32 devices in a mesh: groups: 2 (over y), lat: 4 (over z), lev: 4 (over x, core).
Axes of the slice: x: 2, y: 2, z: 4, core: 2. Of those that a mesh axis runs over, the one named last changes fastest.
Arguments:
- tracers: float32 [8, 8, 144, 1152], P(None, 'lev', ('groups', 'lat')), parts along dimension 2, may hold values from -1 to 8
- wind_x: float32 [8, 144, 1152], P('lev', ('groups', 'lat')), parts along dimension 1, may hold values from -0.9 to 0.9
- wind_y: float32 [8, 144, 1152], P('lev', ('groups', 'lat')), parts along dimension 1, may hold values from -0.9 to 0.9
- level_counts: int32 [4], replicated, may hold values from 1 to 2, 6 in all
- source_level: int32 [6, 144, 1152], P(None, ('groups', 'lat'), 'lev'), parts along dimension 1, may hold values from 0 to 2, as said below
- remap_weight: float32 [4, 6, 144, 1152], P(None, None, ('groups', 'lat'), 'lev'), parts along dimension 2, may hold values from 0.05 to 0.6
Outputs:
- remapped: float32 [8, 6, 144, 1152], P(None, None, ('groups', 'lat'), 'lev'), parts along dimension 2
The draws below stay inside these ranges and needn't reach their ends.
There are 2 independent parts, one for each index of `groups`. The reference program is written for one: setup_inputs(seed, part) draws one part's arguments, and reference() takes and returns one part's arrays. A program takes and returns all parts, laid end to end along the dimension named above; an argument that names none is the same for every part. Nothing has to cross between parts.
Inputs may be any that keep to these rules, and one draw needn't show every extreme that they name: `level_counts`: the counts sum to 6. source_level[k] lies between max(k - 3, 0) and min(k, 2).
All inputs are finite; a program needn't handle non-finite values.
Results may differ from the reference program's by a relative error of at most 0.0003.
Values sent between devices are 32-bit elements; how exact they have to be, the bound alone decides.
No kernel may reach another device: no remote copies, remote signals or barrier semaphores. Data moves between devices by JAX's collectives and lax.ppermute only.
A program may use at most 64 MiB of HBM per device.

```python
import math
import jax
import jax.numpy as jnp
import numpy as np
from jax import lax

NLON = 1152
TRACERS = 8
LEV_DEV = 2
SUBSTEPS = 2
TAPS = 4
NLEV = 6
SLOTS = 8
NLAT = 72
N_LEV = 4


def draw_source_level(key, part):
    key = jax.random.fold_in(key, 7)
    jitter = jax.random.randint(key, (NLEV, NLAT, NLON), -3, 1)
    levels = jnp.arange(NLEV, dtype=jnp.int32)[:, None, None]
    return jnp.clip(levels + jitter, 0, NLEV - TAPS).astype(jnp.int32)


def draw_tracers(key, part):
    key = jax.random.fold_in(key, 11)
    rough_key = jax.random.fold_in(key, 0)
    shape = (TRACERS, SLOTS, NLAT, NLON)
    rough = jnp.clip(jax.random.normal(rough_key, shape, jnp.float32), -4.0, 4.0)
    values = 3.0 + rough
    return values.astype(jnp.float32)


def level_of(key, extent, cuts, least, top_value):
    level, own = 1.0, jax.random.fold_in(key, 6)
    for dim, blocks in cuts:
        draws = jnp.exp(jax.random.uniform(jax.random.fold_in(own, dim), (blocks,), jnp.float32, least / len(cuts), top_value / len(cuts)))
        level = level * jnp.repeat(draws, extent[dim] // blocks).reshape([-1 if axis == dim else 1 for axis in range(len(extent))])
    return level


def split_up(amount, total, most, skew):
    loads = [(1 << 20) // math.isqrt(grade ** skew) + 1 for grade in range(2, amount + 1)]
    rest, given = total - most - (amount - 1), [1] * (amount - 1)
    while rest > 0:
        movable = [i for i in range(amount - 1) if given[i] < most]
        whole, remaining = sum([loads[i] for i in movable]), rest
        for i in movable:
            addition = min(most - given[i], max(1, remaining * loads[i] // whole), rest)
            given[i] = given[i] + addition
            rest = rest - addition
    return np.array([most] + given)


def uneven_parts(rng, count, total, bound, skew):
    if count == 2:
        one = jax.random.randint(rng, (), max(1, total - bound), min(bound, total - 1) + 1)
        return jnp.stack([one, total - one])
    sizes = jnp.asarray(split_up(count, total, bound, skew), jnp.int32)
    twos = (count - 1) // 2
    donor, receiver = sizes[1:1 + 2 * twos:2], sizes[2:2 + 2 * twos:2]
    margin = jnp.minimum(donor - 1, bound - receiver)
    moved = jax.random.randint(jax.random.fold_in(rng, 1), (twos,), 0, 1 << 20) % (margin + 1)
    sizes = sizes.at[1:1 + 2 * twos:2].set(donor - moved).at[2:2 + 2 * twos:2].set(receiver + moved)
    return sizes[jax.random.permutation(jax.random.fold_in(rng, 2), count)]


def setup_inputs(seed: int = 0, part: int = 0) -> dict:
    seeds = jax.random.split(jax.random.key(seed), 7)
    part_splits = jax.random.split(jax.random.fold_in(seeds[6], part), 7)
    tracers = draw_tracers(jax.random.fold_in(jax.random.fold_in(seeds[6], part), 71), part)
    wind_x = jnp.clip(jax.random.uniform(part_splits[1], (SLOTS, NLAT, NLON), jnp.float32, -0.9, 0.9) * level_of(part_splits[1], (SLOTS, NLAT, NLON), ((0, 4), (1, 4)), -0.4, 0.0), -0.9, 0.9)
    wind_y = jnp.clip(jax.random.uniform(part_splits[2], (SLOTS, NLAT, NLON), jnp.float32, -0.9, 0.9) * level_of(part_splits[2], (SLOTS, NLAT, NLON), ((0, 4), (1, 4)), -0.4, 0.0), -0.9, 0.9)
    level_counts = uneven_parts(seeds[3], N_LEV, NLEV, LEV_DEV, 2).astype(jnp.int32)
    source_level = draw_source_level(jax.random.fold_in(jax.random.fold_in(seeds[6], part), 71), part)
    remap_weight = jnp.clip(0.05 + 0.55 * jax.random.uniform(part_splits[5], (TAPS, NLEV, NLAT, NLON), jnp.float32) ** level_of(part_splits[5], (TAPS, NLEV, NLAT, NLON), ((2, 4), (3, 4)), -0.2, 0.2), 0.05, 0.6)
    return {"tracers": tracers, "wind_x": wind_x, "wind_y": wind_y, "level_counts": level_counts, "source_level": source_level, "remap_weight": remap_weight}


def cut(array, start, stop, axis):
    return lax.slice_in_dim(array, start, stop, axis=axis)


def ppm_fluxes(ext, courant, axis):
    cells = ext.shape[axis] - 6
    faces = courant.shape[axis - 1]
    inter = (7.0 / 12.0) * (cut(ext, 1, cells + 4, axis) + cut(ext, 2, cells + 5, axis)) - (1.0 / 12.0) * (cut(ext, 0, cells + 3, axis) + cut(ext, 3, cells + 6, axis))
    left = cut(inter, 0, cells + 2, axis)
    right = cut(inter, 1, cells + 3, axis)
    center = cut(ext, 2, cells + 4, axis)
    slope = right - left
    curve = 6.0 * (center - 0.5 * (left + right))
    speed = courant[None]
    upper = cut(right, 0, faces, axis) - 0.5 * speed * (cut(slope, 0, faces, axis) - (1.0 - speed * (2.0 / 3.0)) * cut(curve, 0, faces, axis))
    lower = cut(left, 1, faces + 1, axis) - 0.5 * speed * (cut(slope, 1, faces + 1, axis) + (1.0 + speed * (2.0 / 3.0)) * cut(curve, 1, faces + 1, axis))
    return speed * jnp.where(speed > 0, upper, lower)


def lat_step(ext, faces):
    flux = ppm_fluxes(ext, faces, 2)
    cells = ext.shape[2] - 6
    return cut(ext, 3, cells + 3, 2) - (cut(flux, 1, cells + 1, 2) - cut(flux, 0, cells, 2))


def lon_step(field, wind):
    ext = jnp.concatenate([field[..., -3:], field, field[..., :3]], axis=3)
    flux = ppm_fluxes(ext, wind, 3)
    return field - (jnp.roll(flux, -1, axis=3) - flux)


def reference(tracers, wind_x, wind_y, level_counts, source_level, remap_weight):
    edge = jnp.zeros_like(wind_y[:, :1])
    faces_y = jnp.concatenate([edge, wind_y[:, 1:], edge], axis=1)
    state = tracers
    for step in range(SUBSTEPS):
        ext = jnp.pad(state, ((0, 0), (0, 0), (3, 3), (0, 0)))
        state = lon_step(lat_step(ext, faces_y), wind_x)
    starts = (jnp.cumsum(level_counts) - level_counts).astype(jnp.int32)
    levels = jnp.arange(NLEV, dtype=jnp.int32)
    owner = (jnp.sum((starts[:, None] <= levels[None]).astype(jnp.int32), axis=0) - 1).astype(jnp.int32)
    table = (owner * LEV_DEV + levels - starts[owner]).astype(jnp.int32)
    remapped = jnp.zeros((TRACERS, NLEV, NLAT, NLON), jnp.float32)
    for tap in range(TAPS):
        index = jnp.take(table, source_level + tap).astype(jnp.int32)
        index = jnp.broadcast_to(index[None], (TRACERS,) + index.shape)
        picked = jnp.take_along_axis(state, index, axis=1)
        remapped = remapped + remap_weight[tap][None] * picked
    return remapped
```

```python
import functools

import jax
import jax.numpy as jnp
from jax import lax
from jax.experimental import pallas as pl
from jax.experimental.pallas import tpu as pltpu
from jax.sharding import PartitionSpec as P

SUBSTEPS = 2
TAPS = 4
REACH = 3
HALO = REACH * SUBSTEPS
BLOCK = 6
LANES = 128
SUB = 8
FACES = 32


def spread(row):
    return jnp.broadcast_to(row, (SUB, LANES))


def lane_ids():
    return lax.broadcasted_iota(jnp.int32, (SUB, LANES), 1)


def from_west(tiles, steps, lane):
    turned = [pltpu.roll(t, steps, 1) for t in tiles]
    return [jnp.where(lane < steps, turned[j - 1], turned[j]) for j in range(len(tiles))]


def from_east(tiles, lane):
    turned = [pltpu.roll(t, LANES - 1, 1) for t in tiles]
    count = len(tiles)
    return [jnp.where(lane == LANES - 1, turned[(j + 1) % count], turned[j]) for j in range(count)]


def coefficients(wind):
    size = jnp.abs(wind)
    rest = 1.0 - size
    alpha = wind * rest * rest * (1.0 / 12.0)
    beta = wind * size * rest * (-1.0 / 12.0)
    gamma = wind * size * (3.0 - 2.0 * size)
    return alpha, beta, gamma


def packed_sizes(nlon, count):
    width = nlon // count
    mains, tail = width // LANES, width % LANES
    per = LANES // tail if tail else 1
    tails = -(-BLOCK // per) if tail else 0
    return width, mains, tail, per, BLOCK * mains + tails


def prep_kernel(rows, tracers, wx, wy, state, down, up):
    levels, nlon = state.shape[0], state.shape[3]
    nj = nlon // LANES
    row_stride = nj * levels
    tracer_stride = rows * row_stride

    def body(row, _):
        for level in range(levels):
            for j in range(nj):
                start = row * row_stride + j * levels + level
                state[level, row, :, j * LANES:(j + 1) * LANES] = tracers[pl.ds(start, SUB, stride=tracer_stride), :]
        return 0

    lax.fori_loop(0, rows, body, 0)
    for level in range(levels):
        for row in range(HALO):
            down[level, row] = state[level, row]
            up[level, row] = state[level, rows - HALO + row]
        for j in range(nj):
            lanes = slice(j * LANES, (j + 1) * LANES)
            at = lambda row: row * row_stride + j * levels + level
            down[level, HALO, 0:REACH, lanes] = wx[pl.ds(at(0), REACH, stride=row_stride), :]
            down[level, HALO, REACH:2 * REACH + 1, lanes] = wy[pl.ds(at(0), REACH + 1, stride=row_stride), :]
            up[level, HALO, 0:REACH, lanes] = wx[pl.ds(at(rows - REACH), REACH, stride=row_stride), :]
            up[level, HALO, REACH:2 * REACH + 1, lanes] = wy[pl.ds(at(rows - REACH - 1), REACH + 1, stride=row_stride), :]


def lat_pass(levels, nj, rows, cell, coef, store):
    def body(i, _):
        level = i // nj
        lanes = pl.ds(pl.multiple_of((i % nj) * LANES, LANES), LANES)
        for first, last in rows:
            a = {r: cell(level, r, lanes) for r in range(first - REACH, last + REACH)}
            inter = {f: 7.0 * (a[f - 1] + a[f]) - (a[f - 2] + a[f + 1]) for f in range(first - 1, last + 2)}
            flux = {}
            for f in range(first, last + 1):
                at = slice(f + REACH, f + REACH + 1)
                alpha, beta, gamma = [spread(coef[i, level, at, lanes]) for i in range(3)]
                north = gamma > 0
                behind = jnp.where(north, inter[f - 1], inter[f + 1])
                upwind = jnp.where(north, a[f - 1], a[f])
                flux[f] = alpha * inter[f] + beta * behind + gamma * upwind
                if f > first:
                    store(level, f - 1, lanes, a[f - 1] - (flux[f] - flux[f - 1]))
        return 0

    lax.fori_loop(0, levels * nj, body, 0)


def lon_row(b, alpha, beta, gamma, lane):
    count = len(b)
    each = range(count)
    west = from_west(b, 1, lane)
    west2 = from_west(b, 2, lane)
    east = from_east(b, lane)
    inter = [7.0 * (west[j] + b[j]) - (west2[j] + east[j]) for j in each]
    inter_w = from_west(inter, 1, lane)
    inter_e = from_east(inter, lane)
    flux = []
    for j in each:
        right = gamma[j] > 0
        behind = jnp.where(right, inter_w[j], inter_e[j])
        upwind = jnp.where(right, west[j], b[j])
        flux.append(alpha[j] * inter[j] + beta[j] * behind + gamma[j] * upwind)
    flux_e = from_east(flux, lane)
    return [b[j] - (flux_e[j] - flux[j]) for j in each]


def lon_block(level, row0, swept, coef, lane):
    nj = swept.shape[3] // LANES
    out = []
    for q in range(BLOCK):
        b = [swept[level, row0 + q, :, j * LANES:(j + 1) * LANES] for j in range(nj)]
        c = [[spread(coef[i, pl.ds((level * nj + j) * FACES + row0 + q, 1), :]) for j in range(nj)] for i in range(3)]
        out.append(lon_row(b, c[0], c[1], c[2], lane))
    return out


def pack_block(block, packed, level, number, count, lane):
    nlon = len(block[0]) * LANES
    width, mains, tail, per, size = packed_sizes(nlon, count)
    for d in range(count):
        j0, off = (d * width) // LANES, (d * width) % LANES
        for q, tiles in enumerate(block):
            turned = [pltpu.roll(tiles[j0 + m], LANES - off, 1) if off else tiles[j0 + m]
                      for m in range(mains + (1 if off else 0))]
            for m in range(mains):
                whole = jnp.where(lane < LANES - off, turned[m], turned[m + 1]) if off else turned[m]
                packed[d, level, number, q * mains + m] = whole
        if tail:
            for g in range(-(-BLOCK // per)):
                total = None
                for place in range(min(per, BLOCK - g * per)):
                    shift = (place * tail - off) % LANES
                    source = block[g * per + place][j0 + mains]
                    moved = pltpu.roll(source, shift, 1) if shift else source
                    total = moved if total is None else jnp.where(lane < place * tail, total, moved)
                packed[d, level, number, BLOCK * mains + g] = total


def transport_kernel(count, rows, state, low, high, wx, wy, packed, winds, cy, cx, swept, first):
    levels, nlon = state.shape[0], state.shape[3]
    nj = nlon // LANES
    row_stride = nj * levels
    lane = lane_ids()
    keep = (lax.axis_index("lat") != 0).astype(jnp.float32)

    for level in range(levels):
        winds[0, level, 0:REACH, :] = low[level, HALO, 0:REACH, :]
        winds[1, level, 0:REACH, :] = low[level, HALO, REACH + 1:2 * REACH + 1, :]
        winds[0, level, rows + REACH:rows + 2 * REACH, :] = high[level, HALO, 0:REACH, :]
        winds[1, level, rows + REACH:rows + 2 * REACH + 1, :] = high[level, HALO, REACH:2 * REACH + 1, :]
        for j in range(nj):
            lanes = slice(j * LANES, (j + 1) * LANES)
            own = pl.ds(j * levels + level, rows, stride=row_stride)
            winds[0, level, REACH:rows + REACH, lanes] = wx[own, :]
            winds[1, level, REACH:rows + REACH, lanes] = wy[own, :]
        winds[1, level, REACH:REACH + 1, :] = winds[1, level, REACH:REACH + 1, :] * keep

    def make(i, _):
        level = i // nj
        lanes = pl.ds(pl.multiple_of((i % nj) * LANES, LANES), LANES)
        parts = coefficients(winds[0, level, :, lanes])
        for p in range(3):
            cx[p, pl.ds(pl.multiple_of(i * FACES, FACES), FACES), :] = parts[p]
        parts = coefficients(winds[1, level, :, lanes])
        for p in range(3):
            cy[p, level, :, lanes] = parts[p]
        return 0

    lax.fori_loop(0, levels * nj, make, 0)

    def cell(level, row, lanes):
        if row < 0:
            return low[level, row + HALO, :, lanes]
        if row >= rows:
            return high[level, row - rows, :, lanes]
        return state[level, row, :, lanes]

    def put(level, row, lanes, value):
        swept[level, row + REACH, :, lanes] = value

    lat_pass(levels, nj, [(-REACH, rows + REACH)], cell, cy, put)
    blocks = (rows + 2 * REACH) // BLOCK

    def step(i, _):
        level, row0 = i // blocks, (i % blocks) * BLOCK
        done = lon_block(level, row0, swept, cx, lane)
        for q in range(BLOCK):
            for j in range(nj):
                first[level, row0 + q, :, j * LANES:(j + 1) * LANES] = done[q][j]
        return 0

    lax.fori_loop(0, levels * blocks, step, 0)

    def cell_first(level, row, lanes):
        return first[level, row + REACH, :, lanes]

    lat_pass(levels, nj, [(0, rows)], cell_first, cy, put)
    finals = rows // BLOCK

    def last(i, _):
        level, number = i // finals, i % finals
        done = lon_block(level, REACH + number * BLOCK, swept, cx, lane)
        pack_block(done, packed, level, number, count, lane)
        return 0

    lax.fori_loop(0, levels * finals, last, 0)


def weights_kernel(weights, source, out):
    targets, rows, taps, width = weights.shape

    for row in range(rows):
        for k in range(targets):
            lowest, highest = max(k - (TAPS - 1), 0), min(k, targets - TAPS)
            w = weights[k, row]
            w = jnp.concatenate([w, jnp.zeros((SUB - taps, width), jnp.float32)], axis=0)
            at = jnp.broadcast_to(source[k, row:row + 1, :], (SUB, width))
            total = w
            for g in range(lowest + 1, highest + 1):
                total = jnp.where(at == g, pltpu.roll(w, g - lowest, 0), total)
            out[k, row] = total


def remap_kernel(count, depth, counts, columns, weights, out):
    targets, rows, _, width = out.shape
    _, mains, tail, per, _ = packed_sizes(width * count, count)
    slots = []
    for level in range(targets):
        slot, start = jnp.int32(level), jnp.int32(0)
        for d in range(count):
            slot = jnp.where(level >= start, d * depth + level - start, slot)
            start = start + counts[d]
        slots.append(slot)

    def body(number, _):
        for q in range(BLOCK):
            row = number * BLOCK + q
            for m in range(mains + (1 if tail else 0)):
                wide = LANES if m < mains else tail
                lanes = slice(m * LANES, m * LANES + wide)
                values = []
                for level in range(targets):
                    if m < mains:
                        values.append(columns[slots[level], number, q * mains + m])
                    else:
                        tile = columns[slots[level], number, BLOCK * mains + q // per]
                        shift = (q % per) * tail
                        tile = pltpu.roll(tile, LANES - shift, 1) if shift else tile
                        values.append(tile[:, :wide])
                for k in range(targets):
                    lowest, highest = max(k - (TAPS - 1), 0), min(k, targets - TAPS) + TAPS - 1
                    total = None
                    for level in range(lowest, highest + 1):
                        j = level - lowest
                        w = jnp.broadcast_to(weights[k, row, j:j + 1, lanes], (SUB, wide))
                        term = w * values[level]
                        total = term if total is None else total + term
                    out[k, row, :, lanes] = total
        return 0

    lax.fori_loop(0, rows // BLOCK, body, 0)


def tiles_of(array):
    lead, levels, nlon = array.shape[:-2], array.shape[-2], array.shape[-1]
    split = array.reshape(lead + (levels, nlon // LANES, LANES))
    return jnp.swapaxes(split, -3, -2).reshape(-1, LANES)


VMEM = pl.BlockSpec(memory_space=pltpu.VMEM)
SMEM = pl.BlockSpec(memory_space=pltpu.SMEM)


def call(kernel, outs, args, specs=None, scratch=(), cost=None):
    return pl.pallas_call(
        kernel,
        out_shape=outs,
        in_specs=specs or [VMEM] * len(args),
        out_specs=jax.tree.map(lambda _: VMEM, outs),
        scratch_shapes=list(scratch),
        compiler_params=pltpu.CompilerParams(vmem_limit_bytes=40 << 20),
        cost_estimate=cost,
    )(*args)


def cost(flops, size):
    return pl.CostEstimate(flops=int(flops), bytes_accessed=int(size), transcendentals=0)


def f32(*shape):
    return jax.ShapeDtypeStruct(shape, jnp.float32)


def shards(tracers, wind_x, wind_y, level_counts, source_level, remap_weight):
    count = lax.axis_size("lev")
    bands = lax.axis_size("lat")
    number, depth, rows, nlon = tracers.shape
    targets, _, width = source_level.shape
    _, mains, tail, per, size = packed_sizes(nlon, count)
    finals = rows // BLOCK

    raw = tiles_of(jnp.transpose(tracers, (0, 2, 1, 3)))
    wx = tiles_of(jnp.transpose(wind_x, (1, 0, 2)))
    wy = tiles_of(jnp.transpose(wind_y, (1, 0, 2)))
    halo = f32(depth, HALO + 1, number, nlon)
    state, down, up = call(
        functools.partial(prep_kernel, rows),
        (f32(depth, rows, number, nlon), halo, halo), (raw, wx, wy),
        cost=cost(1, 8 * tracers.size))
    low = lax.ppermute(up, "lat", [(i, i + 1) for i in range(bands - 1)])
    high = lax.ppermute(down, "lat", [(i + 1, i) for i in range(bands - 1)])
    taps = call(
        weights_kernel, f32(targets, rows, SUB, width),
        (jnp.transpose(remap_weight, (1, 2, 0, 3)), source_level),
        cost=cost(20 * remap_weight.size, 16 * remap_weight.size))
    ext = rows + 2 * REACH
    packed = call(
        functools.partial(transport_kernel, count, rows),
        f32(count, depth, finals, size, SUB, LANES), (state, low, high, wx, wy),
        scratch=[
            pltpu.VMEM((2, depth, FACES, nlon), jnp.float32),
            pltpu.VMEM((3, depth, FACES, nlon), jnp.float32),
            pltpu.VMEM((3, depth * (nlon // LANES) * FACES, LANES), jnp.float32),
            pltpu.VMEM((depth, ext, number, nlon), jnp.float32),
            pltpu.VMEM((depth, ext, number, nlon), jnp.float32),
        ],
        cost=cost(120 * tracers.size, 8 * tracers.size))
    columns = lax.all_to_all(packed, "lev", split_axis=0, concat_axis=0, tiled=True)
    columns = columns.reshape(count * depth, finals, size, SUB, LANES)
    out = call(
        functools.partial(remap_kernel, count, depth),
        f32(targets, rows, number, width), (level_counts, columns, taps),
        specs=[SMEM, VMEM, VMEM],
        cost=cost(60 * remap_weight.size, 16 * remap_weight.size))
    return jnp.transpose(out, (2, 0, 1, 3))


def solution(mesh):
    in_specs = (
        P(None, "lev", ("groups", "lat"), None),
        P("lev", ("groups", "lat"), None),
        P("lev", ("groups", "lat"), None),
        P(),
        P(None, ("groups", "lat"), "lev"),
        P(None, None, ("groups", "lat"), "lev"),
    )
    out_specs = P(None, None, ("groups", "lat"), "lev")
    return jax.shard_map(shards, mesh=mesh, in_specs=in_specs, out_specs=out_specs, check_vma=False)
```

```python
import functools

import jax
import jax.numpy as jnp
from jax import lax
from jax.experimental import pallas as pl
from jax.experimental.layout import Layout, with_layout_constraint
from jax.experimental.pallas import tpu as pltpu
from jax.sharding import PartitionSpec as P

SUBSTEPS = 2
TAPS = 4
REACH = 3
HALO = REACH * SUBSTEPS
BLOCK = 6
LANES = 128
SUB = 8


def spread(row):
    return jnp.broadcast_to(row, (SUB, LANES))


def lane_ids():
    return lax.broadcasted_iota(jnp.int32, (SUB, LANES), 1)


def from_west(tiles, steps, lane):
    turned = [pltpu.roll(t, steps, 1) for t in tiles]
    return [jnp.where(lane < steps, turned[j - 1], turned[j]) for j in range(len(tiles))]


def from_east(tiles, lane):
    turned = [pltpu.roll(t, LANES - 1, 1) for t in tiles]
    count = len(tiles)
    return [jnp.where(lane == LANES - 1, turned[(j + 1) % count], turned[j]) for j in range(count)]


def coefficients(wind):
    size = jnp.abs(wind)
    rest = 1.0 - size
    alpha = wind * rest * rest * (1.0 / 12.0)
    beta = wind * size * rest * (-1.0 / 12.0)
    gamma = wind * size * (3.0 - 2.0 * size)
    return alpha, beta, gamma


def packed_sizes(nlon, count):
    width = nlon // count
    mains, tail = width // LANES, width % LANES
    per = LANES // tail if tail else 1
    tails = -(-BLOCK // per) if tail else 0
    return width, mains, tail, per, BLOCK * mains + tails


def prep_kernel(rows, tracers, wx, wy, state, down, up):
    levels, nlon = state.shape[0], state.shape[3]
    nj = nlon // LANES
    row_stride = nj * levels
    tracer_stride = rows * row_stride

    def body(row, _):
        for level in range(levels):
            for j in range(nj):
                start = row * row_stride + j * levels + level
                state[level, row, :, j * LANES:(j + 1) * LANES] = tracers[pl.ds(start, SUB, stride=tracer_stride), :]
        return 0

    lax.fori_loop(0, rows, body, 0)
    for level in range(levels):
        for row in range(HALO):
            down[level, row] = state[level, row]
            up[level, row] = state[level, rows - HALO + row]
        for j in range(nj):
            lanes = slice(j * LANES, (j + 1) * LANES)
            at = lambda row: row * row_stride + j * levels + level
            down[level, HALO, 0:REACH, lanes] = wx[pl.ds(at(0), REACH, stride=row_stride), :]
            down[level, HALO, REACH:2 * REACH + 1, lanes] = wy[pl.ds(at(0), REACH + 1, stride=row_stride), :]
            up[level, HALO, 0:REACH, lanes] = wx[pl.ds(at(rows - REACH), REACH, stride=row_stride), :]
            up[level, HALO, REACH:2 * REACH + 1, lanes] = wy[pl.ds(at(rows - REACH - 1), REACH + 1, stride=row_stride), :]


def lat_pass(levels, nj, ranges, cell, coef, store):
    def body(i, _):
        level = i // nj
        lanes = pl.ds(pl.multiple_of((i % nj) * LANES, LANES), LANES)
        for first, last in ranges:
            a = {r: cell(level, r, lanes) for r in range(first - REACH, last + REACH)}
            inter = {f: 7.0 * (a[f - 1] + a[f]) - (a[f - 2] + a[f + 1]) for f in range(first - 1, last + 2)}
            flux = {}
            for f in range(first, last + 1):
                alpha, beta, gamma = [spread(coef(i, level, f, lanes)) for i in range(3)]
                north = gamma > 0
                behind = jnp.where(north, inter[f - 1], inter[f + 1])
                upwind = jnp.where(north, a[f - 1], a[f])
                flux[f] = alpha * inter[f] + beta * behind + gamma * upwind
                if f > first:
                    store(level, f - 1, lanes, a[f - 1] - (flux[f] - flux[f - 1]))
        return 0

    lax.fori_loop(0, levels * nj, body, 0)


def tile(j):
    return slice(j * LANES, (j + 1) * LANES)


def lon_block(level, row0, swept, at, coef, inter, west, flux, lane):
    nj = swept.shape[3] // LANES
    each = range(nj)
    out = []
    for q in range(BLOCK):
        b = [swept[level, at + q, :, tile(j)] for j in each]
        w1, w2, e1 = from_west(b, 1, lane), from_west(b, 2, lane), from_east(b, lane)
        for j in each:
            inter[q, :, tile(j)] = 7.0 * (w1[j] + b[j]) - (w2[j] + e1[j])
            west[q, :, tile(j)] = w1[j]
    for q in range(BLOCK):
        mid = [inter[q, :, tile(j)] for j in each]
        w1, e1 = from_west(mid, 1, lane), from_east(mid, lane)
        for j in each:
            alpha, beta, gamma = [spread(coef(i, level, row0 + q, tile(j))) for i in range(3)]
            right = gamma > 0
            behind = jnp.where(right, w1[j], e1[j])
            upwind = jnp.where(right, west[q, :, tile(j)], swept[level, at + q, :, tile(j)])
            flux[q, :, tile(j)] = alpha * mid[j] + beta * behind + gamma * upwind
    for q in range(BLOCK):
        here = [flux[q, :, tile(j)] for j in each]
        e1 = from_east(here, lane)
        out.append([swept[level, at + q, :, tile(j)] - (e1[j] - here[j]) for j in each])
    return out


def pack_block(block, packed, level, number, count, lane):
    nlon = len(block[0]) * LANES
    width, mains, tail, per, size = packed_sizes(nlon, count)
    for d in range(count):
        j0, off = (d * width) // LANES, (d * width) % LANES
        for q, tiles in enumerate(block):
            turned = [pltpu.roll(tiles[j0 + m], LANES - off, 1) if off else tiles[j0 + m]
                      for m in range(mains + (1 if off else 0))]
            for m in range(mains):
                whole = jnp.where(lane < LANES - off, turned[m], turned[m + 1]) if off else turned[m]
                packed[d, level, number, q * mains + m] = whole
        if tail:
            for g in range(-(-BLOCK // per)):
                total = None
                for place in range(min(per, BLOCK - g * per)):
                    shift = (place * tail - off) % LANES
                    source = block[g * per + place][j0 + mains]
                    moved = pltpu.roll(source, shift, 1) if shift else source
                    total = moved if total is None else jnp.where(lane < place * tail, total, moved)
                packed[d, level, number, BLOCK * mains + g] = total


def own_coefficients(rows, wx, wy, cx, cy):
    levels, nlon = cx.shape[1], cx.shape[3]
    nj = nlon // LANES
    keep = jnp.where(lax.axis_index("lat") == 0, 0.0, 1.0)
    south = lax.broadcasted_iota(jnp.int32, (rows, LANES), 0) == 0
    for level in range(levels):
        for j in range(nj):
            own = pl.ds(j * levels + level, rows, stride=nj * levels)
            parts = coefficients(wx[own, :])
            for p in range(3):
                cx[p, level, 0:rows, tile(j)] = parts[p]
            wind = wy[own, :]
            parts = coefficients(jnp.where(south, wind * keep, wind))
            for p in range(3):
                cy[p, level, 0:rows, tile(j)] = parts[p]


def interior_kernel(count, rows, state, wx, wy, packed, first, cx, cy, swept, inter, west, flux):
    levels, nlon = state.shape[0], state.shape[3]
    nj = nlon // LANES
    lane = lane_ids()
    own_coefficients(rows, wx, wy, cx, cy)
    coef_x = lambda i, level, r, lanes: cx[i, level, r:r + 1, lanes]
    coef_y = lambda i, level, f, lanes: cy[i, level, f:f + 1, lanes]

    def put(level, row, lanes, value):
        swept[level, row - REACH, :, lanes] = value

    lat_pass(levels, nj, [(REACH, rows - REACH)], lambda level, r, lanes: state[level, r, :, lanes], coef_y, put)

    def step(level, _):
        for at in range(0, rows - 2 * REACH, BLOCK):
            done = lon_block(level, REACH + at, swept, at, coef_x, inter, west, flux, lane)
            for q in range(BLOCK):
                for j in range(nj):
                    first[level, at + q, :, tile(j)] = done[q][j]
        return 0

    lax.fori_loop(0, levels, step, 0)
    lat_pass(levels, nj, [(HALO, rows - HALO)], lambda level, r, lanes: first[level, r - REACH, :, lanes], coef_y, put)

    def last(level, _):
        for number in range((rows - 2 * HALO) // BLOCK):
            row0 = HALO + number * BLOCK
            done = lon_block(level, row0, swept, row0 - REACH, coef_x, inter, west, flux, lane)
            pack_block(done, packed, level, number, count, lane)
        return 0

    lax.fori_loop(0, levels, last, 0)


def edge_kernel(count, rows, state, low, high, first, cx, cy, packed, near, far, swept, edge, inter, west, flux):
    levels, nlon = state.shape[0], state.shape[3]
    nj = nlon // LANES
    lane = lane_ids()
    for level in range(levels):
        for source, target in ((low, near), (high, far)):
            parts = coefficients(source[level, HALO])
            for p in range(3):
                target[p, level] = parts[p]

    def coef_x(i, level, r, lanes):
        if r < 0:
            return near[i, level, r + REACH:r + REACH + 1, lanes]
        if r >= rows:
            return far[i, level, r - rows:r - rows + 1, lanes]
        return cx[i, level, r:r + 1, lanes]

    def coef_y(i, level, f, lanes):
        if f < 0:
            return near[i, level, f + 2 * REACH + 1:f + 2 * REACH + 2, lanes]
        if f >= rows:
            return far[i, level, f - rows + REACH:f - rows + REACH + 1, lanes]
        return cy[i, level, f:f + 1, lanes]

    def cell(level, r, lanes):
        if r < 0:
            return low[level, r + HALO, :, lanes]
        if r >= rows:
            return high[level, r - rows, :, lanes]
        return state[level, r, :, lanes]

    def cell_first(level, r, lanes):
        if r < REACH:
            return edge[level, r + REACH, :, lanes]
        if r >= rows - REACH:
            return edge[level, r - (rows - REACH) + BLOCK, :, lanes]
        return first[level, r - REACH, :, lanes]

    ends = [(-REACH, REACH), (rows - REACH, rows + REACH)]

    def put(level, row, lanes, value):
        swept[level, row + REACH if row < REACH else row - (rows - REACH) + BLOCK, :, lanes] = value

    lat_pass(levels, nj, ends, cell, coef_y, put)

    def step(level, _):
        for at, (row0, _) in zip((0, BLOCK), ends):
            done = lon_block(level, row0, swept, at, coef_x, inter, west, flux, lane)
            for q in range(BLOCK):
                for j in range(nj):
                    edge[level, at + q, :, tile(j)] = done[q][j]
        return 0

    lax.fori_loop(0, levels, step, 0)
    ends_last = [(0, HALO), (rows - HALO, rows)]

    def put_last(level, row, lanes, value):
        swept[level, row if row < HALO else row - (rows - HALO) + BLOCK, :, lanes] = value

    lat_pass(levels, nj, ends_last, cell_first, coef_y, put_last)

    def last(level, _):
        for number, (row0, _) in enumerate(ends_last):
            done = lon_block(level, row0, swept, number * BLOCK, coef_x, inter, west, flux, lane)
            pack_block(done, packed, level, number, count, lane)
        return 0

    lax.fori_loop(0, levels, last, 0)


def weights_kernel(weights, source, out):
    targets, rows, taps, width = weights.shape

    for row in range(rows):
        for k in range(targets):
            lowest, highest = max(k - (TAPS - 1), 0), min(k, targets - TAPS)
            w = weights[k, row]
            w = jnp.concatenate([w, jnp.zeros((SUB - taps, width), jnp.float32)], axis=0)
            at = jnp.broadcast_to(source[k, row:row + 1, :], (SUB, width))
            total = w
            for g in range(lowest + 1, highest + 1):
                total = jnp.where(at == g, pltpu.roll(w, g - lowest, 0), total)
            out[k, row] = total


def remap_kernel(count, depth, parts, counts, *refs):
    columns, weights, out = refs[:len(parts)], refs[-2], refs[-1]
    targets, rows, _, width = out.shape
    _, mains, tail, per, _ = packed_sizes(width * count, count)
    slots = []
    for level in range(targets):
        slot, start = jnp.int32(level), jnp.int32(0)
        for d in range(count):
            slot = jnp.where(level >= start, d * depth + level - start, slot)
            start = start + counts[d]
        slots.append(slot)

    def block(source, number, row0):
        for q in range(BLOCK):
            row = row0 + q
            for m in range(mains + (1 if tail else 0)):
                wide = LANES if m < mains else tail
                lanes = slice(m * LANES, m * LANES + wide)
                values = []
                for level in range(targets):
                    if m < mains:
                        values.append(source[slots[level], number, q * mains + m])
                    else:
                        last = source[slots[level], number, BLOCK * mains + q // per]
                        shift = (q % per) * tail
                        last = pltpu.roll(last, LANES - shift, 1) if shift else last
                        values.append(last[:, :wide])
                for k in range(targets):
                    lowest, highest = max(k - (TAPS - 1), 0), min(k, targets - TAPS) + TAPS - 1
                    total = None
                    for level in range(lowest, highest + 1):
                        j = level - lowest
                        w = jnp.broadcast_to(weights[k, row, j:j + 1, lanes], (SUB, wide))
                        term = w * values[level]
                        total = term if total is None else total + term
                    out[k, row, :, lanes] = total

    for source, row0s in zip(columns, parts):
        for number, row0 in enumerate(row0s):
            block(source, number, row0)


def tiles_of(array):
    lead, levels, nlon = array.shape[:-2], array.shape[-2], array.shape[-1]
    split = array.reshape(lead + (levels, nlon // LANES, LANES))
    order = tuple(range(len(lead))) + (len(lead) + 1, len(lead), len(lead) + 2)
    split = with_layout_constraint(split, Layout(major_to_minor=order))
    return jnp.swapaxes(split, -3, -2).reshape(-1, LANES)


VMEM = pl.BlockSpec(memory_space=pltpu.VMEM)
SMEM = pl.BlockSpec(memory_space=pltpu.SMEM)


def call(kernel, outs, args, specs=None, scratch=(), cost=None):
    return pl.pallas_call(
        kernel,
        out_shape=outs,
        in_specs=specs or [VMEM] * len(args),
        out_specs=jax.tree.map(lambda _: VMEM, outs),
        scratch_shapes=list(scratch),
        compiler_params=pltpu.CompilerParams(vmem_limit_bytes=40 << 20),
        cost_estimate=cost,
    )(*args)


def cost(flops, size):
    return pl.CostEstimate(flops=int(flops), bytes_accessed=int(size), transcendentals=0)


def f32(*shape):
    return jax.ShapeDtypeStruct(shape, jnp.float32)


def exchanged(packed, slots):
    columns = lax.all_to_all(packed, "lev", split_axis=0, concat_axis=0, tiled=True)
    return columns.reshape((slots,) + packed.shape[2:])


def shards(tracers, wind_x, wind_y, level_counts, source_level, remap_weight):
    count = lax.axis_size("lev")
    bands = lax.axis_size("lat")
    number, depth, rows, nlon = tracers.shape
    targets, _, width = source_level.shape
    _, mains, tail, per, size = packed_sizes(nlon, count)

    raw = tiles_of(jnp.transpose(tracers, (0, 2, 1, 3)))
    wx = tiles_of(jnp.transpose(wind_x, (1, 0, 2)))
    wy = tiles_of(jnp.transpose(wind_y, (1, 0, 2)))
    halo = f32(depth, HALO + 1, number, nlon)
    state, down, up = call(
        functools.partial(prep_kernel, rows),
        (f32(depth, rows, number, nlon), halo, halo), (raw, wx, wy),
        cost=cost(1, 8 * tracers.size))
    low = lax.ppermute(up, "lat", [(i, i + 1) for i in range(bands - 1)])
    high = lax.ppermute(down, "lat", [(i + 1, i) for i in range(bands - 1)])
    taps = call(
        weights_kernel, f32(targets, rows, SUB, width),
        (jnp.transpose(remap_weight, (1, 2, 0, 3)), source_level),
        cost=cost(20 * remap_weight.size, 16 * remap_weight.size))
    swept = pltpu.VMEM((depth, 2 * BLOCK, number, nlon), jnp.float32)
    block = pltpu.VMEM((BLOCK, number, nlon), jnp.float32)
    halo_coef = pltpu.VMEM((3, depth, SUB, nlon), jnp.float32)
    held = -(-rows // SUB) * SUB
    coef = f32(3, depth, held, nlon)
    inner = rows - 2 * HALO
    inner_packed, first, cx, cy = call(
        functools.partial(interior_kernel, count, rows),
        (f32(count, depth, inner // BLOCK, size, SUB, LANES), f32(depth, rows - 2 * REACH, number, nlon), coef, coef),
        (state, wx, wy), scratch=[swept, block, block, block],
        cost=cost(50 * tracers.size, 8 * tracers.size))
    inner_columns = exchanged(inner_packed, count * depth)
    edge_packed = call(
        functools.partial(edge_kernel, count, rows),
        f32(count, depth, 2 * HALO // BLOCK, size, SUB, LANES), (state, low, high, first, cx, cy),
        scratch=[halo_coef, halo_coef, swept, swept, block, block, block],
        cost=cost(60 * tracers.size, 8 * tracers.size))
    edge_columns = exchanged(edge_packed, count * depth)
    parts = (tuple(range(HALO, rows - HALO, BLOCK)), (0, rows - HALO))
    out = call(
        functools.partial(remap_kernel, count, depth, parts),
        f32(targets, rows, number, width), (level_counts, inner_columns, edge_columns, taps),
        specs=[SMEM, VMEM, VMEM, VMEM],
        cost=cost(60 * remap_weight.size, 16 * remap_weight.size))
    return jnp.transpose(out, (2, 0, 1, 3))


def solution(mesh):
    in_specs = (
        P(None, "lev", ("groups", "lat"), None),
        P("lev", ("groups", "lat"), None),
        P("lev", ("groups", "lat"), None),
        P(),
        P(None, ("groups", "lat"), "lev"),
        P(None, None, ("groups", "lat"), "lev"),
    )
    out_specs = P(None, None, ("groups", "lat"), "lev")
    return jax.shard_map(shards, mesh=mesh, in_specs=in_specs, out_specs=out_specs, check_vma=False)
```

```python
import functools

import jax
import jax.numpy as jnp
from jax import lax
from jax.experimental import pallas as pl
from jax.experimental.layout import Layout, with_layout_constraint
from jax.experimental.pallas import tpu as pltpu
from jax.sharding import PartitionSpec as P

SUBSTEPS = 2
TAPS = 4
REACH = 3
HALO = REACH * SUBSTEPS
BLOCK = 6
LANES = 128
SUB = 8


def spread(row):
    return jnp.broadcast_to(row, (SUB, LANES))


def lane_ids():
    return lax.broadcasted_iota(jnp.int32, (SUB, LANES), 1)


def from_west(tiles, steps, lane):
    turned = [pltpu.roll(t, steps, 1) for t in tiles]
    return [jnp.where(lane < steps, turned[j - 1], turned[j]) for j in range(len(tiles))]


def from_east(tiles, lane):
    turned = [pltpu.roll(t, LANES - 1, 1) for t in tiles]
    count = len(tiles)
    return [jnp.where(lane == LANES - 1, turned[(j + 1) % count], turned[j]) for j in range(count)]


def coefficients(wind):
    size = jnp.abs(wind)
    rest = 1.0 - size
    alpha = wind * rest * rest * (1.0 / 12.0)
    beta = wind * size * rest * (-1.0 / 12.0)
    gamma = wind * size * (3.0 - 2.0 * size)
    return alpha, beta, gamma


def packed_sizes(nlon, count):
    width = nlon // count
    mains, tail = width // LANES, width % LANES
    per = LANES // tail if tail else 1
    tails = -(-BLOCK // per) if tail else 0
    return width, mains, tail, per, BLOCK * mains + tails


def prep_kernel(rows, tracers, wind_x, wind_y, state, down, up, wx, wy, raw, sems):
    levels, nlon = state.shape[0], state.shape[3]
    nj = nlon // LANES
    row_stride = nj * levels
    tracer_stride = rows * row_stride
    copies = [pltpu.make_async_copy(source, target, sems.at[i])
              for i, (source, target) in enumerate(((tracers, raw), (wind_x, wx), (wind_y, wy)))]
    for copy in copies:
        copy.start()
    for copy in copies[1:]:
        copy.wait()
    for level in range(levels):
        for target, row_x, row_y in ((down, 0, 0), (up, rows - REACH, rows - REACH - 1)):
            for q in range(REACH):
                target[level, HALO, q:q + 1, :] = wx[row_x + q, level:level + 1, :]
            for q in range(REACH + 1):
                target[level, HALO, REACH + q:REACH + q + 1, :] = wy[row_y + q, level:level + 1, :]
    copies[0].wait()

    def body(row, _):
        for level in range(levels):
            for j in range(nj):
                start = row * row_stride + j * levels + level
                state[level, row, :, tile(j)] = raw[pl.ds(start, SUB, stride=tracer_stride), :]
        return 0

    lax.fori_loop(0, rows, body, 0)
    for level in range(levels):
        for row in range(HALO):
            down[level, row] = state[level, row]
            up[level, row] = state[level, rows - HALO + row]


def lat_pass(levels, nj, ranges, cell, coef, store):
    group = 3 if nj % 3 == 0 else 1

    def body(i, _):
        level = i // (nj // group)
        for u in range(group):
            one(level, pl.ds(pl.multiple_of(((i % (nj // group)) * group + u) * LANES, LANES), LANES))
        return 0

    def one(level, lanes):
        for first, last in ranges:
            a = {r: cell(level, r, lanes) for r in range(first - REACH, last + REACH)}
            inter = {f: 7.0 * (a[f - 1] + a[f]) - (a[f - 2] + a[f + 1]) for f in range(first - 1, last + 2)}
            flux = {}
            for f in range(first, last + 1):
                alpha, beta, gamma = [spread(coef(i, level, f, lanes)) for i in range(3)]
                north = gamma > 0
                behind = jnp.where(north, inter[f - 1], inter[f + 1])
                upwind = jnp.where(north, a[f - 1], a[f])
                flux[f] = alpha * inter[f] + beta * behind + gamma * upwind
                if f > first:
                    store(level, f - 1, lanes, a[f - 1] - (flux[f] - flux[f - 1]))

    lax.fori_loop(0, levels * nj // group, body, 0)


def tile(j):
    return slice(j * LANES, (j + 1) * LANES)


def lon_pass(work, swept, coef, inter, west, flux, lane, finish):
    nj = swept.shape[3] // LANES
    each = range(nj)

    def interfaces(n):
        level, _, at = work[n]
        b = [swept[level, at, :, tile(j)] for j in each]
        w1, w2, e1 = from_west(b, 1, lane), from_west(b, 2, lane), from_east(b, lane)
        for j in each:
            inter[n, :, tile(j)] = 7.0 * (w1[j] + b[j]) - (w2[j] + e1[j])
            west[n, :, tile(j)] = w1[j]

    def fluxes(n):
        level, row, at = work[n]
        mid = [inter[n, :, tile(j)] for j in each]
        w1, e1 = from_west(mid, 1, lane), from_east(mid, lane)
        for j in each:
            alpha, beta, gamma = [spread(coef(i, level, row, tile(j))) for i in range(3)]
            right = gamma > 0
            behind = jnp.where(right, w1[j], e1[j])
            upwind = jnp.where(right, west[n, :, tile(j)], swept[level, at, :, tile(j)])
            flux[n, :, tile(j)] = alpha * mid[j] + beta * behind + gamma * upwind

    def update(n):
        level, _, at = work[n]
        here = [flux[n, :, tile(j)] for j in each]
        e1 = from_east(here, lane)
        return [swept[level, at, :, tile(j)] - (e1[j] - here[j]) for j in each]

    groups = len(work) // BLOCK
    for g in range(groups + 2):
        if g < groups:
            for q in range(BLOCK):
                interfaces(g * BLOCK + q)
        if 1 <= g <= groups:
            for q in range(BLOCK):
                fluxes((g - 1) * BLOCK + q)
        if g >= 2:
            finish(g - 2, [update((g - 2) * BLOCK + q) for q in range(BLOCK)])


def pack_block(block, packed, level, number, count, lane):
    nlon = len(block[0]) * LANES
    width, mains, tail, per, size = packed_sizes(nlon, count)
    for d in range(count):
        j0, off = (d * width) // LANES, (d * width) % LANES
        for q, tiles in enumerate(block):
            turned = [pltpu.roll(tiles[j0 + m], LANES - off, 1) if off else tiles[j0 + m]
                      for m in range(mains + (1 if off else 0))]
            for m in range(mains):
                whole = jnp.where(lane < LANES - off, turned[m], turned[m + 1]) if off else turned[m]
                packed[d, level, number, q * mains + m] = whole
        if tail:
            for g in range(-(-BLOCK // per)):
                total = None
                for place in range(min(per, BLOCK - g * per)):
                    shift = (place * tail - off) % LANES
                    source = block[g * per + place][j0 + mains]
                    moved = pltpu.roll(source, shift, 1) if shift else source
                    total = moved if total is None else jnp.where(lane < place * tail, total, moved)
                packed[d, level, number, BLOCK * mains + g] = total


def own_coefficients(rows, wx, wy, winds, cx, cy):
    levels, held, nlon = cx.shape[1:]
    keep = jnp.where(lax.axis_index("lat") == 0, 0.0, 1.0)
    for level in range(levels):
        for way, source in enumerate((wx, wy)):
            for row in range(rows):
                winds[way, level, row:row + 1, :] = source[row, level:level + 1, :]
        winds[1, level, 0:1, :] = winds[1, level, 0:1, :] * keep
        for way, target in enumerate((cx, cy)):
            for j in range(nlon // LANES):
                parts = coefficients(winds[way, level, :, tile(j)])
                for p in range(3):
                    target[p, level, :, tile(j)] = parts[p]


def put_rows(target, level, at, rows):
    for q, row in enumerate(rows):
        for j, part in enumerate(row):
            target[level, at + q, :, tile(j)] = part


def interior_kernel(count, rows, state, wx, wy, packed, first, cx, cy, winds, swept, inter, west, flux):
    levels, nlon = state.shape[0], state.shape[3]
    nj = nlon // LANES
    lane = lane_ids()
    own_coefficients(rows, wx, wy, winds, cx, cy)
    coef_x = lambda i, level, r, lanes: cx[i, level, r:r + 1, lanes]
    coef_y = lambda i, level, f, lanes: cy[i, level, f:f + 1, lanes]

    def put(level, row, lanes, value):
        swept[level, row - REACH, :, lanes] = value

    lat_pass(levels, nj, [(REACH, rows - REACH)], lambda level, r, lanes: state[level, r, :, lanes], coef_y, put)
    work = [(level, row, row - REACH) for level in range(levels) for row in range(REACH, rows - REACH)]

    def keep_first(group, done):
        level, _, at = work[group * BLOCK]
        put_rows(first, level, at, done)

    lon_pass(work, swept, coef_x, inter, west, flux, lane, keep_first)
    lat_pass(levels, nj, [(HALO, rows - HALO)], lambda level, r, lanes: first[level, r - REACH, :, lanes], coef_y, put)
    work_last = [(level, row, row - REACH) for level in range(levels) for row in range(HALO, rows - HALO)]

    def send(group, done):
        level, row, _ = work_last[group * BLOCK]
        pack_block(done, packed, level, (row - HALO) // BLOCK, count, lane)

    lon_pass(work_last, swept, coef_x, inter, west, flux, lane, send)


def edge_kernel(count, rows, state, low, high, first, cx, cy, packed, near, far, swept, edge, inter, west, flux):
    levels, nlon = state.shape[0], state.shape[3]
    nj = nlon // LANES
    lane = lane_ids()
    for level in range(levels):
        for source, target in ((low, near), (high, far)):
            for j in range(nj):
                parts = coefficients(source[level, HALO, :, tile(j)])
                for p in range(3):
                    target[p, level, :, tile(j)] = parts[p]

    def coef_x(i, level, r, lanes):
        if r < 0:
            return near[i, level, r + REACH:r + REACH + 1, lanes]
        if r >= rows:
            return far[i, level, r - rows:r - rows + 1, lanes]
        return cx[i, level, r:r + 1, lanes]

    def coef_y(i, level, f, lanes):
        if f < 0:
            return near[i, level, f + 2 * REACH + 1:f + 2 * REACH + 2, lanes]
        if f >= rows:
            return far[i, level, f - rows + REACH:f - rows + REACH + 1, lanes]
        return cy[i, level, f:f + 1, lanes]

    def cell(level, r, lanes):
        if r < 0:
            return low[level, r + HALO, :, lanes]
        if r >= rows:
            return high[level, r - rows, :, lanes]
        return state[level, r, :, lanes]

    def cell_first(level, r, lanes):
        if r < REACH:
            return edge[level, r + REACH, :, lanes]
        if r >= rows - REACH:
            return edge[level, r - (rows - REACH) + BLOCK, :, lanes]
        return first[level, r - REACH, :, lanes]

    ends = [(-REACH, REACH), (rows - REACH, rows + REACH)]
    ends_last = [(0, HALO), (rows - HALO, rows)]

    def place(row, ranges):
        (a, b), (c, _) = ranges
        return row - a if row < b else row - c + BLOCK

    def put(level, row, lanes, value):
        swept[level, place(row, ends), :, lanes] = value

    def put_last(level, row, lanes, value):
        swept[level, place(row, ends_last), :, lanes] = value

    def listed(ranges):
        return [(level, row, place(row, ranges)) for level in range(levels) for a, b in ranges for row in range(a, b)]

    lat_pass(levels, nj, ends, cell, coef_y, put)
    work, work_last = listed(ends), listed(ends_last)

    def keep_edge(group, done):
        level, _, at = work[group * BLOCK]
        put_rows(edge, level, at, done)

    def send(group, done):
        level, _, at = work_last[group * BLOCK]
        pack_block(done, packed, level, at // BLOCK, count, lane)

    lon_pass(work, swept, coef_x, inter, west, flux, lane, keep_edge)
    lat_pass(levels, nj, ends_last, cell_first, coef_y, put_last)
    lon_pass(work_last, swept, coef_x, inter, west, flux, lane, send)


def weights_kernel(weights, source, out):
    targets, rows, taps, width = weights.shape

    for row in range(rows):
        for k in range(targets):
            lowest, highest = max(k - (TAPS - 1), 0), min(k, targets - TAPS)
            w = weights[k, row]
            w = jnp.concatenate([w, jnp.zeros((SUB - taps, width), jnp.float32)], axis=0)
            at = jnp.broadcast_to(source[k, row:row + 1, :], (SUB, width))
            total = w
            for g in range(lowest + 1, highest + 1):
                total = jnp.where(at == g, pltpu.roll(w, g - lowest, 0), total)
            out[k, row] = total


def remap_kernel(count, depth, parts, counts, *refs):
    columns, weights, out = refs[:len(parts)], refs[-2], refs[-1]
    targets, rows, _, width = out.shape
    _, mains, tail, per, _ = packed_sizes(width * count, count)
    slots = []
    for level in range(targets):
        slot, start = jnp.int32(level), jnp.int32(0)
        for d in range(count):
            slot = jnp.where(level >= start, d * depth + level - start, slot)
            start = start + counts[d]
        slots.append(slot)

    def block(source, number, row0):
        for q in range(BLOCK):
            row = row0 + q
            for m in range(mains + (1 if tail else 0)):
                wide = LANES if m < mains else tail
                lanes = slice(m * LANES, m * LANES + wide)
                values = []
                for level in range(targets):
                    if m < mains:
                        values.append(source[slots[level], number, q * mains + m])
                    else:
                        last = source[slots[level], number, BLOCK * mains + q // per]
                        shift = (q % per) * tail
                        last = pltpu.roll(last, LANES - shift, 1) if shift else last
                        values.append(last[:, :wide])
                for k in range(targets):
                    lowest, highest = max(k - (TAPS - 1), 0), min(k, targets - TAPS) + TAPS - 1
                    total = None
                    for level in range(lowest, highest + 1):
                        j = level - lowest
                        w = jnp.broadcast_to(weights[k, row, j:j + 1, lanes], (SUB, wide))
                        term = w * values[level]
                        total = term if total is None else total + term
                    out[k, row, :, lanes] = total

    for source, row0s in zip(columns, parts):
        for number, row0 in enumerate(row0s):
            block(source, number, row0)


def tiles_of(array):
    lead, levels, nlon = array.shape[:-2], array.shape[-2], array.shape[-1]
    split = array.reshape(lead + (levels, nlon // LANES, LANES))
    order = tuple(range(len(lead))) + (len(lead) + 1, len(lead), len(lead) + 2)
    split = with_layout_constraint(split, Layout(major_to_minor=order))
    return jnp.swapaxes(split, -3, -2).reshape(-1, LANES)


VMEM = pl.BlockSpec(memory_space=pltpu.VMEM)
HBM = pl.BlockSpec(memory_space=pltpu.HBM)
SMEM = pl.BlockSpec(memory_space=pltpu.SMEM)


def call(kernel, outs, args, specs=None, scratch=(), cost=None):
    return pl.pallas_call(
        kernel,
        out_shape=outs,
        in_specs=specs or [VMEM] * len(args),
        out_specs=jax.tree.map(lambda _: VMEM, outs),
        scratch_shapes=list(scratch),
        compiler_params=pltpu.CompilerParams(vmem_limit_bytes=16 << 20),
        cost_estimate=cost,
    )(*args)


def cost(flops, size):
    return pl.CostEstimate(flops=int(flops), bytes_accessed=int(size), transcendentals=0)


def f32(*shape):
    return jax.ShapeDtypeStruct(shape, jnp.float32)


def exchanged(packed, slots):
    columns = lax.all_to_all(packed, "lev", split_axis=0, concat_axis=0, tiled=True)
    return columns.reshape((slots,) + packed.shape[2:])


def shards(tracers, wind_x, wind_y, level_counts, source_level, remap_weight):
    count = lax.axis_size("lev")
    bands = lax.axis_size("lat")
    number, depth, rows, nlon = tracers.shape
    targets, _, width = source_level.shape
    _, mains, tail, per, size = packed_sizes(nlon, count)

    raw = tiles_of(jnp.transpose(tracers, (0, 2, 1, 3)))
    wind = f32(rows, depth, nlon)
    halo = f32(depth, HALO + 1, number, nlon)
    state, down, up, wx, wy = call(
        functools.partial(prep_kernel, rows),
        (f32(depth, rows, number, nlon), halo, halo, wind, wind),
        (raw, jnp.transpose(wind_x, (1, 0, 2)), jnp.transpose(wind_y, (1, 0, 2))),
        specs=[HBM, HBM, HBM],
        scratch=[pltpu.VMEM(raw.shape, jnp.float32), pltpu.SemaphoreType.DMA((3,))],
        cost=cost(1, 8 * tracers.size))
    low = lax.ppermute(up, "lat", [(i, i + 1) for i in range(bands - 1)])
    high = lax.ppermute(down, "lat", [(i + 1, i) for i in range(bands - 1)])
    taps = call(
        weights_kernel, f32(targets, rows, SUB, width),
        (jnp.transpose(remap_weight, (1, 2, 0, 3)), source_level),
        cost=cost(20 * remap_weight.size, 16 * remap_weight.size))
    swept = pltpu.VMEM((depth, 2 * BLOCK, number, nlon), jnp.float32)
    stage = pltpu.VMEM((2 * BLOCK * depth, number, nlon), jnp.float32)
    halo_coef = pltpu.VMEM((3, depth, SUB, nlon), jnp.float32)
    held = -(-rows // SUB) * SUB
    coef = f32(3, depth, held, nlon)
    inner = rows - 2 * HALO
    inner_packed, first, cx, cy = call(
        functools.partial(interior_kernel, count, rows),
        (f32(count, depth, inner // BLOCK, size, SUB, LANES), f32(depth, rows - 2 * REACH, number, nlon), coef, coef),
        (state, wx, wy), scratch=[pltpu.VMEM((2, depth, held, nlon), jnp.float32), swept, stage, stage, stage],
        cost=cost(50 * tracers.size, 8 * tracers.size))
    inner_columns = exchanged(inner_packed, count * depth)
    edge_packed = call(
        functools.partial(edge_kernel, count, rows),
        f32(count, depth, 2 * HALO // BLOCK, size, SUB, LANES), (state, low, high, first, cx, cy),
        scratch=[halo_coef, halo_coef, swept, swept, stage, stage, stage],
        cost=cost(60 * tracers.size, 8 * tracers.size))
    edge_columns = exchanged(edge_packed, count * depth)
    parts = (tuple(range(HALO, rows - HALO, BLOCK)), (0, rows - HALO))
    out = call(
        functools.partial(remap_kernel, count, depth, parts),
        f32(targets, rows, number, width), (level_counts, inner_columns, edge_columns, taps),
        specs=[SMEM, VMEM, VMEM, VMEM],
        cost=cost(60 * remap_weight.size, 16 * remap_weight.size))
    return jnp.transpose(out, (2, 0, 1, 3))


def solution(mesh):
    in_specs = (
        P(None, "lev", ("groups", "lat"), None),
        P("lev", ("groups", "lat"), None),
        P("lev", ("groups", "lat"), None),
        P(),
        P(None, ("groups", "lat"), "lev"),
        P(None, None, ("groups", "lat"), "lev"),
    )
    out_specs = P(None, None, ("groups", "lat"), "lev")
    return jax.shard_map(shards, mesh=mesh, in_specs=in_specs, out_specs=out_specs, check_vma=False)
```

```python
import functools

import jax
import jax.numpy as jnp
from jax import lax
from jax.experimental import pallas as pl
from jax.experimental.layout import Layout, with_layout_constraint
from jax.experimental.pallas import tpu as pltpu
from jax.sharding import PartitionSpec as P

SUBSTEPS = 2
TAPS = 4
REACH = 3
HALO = REACH * SUBSTEPS
BLOCK = 6
LANES = 128
SUB = 8


def spread(row):
    return jnp.broadcast_to(row, (SUB, LANES))


def lane_ids():
    return lax.broadcasted_iota(jnp.int32, (SUB, LANES), 1)


def from_west(tiles, steps, lane):
    turned = [pltpu.roll(t, steps, 1) for t in tiles]
    return [jnp.where(lane < steps, turned[j - 1], turned[j]) for j in range(len(tiles))]


def from_east(tiles, lane):
    turned = [pltpu.roll(t, LANES - 1, 1) for t in tiles]
    count = len(tiles)
    return [jnp.where(lane == LANES - 1, turned[(j + 1) % count], turned[j]) for j in range(count)]


def coefficients(wind):
    size = jnp.abs(wind)
    rest = 1.0 - size
    alpha = wind * rest * rest * (1.0 / 12.0)
    beta = wind * size * rest * (-1.0 / 12.0)
    gamma = wind * size * (3.0 - 2.0 * size)
    return alpha, beta, gamma


def packed_sizes(nlon, count):
    width = nlon // count
    mains, tail = width // LANES, width % LANES
    per = LANES // tail if tail else 1
    tails = -(-BLOCK // per) if tail else 0
    return width, mains, tail, per, BLOCK * mains + tails


def prep_kernel(rows, tracers, winds, state, down, up):
    levels, nlon = state.shape[0], state.shape[3]
    nj = nlon // LANES
    row_stride = nj * levels
    tracer_stride = rows * row_stride

    def body(row, _):
        for level in range(levels):
            for j in range(nj):
                start = row * row_stride + j * levels + level
                state[level, row, :, tile(j)] = tracers[pl.ds(start, SUB, stride=tracer_stride), :]
        return 0

    lax.fori_loop(0, rows, body, 0)
    for level in range(levels):
        for row in range(HALO):
            down[level, row] = state[level, row]
            up[level, row] = state[level, rows - HALO + row]
        for target, row_x, row_y in ((down, 0, 0), (up, rows - REACH, rows - REACH - 1)):
            for q in range(REACH):
                target[level, HALO, q:q + 1, :] = winds[row_x + q, level:level + 1, :]
            for q in range(REACH + 1):
                target[level, HALO, REACH + q:REACH + q + 1, :] = winds[rows + row_y + q, level:level + 1, :]


def lat_pass(levels, nj, ranges, cell, coef, store):
    group = 3 if nj % 3 == 0 else 1

    def body(i, _):
        level = i // (nj // group)
        for u in range(group):
            one(level, pl.ds(pl.multiple_of(((i % (nj // group)) * group + u) * LANES, LANES), LANES))
        return 0

    def one(level, lanes):
        for first, last in ranges:
            a = {r: cell(level, r, lanes) for r in range(first - REACH, last + REACH)}
            inter = {f: 7.0 * (a[f - 1] + a[f]) - (a[f - 2] + a[f + 1]) for f in range(first - 1, last + 2)}
            flux = {}
            for f in range(first, last + 1):
                alpha, beta, gamma = [spread(coef(i, level, f, lanes)) for i in range(3)]
                north = gamma > 0
                behind = jnp.where(north, inter[f - 1], inter[f + 1])
                upwind = jnp.where(north, a[f - 1], a[f])
                flux[f] = alpha * inter[f] + beta * behind + gamma * upwind
                if f > first:
                    store(level, f - 1, lanes, a[f - 1] - (flux[f] - flux[f - 1]))

    lax.fori_loop(0, levels * nj // group, body, 0)


def tile(j):
    return slice(j * LANES, (j + 1) * LANES)


def lon_pass(work, swept, coef, inter, west, flux, lane, finish):
    nj = swept.shape[3] // LANES
    each = range(nj)

    def interfaces(n):
        level, _, at = work[n]
        b = [swept[level, at, :, tile(j)] for j in each]
        w1, w2, e1 = from_west(b, 1, lane), from_west(b, 2, lane), from_east(b, lane)
        for j in each:
            inter[n, :, tile(j)] = 7.0 * (w1[j] + b[j]) - (w2[j] + e1[j])
            west[n, :, tile(j)] = w1[j]

    def fluxes(n):
        level, row, at = work[n]
        mid = [inter[n, :, tile(j)] for j in each]
        w1, e1 = from_west(mid, 1, lane), from_east(mid, lane)
        for j in each:
            alpha, beta, gamma = [spread(coef(i, level, row, tile(j))) for i in range(3)]
            right = gamma > 0
            behind = jnp.where(right, w1[j], e1[j])
            upwind = jnp.where(right, west[n, :, tile(j)], swept[level, at, :, tile(j)])
            flux[n, :, tile(j)] = alpha * mid[j] + beta * behind + gamma * upwind

    def update(n):
        level, _, at = work[n]
        here = [flux[n, :, tile(j)] for j in each]
        e1 = from_east(here, lane)
        return [swept[level, at, :, tile(j)] - (e1[j] - here[j]) for j in each]

    groups = len(work) // BLOCK
    for g in range(groups + 2):
        if g < groups:
            for q in range(BLOCK):
                interfaces(g * BLOCK + q)
        if 1 <= g <= groups:
            for q in range(BLOCK):
                fluxes((g - 1) * BLOCK + q)
        if g >= 2:
            finish(g - 2, [update((g - 2) * BLOCK + q) for q in range(BLOCK)])


def pack_block(block, packed, level, number, count, lane):
    me = lax.axis_index("lev")
    nlon = len(block[0]) * LANES
    width, mains, tail, per, size = packed_sizes(nlon, count)
    for d in range(count):
        j0, off = (d * width) // LANES, (d * width) % LANES
        for q, tiles in enumerate(block):
            turned = [pltpu.roll(tiles[j0 + m], LANES - off, 1) if off else tiles[j0 + m]
                      for m in range(mains + (1 if off else 0))]
            for m in range(mains):
                whole = jnp.where(lane < LANES - off, turned[m], turned[m + 1]) if off else turned[m]
                packed[d ^ me, level, number, q * mains + m] = whole
        if tail:
            for g in range(-(-BLOCK // per)):
                total = None
                for place in range(min(per, BLOCK - g * per)):
                    shift = (place * tail - off) % LANES
                    source = block[g * per + place][j0 + mains]
                    moved = pltpu.roll(source, shift, 1) if shift else source
                    total = moved if total is None else jnp.where(lane < place * tail, total, moved)
                packed[d ^ me, level, number, BLOCK * mains + g] = total


def copy_blocks(source, target, start=0):
    levels, blocks, size = source.shape[:3]
    for level in range(levels):
        for number in range(blocks):
            for i in range(size):
                target[level, start + number, i] = source[level, number, i]


def own_coefficients(rows, joined, winds, cx, cy):
    levels, held, nlon = cx.shape[1:]
    keep = jnp.where(lax.axis_index("lat") == 0, 0.0, 1.0)
    for level in range(levels):
        for way in range(2):
            for row in range(rows):
                winds[way, level, row:row + 1, :] = joined[way * rows + row, level:level + 1, :]
        winds[1, level, 0:1, :] = winds[1, level, 0:1, :] * keep
        for way, target in enumerate((cx, cy)):
            for j in range(nlon // LANES):
                parts = coefficients(winds[way, level, :, tile(j)])
                for p in range(3):
                    target[p, level, :, tile(j)] = parts[p]


def put_rows(target, level, at, rows):
    for q, row in enumerate(rows):
        for j, part in enumerate(row):
            target[level, at + q, :, tile(j)] = part


def interior_kernel(count, rows, state, joined, *refs):
    outs, (first, cx, cy, packed, winds, swept, inter, west, flux) = refs[:count], refs[count:]
    levels, nlon = state.shape[0], state.shape[3]
    nj = nlon // LANES
    lane = lane_ids()
    own_coefficients(rows, joined, winds, cx, cy)
    coef_x = lambda i, level, r, lanes: cx[i, level, r:r + 1, lanes]
    coef_y = lambda i, level, f, lanes: cy[i, level, f:f + 1, lanes]

    def put(level, row, lanes, value):
        swept[level, row - REACH, :, lanes] = value

    lat_pass(levels, nj, [(REACH, rows - REACH)], lambda level, r, lanes: state[level, r, :, lanes], coef_y, put)
    work = [(level, row, row - REACH) for level in range(levels) for row in range(REACH, rows - REACH)]

    def keep_first(group, done):
        level, _, at = work[group * BLOCK]
        put_rows(first, level, at, done)

    lon_pass(work, swept, coef_x, inter, west, flux, lane, keep_first)
    lat_pass(levels, nj, [(HALO, rows - HALO)], lambda level, r, lanes: first[level, r - REACH, :, lanes], coef_y, put)
    work_last = [(level, row, row - REACH) for level in range(levels) for row in range(HALO, rows - HALO)]

    def send(group, done):
        level, row, _ = work_last[group * BLOCK]
        pack_block(done, packed, level, (row - HALO) // BLOCK, count, lane)

    lon_pass(work_last, swept, coef_x, inter, west, flux, lane, send)
    for k in range(count):
        copy_blocks(packed.at[k], outs[k])


def edge_kernel(count, rows, south, state, halo, first, cx, cy, *refs):
    others = () if south else refs[:2]
    outs, (packed, beyond, swept, edge, inter, west, flux) = refs[len(others):len(others) + count], refs[len(others) + count:]
    levels, nlon = state.shape[0], state.shape[3]
    nj = nlon // LANES
    lane = lane_ids()
    for level in range(levels):
        for j in range(nj):
            parts = coefficients(halo[level, HALO, :, tile(j)])
            for p in range(3):
                beyond[p, level, :, tile(j)] = parts[p]

    def coef_x(i, level, r, lanes):
        if 0 <= r < rows:
            return cx[i, level, r:r + 1, lanes]
        at = r + REACH if south else r - rows
        return beyond[i, level, at:at + 1, lanes]

    def coef_y(i, level, f, lanes):
        if 0 <= f < rows:
            return cy[i, level, f:f + 1, lanes]
        at = f + 2 * REACH + 1 if south else f - rows + REACH
        return beyond[i, level, at:at + 1, lanes]

    def cell(level, r, lanes):
        if 0 <= r < rows:
            return state[level, r, :, lanes]
        return halo[level, r + HALO if south else r - rows, :, lanes]

    base = -REACH if south else rows - REACH
    base_last = 0 if south else rows - HALO

    def cell_first(level, r, lanes):
        if REACH <= r < rows - REACH:
            return first[level, r - REACH, :, lanes]
        return edge[level, r - base, :, lanes]

    def put(level, row, lanes, value):
        swept[level, row - base, :, lanes] = value

    def put_last(level, row, lanes, value):
        swept[level, row - base_last, :, lanes] = value

    def listed(start):
        return [(level, start + q, q) for level in range(levels) for q in range(BLOCK)]

    def keep_edge(group, done):
        put_rows(edge, group, 0, done)

    def send(group, done):
        pack_block(done, packed, group, 0, count, lane)

    lat_pass(levels, nj, [(base, base + BLOCK)], cell, coef_y, put)
    lon_pass(listed(base), swept, coef_x, inter, west, flux, lane, keep_edge)
    lat_pass(levels, nj, [(base_last, base_last + BLOCK)], cell_first, coef_y, put_last)
    lon_pass(listed(base_last), swept, coef_x, inter, west, flux, lane, send)
    for k in range(count):
        start = 0
        for other in others if k == 1 else ():
            copy_blocks(other, outs[k], start)
            start += other.shape[1]
        copy_blocks(packed.at[k], outs[k], start)


def weights_kernel(weights, source, out):
    targets, rows, taps, width = weights.shape

    for row in range(rows):
        for k in range(targets):
            lowest, highest = max(k - (TAPS - 1), 0), min(k, targets - TAPS)
            w = weights[k, row]
            w = jnp.concatenate([w, jnp.zeros((SUB - taps, width), jnp.float32)], axis=0)
            at = jnp.broadcast_to(source[k, row:row + 1, :], (SUB, width))
            total = w
            for g in range(lowest + 1, highest + 1):
                total = jnp.where(at == g, pltpu.roll(w, g - lowest, 0), total)
            out[k, row] = total


def remap_kernel(count, depth, plan, counts, *refs):
    chunks, (weights, out, columns) = refs[:len(plan)], refs[len(plan):]
    me = lax.axis_index("lev")
    for (k, start), chunk in zip(plan, chunks):
        copy_blocks(chunk, columns.at[pl.ds((me ^ k) * depth, depth)], start)
    targets, rows, _, width = out.shape
    _, mains, tail, per, _ = packed_sizes(width * count, count)
    slots = []
    for level in range(targets):
        slot, start = jnp.int32(level), jnp.int32(0)
        for d in range(count):
            slot = jnp.where(level >= start, d * depth + level - start, slot)
            start = start + counts[d]
        slots.append(slot)

    def block(number):
        for q in range(BLOCK):
            row = number * BLOCK + q
            for m in range(mains + (1 if tail else 0)):
                wide = LANES if m < mains else tail
                lanes = slice(m * LANES, m * LANES + wide)
                values = []
                for level in range(targets):
                    if m < mains:
                        values.append(columns[slots[level], number, q * mains + m])
                    else:
                        last = columns[slots[level], number, BLOCK * mains + q // per]
                        shift = (q % per) * tail
                        last = pltpu.roll(last, LANES - shift, 1) if shift else last
                        values.append(last[:, :wide])
                for k in range(targets):
                    lowest, highest = max(k - (TAPS - 1), 0), min(k, targets - TAPS) + TAPS - 1
                    total = None
                    for level in range(lowest, highest + 1):
                        j = level - lowest
                        w = jnp.broadcast_to(weights[k, row, j:j + 1, lanes], (SUB, wide))
                        term = w * values[level]
                        total = term if total is None else total + term
                    out[k, row, :, lanes] = total

    for number in range(rows // BLOCK):
        block(number)


def tiles_of(array):
    lead, levels, nlon = array.shape[:-2], array.shape[-2], array.shape[-1]
    split = array.reshape(lead + (levels, nlon // LANES, LANES))
    order = tuple(range(len(lead))) + (len(lead) + 1, len(lead), len(lead) + 2)
    split = with_layout_constraint(split, Layout(major_to_minor=order))
    return jnp.swapaxes(split, -3, -2).reshape(-1, LANES)


VMEM = pl.BlockSpec(memory_space=pltpu.VMEM)
SMEM = pl.BlockSpec(memory_space=pltpu.SMEM)


def call(kernel, outs, args, specs=None, scratch=(), cost=None):
    return pl.pallas_call(
        kernel,
        out_shape=outs,
        in_specs=specs or [VMEM] * len(args),
        out_specs=jax.tree.map(lambda _: VMEM, outs),
        scratch_shapes=list(scratch),
        compiler_params=pltpu.CompilerParams(vmem_limit_bytes=16 << 20),
        cost_estimate=cost,
    )(*args)


def cost(flops, size):
    return pl.CostEstimate(flops=int(flops), bytes_accessed=int(size), transcendentals=0)


def f32(*shape):
    return jax.ShapeDtypeStruct(shape, jnp.float32)


def swapped(value, k):
    count = lax.axis_size("lev")
    return lax.ppermute(value, "lev", [(i, i ^ k) for i in range(count)])


def shards(tracers, wind_x, wind_y, level_counts, source_level, remap_weight):
    count = lax.axis_size("lev")
    bands = lax.axis_size("lat")
    number, depth, rows, nlon = tracers.shape
    targets, _, width = source_level.shape
    size = packed_sizes(nlon, count)[-1]
    blocks = rows // BLOCK
    inner = (rows - 2 * HALO) // BLOCK
    partners = range(count - 1, 1, -1)

    raw = tiles_of(jnp.transpose(tracers, (0, 2, 1, 3)))
    joined = jnp.concatenate([jnp.transpose(wind_x, (1, 0, 2)), jnp.transpose(wind_y, (1, 0, 2))], axis=0)
    halo = f32(depth, HALO + 1, number, nlon)
    state, down, up = call(
        functools.partial(prep_kernel, rows),
        (f32(depth, rows, number, nlon), halo, halo), (raw, joined),
        cost=cost(1, 8 * tracers.size))
    low = lax.ppermute(up, "lat", [(i, i + 1) for i in range(bands - 1)])
    high = lax.ppermute(down, "lat", [(i + 1, i) for i in range(bands - 1)])
    taps = call(
        weights_kernel, f32(targets, rows, SUB, width),
        (jnp.transpose(remap_weight, (1, 2, 0, 3)), source_level),
        cost=cost(20 * remap_weight.size, 16 * remap_weight.size))

    def box(n, *lead):
        return lead + (depth, n, size, SUB, LANES)

    def vmem(*shape):
        return pltpu.VMEM(shape, jnp.float32)

    held = -(-rows // SUB) * SUB
    coef = f32(3, depth, held, nlon)
    swept = vmem(depth, rows - 2 * REACH, number, nlon)
    stage = vmem(depth * (rows - 2 * REACH), number, nlon)
    result = call(
        functools.partial(interior_kernel, count, rows),
        [f32(*box(inner))] * count + [f32(depth, rows - 2 * REACH, number, nlon), coef, coef],
        (state, joined), scratch=[vmem(*box(inner, count)), vmem(2, depth, held, nlon), swept, stage, stage, stage],
        cost=cost(50 * tracers.size, 8 * tracers.size))
    middle, (first, cx, cy) = result[:count], result[count:]
    plan, chunks = [], []

    def received(k, start, chunk):
        plan.append((k, start))
        chunks.append(chunk)

    def send(sent, start):
        received(0, start, sent[0])
        for k in partners:
            received(k, start, swapped(sent[k], k))

    send(middle, 1)
    swept = vmem(depth, BLOCK, number, nlon)
    stage = vmem(depth * BLOCK, number, nlon)
    scratch = [vmem(*box(1, count)), vmem(3, depth, SUB, nlon), swept, swept, stage, stage, stage]
    south = call(
        functools.partial(edge_kernel, count, rows, True),
        [f32(*box(1))] * count, (state, low, first, cx, cy), scratch=scratch,
        cost=cost(30 * tracers.size, 4 * tracers.size))
    send(south, 0)
    north = call(
        functools.partial(edge_kernel, count, rows, False),
        [f32(*box(blocks if k == 1 else 1)) for k in range(count)],
        (state, high, first, cx, cy, south[1], middle[1]), scratch=scratch,
        cost=cost(30 * tracers.size, 4 * tracers.size))
    send(north, blocks - 1)
    received(1, 0, swapped(north[1], 1))
    out = call(
        functools.partial(remap_kernel, count, depth, tuple(plan)),
        f32(targets, rows, number, width), (level_counts, *chunks, taps),
        specs=[SMEM] + [VMEM] * (len(chunks) + 1),
        scratch=[vmem(count * depth, blocks, size, SUB, LANES)],
        cost=cost(60 * remap_weight.size, 16 * remap_weight.size))
    return jnp.transpose(out, (2, 0, 1, 3))


def solution(mesh):
    in_specs = (
        P(None, "lev", ("groups", "lat"), None),
        P("lev", ("groups", "lat"), None),
        P("lev", ("groups", "lat"), None),
        P(),
        P(None, ("groups", "lat"), "lev"),
        P(None, None, ("groups", "lat"), "lev"),
    )
    out_specs = P(None, None, ("groups", "lat"), "lev")
    return jax.shard_map(shards, mesh=mesh, in_specs=in_specs, out_specs=out_specs, check_vma=False)
```

```python
import functools

import jax
import jax.numpy as jnp
from jax import lax
from jax.experimental import pallas as pl
from jax.experimental.layout import Layout, with_layout_constraint
from jax.experimental.pallas import tpu as pltpu
from jax.sharding import PartitionSpec as P

SUBSTEPS = 2
TAPS = 4
REACH = 3
HALO = REACH * SUBSTEPS
BLOCK = 6
LANES = 128
SUB = 8


def spread(row):
    return jnp.broadcast_to(row, (SUB, LANES))


def lane_ids():
    return lax.broadcasted_iota(jnp.int32, (SUB, LANES), 1)


def from_west(tiles, steps, lane):
    turned = [pltpu.roll(t, steps, 1) for t in tiles]
    return [jnp.where(lane < steps, turned[j - 1], turned[j]) for j in range(len(tiles))]


def from_east(tiles, lane):
    turned = [pltpu.roll(t, LANES - 1, 1) for t in tiles]
    count = len(tiles)
    return [jnp.where(lane == LANES - 1, turned[(j + 1) % count], turned[j]) for j in range(count)]


def coefficients(wind):
    size = jnp.abs(wind)
    rest = 1.0 - size
    alpha = wind * rest * rest * (1.0 / 12.0)
    beta = wind * size * rest * (-1.0 / 12.0)
    gamma = wind * size * (3.0 - 2.0 * size)
    return alpha, beta, gamma


def packed_sizes(nlon, count):
    width = nlon // count
    mains, tail = width // LANES, width % LANES
    per = LANES // tail if tail else 1
    tails = -(-BLOCK // per) if tail else 0
    return width, mains, tail, per, BLOCK * mains + tails


def prep_kernel(rows, tracers, winds, state, first_round, second_round):
    levels, nlon = state.shape[0], state.shape[3]
    nj = nlon // LANES
    row_stride = nj * levels
    tracer_stride = rows * row_stride
    band, bands = lax.axis_index("lat"), lax.axis_size("lat")
    even = band % 2 == 0
    alone = (band == 0) | (band == bands - 1)
    keep = jnp.where(alone, 0.0, 1.0)

    def body(row, _):
        for level in range(levels):
            for j in range(nj):
                start = row * row_stride + j * levels + level
                state[level, row, :, tile(j)] = tracers[pl.ds(start, SUB, stride=tracer_stride), :]
        return 0

    lax.fori_loop(0, rows, body, 0)
    for target, north, scale in ((first_round, even, None), (second_round, jnp.logical_not(even), keep)):
        scaled = (lambda v: v) if scale is None else (lambda v: v * scale)
        row_t = jnp.where(north, rows - HALO, 0)
        row_x = jnp.where(north, rows - REACH, 0)
        row_y = jnp.where(north, rows - REACH - 1, 0)
        for level in range(levels):
            for row in range(HALO):
                target[level, row] = scaled(state[level, row_t + row])
            for q in range(REACH):
                target[level, HALO, q:q + 1, :] = scaled(winds[row_x + q, level:level + 1, :])
            for q in range(REACH + 1):
                target[level, HALO, REACH + q:REACH + q + 1, :] = scaled(winds[rows + row_y + q, level:level + 1, :])


def lat_pass(levels, nj, ranges, cell, coef, store):
    group = 3 if nj % 3 == 0 else 1

    def body(i, _):
        level = i // (nj // group)
        for u in range(group):
            one(level, pl.ds(pl.multiple_of(((i % (nj // group)) * group + u) * LANES, LANES), LANES))
        return 0

    def one(level, lanes):
        for first, last in ranges:
            a = {r: cell(level, r, lanes) for r in range(first - REACH, last + REACH)}
            inter = {f: 7.0 * (a[f - 1] + a[f]) - (a[f - 2] + a[f + 1]) for f in range(first - 1, last + 2)}
            flux = {}
            for f in range(first, last + 1):
                alpha, beta, gamma = [spread(coef(i, level, f, lanes)) for i in range(3)]
                north = gamma > 0
                behind = jnp.where(north, inter[f - 1], inter[f + 1])
                upwind = jnp.where(north, a[f - 1], a[f])
                flux[f] = alpha * inter[f] + beta * behind + gamma * upwind
                if f > first:
                    store(level, f - 1, lanes, a[f - 1] - (flux[f] - flux[f - 1]))

    lax.fori_loop(0, levels * nj // group, body, 0)


def tile(j):
    return slice(j * LANES, (j + 1) * LANES)


def lon_pass(work, swept, coef, inter, west, flux, lane, finish):
    nj = swept.shape[3] // LANES
    each = range(nj)

    def interfaces(n):
        level, _, at = work[n]
        b = [swept[level, at, :, tile(j)] for j in each]
        w1, w2, e1 = from_west(b, 1, lane), from_west(b, 2, lane), from_east(b, lane)
        for j in each:
            inter[n, :, tile(j)] = 7.0 * (w1[j] + b[j]) - (w2[j] + e1[j])
            west[n, :, tile(j)] = w1[j]

    def fluxes(n):
        level, row, at = work[n]
        mid = [inter[n, :, tile(j)] for j in each]
        w1, e1 = from_west(mid, 1, lane), from_east(mid, lane)
        for j in each:
            alpha, beta, gamma = [spread(coef(i, level, row, tile(j))) for i in range(3)]
            right = gamma > 0
            behind = jnp.where(right, w1[j], e1[j])
            upwind = jnp.where(right, west[n, :, tile(j)], swept[level, at, :, tile(j)])
            flux[n, :, tile(j)] = alpha * mid[j] + beta * behind + gamma * upwind

    def update(n):
        level, _, at = work[n]
        here = [flux[n, :, tile(j)] for j in each]
        e1 = from_east(here, lane)
        return [swept[level, at, :, tile(j)] - (e1[j] - here[j]) for j in each]

    groups = len(work) // BLOCK
    for g in range(groups + 2):
        if g < groups:
            for q in range(BLOCK):
                interfaces(g * BLOCK + q)
        if 1 <= g <= groups:
            for q in range(BLOCK):
                fluxes((g - 1) * BLOCK + q)
        if g >= 2:
            finish(g - 2, [update((g - 2) * BLOCK + q) for q in range(BLOCK)])


def pack_block(block, packed, level, number, count, lane):
    me = lax.axis_index("lev")
    nlon = len(block[0]) * LANES
    width, mains, tail, per, size = packed_sizes(nlon, count)
    for d in range(count):
        j0, off = (d * width) // LANES, (d * width) % LANES
        for q, tiles in enumerate(block):
            turned = [pltpu.roll(tiles[j0 + m], LANES - off, 1) if off else tiles[j0 + m]
                      for m in range(mains + (1 if off else 0))]
            for m in range(mains):
                whole = jnp.where(lane < LANES - off, turned[m], turned[m + 1]) if off else turned[m]
                packed[d ^ me, level, number, q * mains + m] = whole
        if tail:
            for g in range(-(-BLOCK // per)):
                total = None
                for place in range(min(per, BLOCK - g * per)):
                    shift = (place * tail - off) % LANES
                    source = block[g * per + place][j0 + mains]
                    moved = pltpu.roll(source, shift, 1) if shift else source
                    total = moved if total is None else jnp.where(lane < place * tail, total, moved)
                packed[d ^ me, level, number, BLOCK * mains + g] = total


def copy_blocks(source, target, start=0):
    levels, blocks, size = source.shape[:3]
    for level in range(levels):
        for number in range(blocks):
            for i in range(size):
                target[level, start + number, i] = source[level, number, i]


def own_coefficients(rows, joined, winds, cx, cy):
    levels, held, nlon = cx.shape[1:]
    keep = jnp.where(lax.axis_index("lat") == 0, 0.0, 1.0)
    for level in range(levels):
        for way in range(2):
            for row in range(rows):
                winds[way, level, row:row + 1, :] = joined[way * rows + row, level:level + 1, :]
        winds[1, level, 0:1, :] = winds[1, level, 0:1, :] * keep
        for way, target in enumerate((cx, cy)):
            for j in range(nlon // LANES):
                parts = coefficients(winds[way, level, :, tile(j)])
                for p in range(3):
                    target[p, level, :, tile(j)] = parts[p]


def put_rows(target, level, at, rows):
    for q, row in enumerate(rows):
        for j, part in enumerate(row):
            target[level, at + q, :, tile(j)] = part


def interior_kernel(count, rows, state, joined, *refs):
    outs, (first, cx, cy, packed, winds, swept, inter, west, flux) = refs[:count], refs[count:]
    levels, nlon = state.shape[0], state.shape[3]
    nj = nlon // LANES
    lane = lane_ids()
    own_coefficients(rows, joined, winds, cx, cy)
    coef_x = lambda i, level, r, lanes: cx[i, level, r:r + 1, lanes]
    coef_y = lambda i, level, f, lanes: cy[i, level, f:f + 1, lanes]

    def put(level, row, lanes, value):
        swept[level, row - REACH, :, lanes] = value

    lat_pass(levels, nj, [(REACH, rows - REACH)], lambda level, r, lanes: state[level, r, :, lanes], coef_y, put)
    work = [(level, row, row - REACH) for level in range(levels) for row in range(REACH, rows - REACH)]

    def keep_first(group, done):
        level, _, at = work[group * BLOCK]
        put_rows(first, level, at, done)

    lon_pass(work, swept, coef_x, inter, west, flux, lane, keep_first)
    lat_pass(levels, nj, [(HALO, rows - HALO)], lambda level, r, lanes: first[level, r - REACH, :, lanes], coef_y, put)
    work_last = [(level, row, row - REACH) for level in range(levels) for row in range(HALO, rows - HALO)]

    def send(group, done):
        level, row, _ = work_last[group * BLOCK]
        pack_block(done, packed, level, (row - HALO) // BLOCK, count, lane)

    lon_pass(work_last, swept, coef_x, inter, west, flux, lane, send)
    for k in range(count):
        copy_blocks(packed.at[k], outs[k])


def edge_kernel(count, rows, south, joint, state, first_round, second_round, first, cx, cy, *refs):
    others = refs[:joint]
    outs, (packed, beyond, swept, edge, inter, west, flux) = refs[-7 - count:-7], refs[-7:]
    odd = lax.axis_index("lat") % 2 == 1
    from_first = odd if south else jnp.logical_not(odd)

    def halo(*at):
        return jnp.where(from_first, first_round[at], second_round[at])

    levels, nlon = state.shape[0], state.shape[3]
    nj = nlon // LANES
    lane = lane_ids()
    for level in range(levels):
        for j in range(nj):
            parts = coefficients(halo(level, HALO, slice(None), tile(j)))
            for p in range(3):
                beyond[p, level, :, tile(j)] = parts[p]

    def coef_x(i, level, r, lanes):
        if 0 <= r < rows:
            return cx[i, level, r:r + 1, lanes]
        at = r + REACH if south else r - rows
        return beyond[i, level, at:at + 1, lanes]

    def coef_y(i, level, f, lanes):
        if 0 <= f < rows:
            return cy[i, level, f:f + 1, lanes]
        at = f + 2 * REACH + 1 if south else f - rows + REACH
        return beyond[i, level, at:at + 1, lanes]

    def cell(level, r, lanes):
        if 0 <= r < rows:
            return state[level, r, :, lanes]
        return halo(level, r + HALO if south else r - rows, slice(None), lanes)

    base = -REACH if south else rows - REACH
    base_last = 0 if south else rows - HALO

    def cell_first(level, r, lanes):
        if REACH <= r < rows - REACH:
            return first[level, r - REACH, :, lanes]
        return edge[level, r - base, :, lanes]

    def put(level, row, lanes, value):
        swept[level, row - base, :, lanes] = value

    def put_last(level, row, lanes, value):
        swept[level, row - base_last, :, lanes] = value

    def listed(start):
        return [(level, start + q, q) for level in range(levels) for q in range(BLOCK)]

    def keep_edge(group, done):
        put_rows(edge, group, 0, done)

    def send(group, done):
        pack_block(done, packed, group, 0, count, lane)

    lat_pass(levels, nj, [(base, base + BLOCK)], cell, coef_y, put)
    lon_pass(listed(base), swept, coef_x, inter, west, flux, lane, keep_edge)
    lat_pass(levels, nj, [(base_last, base_last + BLOCK)], cell_first, coef_y, put_last)
    lon_pass(listed(base_last), swept, coef_x, inter, west, flux, lane, send)
    for k in range(count):
        copy_blocks(packed.at[k], outs[k])
    start = 1
    for other in others:
        copy_blocks(other, outs[1], start)
        start += other.shape[1]


def weights_kernel(weights, source, out):
    targets, rows, taps, width = weights.shape

    for row in range(rows):
        for k in range(targets):
            lowest, highest = max(k - (TAPS - 1), 0), min(k, targets - TAPS)
            w = weights[k, row]
            w = jnp.concatenate([w, jnp.zeros((SUB - taps, width), jnp.float32)], axis=0)
            at = jnp.broadcast_to(source[k, row:row + 1, :], (SUB, width))
            total = w
            for g in range(lowest + 1, highest + 1):
                total = jnp.where(at == g, pltpu.roll(w, g - lowest, 0), total)
            out[k, row] = total


def remap_kernel(count, depth, plan, counts, *refs):
    chunks, (weights, out, columns) = refs[:len(plan)], refs[len(plan):]
    me = lax.axis_index("lev")
    for (k, start), chunk in zip(plan, chunks):
        copy_blocks(chunk, columns.at[pl.ds((me ^ k) * depth, depth)], start)
    targets, rows, _, width = out.shape
    _, mains, tail, per, _ = packed_sizes(width * count, count)
    slots = []
    for level in range(targets):
        slot, start = jnp.int32(level), jnp.int32(0)
        for d in range(count):
            slot = jnp.where(level >= start, d * depth + level - start, slot)
            start = start + counts[d]
        slots.append(slot)

    def block(number):
        for q in range(BLOCK):
            row = number * BLOCK + q
            for m in range(mains + (1 if tail else 0)):
                wide = LANES if m < mains else tail
                lanes = slice(m * LANES, m * LANES + wide)
                values = []
                for level in range(targets):
                    if m < mains:
                        values.append(columns[slots[level], number, q * mains + m])
                    else:
                        last = columns[slots[level], number, BLOCK * mains + q // per]
                        shift = (q % per) * tail
                        last = pltpu.roll(last, LANES - shift, 1) if shift else last
                        values.append(last[:, :wide])
                for k in range(targets):
                    lowest, highest = max(k - (TAPS - 1), 0), min(k, targets - TAPS) + TAPS - 1
                    total = None
                    for level in range(lowest, highest + 1):
                        j = level - lowest
                        w = jnp.broadcast_to(weights[k, row, j:j + 1, lanes], (SUB, wide))
                        term = w * values[level]
                        total = term if total is None else total + term
                    out[k, row, :, lanes] = total

    for number in range(rows // BLOCK):
        block(number)


def tiles_of(array):
    lead, levels, nlon = array.shape[:-2], array.shape[-2], array.shape[-1]
    split = array.reshape(lead + (levels, nlon // LANES, LANES))
    order = tuple(range(len(lead))) + (len(lead) + 1, len(lead), len(lead) + 2)
    split = with_layout_constraint(split, Layout(major_to_minor=order))
    return jnp.swapaxes(split, -3, -2).reshape(-1, LANES)


VMEM = pl.BlockSpec(memory_space=pltpu.VMEM)
ANY = pl.BlockSpec(memory_space=pl.ANY)
SMEM = pl.BlockSpec(memory_space=pltpu.SMEM)


def call(kernel, outs, args, specs=None, scratch=(), cost=None):
    return pl.pallas_call(
        kernel,
        out_shape=outs,
        in_specs=specs or [VMEM] * len(args),
        out_specs=jax.tree.map(lambda _: VMEM, outs),
        scratch_shapes=list(scratch),
        compiler_params=pltpu.CompilerParams(vmem_limit_bytes=16 << 20),
        cost_estimate=cost,
    )(*args)


def cost(flops, size):
    return pl.CostEstimate(flops=int(flops), bytes_accessed=int(size), transcendentals=0)


def f32(*shape):
    return jax.ShapeDtypeStruct(shape, jnp.float32)


def swapped(value, k):
    count = lax.axis_size("lev")
    return lax.ppermute(value, "lev", [(i, i ^ k) for i in range(count)])


def shards(tracers, wind_x, wind_y, level_counts, source_level, remap_weight):
    count = lax.axis_size("lev")
    bands = lax.axis_size("lat")
    number, depth, rows, nlon = tracers.shape
    targets, _, width = source_level.shape
    size = packed_sizes(nlon, count)[-1]
    blocks = rows // BLOCK
    inner = (rows - 2 * HALO) // BLOCK
    partners = range(count - 1, 1, -1)

    raw = tiles_of(jnp.transpose(tracers, (0, 2, 1, 3)))
    joined = jnp.concatenate([jnp.transpose(wind_x, (1, 0, 2)), jnp.transpose(wind_y, (1, 0, 2))], axis=0)
    halo = f32(depth, HALO + 1, number, nlon)
    state, *rounds = call(
        functools.partial(prep_kernel, rows),
        (f32(depth, rows, number, nlon), halo, halo), (raw, joined),
        cost=cost(1, 8 * tracers.size))
    swaps = [[(i, i ^ 1) for i in range(bands)],
             [(i, i if i in (0, bands - 1) else ((i - 1) ^ 1) + 1) for i in range(bands)]]
    rounds = [lax.ppermute(sent, "lat", pairs) for sent, pairs in zip(rounds, swaps)]
    taps = call(
        weights_kernel, f32(targets, rows, SUB, width),
        (jnp.transpose(remap_weight, (1, 2, 0, 3)), source_level),
        cost=cost(20 * remap_weight.size, 16 * remap_weight.size))

    def box(n, *lead):
        return lead + (depth, n, size, SUB, LANES)

    def vmem(*shape):
        return pltpu.VMEM(shape, jnp.float32)

    held = -(-rows // SUB) * SUB
    coef = f32(3, depth, held, nlon)
    swept = vmem(depth, rows - 2 * REACH, number, nlon)
    stage = vmem(depth * (rows - 2 * REACH), number, nlon)
    result = call(
        functools.partial(interior_kernel, count, rows),
        [f32(*box(inner))] * count + [f32(depth, rows - 2 * REACH, number, nlon), coef, coef],
        (state, joined), scratch=[vmem(*box(inner, count)), vmem(2, depth, held, nlon), swept, stage, stage, stage],
        cost=cost(50 * tracers.size, 8 * tracers.size))
    middle, (first, cx, cy) = result[:count], result[count:]
    plan, chunks = [], []

    def received(k, start, chunk):
        plan.append((k, start))
        chunks.append(chunk)
        return chunk

    def send(sent, start):
        received(0, start, sent[0])
        return [received(k, start, swapped(sent[k], k)) for k in partners]

    swept = vmem(depth, BLOCK, number, nlon)
    stage = vmem(depth * BLOCK, number, nlon)

    def edge(south, joint, after):
        args = (state, *rounds, first, cx, cy, *joint, *after)
        return call(
            functools.partial(edge_kernel, count, rows, south, len(joint)),
            [f32(*box(1 + sum(c.shape[1] for c in joint) if k == 1 else 1)) for k in range(count)], args,
            specs=[VMEM] * (len(args) - len(after)) + [ANY] * len(after),
            scratch=[vmem(*box(1, count)), vmem(3, depth, SUB, nlon), swept, swept, stage, stage, stage],
            cost=cost(30 * tracers.size, 4 * tracers.size))

    arrived = send(middle, 1)
    south = edge(True, (middle[1],), (taps,))
    send(south, 0)
    received(1, 0, swapped(south[1], 1))
    north = edge(False, (), arrived)
    send(north, blocks - 1)
    received(1, blocks - 1, swapped(north[1], 1))
    out = call(
        functools.partial(remap_kernel, count, depth, tuple(plan)),
        f32(targets, rows, number, width), (level_counts, *chunks, taps),
        specs=[SMEM] + [VMEM] * (len(chunks) + 1),
        scratch=[vmem(count * depth, blocks, size, SUB, LANES)],
        cost=cost(60 * remap_weight.size, 16 * remap_weight.size))
    return jnp.transpose(out, (2, 0, 1, 3))


def solution(mesh):
    in_specs = (
        P(None, "lev", ("groups", "lat"), None),
        P("lev", ("groups", "lat"), None),
        P("lev", ("groups", "lat"), None),
        P(),
        P(None, ("groups", "lat"), "lev"),
        P(None, None, ("groups", "lat"), "lev"),
    )
    out_specs = P(None, None, ("groups", "lat"), "lev")
    return jax.shard_map(shards, mesh=mesh, in_specs=in_specs, out_specs=out_specs, check_vma=False)
```

```python
import functools

import jax
import jax.numpy as jnp
from jax import lax
from jax.experimental import pallas as pl
from jax.experimental.layout import Layout, with_layout_constraint
from jax.experimental.pallas import tpu as pltpu
from jax.sharding import PartitionSpec as P

SUBSTEPS = 2
TAPS = 4
REACH = 3
HALO = REACH * SUBSTEPS
BLOCK = 6
LANES = 128
SUB = 8


def spread(row):
    return jnp.broadcast_to(row, (SUB, LANES))


def lane_ids():
    return lax.broadcasted_iota(jnp.int32, (SUB, LANES), 1)


def from_west(tiles, steps, lane):
    turned = [pltpu.roll(t, steps, 1) for t in tiles]
    return [jnp.where(lane < steps, turned[j - 1], turned[j]) for j in range(len(tiles))]


def from_east(tiles, lane):
    turned = [pltpu.roll(t, LANES - 1, 1) for t in tiles]
    count = len(tiles)
    return [jnp.where(lane == LANES - 1, turned[(j + 1) % count], turned[j]) for j in range(count)]


def coefficients(wind):
    size = jnp.abs(wind)
    rest = 1.0 - size
    alpha = wind * rest * rest * (1.0 / 12.0)
    beta = wind * size * rest * (-1.0 / 12.0)
    gamma = wind * size * (3.0 - 2.0 * size)
    return alpha, beta, gamma


def packed_sizes(nlon, count):
    width = nlon // count
    mains, tail = width // LANES, width % LANES
    per = LANES // tail if tail else 1
    tails = -(-BLOCK // per) if tail else 0
    return width, mains, tail, per, BLOCK * mains + tails


def prep_kernel(rows, tracers, winds, state, *sent):
    levels, nlon = state.shape[0], state.shape[3]
    nj = nlon // LANES
    row_stride = nj * levels
    tracer_stride = rows * row_stride
    band, bands = lax.axis_index("lat"), lax.axis_size("lat")
    even = band % 2 == 0
    alone = (band == 0) | (band == bands - 1)
    keep = jnp.where(alone, 0.0, 1.0)

    def body(row, _):
        for level in range(levels):
            for j in range(nj):
                start = row * row_stride + j * levels + level
                state[level, row, :, tile(j)] = tracers[pl.ds(start, SUB, stride=tracer_stride), :]
        return 0

    lax.fori_loop(0, rows, body, 0)
    for level in range(levels):
        for target, north, scale in ((sent[2 * level], even, None), (sent[2 * level + 1], jnp.logical_not(even), keep)):
            scaled = (lambda v: v) if scale is None else (lambda v: v * scale)
            row_t = jnp.where(north, rows - HALO, 0)
            row_x = jnp.where(north, rows - REACH, 0)
            row_y = jnp.where(north, rows - REACH - 1, 0)
            for row in range(HALO):
                target[row] = scaled(state[level, row_t + row])
            for q in range(REACH):
                target[HALO, q:q + 1, :] = scaled(winds[row_x + q, level:level + 1, :])
            for q in range(REACH + 1):
                target[HALO, REACH + q:REACH + q + 1, :] = scaled(winds[rows + row_y + q, level:level + 1, :])


def lat_pass(levels, nj, ranges, cell, coef, store):
    group = 3 if nj % 3 == 0 else 1

    def body(i, _):
        level = i // (nj // group)
        for u in range(group):
            one(level, pl.ds(pl.multiple_of(((i % (nj // group)) * group + u) * LANES, LANES), LANES))
        return 0

    def one(level, lanes):
        for first, last in ranges:
            a = {r: cell(level, r, lanes) for r in range(first - REACH, last + REACH)}
            inter = {f: 7.0 * (a[f - 1] + a[f]) - (a[f - 2] + a[f + 1]) for f in range(first - 1, last + 2)}
            flux = {}
            for f in range(first, last + 1):
                alpha, beta, gamma = [spread(coef(i, level, f, lanes)) for i in range(3)]
                north = gamma > 0
                behind = jnp.where(north, inter[f - 1], inter[f + 1])
                upwind = jnp.where(north, a[f - 1], a[f])
                flux[f] = alpha * inter[f] + beta * behind + gamma * upwind
                if f > first:
                    store(level, f - 1, lanes, a[f - 1] - (flux[f] - flux[f - 1]))

    lax.fori_loop(0, levels * nj // group, body, 0)


def tile(j):
    return slice(j * LANES, (j + 1) * LANES)


def lon_pass(work, swept, coef, inter, west, flux, lane, finish):
    nj = swept.shape[3] // LANES
    each = range(nj)

    def interfaces(n):
        level, _, at = work[n]
        b = [swept[level, at, :, tile(j)] for j in each]
        w1, w2, e1 = from_west(b, 1, lane), from_west(b, 2, lane), from_east(b, lane)
        for j in each:
            inter[n, :, tile(j)] = 7.0 * (w1[j] + b[j]) - (w2[j] + e1[j])
            west[n, :, tile(j)] = w1[j]

    def fluxes(n):
        level, row, at = work[n]
        mid = [inter[n, :, tile(j)] for j in each]
        w1, e1 = from_west(mid, 1, lane), from_east(mid, lane)
        for j in each:
            alpha, beta, gamma = [spread(coef(i, level, row, tile(j))) for i in range(3)]
            right = gamma > 0
            behind = jnp.where(right, w1[j], e1[j])
            upwind = jnp.where(right, west[n, :, tile(j)], swept[level, at, :, tile(j)])
            flux[n, :, tile(j)] = alpha * mid[j] + beta * behind + gamma * upwind

    def update(n):
        level, _, at = work[n]
        here = [flux[n, :, tile(j)] for j in each]
        e1 = from_east(here, lane)
        return [swept[level, at, :, tile(j)] - (e1[j] - here[j]) for j in each]

    groups = len(work) // BLOCK
    for g in range(groups + 2):
        if g < groups:
            for q in range(BLOCK):
                interfaces(g * BLOCK + q)
        if 1 <= g <= groups:
            for q in range(BLOCK):
                fluxes((g - 1) * BLOCK + q)
        if g >= 2:
            finish(g - 2, [update((g - 2) * BLOCK + q) for q in range(BLOCK)])


def pack_block(block, packed, unit, count, lane):
    me = lax.axis_index("lev")
    nlon = len(block[0]) * LANES
    width, mains, tail, per, size = packed_sizes(nlon, count)
    for d in range(count):
        j0, off = (d * width) // LANES, (d * width) % LANES
        for q, tiles in enumerate(block):
            turned = [pltpu.roll(tiles[j0 + m], LANES - off, 1) if off else tiles[j0 + m]
                      for m in range(mains + (1 if off else 0))]
            for m in range(mains):
                whole = jnp.where(lane < LANES - off, turned[m], turned[m + 1]) if off else turned[m]
                packed[d ^ me, unit, q * mains + m] = whole
        if tail:
            for g in range(-(-BLOCK // per)):
                total = None
                for place in range(min(per, BLOCK - g * per)):
                    shift = (place * tail - off) % LANES
                    source = block[g * per + place][j0 + mains]
                    moved = pltpu.roll(source, shift, 1) if shift else source
                    total = moved if total is None else jnp.where(lane < place * tail, total, moved)
                packed[d ^ me, unit, BLOCK * mains + g] = total


def copy_units(source, target, start=0):
    for unit in range(source.shape[0]):
        for i in range(source.shape[1]):
            target[start + unit, i] = source[unit, i]


def own_coefficients(rows, joined, winds, cx, cy):
    levels, held, nlon = cx.shape[1:]
    keep = jnp.where(lax.axis_index("lat") == 0, 0.0, 1.0)
    for level in range(levels):
        for way in range(2):
            for row in range(rows):
                winds[way, level, row:row + 1, :] = joined[way * rows + row, level:level + 1, :]
        winds[1, level, 0:1, :] = winds[1, level, 0:1, :] * keep
        for way, target in enumerate((cx, cy)):
            for j in range(nlon // LANES):
                parts = coefficients(winds[way, level, :, tile(j)])
                for p in range(3):
                    target[p, level, :, tile(j)] = parts[p]


def put_rows(target, level, at, rows):
    for q, row in enumerate(rows):
        for j, part in enumerate(row):
            target[level, at + q, :, tile(j)] = part


def interior_kernel(count, rows, state, joined, *refs):
    outs, (first, cx, cy, packed, winds, swept, inter, west, flux) = refs[:count], refs[count:]
    levels, nlon = state.shape[0], state.shape[3]
    nj = nlon // LANES
    lane = lane_ids()
    own_coefficients(rows, joined, winds, cx, cy)
    coef_x = lambda i, level, r, lanes: cx[i, level, r:r + 1, lanes]
    coef_y = lambda i, level, f, lanes: cy[i, level, f:f + 1, lanes]

    def put(level, row, lanes, value):
        swept[level, row - REACH, :, lanes] = value

    lat_pass(levels, nj, [(REACH, rows - REACH)], lambda level, r, lanes: state[level, r, :, lanes], coef_y, put)
    work = [(level, row, row - REACH) for level in range(levels) for row in range(REACH, rows - REACH)]

    def keep_first(group, done):
        level, _, at = work[group * BLOCK]
        put_rows(first, level, at, done)

    lon_pass(work, swept, coef_x, inter, west, flux, lane, keep_first)
    lat_pass(levels, nj, [(HALO, rows - HALO)], lambda level, r, lanes: first[level, r - REACH, :, lanes], coef_y, put)
    work_last = [(level, row, row - REACH) for level in range(levels) for row in range(HALO, rows - HALO)]

    def send(group, done):
        pack_block(done, packed, group, count, lane)

    lon_pass(work_last, swept, coef_x, inter, west, flux, lane, send)
    for k in range(count):
        copy_units(packed.at[k], outs[k])


def edge_kernel(count, rows, slot, joint, state, first_round, second_round, first, cx, cy, *refs):
    others = refs[:joint]
    outs, (packed, beyond, swept, edge, inter, west, flux) = refs[-7 - count:-7], refs[-7:]
    nlon = state.shape[3]
    nj = nlon // LANES
    lane = lane_ids()
    odd = lax.axis_index("lat") % 2 == 1

    def halo(south, *at):
        one, two = first_round[at], second_round[at]
        return jnp.where(odd, one, two) if south else jnp.where(odd, two, one)

    for end, south in enumerate((True, False)):
        for j in range(nj):
            parts = coefficients(halo(south, HALO, slice(None), tile(j)))
            for p in range(3):
                beyond[p, end, :, tile(j)] = parts[p]

    def coef_x(i, _, r, lanes):
        if 0 <= r < rows:
            return cx[i, slot, r:r + 1, lanes]
        end, at = (0, r + REACH) if r < 0 else (1, r - rows)
        return beyond[i, end, at:at + 1, lanes]

    def coef_y(i, _, f, lanes):
        if 0 <= f < rows:
            return cy[i, slot, f:f + 1, lanes]
        end, at = (0, f + 2 * REACH + 1) if f < 0 else (1, f - rows + REACH)
        return beyond[i, end, at:at + 1, lanes]

    def cell(_, r, lanes):
        if 0 <= r < rows:
            return state[slot, r, :, lanes]
        return halo(r < 0, r + HALO if r < 0 else r - rows, slice(None), lanes)

    ends = [(-REACH, REACH), (rows - REACH, rows + REACH)]
    ends_last = [(0, HALO), (rows - HALO, rows)]

    def place(row, ranges):
        (a, b), (c, _) = ranges
        return row - a if row < b else row - c + BLOCK

    def cell_first(_, r, lanes):
        if REACH <= r < rows - REACH:
            return first[slot, r - REACH, :, lanes]
        return edge[0, place(r, ends), :, lanes]

    def put(_, row, lanes, value):
        swept[0, place(row, ends), :, lanes] = value

    def put_last(_, row, lanes, value):
        swept[0, place(row, ends_last), :, lanes] = value

    def listed(ranges):
        return [(0, row, place(row, ranges)) for a, b in ranges for row in range(a, b)]

    def keep_edge(group, done):
        put_rows(edge, 0, group * BLOCK, done)

    def send(group, done):
        pack_block(done, packed, group, count, lane)

    lat_pass(1, nj, ends, cell, coef_y, put)
    lon_pass(listed(ends), swept, coef_x, inter, west, flux, lane, keep_edge)
    lat_pass(1, nj, ends_last, cell_first, coef_y, put_last)
    lon_pass(listed(ends_last), swept, coef_x, inter, west, flux, lane, send)
    for k in range(count):
        copy_units(packed.at[k], outs[k])
    for other, out in zip(others, outs):
        copy_units(other, out, packed.shape[1])


def weights_kernel(weights, source, out):
    targets, rows, taps, width = weights.shape

    for row in range(rows):
        for k in range(targets):
            lowest, highest = max(k - (TAPS - 1), 0), min(k, targets - TAPS)
            w = weights[k, row]
            w = jnp.concatenate([w, jnp.zeros((SUB - taps, width), jnp.float32)], axis=0)
            at = jnp.broadcast_to(source[k, row:row + 1, :], (SUB, width))
            total = w
            for g in range(lowest + 1, highest + 1):
                total = jnp.where(at == g, pltpu.roll(w, g - lowest, 0), total)
            out[k, row] = total


def remap_kernel(count, depth, plan, numbers, counts, *refs):
    chunks, (weights, *ready, out, columns) = refs[:len(plan)], refs[len(plan):]
    me = lax.axis_index("lev")
    for (k, units), chunk in zip(plan, chunks):
        for unit, (slot, number) in enumerate(units):
            if number in numbers:
                for i in range(chunk.shape[1]):
                    columns[(me ^ k) * depth + slot, number, i] = chunk[unit, i]
    first_out = 0 if ready else numbers[0]
    if ready:
        copied = [n for n in range(out.shape[1] // BLOCK) if n not in numbers]
        for k in range(out.shape[0]):
            for row in range(len(copied) * BLOCK):
                out[k, copied[0] * BLOCK + row] = ready[0][k, row]
    targets, _, _, width = out.shape
    _, mains, tail, per, _ = packed_sizes(width * count, count)
    slots = []
    for level in range(targets):
        slot, start = jnp.int32(level), jnp.int32(0)
        for d in range(count):
            slot = jnp.where(level >= start, d * depth + level - start, slot)
            start = start + counts[d]
        slots.append(slot)

    def block(number):
        for q in range(BLOCK):
            row = number * BLOCK + q
            for m in range(mains + (1 if tail else 0)):
                wide = LANES if m < mains else tail
                lanes = slice(m * LANES, m * LANES + wide)
                values = []
                for level in range(targets):
                    if m < mains:
                        values.append(columns[slots[level], number, q * mains + m])
                    else:
                        last = columns[slots[level], number, BLOCK * mains + q // per]
                        shift = (q % per) * tail
                        last = pltpu.roll(last, LANES - shift, 1) if shift else last
                        values.append(last[:, :wide])
                for k in range(targets):
                    lowest, highest = max(k - (TAPS - 1), 0), min(k, targets - TAPS) + TAPS - 1
                    total = None
                    for level in range(lowest, highest + 1):
                        j = level - lowest
                        w = jnp.broadcast_to(weights[k, row, j:j + 1, lanes], (SUB, wide))
                        term = w * values[level]
                        total = term if total is None else total + term
                    out[k, row - first_out * BLOCK, :, lanes] = total

    for number in numbers:
        block(number)


def tiles_of(array):
    lead, levels, nlon = array.shape[:-2], array.shape[-2], array.shape[-1]
    split = array.reshape(lead + (levels, nlon // LANES, LANES))
    order = tuple(range(len(lead))) + (len(lead) + 1, len(lead), len(lead) + 2)
    split = with_layout_constraint(split, Layout(major_to_minor=order))
    return jnp.swapaxes(split, -3, -2).reshape(-1, LANES)


VMEM = pl.BlockSpec(memory_space=pltpu.VMEM)
ANY = pl.BlockSpec(memory_space=pl.ANY)
SMEM = pl.BlockSpec(memory_space=pltpu.SMEM)


def call(kernel, outs, args, specs=None, scratch=(), cost=None):
    return pl.pallas_call(
        kernel,
        out_shape=outs,
        in_specs=specs or [VMEM] * len(args),
        out_specs=jax.tree.map(lambda _: VMEM, outs),
        scratch_shapes=list(scratch),
        compiler_params=pltpu.CompilerParams(vmem_limit_bytes=16 << 20),
        cost_estimate=cost,
    )(*args)


def cost(flops, size):
    return pl.CostEstimate(flops=int(flops), bytes_accessed=int(size), transcendentals=0)


def f32(*shape):
    return jax.ShapeDtypeStruct(shape, jnp.float32)


def shards(tracers, wind_x, wind_y, level_counts, source_level, remap_weight):
    count = lax.axis_size("lev")
    bands = lax.axis_size("lat")
    number, depth, rows, nlon = tracers.shape
    targets, _, width = source_level.shape
    size = packed_sizes(nlon, count)[-1]
    blocks = rows // BLOCK
    inner = (rows - 2 * HALO) // BLOCK

    raw = tiles_of(jnp.transpose(tracers, (0, 2, 1, 3)))
    joined = jnp.concatenate([jnp.transpose(wind_x, (1, 0, 2)), jnp.transpose(wind_y, (1, 0, 2))], axis=0)
    halo = f32(HALO + 1, number, nlon)
    state, *sent = call(
        functools.partial(prep_kernel, rows),
        [f32(depth, rows, number, nlon)] + [halo] * (2 * depth), (raw, joined),
        cost=cost(1, 1))
    swaps = [[(i, i ^ 1) for i in range(bands)],
             [(i, i if i in (0, bands - 1) else ((i - 1) ^ 1) + 1) for i in range(bands)]]
    rounds = [lax.ppermute(buffer, "lat", swaps[i % 2]) for i, buffer in enumerate(sent)]
    taps = call(
        weights_kernel, f32(targets, rows, SUB, width),
        (jnp.transpose(remap_weight, (1, 2, 0, 3)), source_level),
        cost=cost(1, 1))

    def box(units, *lead):
        return lead + (units, size, SUB, LANES)

    def vmem(*shape):
        return pltpu.VMEM(shape, jnp.float32)

    held = -(-rows // SUB) * SUB
    coef = f32(3, depth, held, nlon)
    swept = vmem(depth, rows - 2 * REACH, number, nlon)
    stage = vmem(depth * (rows - 2 * REACH), number, nlon)
    result = call(
        functools.partial(interior_kernel, count, rows),
        [f32(*box(depth * inner))] * count + [f32(depth, rows - 2 * REACH, number, nlon), coef, coef],
        (state, joined), scratch=[vmem(*box(depth * inner, count)), vmem(2, depth, held, nlon), swept, stage, stage, stage],
        cost=cost(1, 1))
    middle, (first, cx, cy) = result[:count], result[count:]
    plan, chunks = [], []
    swept = vmem(1, 2 * HALO, number, nlon)
    stage = vmem(2 * HALO, number, nlon)

    def edge(slot, joint, after):
        args = (state, *rounds[2 * slot:2 * slot + 2], first, cx, cy, *joint, after)
        units = 2 + (joint[0].shape[0] if joint else 0)
        return call(
            functools.partial(edge_kernel, count, rows, slot, len(joint)),
            [f32(*box(units))] * count, args,
            specs=[VMEM] * (len(args) - 1) + [ANY],
            scratch=[vmem(*box(2, count)), vmem(3, 2, SUB, nlon), swept, swept, stage, stage, stage],
            cost=cost(60 * tracers.size, 8 * tracers.size))

    after, joint, joint_units = taps, middle, tuple((slot, 1 + b) for slot in range(depth) for b in range(inner))
    for slot in range(depth):
        done = edge(slot, joint, after)
        plan += [(k, ((slot, 0), (slot, blocks - 1)) + joint_units) for k in range(count)]
        chunks += [done[0]] + [None] * (count - 1)
        for k in range(count - 1, 0, -1):
            chunks[k - count] = lax.ppermute(done[k], "lev", [(i, i ^ k) for i in range(count)])
        after, joint, joint_units = done[0], (), ()
    def remap(part, numbers, height, ready):
        args = (level_counts, *chunks[:part], taps, *ready)
        return call(
            functools.partial(remap_kernel, count, depth, tuple(plan[:part]), numbers),
            f32(targets, height, number, width), args,
            specs=[SMEM] + [VMEM] * (len(args) - 1),
            scratch=[vmem(count * depth, blocks, size, SUB, LANES)],
            cost=cost(1, 1))

    middle_rows = remap(count, tuple(range(1, blocks - 1)), inner * BLOCK, ())
    out = remap(len(chunks), (0, blocks - 1), rows, (middle_rows,))
    return jnp.transpose(out, (2, 0, 1, 3))


def solution(mesh):
    in_specs = (
        P(None, "lev", ("groups", "lat"), None),
        P("lev", ("groups", "lat"), None),
        P("lev", ("groups", "lat"), None),
        P(),
        P(None, ("groups", "lat"), "lev"),
        P(None, None, ("groups", "lat"), "lev"),
    )
    out_specs = P(None, None, ("groups", "lat"), "lev")
    return jax.shard_map(shards, mesh=mesh, in_specs=in_specs, out_specs=out_specs, check_vma=False)
```

```python
import functools

import jax
import jax.numpy as jnp
from jax import lax
from jax.experimental import pallas as pl
from jax.experimental.layout import Layout, with_layout_constraint
from jax.experimental.pallas import tpu as pltpu
from jax.sharding import PartitionSpec as P

SUBSTEPS = 2
TAPS = 4
REACH = 3
HALO = REACH * SUBSTEPS
BLOCK = 6
LANES = 128
SUB = 8


def spread(row):
    return jnp.broadcast_to(row, (SUB, LANES))


def lane_ids():
    return lax.broadcasted_iota(jnp.int32, (SUB, LANES), 1)


def from_west(tiles, steps, lane):
    turned = [pltpu.roll(t, steps, 1) for t in tiles]
    return [jnp.where(lane < steps, turned[j - 1], turned[j]) for j in range(len(tiles))]


def from_east(tiles, lane):
    turned = [pltpu.roll(t, LANES - 1, 1) for t in tiles]
    count = len(tiles)
    return [jnp.where(lane == LANES - 1, turned[(j + 1) % count], turned[j]) for j in range(count)]


def coefficients(wind):
    size = jnp.abs(wind)
    rest = 1.0 - size
    alpha = wind * rest * rest * (1.0 / 12.0)
    beta = wind * size * rest * (-1.0 / 12.0)
    gamma = wind * size * (3.0 - 2.0 * size)
    return alpha, beta, gamma


def packed_sizes(nlon, count):
    width = nlon // count
    mains, tail = width // LANES, width % LANES
    per = LANES // tail if tail else 1
    tails = -(-BLOCK // per) if tail else 0
    return width, mains, tail, per, BLOCK * mains + tails


def prep_kernel(rows, tracers, winds, state, first_round, *second_rounds):
    levels, nlon = state.shape[0], state.shape[3]
    nj = nlon // LANES
    row_stride = nj * levels
    tracer_stride = rows * row_stride
    band, bands = lax.axis_index("lat"), lax.axis_size("lat")
    even = band % 2 == 0
    alone = (band == 0) | (band == bands - 1)
    keep = jnp.where(alone, 0.0, 1.0)

    def body(row, _):
        for level in range(levels):
            for j in range(nj):
                start = row * row_stride + j * levels + level
                state[level, row, :, tile(j)] = tracers[pl.ds(start, SUB, stride=tracer_stride), :]
        return 0

    lax.fori_loop(0, rows, body, 0)
    for level in range(levels):
        for target, north, scale in ((first_round.at[level], even, None), (second_rounds[level], jnp.logical_not(even), keep)):
            scaled = (lambda v: v) if scale is None else (lambda v: v * scale)
            row_t = jnp.where(north, rows - HALO, 0)
            row_x = jnp.where(north, rows - REACH, 0)
            row_y = jnp.where(north, rows - REACH - 1, 0)
            for row in range(HALO):
                target[row] = scaled(state[level, row_t + row])
            for q in range(REACH):
                target[HALO, q:q + 1, :] = scaled(winds[row_x + q, level:level + 1, :])
            for q in range(REACH + 1):
                target[HALO, REACH + q:REACH + q + 1, :] = scaled(winds[rows + row_y + q, level:level + 1, :])


def lat_pass(levels, nj, ranges, cell, coef, store):
    group = 3 if nj % 3 == 0 else 1

    def body(i, _):
        level = i // (nj // group)
        for u in range(group):
            one(level, pl.ds(pl.multiple_of(((i % (nj // group)) * group + u) * LANES, LANES), LANES))
        return 0

    def one(level, lanes):
        for first, last in ranges:
            a = {r: cell(level, r, lanes) for r in range(first - REACH, last + REACH)}
            inter = {f: 7.0 * (a[f - 1] + a[f]) - (a[f - 2] + a[f + 1]) for f in range(first - 1, last + 2)}
            flux = {}
            for f in range(first, last + 1):
                alpha, beta, gamma = [spread(coef(i, level, f, lanes)) for i in range(3)]
                north = gamma > 0
                behind = jnp.where(north, inter[f - 1], inter[f + 1])
                upwind = jnp.where(north, a[f - 1], a[f])
                flux[f] = alpha * inter[f] + beta * behind + gamma * upwind
                if f > first:
                    store(level, f - 1, lanes, a[f - 1] - (flux[f] - flux[f - 1]))

    lax.fori_loop(0, levels * nj // group, body, 0)


def tile(j):
    return slice(j * LANES, (j + 1) * LANES)


def lon_pass(work, swept, coef, inter, west, flux, lane, finish):
    nj = swept.shape[3] // LANES
    each = range(nj)

    def interfaces(n):
        level, _, at = work[n]
        b = [swept[level, at, :, tile(j)] for j in each]
        w1, w2, e1 = from_west(b, 1, lane), from_west(b, 2, lane), from_east(b, lane)
        for j in each:
            inter[n, :, tile(j)] = 7.0 * (w1[j] + b[j]) - (w2[j] + e1[j])
            west[n, :, tile(j)] = w1[j]

    def fluxes(n):
        level, row, at = work[n]
        mid = [inter[n, :, tile(j)] for j in each]
        w1, e1 = from_west(mid, 1, lane), from_east(mid, lane)
        for j in each:
            alpha, beta, gamma = [spread(coef(i, level, row, tile(j))) for i in range(3)]
            right = gamma > 0
            behind = jnp.where(right, w1[j], e1[j])
            upwind = jnp.where(right, west[n, :, tile(j)], swept[level, at, :, tile(j)])
            flux[n, :, tile(j)] = alpha * mid[j] + beta * behind + gamma * upwind

    def update(n):
        level, _, at = work[n]
        here = [flux[n, :, tile(j)] for j in each]
        e1 = from_east(here, lane)
        return [swept[level, at, :, tile(j)] - (e1[j] - here[j]) for j in each]

    groups = len(work) // BLOCK
    for g in range(groups + 2):
        if g < groups:
            for q in range(BLOCK):
                interfaces(g * BLOCK + q)
        if 1 <= g <= groups:
            for q in range(BLOCK):
                fluxes((g - 1) * BLOCK + q)
        if g >= 2:
            finish(g - 2, [update((g - 2) * BLOCK + q) for q in range(BLOCK)])


def pack_block(block, packed, unit, count, lane):
    me = lax.axis_index("lev")
    nlon = len(block[0]) * LANES
    width, mains, tail, per, size = packed_sizes(nlon, count)
    for d in range(count):
        j0, off = (d * width) // LANES, (d * width) % LANES
        for q, tiles in enumerate(block):
            turned = [pltpu.roll(tiles[j0 + m], LANES - off, 1) if off else tiles[j0 + m]
                      for m in range(mains + (1 if off else 0))]
            for m in range(mains):
                whole = jnp.where(lane < LANES - off, turned[m], turned[m + 1]) if off else turned[m]
                packed[d ^ me, unit, q * mains + m] = whole
        if tail:
            for g in range(-(-BLOCK // per)):
                total = None
                for place in range(min(per, BLOCK - g * per)):
                    shift = (place * tail - off) % LANES
                    source = block[g * per + place][j0 + mains]
                    moved = pltpu.roll(source, shift, 1) if shift else source
                    total = moved if total is None else jnp.where(lane < place * tail, total, moved)
                packed[d ^ me, unit, BLOCK * mains + g] = total


def copy_units(source, target, start=0):
    for unit in range(source.shape[0]):
        for i in range(source.shape[1]):
            target[start + unit, i] = source[unit, i]


def own_coefficients(rows, joined, winds, cx, cy):
    levels, held, nlon = cx.shape[1:]
    keep = jnp.where(lax.axis_index("lat") == 0, 0.0, 1.0)
    for level in range(levels):
        for way in range(2):
            for row in range(rows):
                winds[way, level, row:row + 1, :] = joined[way * rows + row, level:level + 1, :]
        winds[1, level, 0:1, :] = winds[1, level, 0:1, :] * keep
        for way, target in enumerate((cx, cy)):
            for j in range(nlon // LANES):
                parts = coefficients(winds[way, level, :, tile(j)])
                for p in range(3):
                    target[p, level, :, tile(j)] = parts[p]


def put_rows(target, level, at, rows):
    for q, row in enumerate(rows):
        for j, part in enumerate(row):
            target[level, at + q, :, tile(j)] = part


def interior_kernel(count, rows, state, joined, *refs):
    outs, (first, cx, cy, packed, winds, swept, inter, west, flux) = refs[:count], refs[count:]
    levels, nlon = state.shape[0], state.shape[3]
    nj = nlon // LANES
    lane = lane_ids()
    own_coefficients(rows, joined, winds, cx, cy)
    coef_x = lambda i, level, r, lanes: cx[i, level, r:r + 1, lanes]
    coef_y = lambda i, level, f, lanes: cy[i, level, f:f + 1, lanes]

    def put(level, row, lanes, value):
        swept[level, row - REACH, :, lanes] = value

    lat_pass(levels, nj, [(REACH, rows - REACH)], lambda level, r, lanes: state[level, r, :, lanes], coef_y, put)
    work = [(level, row, row - REACH) for level in range(levels) for row in range(REACH, rows - REACH)]

    def keep_first(group, done):
        level, _, at = work[group * BLOCK]
        put_rows(first, level, at, done)

    lon_pass(work, swept, coef_x, inter, west, flux, lane, keep_first)
    lat_pass(levels, nj, [(HALO, rows - HALO)], lambda level, r, lanes: first[level, r - REACH, :, lanes], coef_y, put)
    work_last = [(level, row, row - REACH) for level in range(levels) for row in range(HALO, rows - HALO)]

    def send(group, done):
        pack_block(done, packed, group, count, lane)

    lon_pass(work_last, swept, coef_x, inter, west, flux, lane, send)
    for k in range(count):
        copy_units(packed.at[k], outs[k])


def edge_kernel(count, rows, slot, joint, state, first_round, second_round, first, cx, cy, *refs):
    others = refs[:joint]
    outs, (packed, beyond, swept, edge, inter, west, flux) = refs[-7 - count:-7], refs[-7:]
    nlon = state.shape[3]
    nj = nlon // LANES
    lane = lane_ids()
    odd = lax.axis_index("lat") % 2 == 1

    def halo(south, *at):
        one, two = first_round[(slot,) + at], second_round[at]
        return jnp.where(odd, one, two) if south else jnp.where(odd, two, one)

    for end, south in enumerate((True, False)):
        for j in range(nj):
            parts = coefficients(halo(south, HALO, slice(None), tile(j)))
            for p in range(3):
                beyond[p, end, :, tile(j)] = parts[p]

    def coef_x(i, _, r, lanes):
        if 0 <= r < rows:
            return cx[i, slot, r:r + 1, lanes]
        end, at = (0, r + REACH) if r < 0 else (1, r - rows)
        return beyond[i, end, at:at + 1, lanes]

    def coef_y(i, _, f, lanes):
        if 0 <= f < rows:
            return cy[i, slot, f:f + 1, lanes]
        end, at = (0, f + 2 * REACH + 1) if f < 0 else (1, f - rows + REACH)
        return beyond[i, end, at:at + 1, lanes]

    def cell(_, r, lanes):
        if 0 <= r < rows:
            return state[slot, r, :, lanes]
        return halo(r < 0, r + HALO if r < 0 else r - rows, slice(None), lanes)

    ends = [(-REACH, REACH), (rows - REACH, rows + REACH)]
    ends_last = [(0, HALO), (rows - HALO, rows)]

    def place(row, ranges):
        (a, b), (c, _) = ranges
        return row - a if row < b else row - c + BLOCK

    def cell_first(_, r, lanes):
        if REACH <= r < rows - REACH:
            return first[slot, r - REACH, :, lanes]
        return edge[0, place(r, ends), :, lanes]

    def put(_, row, lanes, value):
        swept[0, place(row, ends), :, lanes] = value

    def put_last(_, row, lanes, value):
        swept[0, place(row, ends_last), :, lanes] = value

    def listed(ranges):
        return [(0, row, place(row, ranges)) for a, b in ranges for row in range(a, b)]

    def keep_edge(group, done):
        put_rows(edge, 0, group * BLOCK, done)

    def send(group, done):
        pack_block(done, packed, group, count, lane)

    lat_pass(1, nj, ends, cell, coef_y, put)
    lon_pass(listed(ends), swept, coef_x, inter, west, flux, lane, keep_edge)
    lat_pass(1, nj, ends_last, cell_first, coef_y, put_last)
    lon_pass(listed(ends_last), swept, coef_x, inter, west, flux, lane, send)
    for k in range(count):
        copy_units(packed.at[k], outs[k])
    for other in others:
        copy_units(other, outs[1], packed.shape[1])


def weights_kernel(weights, source, out):
    targets, rows, taps, width = weights.shape

    for row in range(rows):
        for k in range(targets):
            lowest, highest = max(k - (TAPS - 1), 0), min(k, targets - TAPS)
            w = weights[k, row]
            w = jnp.concatenate([w, jnp.zeros((SUB - taps, width), jnp.float32)], axis=0)
            at = jnp.broadcast_to(source[k, row:row + 1, :], (SUB, width))
            total = w
            for g in range(lowest + 1, highest + 1):
                total = jnp.where(at == g, pltpu.roll(w, g - lowest, 0), total)
            out[k, row] = total


def remap_kernel(count, depth, plan, numbers, counts, *refs):
    chunks, (weights, *ready, out, columns) = refs[:len(plan)], refs[len(plan):]
    me = lax.axis_index("lev")
    for (k, units), chunk in zip(plan, chunks):
        for unit, (slot, number) in enumerate(units):
            if number in numbers:
                for i in range(chunk.shape[1]):
                    columns[(me ^ k) * depth + slot, number, i] = chunk[unit, i]
    first_out = 0 if ready else numbers[0]
    if ready:
        copied = [n for n in range(out.shape[1] // BLOCK) if n not in numbers]
        for k in range(out.shape[0]):
            for row in range(len(copied) * BLOCK):
                out[k, copied[0] * BLOCK + row] = ready[0][k, row]
    targets, _, _, width = out.shape
    _, mains, tail, per, _ = packed_sizes(width * count, count)
    slots = []
    for level in range(targets):
        slot, start = jnp.int32(level), jnp.int32(0)
        for d in range(count):
            slot = jnp.where(level >= start, d * depth + level - start, slot)
            start = start + counts[d]
        slots.append(slot)

    def block(number):
        for q in range(BLOCK):
            row = number * BLOCK + q
            for m in range(mains + (1 if tail else 0)):
                wide = LANES if m < mains else tail
                lanes = slice(m * LANES, m * LANES + wide)
                values = []
                for level in range(targets):
                    if m < mains:
                        values.append(columns[slots[level], number, q * mains + m])
                    else:
                        last = columns[slots[level], number, BLOCK * mains + q // per]
                        shift = (q % per) * tail
                        last = pltpu.roll(last, LANES - shift, 1) if shift else last
                        values.append(last[:, :wide])
                for k in range(targets):
                    lowest, highest = max(k - (TAPS - 1), 0), min(k, targets - TAPS) + TAPS - 1
                    total = None
                    for level in range(lowest, highest + 1):
                        j = level - lowest
                        w = jnp.broadcast_to(weights[k, row, j:j + 1, lanes], (SUB, wide))
                        term = w * values[level]
                        total = term if total is None else total + term
                    out[k, row - first_out * BLOCK, :, lanes] = total

    for number in numbers:
        block(number)


def tiles_of(array):
    lead, levels, nlon = array.shape[:-2], array.shape[-2], array.shape[-1]
    split = array.reshape(lead + (levels, nlon // LANES, LANES))
    order = tuple(range(len(lead))) + (len(lead) + 1, len(lead), len(lead) + 2)
    split = with_layout_constraint(split, Layout(major_to_minor=order))
    return jnp.swapaxes(split, -3, -2).reshape(-1, LANES)


VMEM = pl.BlockSpec(memory_space=pltpu.VMEM)
ANY = pl.BlockSpec(memory_space=pl.ANY)
SMEM = pl.BlockSpec(memory_space=pltpu.SMEM)


def call(kernel, outs, args, specs=None, scratch=(), cost=None):
    return pl.pallas_call(
        kernel,
        out_shape=outs,
        in_specs=specs or [VMEM] * len(args),
        out_specs=jax.tree.map(lambda _: VMEM, outs),
        scratch_shapes=list(scratch),
        compiler_params=pltpu.CompilerParams(vmem_limit_bytes=16 << 20),
        cost_estimate=cost,
    )(*args)


def cost(flops, size):
    return pl.CostEstimate(flops=int(flops), bytes_accessed=int(size), transcendentals=0)


def f32(*shape):
    return jax.ShapeDtypeStruct(shape, jnp.float32)


def shards(tracers, wind_x, wind_y, level_counts, source_level, remap_weight):
    count = lax.axis_size("lev")
    bands = lax.axis_size("lat")
    number, depth, rows, nlon = tracers.shape
    targets, _, width = source_level.shape
    size = packed_sizes(nlon, count)[-1]
    blocks = rows // BLOCK
    inner = (rows - 2 * HALO) // BLOCK

    raw = tiles_of(jnp.transpose(tracers, (0, 2, 1, 3)))
    joined = jnp.concatenate([jnp.transpose(wind_x, (1, 0, 2)), jnp.transpose(wind_y, (1, 0, 2))], axis=0)
    halo = (HALO + 1, number, nlon)
    state, *sent = call(
        functools.partial(prep_kernel, rows),
        [f32(depth, rows, number, nlon), f32(depth, *halo)] + [f32(*halo)] * depth, (raw, joined),
        cost=cost(1, 1))
    first_swap = [(i, i ^ 1) for i in range(bands)]
    second_swap = [(i, i if i in (0, bands - 1) else ((i - 1) ^ 1) + 1) for i in range(bands)]
    first_round = lax.ppermute(sent[0], "lat", first_swap)
    second_rounds = [lax.ppermute(buffer, "lat", second_swap) for buffer in sent[1:]]
    taps = call(
        weights_kernel, f32(targets, rows, SUB, width),
        (jnp.transpose(remap_weight, (1, 2, 0, 3)), source_level),
        cost=cost(1, 1))

    def box(units, *lead):
        return lead + (units, size, SUB, LANES)

    def vmem(*shape):
        return pltpu.VMEM(shape, jnp.float32)

    held = -(-rows // SUB) * SUB
    coef = f32(3, depth, held, nlon)
    swept = vmem(depth, rows - 2 * REACH, number, nlon)
    stage = vmem(depth * (rows - 2 * REACH), number, nlon)
    result = call(
        functools.partial(interior_kernel, count, rows),
        [f32(*box(depth * inner))] * count + [f32(depth, rows - 2 * REACH, number, nlon), coef, coef],
        (state, joined), scratch=[vmem(*box(depth * inner, count)), vmem(2, depth, held, nlon), swept, stage, stage, stage],
        cost=cost(1, 1))
    middle, (first, cx, cy) = result[:count], result[count:]
    plan, chunks = [], []
    swept = vmem(1, 2 * HALO, number, nlon)
    stage = vmem(2 * HALO, number, nlon)

    def edge(slot, joint, after):
        args = (state, first_round, second_rounds[slot], first, cx, cy, *joint, *after)
        units = 2 + (joint[0].shape[0] if joint else 0)
        return call(
            functools.partial(edge_kernel, count, rows, slot, len(joint)),
            [f32(*box(units if k == 1 else 2)) for k in range(count)], args,
            specs=[VMEM] * (len(args) - len(after)) + [ANY] * len(after),
            scratch=[vmem(*box(2, count)), vmem(3, 2, SUB, nlon), swept, swept, stage, stage, stage],
            cost=cost(60 * tracers.size, 8 * tracers.size))

    def swapped(sent, k):
        return lax.ppermute(sent, "lev", [(i, i ^ k) for i in range(count)])

    partners = range(count - 1, 1, -1)
    units = tuple((slot, 1 + b) for slot in range(depth) for b in range(inner))
    plan += [(k, units) for k in partners] + [(0, units)]
    chunks += [swapped(middle[k], k) for k in partners] + [middle[0]]
    after, joint = (taps,), (middle[1],)
    for slot in range(depth):
        own = ((slot, 0), (slot, blocks - 1))
        done = edge(slot, joint, after)
        plan += [(k, own) for k in partners] + [(0, own), (1, own + units if joint else own)]
        chunks += [swapped(done[k], k) for k in partners] + [done[0], swapped(done[1], 1)]
        if slot == 0:
            after, joint, early = (done[0], *chunks[:len(partners)]), (), len(chunks)

    def remap(part, numbers, height, ready):
        args = (level_counts, *chunks[:part], taps, *ready)
        return call(
            functools.partial(remap_kernel, count, depth, tuple(plan[:part]), numbers),
            f32(targets, height, number, width), args,
            specs=[SMEM] + [VMEM] * (len(args) - 1),
            scratch=[vmem(count * depth, blocks, size, SUB, LANES)],
            cost=cost(1, 1))

    middle_rows = remap(early, tuple(range(1, blocks - 1)), inner * BLOCK, ())
    out = remap(len(chunks), (0, blocks - 1), rows, (middle_rows,))
    return jnp.transpose(out, (2, 0, 1, 3))


def solution(mesh):
    in_specs = (
        P(None, "lev", ("groups", "lat"), None),
        P("lev", ("groups", "lat"), None),
        P("lev", ("groups", "lat"), None),
        P(),
        P(None, ("groups", "lat"), "lev"),
        P(None, None, ("groups", "lat"), "lev"),
    )
    out_specs = P(None, None, ("groups", "lat"), "lev")
    return jax.shard_map(shards, mesh=mesh, in_specs=in_specs, out_specs=out_specs, check_vma=False)
```

```python
import functools

import jax
import jax.numpy as jnp
from jax import lax
from jax.experimental import pallas as pl
from jax.experimental.layout import Layout, with_layout_constraint
from jax.experimental.pallas import tpu as pltpu
from jax.sharding import PartitionSpec as P

SUBSTEPS = 2
TAPS = 4
REACH = 3
HALO = REACH * SUBSTEPS
BLOCK = 6
LANES = 128
SUB = 8


def spread(row):
    return jnp.broadcast_to(row, (SUB, LANES))


def lane_ids():
    return lax.broadcasted_iota(jnp.int32, (SUB, LANES), 1)


def from_west(tiles, steps, lane):
    turned = [pltpu.roll(t, steps, 1) for t in tiles]
    return [jnp.where(lane < steps, turned[j - 1], turned[j]) for j in range(len(tiles))]


def from_east(tiles, lane):
    turned = [pltpu.roll(t, LANES - 1, 1) for t in tiles]
    count = len(tiles)
    return [jnp.where(lane == LANES - 1, turned[(j + 1) % count], turned[j]) for j in range(count)]


def coefficients(wind):
    size = jnp.abs(wind)
    rest = 1.0 - size
    alpha = wind * rest * rest * (1.0 / 12.0)
    beta = wind * size * rest * (-1.0 / 12.0)
    gamma = wind * size * (3.0 - 2.0 * size)
    return alpha, beta, gamma


def packed_sizes(nlon, count):
    width = nlon // count
    mains, tail = width // LANES, width % LANES
    per = LANES // tail if tail else 1
    tails = -(-BLOCK // per) if tail else 0
    return width, mains, tail, per, BLOCK * mains + tails


def prep_kernel(rows, tracers, winds, state, first_round, *second_rounds):
    levels, nlon = state.shape[0], state.shape[3]
    nj = nlon // LANES
    row_stride = nj * levels
    tracer_stride = rows * row_stride
    band, bands = lax.axis_index("lat"), lax.axis_size("lat")
    even = band % 2 == 0
    alone = (band == 0) | (band == bands - 1)
    keep = jnp.where(alone, 0.0, 1.0)

    def body(row, _):
        for level in range(levels):
            for j in range(nj):
                start = row * row_stride + j * levels + level
                state[level, row, :, tile(j)] = tracers[pl.ds(start, SUB, stride=tracer_stride), :]
        return 0

    lax.fori_loop(0, rows, body, 0)
    for level in range(levels):
        for target, north, scale in ((first_round.at[level], even, None), (second_rounds[level], jnp.logical_not(even), keep)):
            scaled = (lambda v: v) if scale is None else (lambda v: v * scale)
            row_t = jnp.where(north, rows - HALO, 0)
            row_x = jnp.where(north, rows - REACH, 0)
            row_y = jnp.where(north, rows - REACH - 1, 0)
            for row in range(HALO):
                target[row] = scaled(state[level, row_t + row])
            for q in range(REACH):
                target[HALO, q:q + 1, :] = scaled(winds[row_x + q, level:level + 1, :])
            for q in range(REACH + 1):
                target[HALO, REACH + q:REACH + q + 1, :] = scaled(winds[rows + row_y + q, level:level + 1, :])


def lat_pass(levels, nj, ranges, cell, coef, store):
    group = 3 if nj % 3 == 0 else 1

    def body(i, _):
        level = i // (nj // group)
        results = []
        for u in range(group):
            lanes = pl.ds(pl.multiple_of(((i % (nj // group)) * group + u) * LANES, LANES), LANES)
            results += [(level, row, lanes, value) for row, value in one(level, lanes)]
        for result in results:
            store(*result)
        return 0

    def one(level, lanes):
        results = []
        for first, last in ranges:
            a = {r: cell(level, r, lanes) for r in range(first - REACH, last + REACH)}
            inter = {f: 7.0 * (a[f - 1] + a[f]) - (a[f - 2] + a[f + 1]) for f in range(first - 1, last + 2)}
            flux = {}
            for f in range(first, last + 1):
                alpha, beta, gamma = [spread(coef(i, level, f, lanes)) for i in range(3)]
                north = gamma > 0
                behind = jnp.where(north, inter[f - 1], inter[f + 1])
                upwind = jnp.where(north, a[f - 1], a[f])
                flux[f] = alpha * inter[f] + beta * behind + gamma * upwind
                if f > first:
                    results.append((f - 1, a[f - 1] - (flux[f] - flux[f - 1])))
        return results

    lax.fori_loop(0, levels * nj // group, body, 0)


def tile(j):
    return slice(j * LANES, (j + 1) * LANES)


def lon_pass(work, swept, coef, inter, west, flux, lane, finish):
    nj = swept.shape[3] // LANES
    each = range(nj)

    def interfaces(n):
        level, _, at = work[n]
        b = [swept[level, at, :, tile(j)] for j in each]
        w1, w2, e1 = from_west(b, 1, lane), from_west(b, 2, lane), from_east(b, lane)
        for j in each:
            inter[n, :, tile(j)] = 7.0 * (w1[j] + b[j]) - (w2[j] + e1[j])
            west[n, :, tile(j)] = w1[j]

    def fluxes(n):
        level, row, at = work[n]
        mid = [inter[n, :, tile(j)] for j in each]
        w1, e1 = from_west(mid, 1, lane), from_east(mid, lane)
        for j in each:
            alpha, beta, gamma = [spread(coef(i, level, row, tile(j))) for i in range(3)]
            right = gamma > 0
            behind = jnp.where(right, w1[j], e1[j])
            upwind = jnp.where(right, west[n, :, tile(j)], swept[level, at, :, tile(j)])
            flux[n, :, tile(j)] = alpha * mid[j] + beta * behind + gamma * upwind

    def update(n):
        level, _, at = work[n]
        here = [flux[n, :, tile(j)] for j in each]
        e1 = from_east(here, lane)
        return [swept[level, at, :, tile(j)] - (e1[j] - here[j]) for j in each]

    groups = len(work) // BLOCK
    for g in range(groups + 2):
        if g < groups:
            for q in range(BLOCK):
                interfaces(g * BLOCK + q)
        if 1 <= g <= groups:
            for q in range(BLOCK):
                fluxes((g - 1) * BLOCK + q)
        if g >= 2:
            finish(g - 2, [update((g - 2) * BLOCK + q) for q in range(BLOCK)])


def pack_block(block, packed, unit, count, lane):
    nlon = len(block[0]) * LANES
    width, mains, tail, per, size = packed_sizes(nlon, count)
    for d in range(count):
        j0, off = (d * width) // LANES, (d * width) % LANES
        for q, tiles in enumerate(block):
            turned = [pltpu.roll(tiles[j0 + m], LANES - off, 1) if off else tiles[j0 + m]
                      for m in range(mains + (1 if off else 0))]
            for m in range(mains):
                whole = jnp.where(lane < LANES - off, turned[m], turned[m + 1]) if off else turned[m]
                packed[d, unit, q * mains + m] = whole
        if tail:
            for g in range(-(-BLOCK // per)):
                total = None
                for place in range(min(per, BLOCK - g * per)):
                    shift = (place * tail - off) % LANES
                    source = block[g * per + place][j0 + mains]
                    moved = pltpu.roll(source, shift, 1) if shift else source
                    total = moved if total is None else jnp.where(lane < place * tail, total, moved)
                packed[d, unit, BLOCK * mains + g] = total


def copy_tiles(pairs):
    values = [source[at] for (source, at), _ in pairs]
    for value, (_, (target, at)) in zip(values, pairs):
        target[at] = value


def copy_units(source, target, start=0):
    for unit in range(source.shape[0]):
        copy_tiles([((source, (unit, i)), (target, (start + unit, i))) for i in range(source.shape[1])])


def hand_out(packed, outs):
    me = lax.axis_index("lev")
    for k, out in enumerate(outs):
        copy_units(packed.at[me ^ k], out)


def own_coefficients(rows, joined, winds, cx, cy):
    levels, held, nlon = cx.shape[1:]
    keep = jnp.where(lax.axis_index("lat") == 0, 0.0, 1.0)
    for level in range(levels):
        for way in range(2):
            for row in range(rows):
                winds[way, level, row:row + 1, :] = joined[way * rows + row, level:level + 1, :]
        winds[1, level, 0:1, :] = winds[1, level, 0:1, :] * keep
        for way, target in enumerate((cx, cy)):
            for j in range(nlon // LANES):
                parts = coefficients(winds[way, level, :, tile(j)])
                for p in range(3):
                    target[p, level, :, tile(j)] = parts[p]


def put_rows(target, level, at, rows):
    for q, row in enumerate(rows):
        for j, part in enumerate(row):
            target[level, at + q, :, tile(j)] = part


def interior_kernel(count, rows, state, joined, *refs):
    outs, (first, cx, cy, packed, winds, swept, inter, west, flux) = refs[:count], refs[count:]
    levels, nlon = state.shape[0], state.shape[3]
    nj = nlon // LANES
    lane = lane_ids()
    own_coefficients(rows, joined, winds, cx, cy)
    coef_x = lambda i, level, r, lanes: cx[i, level, r:r + 1, lanes]
    coef_y = lambda i, level, f, lanes: cy[i, level, f:f + 1, lanes]

    def put(level, row, lanes, value):
        swept[level, row - REACH, :, lanes] = value

    lat_pass(levels, nj, [(REACH, rows - REACH)], lambda level, r, lanes: state[level, r, :, lanes], coef_y, put)
    work = [(level, row, row - REACH) for level in range(levels) for row in range(REACH, rows - REACH)]

    def keep_first(group, done):
        level, _, at = work[group * BLOCK]
        put_rows(first, level, at, done)

    lon_pass(work, swept, coef_x, inter, west, flux, lane, keep_first)
    lat_pass(levels, nj, [(HALO, rows - HALO)], lambda level, r, lanes: first[level, r - REACH, :, lanes], coef_y, put)
    work_last = [(level, row, row - REACH) for level in range(levels) for row in range(HALO, rows - HALO)]

    def send(group, done):
        pack_block(done, packed, group, count, lane)

    lon_pass(work_last, swept, coef_x, inter, west, flux, lane, send)
    hand_out(packed, outs)


def edge_kernel(count, rows, slot, joint, state, first_round, second_round, first, cx, cy, *refs):
    others = refs[:joint]
    outs, (packed, beyond, swept, edge, inter, west, flux) = refs[-7 - count:-7], refs[-7:]
    nlon = state.shape[3]
    nj = nlon // LANES
    lane = lane_ids()
    odd = lax.axis_index("lat") % 2 == 1

    def halo(south, *at):
        one, two = first_round[(slot,) + at], second_round[at]
        return jnp.where(odd, one, two) if south else jnp.where(odd, two, one)

    for end, south in enumerate((True, False)):
        for j in range(nj):
            parts = coefficients(halo(south, HALO, slice(None), tile(j)))
            for p in range(3):
                beyond[p, end, :, tile(j)] = parts[p]

    def coef_x(i, _, r, lanes):
        if 0 <= r < rows:
            return cx[i, slot, r:r + 1, lanes]
        end, at = (0, r + REACH) if r < 0 else (1, r - rows)
        return beyond[i, end, at:at + 1, lanes]

    def coef_y(i, _, f, lanes):
        if 0 <= f < rows:
            return cy[i, slot, f:f + 1, lanes]
        end, at = (0, f + 2 * REACH + 1) if f < 0 else (1, f - rows + REACH)
        return beyond[i, end, at:at + 1, lanes]

    def cell(_, r, lanes):
        if 0 <= r < rows:
            return state[slot, r, :, lanes]
        return halo(r < 0, r + HALO if r < 0 else r - rows, slice(None), lanes)

    ends = [(-REACH, REACH), (rows - REACH, rows + REACH)]
    ends_last = [(0, HALO), (rows - HALO, rows)]

    def place(row, ranges):
        (a, b), (c, _) = ranges
        return row - a if row < b else row - c + BLOCK

    def cell_first(_, r, lanes):
        if REACH <= r < rows - REACH:
            return first[slot, r - REACH, :, lanes]
        return edge[0, place(r, ends), :, lanes]

    def put(_, row, lanes, value):
        swept[0, place(row, ends), :, lanes] = value

    def put_last(_, row, lanes, value):
        swept[0, place(row, ends_last), :, lanes] = value

    def listed(ranges):
        return [(0, row, place(row, ranges)) for a, b in ranges for row in range(a, b)]

    def keep_edge(group, done):
        put_rows(edge, 0, group * BLOCK, done)

    def send(group, done):
        pack_block(done, packed, group, count, lane)

    lat_pass(1, nj, ends, cell, coef_y, put)
    lon_pass(listed(ends), swept, coef_x, inter, west, flux, lane, keep_edge)
    lat_pass(1, nj, ends_last, cell_first, coef_y, put_last)
    lon_pass(listed(ends_last), swept, coef_x, inter, west, flux, lane, send)
    hand_out(packed, outs)
    for other in others:
        copy_units(other, outs[1], packed.shape[1])


def weights_kernel(weights, source, out):
    targets, rows, taps, width = weights.shape

    for row in range(rows):
        for k in range(targets):
            lowest, highest = max(k - (TAPS - 1), 0), min(k, targets - TAPS)
            w = weights[k, row]
            w = jnp.concatenate([w, jnp.zeros((SUB - taps, width), jnp.float32)], axis=0)
            at = jnp.broadcast_to(source[k, row:row + 1, :], (SUB, width))
            total = w
            for g in range(lowest + 1, highest + 1):
                total = jnp.where(at == g, pltpu.roll(w, g - lowest, 0), total)
            out[k, row] = total


def remap_kernel(count, plan, numbers, counts, *refs):
    chunks, (weights, *ready, out, levels, result, sems) = refs[:len(plan)], refs[len(plan):]
    me = lax.axis_index("lev")
    targets, _, _, width = result.shape
    _, mains, tail, per, _ = packed_sizes(width * count, count)
    copies = []

    def leave(source, target):
        copy = pltpu.make_async_copy(source, target, sems.at[len(copies)])
        copy.start()
        copies.append(copy)

    if ready:
        others = [n for n in range(out.shape[1] // BLOCK) if n not in numbers]
        leave(ready[0], out.at[:, pl.ds(others[0] * BLOCK, len(others) * BLOCK)])

    def level_of(k, slot):
        d = me ^ k
        start = jnp.int32(0)
        for e in range(count):
            start = start + jnp.where(e < d, counts[e], 0)
        return jnp.where(slot < counts[d], start + slot, targets)

    for (k, units), chunk in zip(plan, chunks):
        for unit, (slot, number) in enumerate(units):
            if number in numbers:
                at = numbers.index(number)
                copy_tiles([((chunk, (unit, i)), (levels, (level_of(k, slot), at, i))) for i in range(chunk.shape[1])])

    for at, number in enumerate(numbers):
        for q in range(BLOCK):
            row = number * BLOCK + q
            for m in range(mains + (1 if tail else 0)):
                wide = LANES if m < mains else tail
                lanes = slice(m * LANES, m * LANES + wide)
                values = []
                for level in range(targets):
                    if m < mains:
                        values.append(levels[level, at, q * mains + m])
                    else:
                        last = levels[level, at, BLOCK * mains + q // per]
                        shift = (q % per) * tail
                        values.append(pltpu.roll(last, LANES - shift, 1) if shift else last)
                for k in range(targets):
                    lowest, highest = max(k - (TAPS - 1), 0), min(k, targets - TAPS) + TAPS - 1
                    total = None
                    for level in range(lowest, highest + 1):
                        j = level - lowest
                        term = jnp.broadcast_to(weights[k, row, j:j + 1, lanes], (SUB, wide)) * values[level][:, :wide]
                        total = term if total is None else total + term
                    result[k, at * BLOCK + q, :, lanes] = total
        if ready:
            leave(result.at[:, pl.ds(at * BLOCK, BLOCK)], out.at[:, pl.ds(number * BLOCK, BLOCK)])
    if not ready:
        leave(result, out)
    for copy in copies:
        copy.wait()


def tiles_of(array):
    lead, levels, nlon = array.shape[:-2], array.shape[-2], array.shape[-1]
    split = array.reshape(lead + (levels, nlon // LANES, LANES))
    order = tuple(range(len(lead))) + (len(lead) + 1, len(lead), len(lead) + 2)
    split = with_layout_constraint(split, Layout(major_to_minor=order))
    return jnp.swapaxes(split, -3, -2).reshape(-1, LANES)


VMEM = pl.BlockSpec(memory_space=pltpu.VMEM)
ANY = pl.BlockSpec(memory_space=pl.ANY)
SMEM = pl.BlockSpec(memory_space=pltpu.SMEM)


def call(kernel, outs, args, specs=None, scratch=(), cost=None):
    return pl.pallas_call(
        kernel,
        out_shape=outs,
        in_specs=specs or [VMEM] * len(args),
        out_specs=jax.tree.map(lambda _: VMEM, outs),
        scratch_shapes=list(scratch),
        compiler_params=pltpu.CompilerParams(vmem_limit_bytes=16 << 20),
        cost_estimate=cost,
    )(*args)


def cost(flops, size):
    return pl.CostEstimate(flops=int(flops), bytes_accessed=int(size), transcendentals=0)


def f32(*shape):
    return jax.ShapeDtypeStruct(shape, jnp.float32)


def shards(tracers, wind_x, wind_y, level_counts, source_level, remap_weight):
    count = lax.axis_size("lev")
    bands = lax.axis_size("lat")
    number, depth, rows, nlon = tracers.shape
    targets, _, width = source_level.shape
    size = packed_sizes(nlon, count)[-1]
    blocks = rows // BLOCK
    inner = (rows - 2 * HALO) // BLOCK

    raw = tiles_of(jnp.transpose(tracers, (0, 2, 1, 3)))
    joined = jnp.concatenate([jnp.transpose(wind_x, (1, 0, 2)), jnp.transpose(wind_y, (1, 0, 2))], axis=0)
    halo = (HALO + 1, number, nlon)
    state, *sent = call(
        functools.partial(prep_kernel, rows),
        [f32(depth, rows, number, nlon), f32(depth, *halo)] + [f32(*halo)] * depth, (raw, joined),
        cost=cost(1, 1))
    first_swap = [(i, i ^ 1) for i in range(bands)]
    second_swap = [(i, i if i in (0, bands - 1) else ((i - 1) ^ 1) + 1) for i in range(bands)]
    first_round = lax.ppermute(sent[0], "lat", first_swap)
    second_rounds = [lax.ppermute(buffer, "lat", second_swap) for buffer in sent[1:]]
    taps = call(
        weights_kernel, f32(targets, rows, SUB, width),
        (jnp.transpose(remap_weight, (1, 2, 0, 3)), source_level),
        cost=cost(1, 1))

    def box(units, *lead):
        return lead + (units, size, SUB, LANES)

    def vmem(*shape):
        return pltpu.VMEM(shape, jnp.float32)

    held = -(-rows // SUB) * SUB
    coef = f32(3, depth, held, nlon)
    swept = vmem(depth, rows - 2 * REACH, number, nlon)
    stage = vmem(depth * (rows - 2 * REACH), number, nlon)
    result = call(
        functools.partial(interior_kernel, count, rows),
        [f32(*box(depth * inner))] * count + [f32(depth, rows - 2 * REACH, number, nlon), coef, coef],
        (state, joined), scratch=[vmem(*box(depth * inner, count)), vmem(2, depth, held, nlon), swept, stage, stage, stage],
        cost=cost(1, 1))
    middle, (first, cx, cy) = result[:count], result[count:]
    plan, chunks = [], []
    swept = vmem(1, 2 * HALO, number, nlon)
    stage = vmem(2 * HALO, number, nlon)

    def edge(slot, joint, after):
        args = (state, first_round, second_rounds[slot], first, cx, cy, *joint, *after)
        units = 2 + (joint[0].shape[0] if joint else 0)
        return call(
            functools.partial(edge_kernel, count, rows, slot, len(joint)),
            [f32(*box(units if k == 1 else 2)) for k in range(count)], args,
            specs=[VMEM] * (len(args) - len(after)) + [ANY] * len(after),
            scratch=[vmem(*box(2, count)), vmem(3, 2, SUB, nlon), swept, swept, stage, stage, stage],
            cost=cost(60 * tracers.size, 8 * tracers.size))

    def swapped(sent, k):
        return lax.ppermute(sent, "lev", [(i, i ^ k) for i in range(count)])

    partners = range(count - 1, 1, -1)
    units = tuple((slot, 1 + b) for slot in range(depth) for b in range(inner))
    plan += [(k, units) for k in partners] + [(0, units)]
    chunks += [swapped(middle[k], k) for k in partners] + [middle[0]]
    after, joint = (taps,), (middle[1],)
    for slot in range(depth):
        own = ((slot, 0), (slot, blocks - 1))
        done = edge(slot, joint, after)
        plan += [(k, own) for k in partners] + [(0, own), (1, own + units if joint else own)]
        chunks += [swapped(done[k], k) for k in partners] + [done[0], swapped(done[1], 1)]
        if slot == 0:
            after, joint, early = (done[0], *chunks[:len(partners)]), (), len(chunks)

    def remap(part, numbers, height, ready):
        args = (level_counts, *chunks[:part], taps, *ready)
        return pl.pallas_call(
            functools.partial(remap_kernel, count, tuple(plan[:part]), numbers),
            out_shape=f32(targets, height, number, width),
            in_specs=[SMEM] + [VMEM] * (len(args) - 1),
            out_specs=ANY,
            scratch_shapes=[
                vmem(targets + 1, len(numbers), size, SUB, LANES),
                vmem(targets, len(numbers) * BLOCK, number, width),
                pltpu.SemaphoreType.DMA((len(numbers) + 1,)),
            ],
            compiler_params=pltpu.CompilerParams(vmem_limit_bytes=16 << 20),
            cost_estimate=cost(1, 1),
        )(*args)

    middle_rows = remap(early, tuple(range(1, blocks - 1)), inner * BLOCK, ())
    out = remap(len(chunks), (0, blocks - 1), rows, (middle_rows,))
    return jnp.transpose(out, (2, 0, 1, 3))


def solution(mesh):
    in_specs = (
        P(None, "lev", ("groups", "lat"), None),
        P("lev", ("groups", "lat"), None),
        P("lev", ("groups", "lat"), None),
        P(),
        P(None, ("groups", "lat"), "lev"),
        P(None, None, ("groups", "lat"), "lev"),
    )
    out_specs = P(None, None, ("groups", "lat"), "lev")
    return jax.shard_map(shards, mesh=mesh, in_specs=in_specs, out_specs=out_specs, check_vma=False)
```

```python
import functools

import jax
import jax.numpy as jnp
from jax import lax
from jax.experimental import pallas as pl
from jax.experimental.layout import Layout, with_layout_constraint
from jax.experimental.pallas import tpu as pltpu
from jax.sharding import PartitionSpec as P

SUBSTEPS = 2
TAPS = 4
REACH = 3
HALO = REACH * SUBSTEPS
BLOCK = 6
LANES = 128
SUB = 8


def spread(row):
    return jnp.broadcast_to(row, (SUB, LANES))


def lane_ids():
    return lax.broadcasted_iota(jnp.int32, (SUB, LANES), 1)


def from_west(tiles, steps, lane):
    turned = [pltpu.roll(t, steps, 1) for t in tiles]
    return [jnp.where(lane < steps, turned[j - 1], turned[j]) for j in range(len(tiles))]


def from_east(tiles, lane):
    turned = [pltpu.roll(t, LANES - 1, 1) for t in tiles]
    count = len(tiles)
    return [jnp.where(lane == LANES - 1, turned[(j + 1) % count], turned[j]) for j in range(count)]


def coefficients(wind):
    size = jnp.abs(wind)
    rest = 1.0 - size
    alpha = wind * rest * rest * (1.0 / 12.0)
    beta = wind * size * rest * (-1.0 / 12.0)
    gamma = wind * size * (3.0 - 2.0 * size)
    return alpha, beta, gamma


def packed_sizes(nlon, count):
    width = nlon // count
    mains, tail = width // LANES, width % LANES
    per = LANES // tail if tail else 1
    tails = -(-BLOCK // per) if tail else 0
    return width, mains, tail, per, BLOCK * mains + tails


def fill_halos(rows, slot, state, winds, first_round, second_round):
    band, bands = lax.axis_index("lat"), lax.axis_size("lat")
    even = band % 2 == 0
    keep = jnp.where((band == 0) | (band == bands - 1), 0.0, 1.0)
    for target, north, scale in ((first_round, even, None), (second_round, jnp.logical_not(even), keep)):
        scaled = (lambda v: v) if scale is None else (lambda v: v * scale)
        row_t = jnp.where(north, rows - HALO, 0)
        row_x = jnp.where(north, rows - REACH, 0)
        row_y = jnp.where(north, rows - REACH - 1, 0)
        for row in range(HALO):
            target[row] = scaled(state[slot, row_t + row])
        for q in range(REACH):
            target[HALO, q:q + 1, :] = scaled(winds[row_x + q, slot:slot + 1, :])
        for q in range(REACH + 1):
            target[HALO, REACH + q:REACH + q + 1, :] = scaled(winds[rows + row_y + q, slot:slot + 1, :])


def prep_kernel(rows, tracers, winds, state, first_round, second_round):
    levels, nlon = state.shape[0], state.shape[3]
    nj = nlon // LANES
    row_stride = nj * levels
    tracer_stride = rows * row_stride

    def body(row, _):
        for level in range(levels):
            for j in range(nj):
                start = row * row_stride + j * levels + level
                state[level, row, :, tile(j)] = tracers[pl.ds(start, SUB, stride=tracer_stride), :]
        return 0

    lax.fori_loop(0, rows, body, 0)
    fill_halos(rows, 0, state, winds, first_round, second_round)


def lat_pass(levels, nj, ranges, cell, coef, store):
    group = 3 if nj % 3 == 0 else 1

    def body(i, _):
        level = i // (nj // group)
        results = []
        for u in range(group):
            lanes = pl.ds(pl.multiple_of(((i % (nj // group)) * group + u) * LANES, LANES), LANES)
            results += [(level, row, lanes, value) for row, value in one(level, lanes)]
        for result in results:
            store(*result)
        return 0

    def one(level, lanes):
        results = []
        for first, last in ranges:
            a = {r: cell(level, r, lanes) for r in range(first - REACH, last + REACH)}
            inter = {f: 7.0 * (a[f - 1] + a[f]) - (a[f - 2] + a[f + 1]) for f in range(first - 1, last + 2)}
            flux = {}
            for f in range(first, last + 1):
                alpha, beta, gamma = [spread(coef(i, level, f, lanes)) for i in range(3)]
                north = gamma > 0
                behind = jnp.where(north, inter[f - 1], inter[f + 1])
                upwind = jnp.where(north, a[f - 1], a[f])
                flux[f] = alpha * inter[f] + beta * behind + gamma * upwind
                if f > first:
                    results.append((f - 1, a[f - 1] - (flux[f] - flux[f - 1])))
        return results

    lax.fori_loop(0, levels * nj // group, body, 0)


def tile(j):
    return slice(j * LANES, (j + 1) * LANES)


def lon_pass(work, swept, coef, inter, west, flux, lane, finish):
    nj = swept.shape[3] // LANES
    each = range(nj)

    def interfaces(n):
        level, _, at = work[n]
        b = [swept[level, at, :, tile(j)] for j in each]
        w1, w2, e1 = from_west(b, 1, lane), from_west(b, 2, lane), from_east(b, lane)
        for j in each:
            inter[n, :, tile(j)] = 7.0 * (w1[j] + b[j]) - (w2[j] + e1[j])
            west[n, :, tile(j)] = w1[j]

    def fluxes(n):
        level, row, at = work[n]
        mid = [inter[n, :, tile(j)] for j in each]
        w1, e1 = from_west(mid, 1, lane), from_east(mid, lane)
        for j in each:
            alpha, beta, gamma = [spread(coef(i, level, row, tile(j))) for i in range(3)]
            right = gamma > 0
            behind = jnp.where(right, w1[j], e1[j])
            upwind = jnp.where(right, west[n, :, tile(j)], swept[level, at, :, tile(j)])
            flux[n, :, tile(j)] = alpha * mid[j] + beta * behind + gamma * upwind

    def update(n):
        level, _, at = work[n]
        here = [flux[n, :, tile(j)] for j in each]
        e1 = from_east(here, lane)
        return [swept[level, at, :, tile(j)] - (e1[j] - here[j]) for j in each]

    groups = len(work) // BLOCK
    for g in range(groups + 2):
        if g < groups:
            for q in range(BLOCK):
                interfaces(g * BLOCK + q)
        if 1 <= g <= groups:
            for q in range(BLOCK):
                fluxes((g - 1) * BLOCK + q)
        if g >= 2:
            finish(g - 2, [update((g - 2) * BLOCK + q) for q in range(BLOCK)])


def pack_block(block, packed, unit, count, lane):
    nlon = len(block[0]) * LANES
    width, mains, tail, per, size = packed_sizes(nlon, count)
    for d in range(count):
        j0, off = (d * width) // LANES, (d * width) % LANES
        for q, tiles in enumerate(block):
            turned = [pltpu.roll(tiles[j0 + m], LANES - off, 1) if off else tiles[j0 + m]
                      for m in range(mains + (1 if off else 0))]
            for m in range(mains):
                whole = jnp.where(lane < LANES - off, turned[m], turned[m + 1]) if off else turned[m]
                packed[d, unit, q * mains + m] = whole
        if tail:
            for g in range(-(-BLOCK // per)):
                total = None
                for place in range(min(per, BLOCK - g * per)):
                    shift = (place * tail - off) % LANES
                    source = block[g * per + place][j0 + mains]
                    moved = pltpu.roll(source, shift, 1) if shift else source
                    total = moved if total is None else jnp.where(lane < place * tail, total, moved)
                packed[d, unit, BLOCK * mains + g] = total


def copy_tiles(pairs):
    values = [source[at] for (source, at), _ in pairs]
    for value, (_, (target, at)) in zip(values, pairs):
        target[at] = value


def copy_units(source, target, start=0):
    for unit in range(source.shape[0]):
        copy_tiles([((source, (unit, i)), (target, (start + unit, i))) for i in range(source.shape[1])])


def hand_out(packed, outs):
    me = lax.axis_index("lev")
    for k, out in enumerate(outs):
        copy_units(packed.at[me ^ k], out)


def own_coefficients(rows, joined, winds, cx, cy):
    levels, held, nlon = cx.shape[1:]
    keep = jnp.where(lax.axis_index("lat") == 0, 0.0, 1.0)
    for level in range(levels):
        for way in range(2):
            for row in range(rows):
                winds[way, level, row:row + 1, :] = joined[way * rows + row, level:level + 1, :]
        winds[1, level, 0:1, :] = winds[1, level, 0:1, :] * keep
        for way, target in enumerate((cx, cy)):
            for j in range(nlon // LANES):
                parts = coefficients(winds[way, level, :, tile(j)])
                for p in range(3):
                    target[p, level, :, tile(j)] = parts[p]


def put_rows(target, level, at, rows):
    for q, row in enumerate(rows):
        for j, part in enumerate(row):
            target[level, at + q, :, tile(j)] = part


def interior_kernel(count, rows, state, joined, *refs):
    outs, (first, cx, cy), refs = refs[:count], refs[count:count + 3], refs[count + 3:]
    halos, (packed, winds, swept, inter, west, flux) = refs[:-6], refs[-6:]
    levels, nlon = state.shape[0], state.shape[3]
    nj = nlon // LANES
    lane = lane_ids()
    for slot in range(1, levels):
        fill_halos(rows, slot, state, joined, *halos[2 * slot - 2:2 * slot])
    own_coefficients(rows, joined, winds, cx, cy)
    coef_x = lambda i, level, r, lanes: cx[i, level, r:r + 1, lanes]
    coef_y = lambda i, level, f, lanes: cy[i, level, f:f + 1, lanes]

    def put(level, row, lanes, value):
        swept[level, row - REACH, :, lanes] = value

    lat_pass(levels, nj, [(REACH, rows - REACH)], lambda level, r, lanes: state[level, r, :, lanes], coef_y, put)
    work = [(level, row, row - REACH) for level in range(levels) for row in range(REACH, rows - REACH)]

    def keep_first(group, done):
        level, _, at = work[group * BLOCK]
        put_rows(first, level, at, done)

    lon_pass(work, swept, coef_x, inter, west, flux, lane, keep_first)
    lat_pass(levels, nj, [(HALO, rows - HALO)], lambda level, r, lanes: first[level, r - REACH, :, lanes], coef_y, put)
    work_last = [(level, row, row - REACH) for level in range(levels) for row in range(HALO, rows - HALO)]

    def send(group, done):
        pack_block(done, packed, group, count, lane)

    lon_pass(work_last, swept, coef_x, inter, west, flux, lane, send)
    hand_out(packed, outs)


def edge_kernel(count, rows, slot, joint, state, first_round, second_round, first, cx, cy, *refs):
    others = refs[:joint]
    outs, (packed, beyond, swept, edge, inter, west, flux) = refs[-7 - count:-7], refs[-7:]
    nlon = state.shape[3]
    nj = nlon // LANES
    lane = lane_ids()
    odd = lax.axis_index("lat") % 2 == 1

    def halo(south, *at):
        one, two = first_round[at], second_round[at]
        return jnp.where(odd, one, two) if south else jnp.where(odd, two, one)

    for end, south in enumerate((True, False)):
        for j in range(nj):
            parts = coefficients(halo(south, HALO, slice(None), tile(j)))
            for p in range(3):
                beyond[p, end, :, tile(j)] = parts[p]

    def coef_x(i, _, r, lanes):
        if 0 <= r < rows:
            return cx[i, slot, r:r + 1, lanes]
        end, at = (0, r + REACH) if r < 0 else (1, r - rows)
        return beyond[i, end, at:at + 1, lanes]

    def coef_y(i, _, f, lanes):
        if 0 <= f < rows:
            return cy[i, slot, f:f + 1, lanes]
        end, at = (0, f + 2 * REACH + 1) if f < 0 else (1, f - rows + REACH)
        return beyond[i, end, at:at + 1, lanes]

    def cell(_, r, lanes):
        if 0 <= r < rows:
            return state[slot, r, :, lanes]
        return halo(r < 0, r + HALO if r < 0 else r - rows, slice(None), lanes)

    ends = [(-REACH, REACH), (rows - REACH, rows + REACH)]
    ends_last = [(0, HALO), (rows - HALO, rows)]

    def place(row, ranges):
        (a, b), (c, _) = ranges
        return row - a if row < b else row - c + BLOCK

    def cell_first(_, r, lanes):
        if REACH <= r < rows - REACH:
            return first[slot, r - REACH, :, lanes]
        return edge[0, place(r, ends), :, lanes]

    def put(_, row, lanes, value):
        swept[0, place(row, ends), :, lanes] = value

    def put_last(_, row, lanes, value):
        swept[0, place(row, ends_last), :, lanes] = value

    def listed(ranges):
        return [(0, row, place(row, ranges)) for a, b in ranges for row in range(a, b)]

    def keep_edge(group, done):
        put_rows(edge, 0, group * BLOCK, done)

    def send(group, done):
        pack_block(done, packed, group, count, lane)

    lat_pass(1, nj, ends, cell, coef_y, put)
    lon_pass(listed(ends), swept, coef_x, inter, west, flux, lane, keep_edge)
    lat_pass(1, nj, ends_last, cell_first, coef_y, put_last)
    lon_pass(listed(ends_last), swept, coef_x, inter, west, flux, lane, send)
    hand_out(packed, outs)
    for other in others:
        copy_units(other, outs[1], packed.shape[1])


def weights_kernel(weights, source, out):
    targets, rows, taps, width = weights.shape

    for row in range(rows):
        for k in range(targets):
            lowest, highest = max(k - (TAPS - 1), 0), min(k, targets - TAPS)
            w = weights[k, row]
            w = jnp.concatenate([w, jnp.zeros((SUB - taps, width), jnp.float32)], axis=0)
            at = jnp.broadcast_to(source[k, row:row + 1, :], (SUB, width))
            total = w
            for g in range(lowest + 1, highest + 1):
                total = jnp.where(at == g, pltpu.roll(w, g - lowest, 0), total)
            out[k, row] = total


def remap_kernel(count, plan, numbers, counts, *refs):
    chunks, (weights, *ready, out, levels, result, sems) = refs[:len(plan)], refs[len(plan):]
    me = lax.axis_index("lev")
    targets, _, _, width = result.shape
    _, mains, tail, per, _ = packed_sizes(width * count, count)
    copies = []

    def leave(source, target):
        copy = pltpu.make_async_copy(source, target, sems.at[len(copies)])
        copy.start()
        copies.append(copy)

    if ready:
        others = [n for n in range(out.shape[1] // BLOCK) if n not in numbers]
        leave(ready[0], out.at[:, pl.ds(others[0] * BLOCK, len(others) * BLOCK)])

    def level_of(k, slot):
        d = me ^ k
        start = jnp.int32(0)
        for e in range(count):
            start = start + jnp.where(e < d, counts[e], 0)
        return jnp.where(slot < counts[d], start + slot, targets)

    for (k, units), chunk in zip(plan, chunks):
        for unit, (slot, number) in enumerate(units):
            if number in numbers:
                at = numbers.index(number)
                copy_tiles([((chunk, (unit, i)), (levels, (level_of(k, slot), at, i))) for i in range(chunk.shape[1])])

    for at, number in enumerate(numbers):
        for q in range(BLOCK):
            row = number * BLOCK + q
            for m in range(mains + (1 if tail else 0)):
                wide = LANES if m < mains else tail
                lanes = slice(m * LANES, m * LANES + wide)
                values = []
                for level in range(targets):
                    if m < mains:
                        values.append(levels[level, at, q * mains + m])
                    else:
                        last = levels[level, at, BLOCK * mains + q // per]
                        shift = (q % per) * tail
                        values.append(pltpu.roll(last, LANES - shift, 1) if shift else last)
                for k in range(targets):
                    lowest, highest = max(k - (TAPS - 1), 0), min(k, targets - TAPS) + TAPS - 1
                    total = None
                    for level in range(lowest, highest + 1):
                        j = level - lowest
                        term = jnp.broadcast_to(weights[k, row, j:j + 1, lanes], (SUB, wide)) * values[level][:, :wide]
                        total = term if total is None else total + term
                    result[k, at * BLOCK + q, :, lanes] = total
        if ready:
            leave(result.at[:, pl.ds(at * BLOCK, BLOCK)], out.at[:, pl.ds(number * BLOCK, BLOCK)])
    if not ready:
        leave(result, out)
    for copy in copies:
        copy.wait()


def tiles_of(array):
    lead, levels, nlon = array.shape[:-2], array.shape[-2], array.shape[-1]
    split = array.reshape(lead + (levels, nlon // LANES, LANES))
    order = tuple(range(len(lead))) + (len(lead) + 1, len(lead), len(lead) + 2)
    split = with_layout_constraint(split, Layout(major_to_minor=order))
    return jnp.swapaxes(split, -3, -2).reshape(-1, LANES)


VMEM = pl.BlockSpec(memory_space=pltpu.VMEM)
ANY = pl.BlockSpec(memory_space=pl.ANY)
SMEM = pl.BlockSpec(memory_space=pltpu.SMEM)


def call(kernel, outs, args, specs=None, scratch=(), cost=None):
    return pl.pallas_call(
        kernel,
        out_shape=outs,
        in_specs=specs or [VMEM] * len(args),
        out_specs=jax.tree.map(lambda _: VMEM, outs),
        scratch_shapes=list(scratch),
        compiler_params=pltpu.CompilerParams(vmem_limit_bytes=16 << 20),
        cost_estimate=cost,
    )(*args)


def cost(flops, size):
    return pl.CostEstimate(flops=int(flops), bytes_accessed=int(size), transcendentals=0)


def f32(*shape):
    return jax.ShapeDtypeStruct(shape, jnp.float32)


def shards(tracers, wind_x, wind_y, level_counts, source_level, remap_weight):
    count = lax.axis_size("lev")
    bands = lax.axis_size("lat")
    number, depth, rows, nlon = tracers.shape
    targets, _, width = source_level.shape
    size = packed_sizes(nlon, count)[-1]
    blocks = rows // BLOCK
    inner = (rows - 2 * HALO) // BLOCK

    raw = tiles_of(jnp.transpose(tracers, (0, 2, 1, 3)))
    joined = jnp.concatenate([jnp.transpose(wind_x, (1, 0, 2)), jnp.transpose(wind_y, (1, 0, 2))], axis=0)
    halo = f32(HALO + 1, number, nlon)
    state, *sent = call(
        functools.partial(prep_kernel, rows),
        [f32(depth, rows, number, nlon), halo, halo], (raw, joined),
        cost=cost(1, 1))
    swaps = ([(i, i ^ 1) for i in range(bands)],
             [(i, i if i in (0, bands - 1) else ((i - 1) ^ 1) + 1) for i in range(bands)])

    def beside(sent):
        return [lax.ppermute(buffer, "lat", pairs) for buffer, pairs in zip(sent, swaps)]

    rounds = [beside(sent)]
    taps = call(
        weights_kernel, f32(targets, rows, SUB, width),
        (jnp.transpose(remap_weight, (1, 2, 0, 3)), source_level),
        cost=cost(1, 1))

    def box(units, *lead):
        return lead + (units, size, SUB, LANES)

    def vmem(*shape):
        return pltpu.VMEM(shape, jnp.float32)

    held = -(-rows // SUB) * SUB
    coef = f32(3, depth, held, nlon)
    swept = vmem(depth, rows - 2 * REACH, number, nlon)
    stage = vmem(depth * (rows - 2 * REACH), number, nlon)
    result = call(
        functools.partial(interior_kernel, count, rows),
        [f32(*box(depth * inner))] * count + [f32(depth, rows - 2 * REACH, number, nlon), coef, coef] + [halo] * (2 * depth - 2),
        (state, joined), scratch=[vmem(*box(depth * inner, count)), vmem(2, depth, held, nlon), swept, stage, stage, stage],
        cost=cost(1, 1))
    middle, (first, cx, cy), sent = result[:count], result[count:count + 3], result[count + 3:]
    rounds += [beside(sent[2 * i:2 * i + 2]) for i in range(depth - 1)]
    plan, chunks = [], []
    swept = vmem(1, 2 * HALO, number, nlon)
    stage = vmem(2 * HALO, number, nlon)

    def edge(slot, joint, after):
        args = (state, *rounds[slot], first, cx, cy, *joint, *after)
        units = 2 + (joint[0].shape[0] if joint else 0)
        return call(
            functools.partial(edge_kernel, count, rows, slot, len(joint)),
            [f32(*box(units if k == 1 else 2)) for k in range(count)], args,
            specs=[VMEM] * (len(args) - len(after)) + [ANY] * len(after),
            scratch=[vmem(*box(2, count)), vmem(3, 2, SUB, nlon), swept, swept, stage, stage, stage],
            cost=cost(60 * tracers.size, 8 * tracers.size))

    def swapped(sent, k):
        return lax.ppermute(sent, "lev", [(i, i ^ k) for i in range(count)])

    partners = range(count - 1, 1, -1)
    units = tuple((slot, 1 + b) for slot in range(depth) for b in range(inner))
    plan += [(k, units) for k in partners] + [(0, units)]
    chunks += [swapped(middle[k], k) for k in partners] + [middle[0]]
    after, joint = (taps,), (middle[1],)
    for slot in range(depth):
        own = ((slot, 0), (slot, blocks - 1))
        done = edge(slot, joint, after)
        plan += [(k, own) for k in partners] + [(0, own), (1, own + units if joint else own)]
        chunks += [swapped(done[k], k) for k in partners] + [done[0], swapped(done[1], 1)]
        if slot == 0:
            after, joint, early = (done[0], *chunks[:len(partners)]), (), len(chunks)

    def remap(part, numbers, height, ready):
        args = (level_counts, *chunks[:part], taps, *ready)
        return pl.pallas_call(
            functools.partial(remap_kernel, count, tuple(plan[:part]), numbers),
            out_shape=f32(targets, height, number, width),
            in_specs=[SMEM] + [VMEM] * (len(args) - 1),
            out_specs=ANY,
            scratch_shapes=[
                vmem(targets + 1, len(numbers), size, SUB, LANES),
                vmem(targets, len(numbers) * BLOCK, number, width),
                pltpu.SemaphoreType.DMA((len(numbers) + 1,)),
            ],
            compiler_params=pltpu.CompilerParams(vmem_limit_bytes=16 << 20),
            cost_estimate=cost(1, 1),
        )(*args)

    middle_rows = remap(early, tuple(range(1, blocks - 1)), inner * BLOCK, ())
    out = remap(len(chunks), (0, blocks - 1), rows, (middle_rows,))
    return jnp.transpose(out, (2, 0, 1, 3))


def solution(mesh):
    in_specs = (
        P(None, "lev", ("groups", "lat"), None),
        P("lev", ("groups", "lat"), None),
        P("lev", ("groups", "lat"), None),
        P(),
        P(None, ("groups", "lat"), "lev"),
        P(None, None, ("groups", "lat"), "lev"),
    )
    out_specs = P(None, None, ("groups", "lat"), "lev")
    return jax.shard_map(shards, mesh=mesh, in_specs=in_specs, out_specs=out_specs, check_vma=False)
```

```python
import functools

import jax
import jax.numpy as jnp
from jax import lax
from jax.experimental import pallas as pl
from jax.experimental.layout import Layout, with_layout_constraint
from jax.experimental.pallas import tpu as pltpu
from jax.sharding import PartitionSpec as P

SUBSTEPS = 2
TAPS = 4
REACH = 3
HALO = REACH * SUBSTEPS
BLOCK = 6
LANES = 128
SUB = 8


def spread(row):
    return jnp.broadcast_to(row, (SUB, LANES))


def lane_ids():
    return lax.broadcasted_iota(jnp.int32, (SUB, LANES), 1)


def from_west(tiles, steps, lane):
    turned = [pltpu.roll(t, steps, 1) for t in tiles]
    return [jnp.where(lane < steps, turned[j - 1], turned[j]) for j in range(len(tiles))]


def from_east(tiles, lane):
    turned = [pltpu.roll(t, LANES - 1, 1) for t in tiles]
    count = len(tiles)
    return [jnp.where(lane == LANES - 1, turned[(j + 1) % count], turned[j]) for j in range(count)]


def coefficients(wind):
    size = jnp.abs(wind)
    rest = 1.0 - size
    alpha = wind * rest * rest * (1.0 / 12.0)
    beta = wind * size * rest * (-1.0 / 12.0)
    gamma = wind * size * (3.0 - 2.0 * size)
    return alpha, beta, gamma


def packed_sizes(nlon, count):
    width = nlon // count
    mains, tail = width // LANES, width % LANES
    per = LANES // tail if tail else 1
    tails = -(-BLOCK // per) if tail else 0
    return width, mains, tail, per, BLOCK * mains + tails


def fill_halos(rows, slot, state, winds, first_round, second_round):
    band, bands = lax.axis_index("lat"), lax.axis_size("lat")
    even = band % 2 == 0
    keep = jnp.where((band == 0) | (band == bands - 1), 0.0, 1.0)
    for target, north, scale in ((first_round, even, None), (second_round, jnp.logical_not(even), keep)):
        scaled = (lambda v: v) if scale is None else (lambda v: v * scale)
        row_t = jnp.where(north, rows - HALO, 0)
        row_x = jnp.where(north, rows - REACH, 0)
        row_y = jnp.where(north, rows - REACH - 1, 0)
        for row in range(HALO):
            target[row] = scaled(state[slot, row_t + row])
        for q in range(REACH):
            target[HALO, q:q + 1, :] = scaled(winds[row_x + q, slot:slot + 1, :])
        for q in range(REACH + 1):
            target[HALO, REACH + q:REACH + q + 1, :] = scaled(winds[rows + row_y + q, slot:slot + 1, :])


def prep_kernel(rows, tracers, winds, state, first_round, second_round):
    levels, nlon = state.shape[0], state.shape[3]
    nj = nlon // LANES
    row_stride = nj * levels
    tracer_stride = rows * row_stride

    def body(row, _):
        for level in range(levels):
            for j in range(nj):
                start = row * row_stride + j * levels + level
                state[level, row, :, tile(j)] = tracers[pl.ds(start, SUB, stride=tracer_stride), :]
        return 0

    lax.fori_loop(0, rows, body, 0)
    fill_halos(rows, 0, state, winds, first_round, second_round)


def lat_pass(levels, nj, ranges, cell, coef, store):
    group = 3 if nj % 3 == 0 else 1

    def body(i, _):
        level = i // (nj // group)
        results = []
        for u in range(group):
            lanes = pl.ds(pl.multiple_of(((i % (nj // group)) * group + u) * LANES, LANES), LANES)
            results += [(level, row, lanes, value) for row, value in one(level, lanes)]
        for result in results:
            store(*result)
        return 0

    def one(level, lanes):
        results = []
        for first, last in ranges:
            a = {r: cell(level, r, lanes) for r in range(first - REACH, last + REACH)}
            inter = {f: 7.0 * (a[f - 1] + a[f]) - (a[f - 2] + a[f + 1]) for f in range(first - 1, last + 2)}
            flux = {}
            for f in range(first, last + 1):
                alpha, beta, gamma = [spread(coef(i, level, f, lanes)) for i in range(3)]
                north = gamma > 0
                behind = jnp.where(north, inter[f - 1], inter[f + 1])
                upwind = jnp.where(north, a[f - 1], a[f])
                flux[f] = alpha * inter[f] + beta * behind + gamma * upwind
                if f > first:
                    results.append((f - 1, a[f - 1] - (flux[f] - flux[f - 1])))
        return results

    lax.fori_loop(0, levels * nj // group, body, 0)


def tile(j):
    return slice(j * LANES, (j + 1) * LANES)


def lon_pass(work, swept, coef, inter, west, flux, lane, finish):
    nj = swept.shape[3] // LANES
    each = range(nj)

    def interfaces(n):
        level, _, at = work[n]
        b = [swept[level, at, :, tile(j)] for j in each]
        w1, w2, e1 = from_west(b, 1, lane), from_west(b, 2, lane), from_east(b, lane)
        for j in each:
            inter[n, :, tile(j)] = 7.0 * (w1[j] + b[j]) - (w2[j] + e1[j])
            west[n, :, tile(j)] = w1[j]

    def fluxes(n):
        level, row, at = work[n]
        mid = [inter[n, :, tile(j)] for j in each]
        w1, e1 = from_west(mid, 1, lane), from_east(mid, lane)
        for j in each:
            alpha, beta, gamma = [spread(coef(i, level, row, tile(j))) for i in range(3)]
            right = gamma > 0
            behind = jnp.where(right, w1[j], e1[j])
            upwind = jnp.where(right, west[n, :, tile(j)], swept[level, at, :, tile(j)])
            flux[n, :, tile(j)] = alpha * mid[j] + beta * behind + gamma * upwind

    def update(n):
        level, _, at = work[n]
        here = [flux[n, :, tile(j)] for j in each]
        e1 = from_east(here, lane)
        return [swept[level, at, :, tile(j)] - (e1[j] - here[j]) for j in each]

    groups = len(work) // BLOCK
    for g in range(groups + 2):
        if g < groups:
            for q in range(BLOCK):
                interfaces(g * BLOCK + q)
        if 1 <= g <= groups:
            for q in range(BLOCK):
                fluxes((g - 1) * BLOCK + q)
        if g >= 2:
            finish(g - 2, [update((g - 2) * BLOCK + q) for q in range(BLOCK)])


def pack_block(block, packed, unit, count, lane):
    nlon = len(block[0]) * LANES
    width, mains, tail, per, size = packed_sizes(nlon, count)
    for d in range(count):
        j0, off = (d * width) // LANES, (d * width) % LANES
        for q, tiles in enumerate(block):
            turned = [pltpu.roll(tiles[j0 + m], LANES - off, 1) if off else tiles[j0 + m]
                      for m in range(mains + (1 if off else 0))]
            for m in range(mains):
                whole = jnp.where(lane < LANES - off, turned[m], turned[m + 1]) if off else turned[m]
                packed[d, unit, q * mains + m] = whole
        if tail:
            for g in range(-(-BLOCK // per)):
                total = None
                for place in range(min(per, BLOCK - g * per)):
                    shift = (place * tail - off) % LANES
                    source = block[g * per + place][j0 + mains]
                    moved = pltpu.roll(source, shift, 1) if shift else source
                    total = moved if total is None else jnp.where(lane < place * tail, total, moved)
                packed[d, unit, BLOCK * mains + g] = total


def copy_tiles(pairs):
    values = [source[at] for (source, at), _ in pairs]
    for value, (_, (target, at)) in zip(values, pairs):
        target[at] = value


def copy_units(source, target, start=0):
    for unit in range(source.shape[0]):
        copy_tiles([((source, (unit, i)), (target, (start + unit, i))) for i in range(source.shape[1])])


def hand_out(packed, outs):
    me = lax.axis_index("lev")
    for k, out in enumerate(outs):
        copy_units(packed.at[me ^ k], out)


def own_coefficients(rows, joined, winds, cx, cy):
    levels, held, nlon = cx.shape[1:]
    keep = jnp.where(lax.axis_index("lat") == 0, 0.0, 1.0)
    for level in range(levels):
        for way in range(2):
            for row in range(rows):
                winds[way, level, row:row + 1, :] = joined[way * rows + row, level:level + 1, :]
        winds[1, level, 0:1, :] = winds[1, level, 0:1, :] * keep
        for way, target in enumerate((cx, cy)):
            for j in range(nlon // LANES):
                parts = coefficients(winds[way, level, :, tile(j)])
                for p in range(3):
                    target[p, level, :, tile(j)] = parts[p]


def put_rows(target, level, at, rows):
    for q, row in enumerate(rows):
        for j, part in enumerate(row):
            target[level, at + q, :, tile(j)] = part


def interior_kernel(count, rows, state, joined, *refs):
    outs, (first, cx, cy), refs = refs[:count], refs[count:count + 3], refs[count + 3:]
    halos, (packed, winds, swept, inter, west, flux) = refs[:-6], refs[-6:]
    levels, nlon = state.shape[0], state.shape[3]
    nj = nlon // LANES
    lane = lane_ids()
    for slot in range(1, levels):
        fill_halos(rows, slot, state, joined, *halos[2 * slot - 2:2 * slot])
    own_coefficients(rows, joined, winds, cx, cy)
    coef_x = lambda i, level, r, lanes: cx[i, level, r:r + 1, lanes]
    coef_y = lambda i, level, f, lanes: cy[i, level, f:f + 1, lanes]

    def put(level, row, lanes, value):
        swept[level, row - REACH, :, lanes] = value

    lat_pass(levels, nj, [(REACH, rows - REACH)], lambda level, r, lanes: state[level, r, :, lanes], coef_y, put)
    work = [(level, row, row - REACH) for level in range(levels) for row in range(REACH, rows - REACH)]

    def keep_first(group, done):
        level, _, at = work[group * BLOCK]
        put_rows(first, level, at, done)

    lon_pass(work, swept, coef_x, inter, west, flux, lane, keep_first)
    lat_pass(levels, nj, [(HALO, rows - HALO)], lambda level, r, lanes: first[level, r - REACH, :, lanes], coef_y, put)
    work_last = [(level, row, row - REACH) for level in range(levels) for row in range(HALO, rows - HALO)]

    def send(group, done):
        pack_block(done, packed, group, count, lane)

    lon_pass(work_last, swept, coef_x, inter, west, flux, lane, send)
    hand_out(packed, outs)


def edge_kernel(count, rows, slot, joint, state, first_round, second_round, first, cx, cy, *refs):
    others = refs[:joint]
    outs, (packed, beyond, swept, edge, inter, west, flux) = refs[-7 - count:-7], refs[-7:]
    nlon = state.shape[3]
    nj = nlon // LANES
    lane = lane_ids()
    odd = lax.axis_index("lat") % 2 == 1

    def halo(south, *at):
        one, two = first_round[at], second_round[at]
        return jnp.where(odd, one, two) if south else jnp.where(odd, two, one)

    for end, south in enumerate((True, False)):
        for j in range(nj):
            parts = coefficients(halo(south, HALO, slice(None), tile(j)))
            for p in range(3):
                beyond[p, end, :, tile(j)] = parts[p]

    def coef_x(i, _, r, lanes):
        if 0 <= r < rows:
            return cx[i, slot, r:r + 1, lanes]
        end, at = (0, r + REACH) if r < 0 else (1, r - rows)
        return beyond[i, end, at:at + 1, lanes]

    def coef_y(i, _, f, lanes):
        if 0 <= f < rows:
            return cy[i, slot, f:f + 1, lanes]
        end, at = (0, f + 2 * REACH + 1) if f < 0 else (1, f - rows + REACH)
        return beyond[i, end, at:at + 1, lanes]

    def cell(_, r, lanes):
        if 0 <= r < rows:
            return state[slot, r, :, lanes]
        return halo(r < 0, r + HALO if r < 0 else r - rows, slice(None), lanes)

    ends = [(-REACH, REACH), (rows - REACH, rows + REACH)]
    ends_last = [(0, HALO), (rows - HALO, rows)]

    def place(row, ranges):
        (a, b), (c, _) = ranges
        return row - a if row < b else row - c + BLOCK

    def cell_first(_, r, lanes):
        if REACH <= r < rows - REACH:
            return first[slot, r - REACH, :, lanes]
        return edge[0, place(r, ends), :, lanes]

    def put(_, row, lanes, value):
        swept[0, place(row, ends), :, lanes] = value

    def put_last(_, row, lanes, value):
        swept[0, place(row, ends_last), :, lanes] = value

    def listed(ranges):
        return [(0, row, place(row, ranges)) for a, b in ranges for row in range(a, b)]

    def keep_edge(group, done):
        put_rows(edge, 0, group * BLOCK, done)

    def send(group, done):
        pack_block(done, packed, group, count, lane)

    lat_pass(1, nj, ends, cell, coef_y, put)
    lon_pass(listed(ends), swept, coef_x, inter, west, flux, lane, keep_edge)
    lat_pass(1, nj, ends_last, cell_first, coef_y, put_last)
    lon_pass(listed(ends_last), swept, coef_x, inter, west, flux, lane, send)
    hand_out(packed, outs)
    for other in others:
        copy_units(other, outs[1], packed.shape[1])


def weights_kernel(weights, source, out):
    targets, rows, taps, width = weights.shape

    for row in range(rows):
        for k in range(targets):
            lowest, highest = max(k - (TAPS - 1), 0), min(k, targets - TAPS)
            w = weights[k, row]
            w = jnp.concatenate([w, jnp.zeros((SUB - taps, width), jnp.float32)], axis=0)
            at = jnp.broadcast_to(source[k, row:row + 1, :], (SUB, width))
            total = w
            for g in range(lowest + 1, highest + 1):
                total = jnp.where(at == g, pltpu.roll(w, g - lowest, 0), total)
            out[k, row] = total


def remap_kernel(count, plan, numbers, counts, *refs):
    chunks, (weights, *ready, out, levels, result, sems) = refs[:len(plan)], refs[len(plan):]
    me = lax.axis_index("lev")
    targets, _, _, width = result.shape
    _, mains, tail, per, _ = packed_sizes(width * count, count)
    copies = []

    def leave(source, target):
        copy = pltpu.make_async_copy(source, target, sems.at[len(copies)])
        copy.start()
        copies.append(copy)

    if ready:
        others = [n for n in range(out.shape[1] // BLOCK) if n not in numbers]
        leave(ready[0], out.at[:, pl.ds(others[0] * BLOCK, len(others) * BLOCK)])

    def level_of(k, slot):
        d = me ^ k
        start = jnp.int32(0)
        for e in range(count):
            start = start + jnp.where(e < d, counts[e], 0)
        return jnp.where(slot < counts[d], start + slot, targets)

    for (k, units), chunk in zip(plan, chunks):
        for unit, (slot, number) in enumerate(units):
            if number in numbers:
                at = numbers.index(number)
                copy_tiles([((chunk, (unit, i)), (levels, (level_of(k, slot), at, i))) for i in range(chunk.shape[1])])

    for at, number in enumerate(numbers):
        for q in range(BLOCK):
            row = number * BLOCK + q
            for m in range(mains + (1 if tail else 0)):
                wide = LANES if m < mains else tail
                lanes = slice(m * LANES, m * LANES + wide)
                values = []
                for level in range(targets):
                    if m < mains:
                        values.append(levels[level, at, q * mains + m])
                    else:
                        last = levels[level, at, BLOCK * mains + q // per]
                        shift = (q % per) * tail
                        values.append(pltpu.roll(last, LANES - shift, 1) if shift else last)
                for k in range(targets):
                    lowest, highest = max(k - (TAPS - 1), 0), min(k, targets - TAPS) + TAPS - 1
                    total = None
                    for level in range(lowest, highest + 1):
                        j = level - lowest
                        term = jnp.broadcast_to(weights[k, row, j:j + 1, lanes], (SUB, wide)) * values[level][:, :wide]
                        total = term if total is None else total + term
                    result[k, at * BLOCK + q, :, lanes] = total
        if ready:
            leave(result.at[:, pl.ds(at * BLOCK, BLOCK)], out.at[:, pl.ds(number * BLOCK, BLOCK)])
    if not ready:
        leave(result, out)
    for copy in copies:
        copy.wait()


def tiles_of(array):
    lead, levels, nlon = array.shape[:-2], array.shape[-2], array.shape[-1]
    split = array.reshape(lead + (levels, nlon // LANES, LANES))
    order = tuple(range(len(lead))) + (len(lead) + 1, len(lead), len(lead) + 2)
    split = with_layout_constraint(split, Layout(major_to_minor=order))
    return jnp.swapaxes(split, -3, -2).reshape(-1, LANES)


VMEM = pl.BlockSpec(memory_space=pltpu.VMEM)
ANY = pl.BlockSpec(memory_space=pl.ANY)
SMEM = pl.BlockSpec(memory_space=pltpu.SMEM)


def call(kernel, outs, args, specs=None, scratch=(), cost=None):
    return pl.pallas_call(
        kernel,
        out_shape=outs,
        in_specs=specs or [VMEM] * len(args),
        out_specs=jax.tree.map(lambda _: VMEM, outs),
        scratch_shapes=list(scratch),
        compiler_params=pltpu.CompilerParams(vmem_limit_bytes=16 << 20),
        cost_estimate=cost,
    )(*args)


def cost(flops, size):
    return pl.CostEstimate(flops=int(flops), bytes_accessed=int(size), transcendentals=0)


def f32(*shape):
    return jax.ShapeDtypeStruct(shape, jnp.float32)


def shards(tracers, wind_x, wind_y, level_counts, source_level, remap_weight):
    count = lax.axis_size("lev")
    bands = lax.axis_size("lat")
    number, depth, rows, nlon = tracers.shape
    targets, _, width = source_level.shape
    size = packed_sizes(nlon, count)[-1]
    blocks = rows // BLOCK
    inner = (rows - 2 * HALO) // BLOCK

    raw = tiles_of(jnp.transpose(tracers, (0, 2, 1, 3)))
    joined = jnp.concatenate([jnp.transpose(wind_x, (1, 0, 2)), jnp.transpose(wind_y, (1, 0, 2))], axis=0)
    halo = f32(HALO + 1, number, nlon)
    state, *sent = call(
        functools.partial(prep_kernel, rows),
        [f32(depth, rows, number, nlon), halo, halo], (raw, joined),
        cost=cost(1, 1))
    second = {i: ((i - 1) ^ 1) + 1 for i in range(1, bands - 1)}
    second_pairs = [(i * count + d, second[i] * count + d if i in second else i * count + (d ^ 1))
                    for i in range(bands) for d in range(count)]

    def beside(sent):
        return [lax.ppermute(sent[0], "lat", [(i, i ^ 1) for i in range(bands)]),
                lax.ppermute(sent[1], ("lat", "lev"), second_pairs)]

    rounds = [beside(sent)]
    taps = call(
        weights_kernel, f32(targets, rows, SUB, width),
        (jnp.transpose(remap_weight, (1, 2, 0, 3)), source_level),
        cost=cost(1, 1))

    def box(units, *lead):
        return lead + (units, size, SUB, LANES)

    def vmem(*shape):
        return pltpu.VMEM(shape, jnp.float32)

    held = -(-rows // SUB) * SUB
    coef = f32(3, depth, held, nlon)
    swept = vmem(depth, rows - 2 * REACH, number, nlon)
    stage = vmem(depth * (rows - 2 * REACH), number, nlon)
    result = call(
        functools.partial(interior_kernel, count, rows),
        [f32(*box(depth * inner))] * count + [f32(depth, rows - 2 * REACH, number, nlon), coef, coef] + [halo] * (2 * depth - 2),
        (state, joined), scratch=[vmem(*box(depth * inner, count)), vmem(2, depth, held, nlon), swept, stage, stage, stage],
        cost=cost(1, 1))
    middle, (first, cx, cy), sent = result[:count], result[count:count + 3], result[count + 3:]
    rounds += [beside(sent[2 * i:2 * i + 2]) for i in range(depth - 1)]
    plan, chunks = [], []
    swept = vmem(1, 2 * HALO, number, nlon)
    stage = vmem(2 * HALO, number, nlon)

    def edge(slot, joint, after):
        args = (state, *rounds[slot], first, cx, cy, *joint, *after)
        units = 2 + (joint[0].shape[0] if joint else 0)
        return call(
            functools.partial(edge_kernel, count, rows, slot, len(joint)),
            [f32(*box(units if k == 1 else 2)) for k in range(count)], args,
            specs=[VMEM] * (len(args) - len(after)) + [ANY] * len(after),
            scratch=[vmem(*box(2, count)), vmem(3, 2, SUB, nlon), swept, swept, stage, stage, stage],
            cost=cost(60 * tracers.size, 8 * tracers.size))

    def swapped(sent, k):
        return lax.ppermute(sent, "lev", [(i, i ^ k) for i in range(count)])

    partners = range(count - 1, 1, -1)
    units = tuple((slot, 1 + b) for slot in range(depth) for b in range(inner))
    plan += [(k, units) for k in partners] + [(0, units)]
    chunks += [swapped(middle[k], k) for k in partners] + [middle[0]]
    after, joint = (taps,), (middle[1],)
    for slot in range(depth):
        own = ((slot, 0), (slot, blocks - 1))
        done = edge(slot, joint, after)
        plan += [(k, own) for k in partners] + [(0, own), (1, own + units if joint else own)]
        chunks += [swapped(done[k], k) for k in partners] + [done[0], swapped(done[1], 1)]
        if slot == 0:
            after, joint, early = (done[0], *chunks[:len(partners)]), (), len(chunks)

    def remap(part, numbers, height, ready):
        args = (level_counts, *chunks[:part], taps, *ready)
        return pl.pallas_call(
            functools.partial(remap_kernel, count, tuple(plan[:part]), numbers),
            out_shape=f32(targets, height, number, width),
            in_specs=[SMEM] + [VMEM] * (len(args) - 1),
            out_specs=ANY,
            scratch_shapes=[
                vmem(targets + 1, len(numbers), size, SUB, LANES),
                vmem(targets, len(numbers) * BLOCK, number, width),
                pltpu.SemaphoreType.DMA((len(numbers) + 1,)),
            ],
            compiler_params=pltpu.CompilerParams(vmem_limit_bytes=16 << 20),
            cost_estimate=cost(1, 1),
        )(*args)

    middle_rows = remap(early, tuple(range(1, blocks - 1)), inner * BLOCK, ())
    out = remap(len(chunks), (0, blocks - 1), rows, (middle_rows,))
    return jnp.transpose(out, (2, 0, 1, 3))


def solution(mesh):
    in_specs = (
        P(None, "lev", ("groups", "lat"), None),
        P("lev", ("groups", "lat"), None),
        P("lev", ("groups", "lat"), None),
        P(),
        P(None, ("groups", "lat"), "lev"),
        P(None, None, ("groups", "lat"), "lev"),
    )
    out_specs = P(None, None, ("groups", "lat"), "lev")
    return jax.shard_map(shards, mesh=mesh, in_specs=in_specs, out_specs=out_specs, check_vma=False)
```

```python
import functools

import jax
import jax.numpy as jnp
from jax import lax
from jax.experimental import pallas as pl
from jax.experimental.layout import Layout, with_layout_constraint
from jax.experimental.pallas import tpu as pltpu
from jax.sharding import PartitionSpec as P

SUBSTEPS = 2
TAPS = 4
REACH = 3
HALO = REACH * SUBSTEPS
BLOCK = 6
LANES = 128
SUB = 8


def spread(row):
    return jnp.broadcast_to(row, (SUB, LANES))


def lane_ids():
    return lax.broadcasted_iota(jnp.int32, (SUB, LANES), 1)


def from_west(tiles, steps, lane):
    turned = [pltpu.roll(t, steps, 1) for t in tiles]
    return [jnp.where(lane < steps, turned[j - 1], turned[j]) for j in range(len(tiles))]


def from_east(tiles, lane):
    turned = [pltpu.roll(t, LANES - 1, 1) for t in tiles]
    count = len(tiles)
    return [jnp.where(lane == LANES - 1, turned[(j + 1) % count], turned[j]) for j in range(count)]


def coefficients(wind):
    size = jnp.abs(wind)
    rest = 1.0 - size
    alpha = wind * rest * rest * (1.0 / 12.0)
    beta = wind * size * rest * (-1.0 / 12.0)
    gamma = wind * size * (3.0 - 2.0 * size)
    return alpha, beta, gamma


def packed_sizes(nlon, count):
    width = nlon // count
    mains, tail = width // LANES, width % LANES
    per = LANES // tail if tail else 1
    tails = -(-BLOCK // per) if tail else 0
    return width, mains, tail, per, BLOCK * mains + tails


def fill_halos(rows, slot, state, winds, first_round, second_round):
    band, bands = lax.axis_index("lat"), lax.axis_size("lat")
    even = band % 2 == 0
    keep = jnp.where((band == 0) | (band == bands - 1), 0.0, 1.0)
    for target, north, scale in ((first_round, even, None), (second_round, jnp.logical_not(even), keep)):
        scaled = (lambda v: v) if scale is None else (lambda v: v * scale)
        row_t = jnp.where(north, rows - HALO, 0)
        row_x = jnp.where(north, rows - REACH, 0)
        row_y = jnp.where(north, rows - REACH - 1, 0)
        for row in range(HALO):
            target[row] = scaled(state[slot, row_t + row])
        for q in range(REACH):
            target[HALO, q:q + 1, :] = scaled(winds[row_x + q, slot:slot + 1, :])
        for q in range(REACH + 1):
            target[HALO, REACH + q:REACH + q + 1, :] = scaled(winds[rows + row_y + q, slot:slot + 1, :])


def prep_kernel(rows, tracers, winds, state, first_round, second_round):
    levels, nlon = state.shape[0], state.shape[3]
    nj = nlon // LANES
    row_stride = nj * levels
    tracer_stride = rows * row_stride

    def body(row, _):
        for level in range(levels):
            for j in range(nj):
                start = row * row_stride + j * levels + level
                state[level, row, :, tile(j)] = tracers[pl.ds(start, SUB, stride=tracer_stride), :]
        return 0

    lax.fori_loop(0, rows, body, 0)
    fill_halos(rows, 0, state, winds, first_round, second_round)


def lat_pass(levels, nj, ranges, cell, coef, store):
    group = 3 if nj % 3 == 0 else 1

    def body(i, _):
        level = i // (nj // group)
        results = []
        for u in range(group):
            lanes = pl.ds(pl.multiple_of(((i % (nj // group)) * group + u) * LANES, LANES), LANES)
            results += [(level, row, lanes, value) for row, value in one(level, lanes)]
        for result in results:
            store(*result)
        return 0

    def one(level, lanes):
        results = []
        for first, last in ranges:
            a = {r: cell(level, r, lanes) for r in range(first - REACH, last + REACH)}
            inter = {f: 7.0 * (a[f - 1] + a[f]) - (a[f - 2] + a[f + 1]) for f in range(first - 1, last + 2)}
            flux = {}
            for f in range(first, last + 1):
                alpha, beta, gamma = [spread(coef(i, level, f, lanes)) for i in range(3)]
                north = gamma > 0
                behind = jnp.where(north, inter[f - 1], inter[f + 1])
                upwind = jnp.where(north, a[f - 1], a[f])
                flux[f] = alpha * inter[f] + beta * behind + gamma * upwind
                if f > first:
                    results.append((f - 1, a[f - 1] - (flux[f] - flux[f - 1])))
        return results

    lax.fori_loop(0, levels * nj // group, body, 0)


def tile(j):
    return slice(j * LANES, (j + 1) * LANES)


def lon_pass(work, swept, coef, inter, west, flux, lane, finish):
    nj = swept.shape[3] // LANES
    each = range(nj)

    def interfaces(n):
        level, _, at = work[n]
        b = [swept[level, at, :, tile(j)] for j in each]
        w1, w2, e1 = from_west(b, 1, lane), from_west(b, 2, lane), from_east(b, lane)
        for j in each:
            inter[n, :, tile(j)] = 7.0 * (w1[j] + b[j]) - (w2[j] + e1[j])
            west[n, :, tile(j)] = w1[j]

    def fluxes(n):
        level, row, at = work[n]
        mid = [inter[n, :, tile(j)] for j in each]
        w1, e1 = from_west(mid, 1, lane), from_east(mid, lane)
        for j in each:
            alpha, beta, gamma = [spread(coef(i, level, row, tile(j))) for i in range(3)]
            right = gamma > 0
            behind = jnp.where(right, w1[j], e1[j])
            upwind = jnp.where(right, west[n, :, tile(j)], swept[level, at, :, tile(j)])
            flux[n, :, tile(j)] = alpha * mid[j] + beta * behind + gamma * upwind

    def update(n):
        level, _, at = work[n]
        here = [flux[n, :, tile(j)] for j in each]
        e1 = from_east(here, lane)
        return [swept[level, at, :, tile(j)] - (e1[j] - here[j]) for j in each]

    groups = len(work) // BLOCK
    for g in range(groups + 2):
        if g < groups:
            for q in range(BLOCK):
                interfaces(g * BLOCK + q)
        if 1 <= g <= groups:
            for q in range(BLOCK):
                fluxes((g - 1) * BLOCK + q)
        if g >= 2:
            finish(g - 2, [update((g - 2) * BLOCK + q) for q in range(BLOCK)])


def pack_block(block, packed, unit, count, lane):
    nlon = len(block[0]) * LANES
    width, mains, tail, per, size = packed_sizes(nlon, count)
    for d in range(count):
        j0, off = (d * width) // LANES, (d * width) % LANES
        for q, tiles in enumerate(block):
            turned = [pltpu.roll(tiles[j0 + m], LANES - off, 1) if off else tiles[j0 + m]
                      for m in range(mains + (1 if off else 0))]
            for m in range(mains):
                whole = jnp.where(lane < LANES - off, turned[m], turned[m + 1]) if off else turned[m]
                packed[d, unit, q * mains + m] = whole
        if tail:
            for g in range(-(-BLOCK // per)):
                total = None
                for place in range(min(per, BLOCK - g * per)):
                    shift = (place * tail - off) % LANES
                    source = block[g * per + place][j0 + mains]
                    moved = pltpu.roll(source, shift, 1) if shift else source
                    total = moved if total is None else jnp.where(lane < place * tail, total, moved)
                packed[d, unit, BLOCK * mains + g] = total


def copy_tiles(pairs):
    values = [source[at] for (source, at), _ in pairs]
    for value, (_, (target, at)) in zip(values, pairs):
        target[at] = value


def copy_units(source, target, start=0):
    for unit in range(source.shape[0]):
        copy_tiles([((source, (unit, i)), (target, (start + unit, i))) for i in range(source.shape[1])])


def hand_out(packed, outs, groups):
    me = lax.axis_index("lev")
    for group, out in zip(groups, outs):
        for place, k in enumerate(group):
            copy_units(packed.at[me ^ k], out, place * packed.shape[1])


def own_coefficients(rows, joined, winds, cx, cy):
    levels, held, nlon = cx.shape[1:]
    keep = jnp.where(lax.axis_index("lat") == 0, 0.0, 1.0)
    for level in range(levels):
        for way in range(2):
            for row in range(rows):
                winds[way, level, row:row + 1, :] = joined[way * rows + row, level:level + 1, :]
        winds[1, level, 0:1, :] = winds[1, level, 0:1, :] * keep
        for way, target in enumerate((cx, cy)):
            for j in range(nlon // LANES):
                parts = coefficients(winds[way, level, :, tile(j)])
                for p in range(3):
                    target[p, level, :, tile(j)] = parts[p]


def put_rows(target, level, at, rows):
    for q, row in enumerate(rows):
        for j, part in enumerate(row):
            target[level, at + q, :, tile(j)] = part


def interior_kernel(count, rows, groups, state, joined, *refs):
    outs, (first, cx, cy), refs = refs[:len(groups)], refs[len(groups):len(groups) + 3], refs[len(groups) + 3:]
    halos, (packed, winds, swept, inter, west, flux) = refs[:-6], refs[-6:]
    levels, nlon = state.shape[0], state.shape[3]
    nj = nlon // LANES
    lane = lane_ids()
    for slot in range(1, levels):
        fill_halos(rows, slot, state, joined, *halos[2 * slot - 2:2 * slot])
    own_coefficients(rows, joined, winds, cx, cy)
    coef_x = lambda i, level, r, lanes: cx[i, level, r:r + 1, lanes]
    coef_y = lambda i, level, f, lanes: cy[i, level, f:f + 1, lanes]

    def put(level, row, lanes, value):
        swept[level, row - REACH, :, lanes] = value

    lat_pass(levels, nj, [(REACH, rows - REACH)], lambda level, r, lanes: state[level, r, :, lanes], coef_y, put)
    work = [(level, row, row - REACH) for level in range(levels) for row in range(REACH, rows - REACH)]

    def keep_first(group, done):
        level, _, at = work[group * BLOCK]
        put_rows(first, level, at, done)

    lon_pass(work, swept, coef_x, inter, west, flux, lane, keep_first)
    lat_pass(levels, nj, [(HALO, rows - HALO)], lambda level, r, lanes: first[level, r - REACH, :, lanes], coef_y, put)
    work_last = [(level, row, row - REACH) for level in range(levels) for row in range(HALO, rows - HALO)]

    def send(group, done):
        pack_block(done, packed, group, count, lane)

    lon_pass(work_last, swept, coef_x, inter, west, flux, lane, send)
    hand_out(packed, outs, groups)


def edge_kernel(count, rows, slot, joint, state, first_round, second_round, first, cx, cy, *refs):
    others = refs[:len(joint)]
    outs, (packed, beyond, swept, edge, inter, west, flux) = refs[-7 - count:-7], refs[-7:]
    nlon = state.shape[3]
    nj = nlon // LANES
    lane = lane_ids()
    odd = lax.axis_index("lat") % 2 == 1

    def halo(south, *at):
        one, two = first_round[at], second_round[at]
        return jnp.where(odd, one, two) if south else jnp.where(odd, two, one)

    for end, south in enumerate((True, False)):
        for j in range(nj):
            parts = coefficients(halo(south, HALO, slice(None), tile(j)))
            for p in range(3):
                beyond[p, end, :, tile(j)] = parts[p]

    def coef_x(i, _, r, lanes):
        if 0 <= r < rows:
            return cx[i, slot, r:r + 1, lanes]
        end, at = (0, r + REACH) if r < 0 else (1, r - rows)
        return beyond[i, end, at:at + 1, lanes]

    def coef_y(i, _, f, lanes):
        if 0 <= f < rows:
            return cy[i, slot, f:f + 1, lanes]
        end, at = (0, f + 2 * REACH + 1) if f < 0 else (1, f - rows + REACH)
        return beyond[i, end, at:at + 1, lanes]

    def cell(_, r, lanes):
        if 0 <= r < rows:
            return state[slot, r, :, lanes]
        return halo(r < 0, r + HALO if r < 0 else r - rows, slice(None), lanes)

    ends = [(-REACH, REACH), (rows - REACH, rows + REACH)]
    ends_last = [(0, HALO), (rows - HALO, rows)]

    def place(row, ranges):
        (a, b), (c, _) = ranges
        return row - a if row < b else row - c + BLOCK

    def cell_first(_, r, lanes):
        if REACH <= r < rows - REACH:
            return first[slot, r - REACH, :, lanes]
        return edge[0, place(r, ends), :, lanes]

    def put(_, row, lanes, value):
        swept[0, place(row, ends), :, lanes] = value

    def put_last(_, row, lanes, value):
        swept[0, place(row, ends_last), :, lanes] = value

    def listed(ranges):
        return [(0, row, place(row, ranges)) for a, b in ranges for row in range(a, b)]

    def keep_edge(group, done):
        put_rows(edge, 0, group * BLOCK, done)

    def send(group, done):
        pack_block(done, packed, group, count, lane)

    lat_pass(1, nj, ends, cell, coef_y, put)
    lon_pass(listed(ends), swept, coef_x, inter, west, flux, lane, keep_edge)
    lat_pass(1, nj, ends_last, cell_first, coef_y, put_last)
    lon_pass(listed(ends_last), swept, coef_x, inter, west, flux, lane, send)
    hand_out(packed, outs, [(k,) for k in range(count)])
    place = packed.shape[1]
    for other, (begin, size) in zip(others, joint):
        copy_units(other.at[pl.ds(begin, size)], outs[1], place)
        place += size


def weights_kernel(weights, source, out):
    targets, rows, taps, width = weights.shape

    for row in range(rows):
        for k in range(targets):
            lowest, highest = max(k - (TAPS - 1), 0), min(k, targets - TAPS)
            w = weights[k, row]
            w = jnp.concatenate([w, jnp.zeros((SUB - taps, width), jnp.float32)], axis=0)
            at = jnp.broadcast_to(source[k, row:row + 1, :], (SUB, width))
            total = w
            for g in range(lowest + 1, highest + 1):
                total = jnp.where(at == g, pltpu.roll(w, g - lowest, 0), total)
            out[k, row] = total


def remap_kernel(count, plan, numbers, whole, counts, *refs):
    chunks, weights, ready, (out, levels, result, sems) = refs[:len(plan)], refs[len(plan)], refs[len(plan) + 1:-4], refs[-4:]
    ready = ready if whole else ()
    me = lax.axis_index("lev")
    targets, _, _, width = result.shape
    _, mains, tail, per, _ = packed_sizes(width * count, count)
    copies = []

    def leave(source, target):
        copy = pltpu.make_async_copy(source, target, sems.at[len(copies)])
        copy.start()
        copies.append(copy)

    if ready:
        others = [n for n in range(out.shape[1] // BLOCK) if n not in numbers]
        leave(ready[0], out.at[:, pl.ds(others[0] * BLOCK, len(others) * BLOCK)])

    def level_of(k, slot):
        d = me ^ k
        start = jnp.int32(0)
        for e in range(count):
            start = start + jnp.where(e < d, counts[e], 0)
        return jnp.where(slot < counts[d], start + slot, targets)

    for units, chunk in zip(plan, chunks):
        for unit, (k, slot, number) in enumerate(units):
            if number in numbers:
                at = numbers.index(number)
                copy_tiles([((chunk, (unit, i)), (levels, (level_of(k, slot), at, i))) for i in range(chunk.shape[1])])

    for at, number in enumerate(numbers):
        for q in range(BLOCK):
            row = number * BLOCK + q
            for m in range(mains + (1 if tail else 0)):
                wide = LANES if m < mains else tail
                lanes = slice(m * LANES, m * LANES + wide)
                values = []
                for level in range(targets):
                    if m < mains:
                        values.append(levels[level, at, q * mains + m])
                    else:
                        last = levels[level, at, BLOCK * mains + q // per]
                        shift = (q % per) * tail
                        values.append(pltpu.roll(last, LANES - shift, 1) if shift else last)
                for k in range(targets):
                    lowest, highest = max(k - (TAPS - 1), 0), min(k, targets - TAPS) + TAPS - 1
                    total = None
                    for level in range(lowest, highest + 1):
                        j = level - lowest
                        term = jnp.broadcast_to(weights[k, row, j:j + 1, lanes], (SUB, wide)) * values[level][:, :wide]
                        total = term if total is None else total + term
                    result[k, at * BLOCK + q, :, lanes] = total
        if ready:
            leave(result.at[:, pl.ds(at * BLOCK, BLOCK)], out.at[:, pl.ds(number * BLOCK, BLOCK)])
    if not ready:
        leave(result, out)
    for copy in copies:
        copy.wait()


def tiles_of(array):
    lead, levels, nlon = array.shape[:-2], array.shape[-2], array.shape[-1]
    split = array.reshape(lead + (levels, nlon // LANES, LANES))
    order = tuple(range(len(lead))) + (len(lead) + 1, len(lead), len(lead) + 2)
    split = with_layout_constraint(split, Layout(major_to_minor=order))
    return jnp.swapaxes(split, -3, -2).reshape(-1, LANES)


VMEM = pl.BlockSpec(memory_space=pltpu.VMEM)
ANY = pl.BlockSpec(memory_space=pl.ANY)
SMEM = pl.BlockSpec(memory_space=pltpu.SMEM)


def call(kernel, outs, args, specs=None, scratch=(), cost=None):
    return pl.pallas_call(
        kernel,
        out_shape=outs,
        in_specs=specs or [VMEM] * len(args),
        out_specs=jax.tree.map(lambda _: VMEM, outs),
        scratch_shapes=list(scratch),
        compiler_params=pltpu.CompilerParams(vmem_limit_bytes=16 << 20),
        cost_estimate=cost,
    )(*args)


def cost(flops, size):
    return pl.CostEstimate(flops=int(flops), bytes_accessed=int(size), transcendentals=0)


def f32(*shape):
    return jax.ShapeDtypeStruct(shape, jnp.float32)


def shards(tracers, wind_x, wind_y, level_counts, source_level, remap_weight):
    count = lax.axis_size("lev")
    bands = lax.axis_size("lat")
    number, depth, rows, nlon = tracers.shape
    targets, _, width = source_level.shape
    size = packed_sizes(nlon, count)[-1]
    blocks = rows // BLOCK
    inner = (rows - 2 * HALO) // BLOCK

    raw = tiles_of(jnp.transpose(tracers, (0, 2, 1, 3)))
    joined = jnp.concatenate([jnp.transpose(wind_x, (1, 0, 2)), jnp.transpose(wind_y, (1, 0, 2))], axis=0)
    halo = f32(HALO + 1, number, nlon)
    state, *sent = call(
        functools.partial(prep_kernel, rows),
        [f32(depth, rows, number, nlon), halo, halo], (raw, joined),
        cost=cost(1, 1))
    second = {i: ((i - 1) ^ 1) + 1 for i in range(1, bands - 1)}
    second_pairs = [(i * count + d, second[i] * count + d if i in second else i * count + (d ^ 1))
                    for i in range(bands) for d in range(count)]

    def beside(sent):
        return [lax.ppermute(sent[0], "lat", [(i, i ^ 1) for i in range(bands)]),
                lax.ppermute(sent[1], ("lat", "lev"), second_pairs)]

    rounds = [beside(sent)]
    taps = call(
        weights_kernel, f32(targets, rows, SUB, width),
        (jnp.transpose(remap_weight, (1, 2, 0, 3)), source_level),
        cost=cost(1, 1))

    def box(units, *lead):
        return lead + (units, size, SUB, LANES)

    def vmem(*shape):
        return pltpu.VMEM(shape, jnp.float32)

    held = -(-rows // SUB) * SUB
    coef = f32(3, depth, held, nlon)
    swept = vmem(depth, rows - 2 * REACH, number, nlon)
    stage = vmem(depth * (rows - 2 * REACH), number, nlon)
    chips = tuple(range(2, count, 2))
    groups = ((0,), (1,)) + tuple((k, k ^ 1) for k in chips)
    inner_units = depth * inner
    result = call(
        functools.partial(interior_kernel, count, rows, groups),
        [f32(*box(len(group) * inner_units)) for group in groups]
        + [f32(depth, rows - 2 * REACH, number, nlon), coef, coef] + [halo] * (2 * depth - 2),
        (state, joined), scratch=[vmem(*box(inner_units, count)), vmem(2, depth, held, nlon), swept, stage, stage, stage],
        cost=cost(1, 1))
    middle, (first, cx, cy), sent = result[:len(groups)], result[len(groups):len(groups) + 3], result[len(groups) + 3:]
    rounds += [beside(sent[2 * i:2 * i + 2]) for i in range(depth - 1)]
    swept = vmem(1, 2 * HALO, number, nlon)
    stage = vmem(2 * HALO, number, nlon)

    def edge(slot, joint, after):
        args = (state, *rounds[slot], first, cx, cy, *(chunk for chunk, _ in joint), *after)
        parts = tuple(part for _, part in joint)
        return call(
            functools.partial(edge_kernel, count, rows, slot, parts),
            [f32(*box(2 + sum(size for _, size in parts) if k == 1 else 2)) for k in range(count)], args,
            specs=[VMEM] * (len(args) - len(after)) + [ANY] * len(after),
            scratch=[vmem(*box(2, count)), vmem(3, 2, SUB, nlon), swept, swept, stage, stage, stage],
            cost=cost(60 * tracers.size, 8 * tracers.size))

    def swapped(sent, k):
        return lax.ppermute(sent, "lev", [(i, i ^ k) for i in range(count)])

    def units_of(k, places):
        return tuple((k, slot, block) for slot, block in places)

    def remap(listed, numbers, height, ready, after=()):
        args = (level_counts, *(chunk for _, chunk in listed), taps, *ready, *after)
        return pl.pallas_call(
            functools.partial(remap_kernel, count, tuple(units for units, _ in listed), numbers, bool(ready)),
            out_shape=f32(targets, height, number, width),
            in_specs=[SMEM] + [VMEM] * (len(args) - 1 - len(after)) + [ANY] * len(after),
            out_specs=ANY,
            scratch_shapes=[
                vmem(targets + 1, len(numbers), size, SUB, LANES),
                vmem(targets, len(numbers) * BLOCK, number, width),
                pltpu.SemaphoreType.DMA((len(numbers) + 1,)),
            ],
            compiler_params=pltpu.CompilerParams(vmem_limit_bytes=16 << 20),
            cost_estimate=cost(1, 1),
        )(*args)

    places = tuple((slot, 1 + b) for slot in range(depth) for b in range(inner))
    passing = tuple((None, None, None) for _ in places)
    arrived = [swapped(sent_on, k) for sent_on, k in zip(middle[2:], chips)]
    middle_chunks = [(units_of(k, places) + passing, chunk) for k, chunk in zip(chips, arrived)]
    middle_chunks.append((units_of(0, places), middle[0]))
    joint, joint_units, after = [(middle[1], (0, inner_units))], units_of(1, places), (taps,)
    edge_chunks, far = [], []
    for slot in range(depth):
        own = ((slot, 0), (slot, blocks - 1))
        done = edge(slot, joint, after)
        crossing = [(units_of(k, own), swapped(done[k], k)) for k in range(count - 1, 1, -1)]
        beside_me = (units_of(1, own) + joint_units, swapped(done[1], 1))
        edge_chunks += crossing + [(units_of(0, own), done[0]), beside_me]
        if slot + 1 < depth:
            far += [chunk for _, chunk in crossing]
        middle_chunks.append(beside_me)
        if slot == 0:
            for k, chunk in zip(chips, arrived):
                chunk, _ = lax.optimization_barrier((chunk, done[0]))
                middle_chunks.append((units_of(k ^ 1, places), swapped(chunk[inner_units:], 1)))
        joint, joint_units, after = [], (), (done[0], beside_me[1])
    middle_rows = remap(middle_chunks, tuple(range(1, blocks - 1)), inner * BLOCK, (), far)
    out = remap(edge_chunks, (0, blocks - 1), rows, (middle_rows,))
    return jnp.transpose(out, (2, 0, 1, 3))


def solution(mesh):
    in_specs = (
        P(None, "lev", ("groups", "lat"), None),
        P("lev", ("groups", "lat"), None),
        P("lev", ("groups", "lat"), None),
        P(),
        P(None, ("groups", "lat"), "lev"),
        P(None, None, ("groups", "lat"), "lev"),
    )
    out_specs = P(None, None, ("groups", "lat"), "lev")
    return jax.shard_map(shards, mesh=mesh, in_specs=in_specs, out_specs=out_specs, check_vma=False)
```

```python
import functools

import jax
import jax.numpy as jnp
from jax import lax
from jax.experimental import pallas as pl
from jax.experimental.layout import Layout, with_layout_constraint
from jax.experimental.pallas import tpu as pltpu
from jax.sharding import PartitionSpec as P

SUBSTEPS = 2
TAPS = 4
REACH = 3
HALO = REACH * SUBSTEPS
BLOCK = 6
LANES = 128
SUB = 8


def spread(row):
    return jnp.broadcast_to(row, (SUB, LANES))


def lane_ids():
    return lax.broadcasted_iota(jnp.int32, (SUB, LANES), 1)


def from_west(tiles, steps, lane):
    turned = [pltpu.roll(t, steps, 1) for t in tiles]
    return [jnp.where(lane < steps, turned[j - 1], turned[j]) for j in range(len(tiles))]


def from_east(tiles, lane):
    turned = [pltpu.roll(t, LANES - 1, 1) for t in tiles]
    count = len(tiles)
    return [jnp.where(lane == LANES - 1, turned[(j + 1) % count], turned[j]) for j in range(count)]


def coefficients(wind):
    size = jnp.abs(wind)
    rest = 1.0 - size
    alpha = wind * rest * rest * (1.0 / 12.0)
    beta = wind * size * rest * (-1.0 / 12.0)
    gamma = wind * size * (3.0 - 2.0 * size)
    return alpha, beta, gamma


def packed_sizes(nlon, count):
    width = nlon // count
    mains, tail = width // LANES, width % LANES
    per = LANES // tail if tail else 1
    tails = -(-BLOCK // per) if tail else 0
    return width, mains, tail, per, BLOCK * mains + tails


def fill_halos(rows, slot, state, winds, first_round, second_round):
    band, bands = lax.axis_index("lat"), lax.axis_size("lat")
    even = band % 2 == 0
    keep = jnp.where((band == 0) | (band == bands - 1), 0.0, 1.0)
    for target, north, scale in ((first_round, even, None), (second_round, jnp.logical_not(even), keep)):
        scaled = (lambda v: v) if scale is None else (lambda v: v * scale)
        row_t = jnp.where(north, rows - HALO, 0)
        row_x = jnp.where(north, rows - REACH, 0)
        row_y = jnp.where(north, rows - REACH - 1, 0)
        for row in range(HALO):
            target[row] = scaled(state[slot, row_t + row])
        for q in range(REACH):
            target[HALO, q:q + 1, :] = scaled(winds[row_x + q, slot:slot + 1, :])
        for q in range(REACH + 1):
            target[HALO, REACH + q:REACH + q + 1, :] = scaled(winds[rows + row_y + q, slot:slot + 1, :])


def prep_kernel(rows, tracers, winds, state, first_round, second_round):
    levels, nlon = state.shape[0], state.shape[3]
    nj = nlon // LANES
    row_stride = nj * levels
    tracer_stride = rows * row_stride

    def body(row, _):
        for level in range(levels):
            for j in range(nj):
                start = row * row_stride + j * levels + level
                state[level, row, :, tile(j)] = tracers[pl.ds(start, SUB, stride=tracer_stride), :]
        return 0

    lax.fori_loop(0, rows, body, 0)
    fill_halos(rows, 0, state, winds, first_round, second_round)


def lat_pass(levels, nj, ranges, cell, coef, store):
    group = 3 if nj % 3 == 0 else 1

    def body(i, _):
        level = i // (nj // group)
        results = []
        for u in range(group):
            lanes = pl.ds(pl.multiple_of(((i % (nj // group)) * group + u) * LANES, LANES), LANES)
            results += [(level, row, lanes, value) for row, value in one(level, lanes)]
        for result in results:
            store(*result)
        return 0

    def one(level, lanes):
        results = []
        for first, last in ranges:
            a = {r: cell(level, r, lanes) for r in range(first - REACH, last + REACH)}
            inter = {f: 7.0 * (a[f - 1] + a[f]) - (a[f - 2] + a[f + 1]) for f in range(first - 1, last + 2)}
            flux = {}
            for f in range(first, last + 1):
                alpha, beta, gamma = [spread(coef(i, level, f, lanes)) for i in range(3)]
                north = gamma > 0
                behind = jnp.where(north, inter[f - 1], inter[f + 1])
                upwind = jnp.where(north, a[f - 1], a[f])
                flux[f] = alpha * inter[f] + beta * behind + gamma * upwind
                if f > first:
                    results.append((f - 1, a[f - 1] - (flux[f] - flux[f - 1])))
        return results

    lax.fori_loop(0, levels * nj // group, body, 0)


def tile(j):
    return slice(j * LANES, (j + 1) * LANES)


def lon_pass(work, swept, coef, inter, west, flux, lane, finish):
    nj = swept.shape[3] // LANES
    each = range(nj)

    def interfaces(n):
        level, _, at = work[n]
        b = [swept[level, at, :, tile(j)] for j in each]
        w1, w2, e1 = from_west(b, 1, lane), from_west(b, 2, lane), from_east(b, lane)
        for j in each:
            inter[n, :, tile(j)] = 7.0 * (w1[j] + b[j]) - (w2[j] + e1[j])
            west[n, :, tile(j)] = w1[j]

    def fluxes(n):
        level, row, at = work[n]
        mid = [inter[n, :, tile(j)] for j in each]
        w1, e1 = from_west(mid, 1, lane), from_east(mid, lane)
        for j in each:
            alpha, beta, gamma = [spread(coef(i, level, row, tile(j))) for i in range(3)]
            right = gamma > 0
            behind = jnp.where(right, w1[j], e1[j])
            upwind = jnp.where(right, west[n, :, tile(j)], swept[level, at, :, tile(j)])
            flux[n, :, tile(j)] = alpha * mid[j] + beta * behind + gamma * upwind

    def update(n):
        level, _, at = work[n]
        here = [flux[n, :, tile(j)] for j in each]
        e1 = from_east(here, lane)
        return [swept[level, at, :, tile(j)] - (e1[j] - here[j]) for j in each]

    groups = len(work) // BLOCK
    for g in range(groups + 2):
        if g < groups:
            for q in range(BLOCK):
                interfaces(g * BLOCK + q)
        if 1 <= g <= groups:
            for q in range(BLOCK):
                fluxes((g - 1) * BLOCK + q)
        if g >= 2:
            finish(g - 2, [update((g - 2) * BLOCK + q) for q in range(BLOCK)])


def pack_block(block, packed, unit, count, lane):
    nlon = len(block[0]) * LANES
    width, mains, tail, per, size = packed_sizes(nlon, count)
    for d in range(count):
        j0, off = (d * width) // LANES, (d * width) % LANES
        for q, tiles in enumerate(block):
            turned = [pltpu.roll(tiles[j0 + m], LANES - off, 1) if off else tiles[j0 + m]
                      for m in range(mains + (1 if off else 0))]
            for m in range(mains):
                whole = jnp.where(lane < LANES - off, turned[m], turned[m + 1]) if off else turned[m]
                packed[d, unit, q * mains + m] = whole
        if tail:
            for g in range(-(-BLOCK // per)):
                total = None
                for place in range(min(per, BLOCK - g * per)):
                    shift = (place * tail - off) % LANES
                    source = block[g * per + place][j0 + mains]
                    moved = pltpu.roll(source, shift, 1) if shift else source
                    total = moved if total is None else jnp.where(lane < place * tail, total, moved)
                packed[d, unit, BLOCK * mains + g] = total


def copy_tiles(pairs):
    values = [source[at] for (source, at), _ in pairs]
    for value, (_, (target, at)) in zip(values, pairs):
        target[at] = value


def copy_units(source, target, start=0):
    for unit in range(source.shape[0]):
        copy_tiles([((source, (unit, i)), (target, (start + unit, i))) for i in range(source.shape[1])])


def hand_out(packed, outs, groups):
    me = lax.axis_index("lev")
    for group, out in zip(groups, outs):
        for place, k in enumerate(group):
            copy_units(packed.at[me ^ k], out, place * packed.shape[1])


def own_coefficients(rows, joined, winds, cx, cy):
    levels, held, nlon = cx.shape[1:]
    keep = jnp.where(lax.axis_index("lat") == 0, 0.0, 1.0)
    for level in range(levels):
        for way in range(2):
            for row in range(rows):
                winds[way, level, row:row + 1, :] = joined[way * rows + row, level:level + 1, :]
        winds[1, level, 0:1, :] = winds[1, level, 0:1, :] * keep
        for way, target in enumerate((cx, cy)):
            for j in range(nlon // LANES):
                parts = coefficients(winds[way, level, :, tile(j)])
                for p in range(3):
                    target[p, level, :, tile(j)] = parts[p]


def put_rows(target, level, at, rows):
    for q, row in enumerate(rows):
        for j, part in enumerate(row):
            target[level, at + q, :, tile(j)] = part


def interior_kernel(count, rows, groups, state, joined, *refs):
    outs, (first, cx, cy), refs = refs[:len(groups)], refs[len(groups):len(groups) + 3], refs[len(groups) + 3:]
    halos, (packed, winds, swept, inter, west, flux) = refs[:-6], refs[-6:]
    levels, nlon = state.shape[0], state.shape[3]
    nj = nlon // LANES
    lane = lane_ids()
    for slot in range(1, levels):
        fill_halos(rows, slot, state, joined, *halos[2 * slot - 2:2 * slot])
    own_coefficients(rows, joined, winds, cx, cy)
    coef_x = lambda i, level, r, lanes: cx[i, level, r:r + 1, lanes]
    coef_y = lambda i, level, f, lanes: cy[i, level, f:f + 1, lanes]

    def put(level, row, lanes, value):
        swept[level, row - REACH, :, lanes] = value

    lat_pass(levels, nj, [(REACH, rows - REACH)], lambda level, r, lanes: state[level, r, :, lanes], coef_y, put)
    work = [(level, row, row - REACH) for level in range(levels) for row in range(REACH, rows - REACH)]

    def keep_first(group, done):
        level, _, at = work[group * BLOCK]
        put_rows(first, level, at, done)

    lon_pass(work, swept, coef_x, inter, west, flux, lane, keep_first)
    lat_pass(levels, nj, [(HALO, rows - HALO)], lambda level, r, lanes: first[level, r - REACH, :, lanes], coef_y, put)
    work_last = [(level, row, row - REACH) for level in range(levels) for row in range(HALO, rows - HALO)]

    def send(group, done):
        pack_block(done, packed, group, count, lane)

    lon_pass(work_last, swept, coef_x, inter, west, flux, lane, send)
    hand_out(packed, outs, groups)


def edge_kernel(count, rows, groups, slot, joint, state, first_round, second_round, first, cx, cy, *refs):
    others = refs[:len(joint)]
    outs, (packed, beyond, swept, edge, inter, west, flux) = refs[-7 - len(groups):-7], refs[-7:]
    nlon = state.shape[3]
    nj = nlon // LANES
    lane = lane_ids()
    odd = lax.axis_index("lat") % 2 == 1

    def halo(south, *at):
        one, two = first_round[at], second_round[at]
        return jnp.where(odd, one, two) if south else jnp.where(odd, two, one)

    for end, south in enumerate((True, False)):
        for j in range(nj):
            parts = coefficients(halo(south, HALO, slice(None), tile(j)))
            for p in range(3):
                beyond[p, end, :, tile(j)] = parts[p]

    def coef_x(i, _, r, lanes):
        if 0 <= r < rows:
            return cx[i, slot, r:r + 1, lanes]
        end, at = (0, r + REACH) if r < 0 else (1, r - rows)
        return beyond[i, end, at:at + 1, lanes]

    def coef_y(i, _, f, lanes):
        if 0 <= f < rows:
            return cy[i, slot, f:f + 1, lanes]
        end, at = (0, f + 2 * REACH + 1) if f < 0 else (1, f - rows + REACH)
        return beyond[i, end, at:at + 1, lanes]

    def cell(_, r, lanes):
        if 0 <= r < rows:
            return state[slot, r, :, lanes]
        return halo(r < 0, r + HALO if r < 0 else r - rows, slice(None), lanes)

    ends = [(-REACH, REACH), (rows - REACH, rows + REACH)]
    ends_last = [(0, HALO), (rows - HALO, rows)]

    def place(row, ranges):
        (a, b), (c, _) = ranges
        return row - a if row < b else row - c + BLOCK

    def cell_first(_, r, lanes):
        if REACH <= r < rows - REACH:
            return first[slot, r - REACH, :, lanes]
        return edge[0, place(r, ends), :, lanes]

    def put(_, row, lanes, value):
        swept[0, place(row, ends), :, lanes] = value

    def put_last(_, row, lanes, value):
        swept[0, place(row, ends_last), :, lanes] = value

    def listed(ranges):
        return [(0, row, place(row, ranges)) for a, b in ranges for row in range(a, b)]

    def keep_edge(group, done):
        put_rows(edge, 0, group * BLOCK, done)

    def send(group, done):
        pack_block(done, packed, group, count, lane)

    lat_pass(1, nj, ends, cell, coef_y, put)
    lon_pass(listed(ends), swept, coef_x, inter, west, flux, lane, keep_edge)
    lat_pass(1, nj, ends_last, cell_first, coef_y, put_last)
    lon_pass(listed(ends_last), swept, coef_x, inter, west, flux, lane, send)
    hand_out(packed, outs, groups)
    place = packed.shape[1]
    for other, (begin, size) in zip(others, joint):
        copy_units(other.at[pl.ds(begin, size)], outs[1], place)
        place += size


def weights_kernel(weights, source, out):
    targets, rows, taps, width = weights.shape

    for row in range(rows):
        for k in range(targets):
            lowest, highest = max(k - (TAPS - 1), 0), min(k, targets - TAPS)
            w = weights[k, row]
            w = jnp.concatenate([w, jnp.zeros((SUB - taps, width), jnp.float32)], axis=0)
            at = jnp.broadcast_to(source[k, row:row + 1, :], (SUB, width))
            total = w
            for g in range(lowest + 1, highest + 1):
                total = jnp.where(at == g, pltpu.roll(w, g - lowest, 0), total)
            out[k, row] = total


def remap_kernel(count, plan, numbers, counts, *refs):
    chunks, weights, (out, levels, result, sems) = refs[:len(plan)], refs[len(plan)], refs[-4:]
    me = lax.axis_index("lev")
    targets, _, _, width = result.shape
    _, mains, tail, per, _ = packed_sizes(width * count, count)
    copies = []

    def leave(source, target):
        copy = pltpu.make_async_copy(source, target, sems.at[len(copies)])
        copy.start()
        copies.append(copy)

    def level_of(k, slot):
        d = me ^ k
        start = jnp.int32(0)
        for e in range(count):
            start = start + jnp.where(e < d, counts[e], 0)
        return jnp.where(slot < counts[d], start + slot, targets)

    for units, chunk in zip(plan, chunks):
        for unit, (k, slot, number) in enumerate(units):
            if number in numbers:
                at = numbers.index(number)
                copy_tiles([((chunk, (unit, i)), (levels, (level_of(k, slot), at, i))) for i in range(chunk.shape[1])])

    for at, number in enumerate(numbers):
        for q in range(BLOCK):
            row = number * BLOCK + q
            for m in range(mains + (1 if tail else 0)):
                wide = LANES if m < mains else tail
                lanes = slice(m * LANES, m * LANES + wide)
                values = []
                for level in range(targets):
                    if m < mains:
                        values.append(levels[level, at, q * mains + m])
                    else:
                        last = levels[level, at, BLOCK * mains + q // per]
                        shift = (q % per) * tail
                        values.append(pltpu.roll(last, LANES - shift, 1) if shift else last)
                for k in range(targets):
                    lowest, highest = max(k - (TAPS - 1), 0), min(k, targets - TAPS) + TAPS - 1
                    total = None
                    for level in range(lowest, highest + 1):
                        j = level - lowest
                        term = jnp.broadcast_to(weights[k, row, j:j + 1, lanes], (SUB, wide)) * values[level][:, :wide]
                        total = term if total is None else total + term
                    result[k, at * BLOCK + q, :, lanes] = total
        leave(result.at[:, pl.ds(at * BLOCK, BLOCK)], out.at[:, pl.ds(number * BLOCK, BLOCK)])
    for copy in copies:
        copy.wait()


def mark_kernel(*refs):
    refs[-1][...] = jnp.zeros((SUB, LANES), jnp.float32)


def tiles_of(array):
    lead, levels, nlon = array.shape[:-2], array.shape[-2], array.shape[-1]
    split = array.reshape(lead + (levels, nlon // LANES, LANES))
    order = tuple(range(len(lead))) + (len(lead) + 1, len(lead), len(lead) + 2)
    split = with_layout_constraint(split, Layout(major_to_minor=order))
    return jnp.swapaxes(split, -3, -2).reshape(-1, LANES)


VMEM = pl.BlockSpec(memory_space=pltpu.VMEM)
ANY = pl.BlockSpec(memory_space=pl.ANY)
SMEM = pl.BlockSpec(memory_space=pltpu.SMEM)


def call(kernel, outs, args, specs=None, scratch=(), cost=None):
    return pl.pallas_call(
        kernel,
        out_shape=outs,
        in_specs=specs or [VMEM] * len(args),
        out_specs=jax.tree.map(lambda _: VMEM, outs),
        scratch_shapes=list(scratch),
        compiler_params=pltpu.CompilerParams(vmem_limit_bytes=16 << 20),
        cost_estimate=cost,
    )(*args)


def cost(flops, size):
    return pl.CostEstimate(flops=int(flops), bytes_accessed=int(size), transcendentals=0)


def f32(*shape):
    return jax.ShapeDtypeStruct(shape, jnp.float32)


def shards(tracers, wind_x, wind_y, level_counts, source_level, remap_weight):
    count = lax.axis_size("lev")
    bands = lax.axis_size("lat")
    number, depth, rows, nlon = tracers.shape
    targets, _, width = source_level.shape
    size = packed_sizes(nlon, count)[-1]
    blocks = rows // BLOCK
    inner = (rows - 2 * HALO) // BLOCK

    raw = tiles_of(jnp.transpose(tracers, (0, 2, 1, 3)))
    joined = jnp.concatenate([jnp.transpose(wind_x, (1, 0, 2)), jnp.transpose(wind_y, (1, 0, 2))], axis=0)
    halo = f32(HALO + 1, number, nlon)
    state, *sent = call(
        functools.partial(prep_kernel, rows),
        [f32(depth, rows, number, nlon), halo, halo], (raw, joined),
        cost=cost(1, 1))
    second = {i: ((i - 1) ^ 1) + 1 for i in range(1, bands - 1)}
    second_pairs = [(i * count + d, second[i] * count + d if i in second else i * count + (d ^ 1))
                    for i in range(bands) for d in range(count)]

    def beside(sent):
        return [lax.ppermute(sent[0], "lat", [(i, i ^ 1) for i in range(bands)]),
                lax.ppermute(sent[1], ("lat", "lev"), second_pairs)]

    rounds = [beside(sent)]
    taps = call(
        weights_kernel, f32(targets, rows, SUB, width),
        (jnp.transpose(remap_weight, (1, 2, 0, 3)), source_level),
        cost=cost(1, 1))

    def box(units, *lead):
        return lead + (units, size, SUB, LANES)

    def vmem(*shape):
        return pltpu.VMEM(shape, jnp.float32)

    held = -(-rows // SUB) * SUB
    coef = f32(3, depth, held, nlon)
    swept = vmem(depth, rows - 2 * REACH, number, nlon)
    stage = vmem(depth * (rows - 2 * REACH), number, nlon)
    chips = tuple(range(2, count, 2))
    groups = ((0,), (1,)) + tuple((k, k ^ 1) for k in chips)
    inner_units = depth * inner
    result = call(
        functools.partial(interior_kernel, count, rows, groups),
        [f32(*box(len(group) * inner_units)) for group in groups]
        + [f32(depth, rows - 2 * REACH, number, nlon), coef, coef] + [halo] * (2 * depth - 2),
        (state, joined), scratch=[vmem(*box(inner_units, count)), vmem(2, depth, held, nlon), swept, stage, stage, stage],
        cost=cost(1, 1))
    middle, (first, cx, cy), sent = result[:len(groups)], result[len(groups):len(groups) + 3], result[len(groups) + 3:]
    rounds += [beside(sent[2 * i:2 * i + 2]) for i in range(depth - 1)]
    swept = vmem(1, 2 * HALO, number, nlon)
    stage = vmem(2 * HALO, number, nlon)

    def edge(slot, groups, joint, after):
        args = (state, *rounds[slot], first, cx, cy, *(chunk for chunk, _ in joint), *after)
        parts = tuple(part for _, part in joint)
        units = [2 * len(group) + (sum(size for _, size in parts) if group == (1,) else 0) for group in groups]
        return call(
            functools.partial(edge_kernel, count, rows, groups, slot, parts),
            [f32(*box(n)) for n in units], args,
            specs=[VMEM] * (len(args) - len(after)) + [ANY] * len(after),
            scratch=[vmem(*box(2, count)), vmem(3, 2, SUB, nlon), swept, swept, stage, stage, stage],
            cost=cost(60 * tracers.size, 8 * tracers.size))

    def swapped(sent, k):
        return lax.ppermute(sent, "lev", [(i, i ^ k) for i in range(count)])

    def units_of(k, places):
        return tuple((k, slot, block) for slot, block in places)

    def remap(listed, after):
        args = (level_counts, *(chunk for _, chunk in listed), taps, *after)
        return pl.pallas_call(
            functools.partial(remap_kernel, count, tuple(units for units, _ in listed), tuple(range(blocks))),
            out_shape=f32(targets, rows, number, width),
            in_specs=[SMEM] + [VMEM] * (len(args) - 1 - len(after)) + [ANY] * len(after),
            out_specs=ANY,
            scratch_shapes=[
                vmem(targets + 1, blocks, size, SUB, LANES),
                vmem(targets, rows, number, width),
                pltpu.SemaphoreType.DMA((blocks,)),
            ],
            compiler_params=pltpu.CompilerParams(vmem_limit_bytes=16 << 20),
            cost_estimate=cost(1, 1),
        )(*args)

    def mark(chunks):
        return pl.pallas_call(
            mark_kernel, out_shape=f32(SUB, LANES), in_specs=[ANY] * len(chunks), out_specs=VMEM, cost_estimate=cost(1, 1),
        )(*chunks)

    places = tuple((slot, 1 + b) for slot in range(depth) for b in range(inner))
    passing = tuple((None, None, None) for _ in places)
    arrived = [swapped(chunk, k) for k, chunk in zip(chips, middle[2:])]
    listed = [(units_of(k, places) + passing, chunk) for k, chunk in zip(chips, arrived)]
    listed.append((units_of(0, places), middle[0]))
    beside_me = [(units_of(1, places), middle[1])]
    after, marks = (taps,), []
    for slot in range(depth):
        own = ((slot, 0), (slot, blocks - 1))
        done = edge(slot, tuple((k,) for k in range(count)), [], after)
        crossing = [(units_of(k, own), swapped(done[k], k)) for k in range(count - 1, 1, -1)]
        listed += crossing + [(units_of(0, own), done[0])]
        beside_me.append((units_of(1, own), done[1]))
        marks.append(mark([chunk for _, chunk in crossing]))
        after = (done[0], *arrived)
    beside_me += [(units_of(k ^ 1, places), chunk) for k, chunk in zip(chips, arrived)]
    waiting = lax.optimization_barrier((*(chunk for _, chunk in beside_me), done[0]))
    listed += [(units, swapped(chunk[chunk.shape[0] - len(units):], 1)) for (units, _), chunk in zip(beside_me, waiting)]
    out = remap(listed, marks)
    return jnp.transpose(out, (2, 0, 1, 3))


def solution(mesh):
    in_specs = (
        P(None, "lev", ("groups", "lat"), None),
        P("lev", ("groups", "lat"), None),
        P("lev", ("groups", "lat"), None),
        P(),
        P(None, ("groups", "lat"), "lev"),
        P(None, None, ("groups", "lat"), "lev"),
    )
    out_specs = P(None, None, ("groups", "lat"), "lev")
    return jax.shard_map(shards, mesh=mesh, in_specs=in_specs, out_specs=out_specs, check_vma=False)
```

```python
import functools

import jax
import jax.numpy as jnp
from jax import lax
from jax.experimental import pallas as pl
from jax.experimental.layout import Layout, with_layout_constraint
from jax.experimental.pallas import tpu as pltpu
from jax.sharding import PartitionSpec as P

SUBSTEPS = 2
TAPS = 4
REACH = 3
HALO = REACH * SUBSTEPS
BLOCK = 6
LANES = 128
SUB = 8


def spread(row):
    return jnp.broadcast_to(row, (SUB, LANES))


def lane_ids():
    return lax.broadcasted_iota(jnp.int32, (SUB, LANES), 1)


def from_west(tiles, steps, lane):
    turned = [pltpu.roll(t, steps, 1) for t in tiles]
    return [jnp.where(lane < steps, turned[j - 1], turned[j]) for j in range(len(tiles))]


def from_east(tiles, lane):
    turned = [pltpu.roll(t, LANES - 1, 1) for t in tiles]
    count = len(tiles)
    return [jnp.where(lane == LANES - 1, turned[(j + 1) % count], turned[j]) for j in range(count)]


def coefficients(wind):
    size = jnp.abs(wind)
    rest = 1.0 - size
    alpha = wind * rest * rest * (1.0 / 12.0)
    beta = wind * size * rest * (-1.0 / 12.0)
    gamma = wind * size * (3.0 - 2.0 * size)
    return alpha, beta, gamma


def packed_sizes(nlon, count):
    width = nlon // count
    mains, tail = width // LANES, width % LANES
    per = LANES // tail if tail else 1
    tails = -(-BLOCK // per) if tail else 0
    return width, mains, tail, per, BLOCK * mains + tails


def fill_halos(rows, slot, state, winds, first_round, second_round):
    band, bands = lax.axis_index("lat"), lax.axis_size("lat")
    even = band % 2 == 0
    keep = jnp.where((band == 0) | (band == bands - 1), 0.0, 1.0)
    for target, north, scale in ((first_round, even, None), (second_round, jnp.logical_not(even), keep)):
        scaled = (lambda v: v) if scale is None else (lambda v: v * scale)
        row_t = jnp.where(north, rows - HALO, 0)
        row_x = jnp.where(north, rows - REACH, 0)
        row_y = jnp.where(north, rows - REACH - 1, 0)
        for row in range(HALO):
            target[row] = scaled(state[slot, row_t + row])
        for q in range(REACH):
            target[HALO, q:q + 1, :] = scaled(winds[row_x + q, slot:slot + 1, :])
        for q in range(REACH + 1):
            target[HALO, REACH + q:REACH + q + 1, :] = scaled(winds[rows + row_y + q, slot:slot + 1, :])


def prep_kernel(rows, tracers, winds, state, first_round, second_round):
    levels, nlon = state.shape[0], state.shape[3]
    nj = nlon // LANES
    row_stride = nj * levels
    tracer_stride = rows * row_stride

    def body(row, _):
        for level in range(levels):
            for j in range(nj):
                start = row * row_stride + j * levels + level
                state[level, row, :, tile(j)] = tracers[pl.ds(start, SUB, stride=tracer_stride), :]
        return 0

    lax.fori_loop(0, rows, body, 0)
    fill_halos(rows, 0, state, winds, first_round, second_round)


def lat_pass(levels, nj, ranges, cell, coef, store):
    group = 3 if nj % 3 == 0 else 1

    def body(i, _):
        level = i // (nj // group)
        results = []
        for u in range(group):
            lanes = pl.ds(pl.multiple_of(((i % (nj // group)) * group + u) * LANES, LANES), LANES)
            results += [(level, row, lanes, value) for row, value in one(level, lanes)]
        for result in results:
            store(*result)
        return 0

    def one(level, lanes):
        results = []
        for first, last in ranges:
            a = {r: cell(level, r, lanes) for r in range(first - REACH, last + REACH)}
            inter = {f: 7.0 * (a[f - 1] + a[f]) - (a[f - 2] + a[f + 1]) for f in range(first - 1, last + 2)}
            flux = {}
            for f in range(first, last + 1):
                alpha, beta, gamma = [spread(coef(i, level, f, lanes)) for i in range(3)]
                north = gamma > 0
                behind = jnp.where(north, inter[f - 1], inter[f + 1])
                upwind = jnp.where(north, a[f - 1], a[f])
                flux[f] = alpha * inter[f] + beta * behind + gamma * upwind
                if f > first:
                    results.append((f - 1, a[f - 1] - (flux[f] - flux[f - 1])))
        return results

    lax.fori_loop(0, levels * nj // group, body, 0)


def tile(j):
    return slice(j * LANES, (j + 1) * LANES)


def lon_pass(work, swept, coef, inter, west, flux, lane, finish):
    nj = swept.shape[3] // LANES
    each = range(nj)

    def interfaces(n):
        level, _, at = work[n]
        b = [swept[level, at, :, tile(j)] for j in each]
        w1, w2, e1 = from_west(b, 1, lane), from_west(b, 2, lane), from_east(b, lane)
        for j in each:
            inter[n, :, tile(j)] = 7.0 * (w1[j] + b[j]) - (w2[j] + e1[j])
            west[n, :, tile(j)] = w1[j]

    def fluxes(n):
        level, row, at = work[n]
        mid = [inter[n, :, tile(j)] for j in each]
        w1, e1 = from_west(mid, 1, lane), from_east(mid, lane)
        for j in each:
            alpha, beta, gamma = [spread(coef(i, level, row, tile(j))) for i in range(3)]
            right = gamma > 0
            behind = jnp.where(right, w1[j], e1[j])
            upwind = jnp.where(right, west[n, :, tile(j)], swept[level, at, :, tile(j)])
            flux[n, :, tile(j)] = alpha * mid[j] + beta * behind + gamma * upwind

    def update(n):
        level, _, at = work[n]
        here = [flux[n, :, tile(j)] for j in each]
        e1 = from_east(here, lane)
        return [swept[level, at, :, tile(j)] - (e1[j] - here[j]) for j in each]

    groups = len(work) // BLOCK
    for g in range(groups + 2):
        if g < groups:
            for q in range(BLOCK):
                interfaces(g * BLOCK + q)
        if 1 <= g <= groups:
            for q in range(BLOCK):
                fluxes((g - 1) * BLOCK + q)
        if g >= 2:
            finish(g - 2, [update((g - 2) * BLOCK + q) for q in range(BLOCK)])


def pack_block(block, packed, unit, count, lane):
    nlon = len(block[0]) * LANES
    width, mains, tail, per, size = packed_sizes(nlon, count)
    for d in range(count):
        j0, off = (d * width) // LANES, (d * width) % LANES
        for q, tiles in enumerate(block):
            turned = [pltpu.roll(tiles[j0 + m], LANES - off, 1) if off else tiles[j0 + m]
                      for m in range(mains + (1 if off else 0))]
            for m in range(mains):
                whole = jnp.where(lane < LANES - off, turned[m], turned[m + 1]) if off else turned[m]
                packed[d, unit, q * mains + m] = whole
        if tail:
            for g in range(-(-BLOCK // per)):
                total = None
                for place in range(min(per, BLOCK - g * per)):
                    shift = (place * tail - off) % LANES
                    source = block[g * per + place][j0 + mains]
                    moved = pltpu.roll(source, shift, 1) if shift else source
                    total = moved if total is None else jnp.where(lane < place * tail, total, moved)
                packed[d, unit, BLOCK * mains + g] = total


def copy_tiles(pairs):
    values = [source[at] for (source, at), _ in pairs]
    for value, (_, (target, at)) in zip(values, pairs):
        target[at] = value


def copy_units(source, target, start=0):
    for unit in range(source.shape[0]):
        copy_tiles([((source, (unit, i)), (target, (start + unit, i))) for i in range(source.shape[1])])


def hand_out(packed, outs, groups):
    me = lax.axis_index("lev")
    for group, out in zip(groups, outs):
        for place, k in enumerate(group):
            copy_units(packed.at[me ^ k], out, place * packed.shape[1])


def own_coefficients(rows, joined, winds, cx, cy):
    levels, held, nlon = cx.shape[1:]
    keep = jnp.where(lax.axis_index("lat") == 0, 0.0, 1.0)
    for level in range(levels):
        for way in range(2):
            for row in range(rows):
                winds[way, level, row:row + 1, :] = joined[way * rows + row, level:level + 1, :]
        winds[1, level, 0:1, :] = winds[1, level, 0:1, :] * keep
        for way, target in enumerate((cx, cy)):
            for j in range(nlon // LANES):
                parts = coefficients(winds[way, level, :, tile(j)])
                for p in range(3):
                    target[p, level, :, tile(j)] = parts[p]


def put_rows(target, level, at, rows):
    for q, row in enumerate(rows):
        for j, part in enumerate(row):
            target[level, at + q, :, tile(j)] = part


def interior_kernel(count, rows, groups, state, joined, *refs):
    outs, (first, cx, cy), refs = refs[:len(groups)], refs[len(groups):len(groups) + 3], refs[len(groups) + 3:]
    halos, (packed, winds, swept, inter, west, flux) = refs[:-6], refs[-6:]
    levels, nlon = state.shape[0], state.shape[3]
    nj = nlon // LANES
    lane = lane_ids()
    for slot in range(1, levels):
        fill_halos(rows, slot, state, joined, *halos[2 * slot - 2:2 * slot])
    own_coefficients(rows, joined, winds, cx, cy)
    coef_x = lambda i, level, r, lanes: cx[i, level, r:r + 1, lanes]
    coef_y = lambda i, level, f, lanes: cy[i, level, f:f + 1, lanes]

    def put(level, row, lanes, value):
        swept[level, row - REACH, :, lanes] = value

    lat_pass(levels, nj, [(REACH, rows - REACH)], lambda level, r, lanes: state[level, r, :, lanes], coef_y, put)
    work = [(level, row, row - REACH) for level in range(levels) for row in range(REACH, rows - REACH)]

    def keep_first(group, done):
        level, _, at = work[group * BLOCK]
        put_rows(first, level, at, done)

    lon_pass(work, swept, coef_x, inter, west, flux, lane, keep_first)
    lat_pass(levels, nj, [(HALO, rows - HALO)], lambda level, r, lanes: first[level, r - REACH, :, lanes], coef_y, put)
    work_last = [(level, row, row - REACH) for level in range(levels) for row in range(HALO, rows - HALO)]

    def send(group, done):
        pack_block(done, packed, group, count, lane)

    lon_pass(work_last, swept, coef_x, inter, west, flux, lane, send)
    hand_out(packed, outs, groups)


def edge_kernel(count, rows, groups, slot, joint, state, first_round, second_round, first, cx, cy, *refs):
    others = refs[:len(joint)]
    outs, (packed, beyond, swept, edge, inter, west, flux) = refs[-7 - len(groups):-7], refs[-7:]
    nlon = state.shape[3]
    nj = nlon // LANES
    lane = lane_ids()
    odd = lax.axis_index("lat") % 2 == 1

    def halo(south, *at):
        one, two = first_round[at], second_round[at]
        return jnp.where(odd, one, two) if south else jnp.where(odd, two, one)

    for end, south in enumerate((True, False)):
        for j in range(nj):
            parts = coefficients(halo(south, HALO, slice(None), tile(j)))
            for p in range(3):
                beyond[p, end, :, tile(j)] = parts[p]

    def coef_x(i, _, r, lanes):
        if 0 <= r < rows:
            return cx[i, slot, r:r + 1, lanes]
        end, at = (0, r + REACH) if r < 0 else (1, r - rows)
        return beyond[i, end, at:at + 1, lanes]

    def coef_y(i, _, f, lanes):
        if 0 <= f < rows:
            return cy[i, slot, f:f + 1, lanes]
        end, at = (0, f + 2 * REACH + 1) if f < 0 else (1, f - rows + REACH)
        return beyond[i, end, at:at + 1, lanes]

    def cell(_, r, lanes):
        if 0 <= r < rows:
            return state[slot, r, :, lanes]
        return halo(r < 0, r + HALO if r < 0 else r - rows, slice(None), lanes)

    ends = [(-REACH, REACH), (rows - REACH, rows + REACH)]
    ends_last = [(0, HALO), (rows - HALO, rows)]

    def place(row, ranges):
        (a, b), (c, _) = ranges
        return row - a if row < b else row - c + BLOCK

    def cell_first(_, r, lanes):
        if REACH <= r < rows - REACH:
            return first[slot, r - REACH, :, lanes]
        return edge[0, place(r, ends), :, lanes]

    def put(_, row, lanes, value):
        swept[0, place(row, ends), :, lanes] = value

    def put_last(_, row, lanes, value):
        swept[0, place(row, ends_last), :, lanes] = value

    def listed(ranges):
        return [(0, row, place(row, ranges)) for a, b in ranges for row in range(a, b)]

    def keep_edge(group, done):
        put_rows(edge, 0, group * BLOCK, done)

    def send(group, done):
        pack_block(done, packed, group, count, lane)

    lat_pass(1, nj, ends, cell, coef_y, put)
    lon_pass(listed(ends), swept, coef_x, inter, west, flux, lane, keep_edge)
    lat_pass(1, nj, ends_last, cell_first, coef_y, put_last)
    lon_pass(listed(ends_last), swept, coef_x, inter, west, flux, lane, send)
    hand_out(packed, outs, groups)
    place = packed.shape[1]
    for other, (begin, size) in zip(others, joint):
        copy_units(other.at[pl.ds(begin, size)], outs[1], place)
        place += size


def weights_kernel(weights, source, out):
    targets, rows, taps, width = weights.shape

    for row in range(rows):
        for k in range(targets):
            lowest, highest = max(k - (TAPS - 1), 0), min(k, targets - TAPS)
            w = weights[k, row]
            w = jnp.concatenate([w, jnp.zeros((SUB - taps, width), jnp.float32)], axis=0)
            at = jnp.broadcast_to(source[k, row:row + 1, :], (SUB, width))
            total = w
            for g in range(lowest + 1, highest + 1):
                total = jnp.where(at == g, pltpu.roll(w, g - lowest, 0), total)
            out[k, row] = total


def remap_kernel(count, plan, numbers, counts, *refs):
    chunks, weights, (out, levels, result, sems) = refs[:len(plan)], refs[len(plan)], refs[-4:]
    me = lax.axis_index("lev")
    targets, _, _, width = result.shape
    _, mains, tail, per, _ = packed_sizes(width * count, count)
    copies = []

    def leave(source, target):
        copy = pltpu.make_async_copy(source, target, sems.at[len(copies)])
        copy.start()
        copies.append(copy)

    def level_of(k, slot):
        d = me ^ k
        start = jnp.int32(0)
        for e in range(count):
            start = start + jnp.where(e < d, counts[e], 0)
        return jnp.where(slot < counts[d], start + slot, targets)

    for units, chunk in zip(plan, chunks):
        for unit, (k, slot, number) in enumerate(units):
            if number in numbers:
                at = numbers.index(number)
                copy_tiles([((chunk, (unit, i)), (levels, (level_of(k, slot), at, i))) for i in range(chunk.shape[1])])

    for at, number in enumerate(numbers):
        for q in range(BLOCK):
            row = number * BLOCK + q
            for m in range(mains + (1 if tail else 0)):
                wide = LANES if m < mains else tail
                lanes = slice(m * LANES, m * LANES + wide)
                values = []
                for level in range(targets):
                    if m < mains:
                        values.append(levels[level, at, q * mains + m])
                    else:
                        last = levels[level, at, BLOCK * mains + q // per]
                        shift = (q % per) * tail
                        values.append(pltpu.roll(last, LANES - shift, 1) if shift else last)
                for k in range(targets):
                    lowest, highest = max(k - (TAPS - 1), 0), min(k, targets - TAPS) + TAPS - 1
                    total = None
                    for level in range(lowest, highest + 1):
                        j = level - lowest
                        term = jnp.broadcast_to(weights[k, row, j:j + 1, lanes], (SUB, wide)) * values[level][:, :wide]
                        total = term if total is None else total + term
                    result[k, at * BLOCK + q, :, lanes] = total
        leave(result.at[:, pl.ds(at * BLOCK, BLOCK)], out.at[:, pl.ds(number * BLOCK, BLOCK)])
    for copy in copies:
        copy.wait()


def mark_kernel(*refs):
    refs[-1][...] = jnp.zeros((SUB, LANES), jnp.float32)


def tiles_of(array):
    lead, levels, nlon = array.shape[:-2], array.shape[-2], array.shape[-1]
    split = array.reshape(lead + (levels, nlon // LANES, LANES))
    order = tuple(range(len(lead))) + (len(lead) + 1, len(lead), len(lead) + 2)
    split = with_layout_constraint(split, Layout(major_to_minor=order))
    return jnp.swapaxes(split, -3, -2).reshape(-1, LANES)


VMEM = pl.BlockSpec(memory_space=pltpu.VMEM)
ANY = pl.BlockSpec(memory_space=pl.ANY)
SMEM = pl.BlockSpec(memory_space=pltpu.SMEM)


def call(kernel, outs, args, specs=None, scratch=(), cost=None):
    return pl.pallas_call(
        kernel,
        out_shape=outs,
        in_specs=specs or [VMEM] * len(args),
        out_specs=jax.tree.map(lambda _: VMEM, outs),
        scratch_shapes=list(scratch),
        compiler_params=pltpu.CompilerParams(vmem_limit_bytes=16 << 20),
        cost_estimate=cost,
    )(*args)


def cost(flops, size):
    return pl.CostEstimate(flops=int(flops), bytes_accessed=int(size), transcendentals=0)


def f32(*shape):
    return jax.ShapeDtypeStruct(shape, jnp.float32)


def shards(tracers, wind_x, wind_y, level_counts, source_level, remap_weight):
    count = lax.axis_size("lev")
    bands = lax.axis_size("lat")
    number, depth, rows, nlon = tracers.shape
    targets, _, width = source_level.shape
    size = packed_sizes(nlon, count)[-1]
    blocks = rows // BLOCK
    inner = (rows - 2 * HALO) // BLOCK

    raw = tiles_of(jnp.transpose(tracers, (0, 2, 1, 3)))
    joined = jnp.concatenate([jnp.transpose(wind_x, (1, 0, 2)), jnp.transpose(wind_y, (1, 0, 2))], axis=0)
    halo = f32(HALO + 1, number, nlon)
    state, *sent = call(
        functools.partial(prep_kernel, rows),
        [f32(depth, rows, number, nlon), halo, halo], (raw, joined),
        cost=cost(1, 1))
    second = {i: ((i - 1) ^ 1) + 1 for i in range(1, bands - 1)}
    second_pairs = [(i * count + d, second[i] * count + d if i in second else i * count + (d ^ 1))
                    for i in range(bands) for d in range(count)]

    def beside(sent):
        return [lax.ppermute(sent[0], "lat", [(i, i ^ 1) for i in range(bands)]),
                lax.ppermute(sent[1], ("lat", "lev"), second_pairs)]

    rounds = [beside(sent)]
    taps = call(
        weights_kernel, f32(targets, rows, SUB, width),
        (jnp.transpose(remap_weight, (1, 2, 0, 3)), source_level),
        cost=cost(1, 1))

    def box(units, *lead):
        return lead + (units, size, SUB, LANES)

    def vmem(*shape):
        return pltpu.VMEM(shape, jnp.float32)

    held = -(-rows // SUB) * SUB
    coef = f32(3, depth, held, nlon)
    swept = vmem(depth, rows - 2 * REACH, number, nlon)
    stage = vmem(depth * (rows - 2 * REACH), number, nlon)
    chips = tuple(range(2, count, 2))
    groups = ((0,), (1,)) + tuple((k, k ^ 1) for k in chips)
    inner_units = depth * inner
    result = call(
        functools.partial(interior_kernel, count, rows, groups),
        [f32(*box(len(group) * inner_units)) for group in groups]
        + [f32(depth, rows - 2 * REACH, number, nlon), coef, coef] + [halo] * (2 * depth - 2),
        (state, joined), scratch=[vmem(*box(inner_units, count)), vmem(2, depth, held, nlon), swept, stage, stage, stage],
        cost=cost(1, 1))
    middle, (first, cx, cy), sent = result[:len(groups)], result[len(groups):len(groups) + 3], result[len(groups) + 3:]
    rounds += [beside(sent[2 * i:2 * i + 2]) for i in range(depth - 1)]
    swept = vmem(1, 2 * HALO, number, nlon)
    stage = vmem(2 * HALO, number, nlon)

    def edge(slot, groups, joint, after):
        args = (state, *rounds[slot], first, cx, cy, *(chunk for chunk, _ in joint), *after)
        parts = tuple(part for _, part in joint)
        units = [2 * len(group) + (sum(size for _, size in parts) if group == (1,) else 0) for group in groups]
        return call(
            functools.partial(edge_kernel, count, rows, groups, slot, parts),
            [f32(*box(n)) for n in units], args,
            specs=[VMEM] * (len(args) - len(after)) + [ANY] * len(after),
            scratch=[vmem(*box(2, count)), vmem(3, 2, SUB, nlon), swept, swept, stage, stage, stage],
            cost=cost(60 * tracers.size, 8 * tracers.size))

    def swapped(sent, k):
        return lax.ppermute(sent, "lev", [(i, i ^ k) for i in range(count)])

    def units_of(k, places):
        return tuple((k, slot, block) for slot, block in places)

    def remap(listed, after):
        args = (level_counts, *(chunk for _, chunk in listed), taps, *after)
        return pl.pallas_call(
            functools.partial(remap_kernel, count, tuple(units for units, _ in listed), tuple(range(blocks))),
            out_shape=f32(targets, rows, number, width),
            in_specs=[SMEM] + [VMEM] * (len(args) - 1 - len(after)) + [ANY] * len(after),
            out_specs=ANY,
            scratch_shapes=[
                vmem(targets + 1, blocks, size, SUB, LANES),
                vmem(targets, rows, number, width),
                pltpu.SemaphoreType.DMA((blocks,)),
            ],
            compiler_params=pltpu.CompilerParams(vmem_limit_bytes=16 << 20),
            cost_estimate=cost(1, 1),
        )(*args)

    def mark(chunks):
        return pl.pallas_call(
            mark_kernel, out_shape=f32(SUB, LANES), in_specs=[ANY] * len(chunks), out_specs=VMEM, cost_estimate=cost(1, 1),
            compiler_params=pltpu.CompilerParams(vmem_limit_bytes=1 << 20),
        )(*chunks)

    places = tuple((slot, 1 + b) for slot in range(depth) for b in range(inner))
    passing = tuple((None, None, None) for _ in places)
    arrived = [swapped(chunk, k) for k, chunk in zip(chips, middle[2:])]
    listed = [(units_of(k, places) + passing, chunk) for k, chunk in zip(chips, arrived)]
    listed.append((units_of(0, places), middle[0]))
    beside_me = [(units_of(1, places), middle[1])]
    after, marks = (taps,), []
    for slot in range(depth):
        own = ((slot, 0), (slot, blocks - 1))
        done = edge(slot, tuple((k,) for k in range(count)), [], after)
        crossing = [(units_of(k, own), swapped(done[k], k)) for k in range(count - 1, 1, -1)]
        listed += crossing + [(units_of(0, own), done[0])]
        beside_me.append((units_of(1, own), done[1]))
        marks.append(mark([chunk for _, chunk in crossing]))
        after = (done[0], *arrived)
    beside_me += [(units_of(k ^ 1, places), chunk) for k, chunk in zip(chips, arrived)]
    waiting = lax.optimization_barrier((*(chunk for _, chunk in beside_me), done[0]))
    listed += [(units, swapped(chunk[chunk.shape[0] - len(units):], 1)) for (units, _), chunk in zip(beside_me, waiting)]
    out = remap(listed, marks)
    return jnp.transpose(out, (2, 0, 1, 3))


def solution(mesh):
    in_specs = (
        P(None, "lev", ("groups", "lat"), None),
        P("lev", ("groups", "lat"), None),
        P("lev", ("groups", "lat"), None),
        P(),
        P(None, ("groups", "lat"), "lev"),
        P(None, None, ("groups", "lat"), "lev"),
    )
    out_specs = P(None, None, ("groups", "lat"), "lev")
    return jax.shard_map(shards, mesh=mesh, in_specs=in_specs, out_specs=out_specs, check_vma=False)
```

```python
import functools

import jax
import jax.numpy as jnp
from jax import lax
from jax.experimental import pallas as pl
from jax.experimental.layout import Layout, with_layout_constraint
from jax.experimental.pallas import tpu as pltpu
from jax.sharding import PartitionSpec as P

SUBSTEPS = 2
TAPS = 4
REACH = 3
HALO = REACH * SUBSTEPS
BLOCK = 6
LANES = 128
SUB = 8


def spread(row):
    return jnp.broadcast_to(row, (SUB, LANES))


def lane_ids():
    return lax.broadcasted_iota(jnp.int32, (SUB, LANES), 1)


def from_west(tiles, steps, lane):
    turned = [pltpu.roll(t, steps, 1) for t in tiles]
    return [jnp.where(lane < steps, turned[j - 1], turned[j]) for j in range(len(tiles))]


def from_east(tiles, lane):
    turned = [pltpu.roll(t, LANES - 1, 1) for t in tiles]
    count = len(tiles)
    return [jnp.where(lane == LANES - 1, turned[(j + 1) % count], turned[j]) for j in range(count)]


def coefficients(wind):
    size = jnp.abs(wind)
    rest = 1.0 - size
    alpha = wind * rest * rest * (1.0 / 12.0)
    beta = wind * size * rest * (-1.0 / 12.0)
    gamma = wind * size * (3.0 - 2.0 * size)
    return alpha, beta, gamma


def packed_sizes(nlon, count):
    width = nlon // count
    mains, tail = width // LANES, width % LANES
    per = LANES // tail if tail else 1
    tails = -(-BLOCK // per) if tail else 0
    return width, mains, tail, per, BLOCK * mains + tails


def fill_halos(rows, slot, state, winds, first_round, second_round):
    band, bands = lax.axis_index("lat"), lax.axis_size("lat")
    even = band % 2 == 0
    keep = jnp.where((band == 0) | (band == bands - 1), 0.0, 1.0)
    for target, north, scale in ((first_round, even, None), (second_round, jnp.logical_not(even), keep)):
        scaled = (lambda v: v) if scale is None else (lambda v: v * scale)
        row_t = jnp.where(north, rows - HALO, 0)
        row_x = jnp.where(north, rows - REACH, 0)
        row_y = jnp.where(north, rows - REACH - 1, 0)
        for row in range(HALO):
            target[row] = scaled(state[slot, row_t + row])
        for q in range(REACH):
            target[HALO, q:q + 1, :] = scaled(winds[row_x + q, slot:slot + 1, :])
        for q in range(REACH + 1):
            target[HALO, REACH + q:REACH + q + 1, :] = scaled(winds[rows + row_y + q, slot:slot + 1, :])


def prep_kernel(rows, tracers, winds, state, first_round, second_round):
    levels, nlon = state.shape[0], state.shape[3]
    nj = nlon // LANES
    row_stride = nj * levels
    tracer_stride = rows * row_stride

    def body(row, _):
        for level in range(levels):
            for j in range(nj):
                start = row * row_stride + j * levels + level
                state[level, row, :, tile(j)] = tracers[pl.ds(start, SUB, stride=tracer_stride), :]
        return 0

    lax.fori_loop(0, rows, body, 0)
    fill_halos(rows, 0, state, winds, first_round, second_round)


def lat_pass(levels, nj, ranges, cell, coef, store):
    group = 3 if nj % 3 == 0 else 1

    def body(i, _):
        level = i // (nj // group)
        results = []
        for u in range(group):
            lanes = pl.ds(pl.multiple_of(((i % (nj // group)) * group + u) * LANES, LANES), LANES)
            results += [(level, row, lanes, value) for row, value in one(level, lanes)]
        for result in results:
            store(*result)
        return 0

    def one(level, lanes):
        results = []
        for first, last in ranges:
            a = {r: cell(level, r, lanes) for r in range(first - REACH, last + REACH)}
            inter = {f: 7.0 * (a[f - 1] + a[f]) - (a[f - 2] + a[f + 1]) for f in range(first - 1, last + 2)}
            flux = {}
            for f in range(first, last + 1):
                alpha, beta, gamma = [spread(coef(i, level, f, lanes)) for i in range(3)]
                north = gamma > 0
                behind = jnp.where(north, inter[f - 1], inter[f + 1])
                upwind = jnp.where(north, a[f - 1], a[f])
                flux[f] = alpha * inter[f] + beta * behind + gamma * upwind
                if f > first:
                    results.append((f - 1, a[f - 1] - (flux[f] - flux[f - 1])))
        return results

    lax.fori_loop(0, levels * nj // group, body, 0)


def tile(j):
    return slice(j * LANES, (j + 1) * LANES)


def lon_pass(work, swept, coef, inter, west, flux, lane, finish):
    nj = swept.shape[3] // LANES
    each = range(nj)

    def interfaces(n):
        level, _, at = work[n]
        b = [swept[level, at, :, tile(j)] for j in each]
        w1, w2, e1 = from_west(b, 1, lane), from_west(b, 2, lane), from_east(b, lane)
        for j in each:
            inter[n, :, tile(j)] = 7.0 * (w1[j] + b[j]) - (w2[j] + e1[j])
            west[n, :, tile(j)] = w1[j]

    def fluxes(n):
        level, row, at = work[n]
        mid = [inter[n, :, tile(j)] for j in each]
        w1, e1 = from_west(mid, 1, lane), from_east(mid, lane)
        for j in each:
            alpha, beta, gamma = [spread(coef(i, level, row, tile(j))) for i in range(3)]
            right = gamma > 0
            behind = jnp.where(right, w1[j], e1[j])
            upwind = jnp.where(right, west[n, :, tile(j)], swept[level, at, :, tile(j)])
            flux[n, :, tile(j)] = alpha * mid[j] + beta * behind + gamma * upwind

    def update(n):
        level, _, at = work[n]
        here = [flux[n, :, tile(j)] for j in each]
        e1 = from_east(here, lane)
        return [swept[level, at, :, tile(j)] - (e1[j] - here[j]) for j in each]

    groups = len(work) // BLOCK
    for g in range(groups + 2):
        if g < groups:
            for q in range(BLOCK):
                interfaces(g * BLOCK + q)
        if 1 <= g <= groups:
            for q in range(BLOCK):
                fluxes((g - 1) * BLOCK + q)
        if g >= 2:
            finish(g - 2, [update((g - 2) * BLOCK + q) for q in range(BLOCK)])


def pack_block(block, packed, unit, count, lane):
    nlon = len(block[0]) * LANES
    width, mains, tail, per, size = packed_sizes(nlon, count)
    for d in range(count):
        j0, off = (d * width) // LANES, (d * width) % LANES
        for q, tiles in enumerate(block):
            turned = [pltpu.roll(tiles[j0 + m], LANES - off, 1) if off else tiles[j0 + m]
                      for m in range(mains + (1 if off else 0))]
            for m in range(mains):
                whole = jnp.where(lane < LANES - off, turned[m], turned[m + 1]) if off else turned[m]
                packed[d, unit, q * mains + m] = whole
        if tail:
            for g in range(-(-BLOCK // per)):
                total = None
                for place in range(min(per, BLOCK - g * per)):
                    shift = (place * tail - off) % LANES
                    source = block[g * per + place][j0 + mains]
                    moved = pltpu.roll(source, shift, 1) if shift else source
                    total = moved if total is None else jnp.where(lane < place * tail, total, moved)
                packed[d, unit, BLOCK * mains + g] = total


def copy_tiles(pairs):
    values = [source[at] for (source, at), _ in pairs]
    for value, (_, (target, at)) in zip(values, pairs):
        target[at] = value


def copy_units(source, target, start=0):
    for unit in range(source.shape[0]):
        copy_tiles([((source, (unit, i)), (target, (start + unit, i))) for i in range(source.shape[1])])


def hand_out(packed, outs, groups):
    me = lax.axis_index("lev")
    for group, out in zip(groups, outs):
        for place, k in enumerate(group):
            copy_units(packed.at[me ^ k], out, place * packed.shape[1])


def own_coefficients(rows, joined, winds, cx, cy):
    levels, held, nlon = cx.shape[1:]
    keep = jnp.where(lax.axis_index("lat") == 0, 0.0, 1.0)
    for level in range(levels):
        for way in range(2):
            for row in range(rows):
                winds[way, level, row:row + 1, :] = joined[way * rows + row, level:level + 1, :]
        winds[1, level, 0:1, :] = winds[1, level, 0:1, :] * keep
        for way, target in enumerate((cx, cy)):
            for j in range(nlon // LANES):
                parts = coefficients(winds[way, level, :, tile(j)])
                for p in range(3):
                    target[p, level, :, tile(j)] = parts[p]


def put_rows(target, level, at, rows):
    for q, row in enumerate(rows):
        for j, part in enumerate(row):
            target[level, at + q, :, tile(j)] = part


def interior_kernel(count, rows, groups, state, joined, *refs):
    outs, (first, cx, cy), refs = refs[:len(groups)], refs[len(groups):len(groups) + 3], refs[len(groups) + 3:]
    halos, (packed, winds, swept, inter, west, flux) = refs[:-6], refs[-6:]
    levels, nlon = state.shape[0], state.shape[3]
    nj = nlon // LANES
    lane = lane_ids()
    for slot in range(1, levels):
        fill_halos(rows, slot, state, joined, *halos[2 * slot - 2:2 * slot])
    own_coefficients(rows, joined, winds, cx, cy)
    coef_x = lambda i, level, r, lanes: cx[i, level, r:r + 1, lanes]
    coef_y = lambda i, level, f, lanes: cy[i, level, f:f + 1, lanes]

    def put(level, row, lanes, value):
        swept[level, row - REACH, :, lanes] = value

    lat_pass(levels, nj, [(REACH, rows - REACH)], lambda level, r, lanes: state[level, r, :, lanes], coef_y, put)
    work = [(level, row, row - REACH) for level in range(levels) for row in range(REACH, rows - REACH)]

    def keep_first(group, done):
        level, _, at = work[group * BLOCK]
        put_rows(first, level, at, done)

    lon_pass(work, swept, coef_x, inter, west, flux, lane, keep_first)
    lat_pass(levels, nj, [(HALO, rows - HALO)], lambda level, r, lanes: first[level, r - REACH, :, lanes], coef_y, put)
    work_last = [(level, row, row - REACH) for level in range(levels) for row in range(HALO, rows - HALO)]

    def send(group, done):
        pack_block(done, packed, group, count, lane)

    lon_pass(work_last, swept, coef_x, inter, west, flux, lane, send)
    hand_out(packed, outs, groups)


def edge_kernel(count, rows, groups, slot, joint, state, first_round, second_round, first, cx, cy, *refs):
    others = refs[:len(joint)]
    outs, (packed, beyond, swept, edge, inter, west, flux) = refs[-7 - len(groups):-7], refs[-7:]
    nlon = state.shape[3]
    nj = nlon // LANES
    lane = lane_ids()
    odd = lax.axis_index("lat") % 2 == 1

    def halo(south, *at):
        one, two = first_round[at], second_round[at]
        return jnp.where(odd, one, two) if south else jnp.where(odd, two, one)

    for end, south in enumerate((True, False)):
        for j in range(nj):
            parts = coefficients(halo(south, HALO, slice(None), tile(j)))
            for p in range(3):
                beyond[p, end, :, tile(j)] = parts[p]

    def coef_x(i, _, r, lanes):
        if 0 <= r < rows:
            return cx[i, slot, r:r + 1, lanes]
        end, at = (0, r + REACH) if r < 0 else (1, r - rows)
        return beyond[i, end, at:at + 1, lanes]

    def coef_y(i, _, f, lanes):
        if 0 <= f < rows:
            return cy[i, slot, f:f + 1, lanes]
        end, at = (0, f + 2 * REACH + 1) if f < 0 else (1, f - rows + REACH)
        return beyond[i, end, at:at + 1, lanes]

    def cell(_, r, lanes):
        if 0 <= r < rows:
            return state[slot, r, :, lanes]
        return halo(r < 0, r + HALO if r < 0 else r - rows, slice(None), lanes)

    ends = [(-REACH, REACH), (rows - REACH, rows + REACH)]
    ends_last = [(0, HALO), (rows - HALO, rows)]

    def place(row, ranges):
        (a, b), (c, _) = ranges
        return row - a if row < b else row - c + BLOCK

    def cell_first(_, r, lanes):
        if REACH <= r < rows - REACH:
            return first[slot, r - REACH, :, lanes]
        return edge[0, place(r, ends), :, lanes]

    def put(_, row, lanes, value):
        swept[0, place(row, ends), :, lanes] = value

    def put_last(_, row, lanes, value):
        swept[0, place(row, ends_last), :, lanes] = value

    def listed(ranges):
        return [(0, row, place(row, ranges)) for a, b in ranges for row in range(a, b)]

    def keep_edge(group, done):
        put_rows(edge, 0, group * BLOCK, done)

    def send(group, done):
        pack_block(done, packed, group, count, lane)

    lat_pass(1, nj, ends, cell, coef_y, put)
    lon_pass(listed(ends), swept, coef_x, inter, west, flux, lane, keep_edge)
    lat_pass(1, nj, ends_last, cell_first, coef_y, put_last)
    lon_pass(listed(ends_last), swept, coef_x, inter, west, flux, lane, send)
    hand_out(packed, outs, groups)
    place = packed.shape[1]
    for other, (begin, size) in zip(others, joint):
        copy_units(other.at[pl.ds(begin, size)], outs[1], place)
        place += size


def weights_kernel(weights, source, out):
    targets, rows, taps, width = weights.shape

    for row in range(rows):
        for k in range(targets):
            lowest, highest = max(k - (TAPS - 1), 0), min(k, targets - TAPS)
            w = weights[k, row]
            w = jnp.concatenate([w, jnp.zeros((SUB - taps, width), jnp.float32)], axis=0)
            at = jnp.broadcast_to(source[k, row:row + 1, :], (SUB, width))
            total = w
            for g in range(lowest + 1, highest + 1):
                total = jnp.where(at == g, pltpu.roll(w, g - lowest, 0), total)
            out[k, row] = total


def remap_kernel(count, plan, numbers, counts, *refs):
    chunks, weights, (out, levels, result, sems) = refs[:len(plan)], refs[len(plan)], refs[-4:]
    me = lax.axis_index("lev")
    targets, _, _, width = result.shape
    _, mains, tail, per, _ = packed_sizes(width * count, count)
    copies = []

    def leave(source, target):
        copy = pltpu.make_async_copy(source, target, sems.at[len(copies)])
        copy.start()
        copies.append(copy)

    def level_of(k, slot):
        d = me ^ k
        start = jnp.int32(0)
        for e in range(count):
            start = start + jnp.where(e < d, counts[e], 0)
        return jnp.where(slot < counts[d], start + slot, targets)

    for units, chunk in zip(plan, chunks):
        for unit, (k, slot, number) in enumerate(units):
            if number in numbers:
                at = numbers.index(number)
                copy_tiles([((chunk, (unit, i)), (levels, (level_of(k, slot), at, i))) for i in range(chunk.shape[1])])

    for at, number in enumerate(numbers):
        for q in range(BLOCK):
            row = number * BLOCK + q
            for m in range(mains + (1 if tail else 0)):
                wide = LANES if m < mains else tail
                lanes = slice(m * LANES, m * LANES + wide)
                values = []
                for level in range(targets):
                    if m < mains:
                        values.append(levels[level, at, q * mains + m])
                    else:
                        last = levels[level, at, BLOCK * mains + q // per]
                        shift = (q % per) * tail
                        values.append(pltpu.roll(last, LANES - shift, 1) if shift else last)
                for k in range(targets):
                    lowest, highest = max(k - (TAPS - 1), 0), min(k, targets - TAPS) + TAPS - 1
                    total = None
                    for level in range(lowest, highest + 1):
                        j = level - lowest
                        term = jnp.broadcast_to(weights[k, row, j:j + 1, lanes], (SUB, wide)) * values[level][:, :wide]
                        total = term if total is None else total + term
                    result[k, at * BLOCK + q, :, lanes] = total
        leave(result.at[:, pl.ds(at * BLOCK, BLOCK)], out.at[:, pl.ds(number * BLOCK, BLOCK)])
    for copy in copies:
        copy.wait()


def mark_kernel(*refs):
    refs[-1][...] = jnp.zeros((SUB, LANES), jnp.float32)


def tiles_of(array):
    lead, levels, nlon = array.shape[:-2], array.shape[-2], array.shape[-1]
    split = array.reshape(lead + (levels, nlon // LANES, LANES))
    order = tuple(range(len(lead))) + (len(lead) + 1, len(lead), len(lead) + 2)
    split = with_layout_constraint(split, Layout(major_to_minor=order))
    return jnp.swapaxes(split, -3, -2).reshape(-1, LANES)


VMEM = pl.BlockSpec(memory_space=pltpu.VMEM)
ANY = pl.BlockSpec(memory_space=pl.ANY)
SMEM = pl.BlockSpec(memory_space=pltpu.SMEM)


def call(kernel, outs, args, specs=None, scratch=(), cost=None):
    return pl.pallas_call(
        kernel,
        out_shape=outs,
        in_specs=specs or [VMEM] * len(args),
        out_specs=jax.tree.map(lambda _: VMEM, outs),
        scratch_shapes=list(scratch),
        compiler_params=pltpu.CompilerParams(vmem_limit_bytes=16 << 20),
        cost_estimate=cost,
    )(*args)


def cost(flops, size):
    return pl.CostEstimate(flops=int(flops), bytes_accessed=int(size), transcendentals=0)


def f32(*shape):
    return jax.ShapeDtypeStruct(shape, jnp.float32)


def shards(tracers, wind_x, wind_y, level_counts, source_level, remap_weight):
    count = lax.axis_size("lev")
    bands = lax.axis_size("lat")
    number, depth, rows, nlon = tracers.shape
    targets, _, width = source_level.shape
    size = packed_sizes(nlon, count)[-1]
    blocks = rows // BLOCK
    inner = (rows - 2 * HALO) // BLOCK

    raw = tiles_of(jnp.transpose(tracers, (0, 2, 1, 3)))
    joined = jnp.concatenate([jnp.transpose(wind_x, (1, 0, 2)), jnp.transpose(wind_y, (1, 0, 2))], axis=0)
    halo = f32(HALO + 1, number, nlon)
    state, *sent = call(
        functools.partial(prep_kernel, rows),
        [f32(depth, rows, number, nlon), halo, halo], (raw, joined),
        cost=cost(1, 1))
    second = {i: ((i - 1) ^ 1) + 1 for i in range(1, bands - 1)}
    second_pairs = [(i * count + d, second[i] * count + d if i in second else i * count + (d ^ 1))
                    for i in range(bands) for d in range(count)]

    def beside(sent):
        return [lax.ppermute(sent[0], "lat", [(i, i ^ 1) for i in range(bands)]),
                lax.ppermute(sent[1], ("lat", "lev"), second_pairs)]

    rounds = [beside(sent)]
    taps = call(
        weights_kernel, f32(targets, rows, SUB, width),
        (jnp.transpose(remap_weight, (1, 2, 0, 3)), source_level),
        cost=cost(1, 1))

    def box(units, *lead):
        return lead + (units, size, SUB, LANES)

    def vmem(*shape):
        return pltpu.VMEM(shape, jnp.float32)

    held = -(-rows // SUB) * SUB
    coef = f32(3, depth, held, nlon)
    swept = vmem(depth, rows - 2 * REACH, number, nlon)
    stage = vmem(depth * (rows - 2 * REACH), number, nlon)
    chips = tuple(range(2, count, 2))
    groups = ((0,), (1,)) + tuple((k, k ^ 1) for k in chips)
    inner_units = depth * inner
    result = call(
        functools.partial(interior_kernel, count, rows, groups),
        [f32(*box(len(group) * inner_units)) for group in groups]
        + [f32(depth, rows - 2 * REACH, number, nlon), coef, coef] + [halo] * (2 * depth - 2),
        (state, joined), scratch=[vmem(*box(inner_units, count)), vmem(2, depth, held, nlon), swept, stage, stage, stage],
        cost=cost(1, 1))
    middle, (first, cx, cy), sent = result[:len(groups)], result[len(groups):len(groups) + 3], result[len(groups) + 3:]
    rounds += [beside(sent[2 * i:2 * i + 2]) for i in range(depth - 1)]
    swept = vmem(1, 2 * HALO, number, nlon)
    stage = vmem(2 * HALO, number, nlon)

    def edge(slot, groups, joint, after):
        args = (state, *rounds[slot], first, cx, cy, *(chunk for chunk, _ in joint), *after)
        parts = tuple(part for _, part in joint)
        units = [2 * len(group) + (sum(size for _, size in parts) if group == (1,) else 0) for group in groups]
        return call(
            functools.partial(edge_kernel, count, rows, groups, slot, parts),
            [f32(*box(n)) for n in units], args,
            specs=[VMEM] * (len(args) - len(after)) + [ANY] * len(after),
            scratch=[vmem(*box(2, count)), vmem(3, 2, SUB, nlon), swept, swept, stage, stage, stage],
            cost=cost(60 * tracers.size, 8 * tracers.size))

    def swapped(sent, k):
        return lax.ppermute(sent, "lev", [(i, i ^ k) for i in range(count)])

    def units_of(k, places):
        return tuple((k, slot, block) for slot, block in places)

    def remap(listed, after):
        args = (level_counts, *(chunk for _, chunk in listed), taps, *after)
        return pl.pallas_call(
            functools.partial(remap_kernel, count, tuple(units for units, _ in listed), tuple(range(blocks))),
            out_shape=f32(targets, rows, number, width),
            in_specs=[SMEM] + [VMEM] * (len(args) - 1 - len(after)) + [ANY] * len(after),
            out_specs=ANY,
            scratch_shapes=[
                vmem(targets + 1, blocks, size, SUB, LANES),
                vmem(targets, rows, number, width),
                pltpu.SemaphoreType.DMA((blocks,)),
            ],
            compiler_params=pltpu.CompilerParams(vmem_limit_bytes=16 << 20),
            cost_estimate=cost(1, 1),
        )(*args)

    def mark(chunks):
        return pl.pallas_call(
            mark_kernel, out_shape=f32(SUB, LANES), in_specs=[ANY] * len(chunks), out_specs=VMEM, cost_estimate=cost(1, 1),
            compiler_params=pltpu.CompilerParams(vmem_limit_bytes=1 << 20),
        )(*chunks)

    places = tuple((slot, 1 + b) for slot in range(depth) for b in range(inner))
    passing = tuple((None, None, None) for _ in places)
    arrived = [swapped(chunk, k) for k, chunk in zip(chips, middle[2:])]
    listed = [(units_of(k, places) + passing, chunk) for k, chunk in zip(chips, arrived)]
    listed.append((units_of(0, places), middle[0]))
    beside_me = [(units_of(1, places), middle[1])]
    after, marks = (taps,), []
    for slot in range(depth):
        own = ((slot, 0), (slot, blocks - 1))
        done = edge(slot, tuple((k,) for k in range(count)), [], after)
        crossing = [(units_of(k, own), swapped(done[k], k)) for k in range(count - 1, 1, -1)]
        listed += crossing + [(units_of(0, own), done[0])]
        beside_me.append((units_of(1, own), done[1]))
        marks.append(mark([chunk for _, chunk in crossing]))
        after = (done[0],)
    beside_me += [(units_of(k ^ 1, places), chunk) for k, chunk in zip(chips, arrived)]
    waiting = lax.optimization_barrier((*(chunk for _, chunk in beside_me), done[0]))
    listed += [(units, swapped(chunk[chunk.shape[0] - len(units):], 1)) for (units, _), chunk in zip(beside_me, waiting)]
    out = remap(listed, marks)
    return jnp.transpose(out, (2, 0, 1, 3))


def solution(mesh):
    in_specs = (
        P(None, "lev", ("groups", "lat"), None),
        P("lev", ("groups", "lat"), None),
        P("lev", ("groups", "lat"), None),
        P(),
        P(None, ("groups", "lat"), "lev"),
        P(None, None, ("groups", "lat"), "lev"),
    )
    out_specs = P(None, None, ("groups", "lat"), "lev")
    return jax.shard_map(shards, mesh=mesh, in_specs=in_specs, out_specs=out_specs, check_vma=False)
```

```python
import functools

import jax
import jax.numpy as jnp
from jax import lax
from jax.experimental import pallas as pl
from jax.experimental.layout import Layout, with_layout_constraint
from jax.experimental.pallas import tpu as pltpu
from jax.sharding import PartitionSpec as P

SUBSTEPS = 2
TAPS = 4
REACH = 3
HALO = REACH * SUBSTEPS
BLOCK = 6
LANES = 128
SUB = 8


def spread(row):
    return jnp.broadcast_to(row, (SUB, LANES))


def lane_ids():
    return lax.broadcasted_iota(jnp.int32, (SUB, LANES), 1)


def from_west(tiles, steps, lane):
    turned = [pltpu.roll(t, steps, 1) for t in tiles]
    return [jnp.where(lane < steps, turned[j - 1], turned[j]) for j in range(len(tiles))]


def from_east(tiles, lane):
    turned = [pltpu.roll(t, LANES - 1, 1) for t in tiles]
    count = len(tiles)
    return [jnp.where(lane == LANES - 1, turned[(j + 1) % count], turned[j]) for j in range(count)]


def coefficients(wind):
    size = jnp.abs(wind)
    rest = 1.0 - size
    alpha = wind * rest * rest * (1.0 / 12.0)
    beta = wind * size * rest * (-1.0 / 12.0)
    gamma = wind * size * (3.0 - 2.0 * size)
    return alpha, beta, gamma


def packed_sizes(nlon, count):
    width = nlon // count
    mains, tail = width // LANES, width % LANES
    return width, mains, tail, LANES // tail if tail else 1


def packed_tiles(units, mains, tail, per):
    return units * BLOCK * mains + (-(-units * BLOCK // per) if tail else 0)


def fill_halos(rows, slot, state, winds, first_round, second_round):
    band, bands = lax.axis_index("lat"), lax.axis_size("lat")
    even = band % 2 == 0
    keep = jnp.where((band == 0) | (band == bands - 1), 0.0, 1.0)
    for target, north, scale in ((first_round, even, None), (second_round, jnp.logical_not(even), keep)):
        scaled = (lambda v: v) if scale is None else (lambda v: v * scale)
        row_t = jnp.where(north, rows - HALO, 0)
        row_x = jnp.where(north, rows - REACH, 0)
        row_y = jnp.where(north, rows - REACH - 1, 0)
        for row in range(HALO):
            target[row] = scaled(state[slot, row_t + row])
        for q in range(REACH):
            target[HALO, q:q + 1, :] = scaled(winds[row_x + q, slot:slot + 1, :])
        for q in range(REACH + 1):
            target[HALO, REACH + q:REACH + q + 1, :] = scaled(winds[rows + row_y + q, slot:slot + 1, :])


def prep_kernel(rows, tracers, winds, state, first_round, second_round):
    levels, nlon = state.shape[0], state.shape[3]
    nj = nlon // LANES
    row_stride = nj * levels
    tracer_stride = rows * row_stride

    def body(row, _):
        for level in range(levels):
            for j in range(nj):
                start = row * row_stride + j * levels + level
                state[level, row, :, tile(j)] = tracers[pl.ds(start, SUB, stride=tracer_stride), :]
        return 0

    lax.fori_loop(0, rows, body, 0)
    fill_halos(rows, 0, state, winds, first_round, second_round)


def lat_pass(levels, nj, ranges, cell, coef, store):
    group = 3 if nj % 3 == 0 else 1

    def body(i, _):
        level = i // (nj // group)
        results = []
        for u in range(group):
            lanes = pl.ds(pl.multiple_of(((i % (nj // group)) * group + u) * LANES, LANES), LANES)
            results += [(level, row, lanes, value) for row, value in one(level, lanes)]
        for result in results:
            store(*result)
        return 0

    def one(level, lanes):
        results = []
        for first, last in ranges:
            a = {r: cell(level, r, lanes) for r in range(first - REACH, last + REACH)}
            inter = {f: 7.0 * (a[f - 1] + a[f]) - (a[f - 2] + a[f + 1]) for f in range(first - 1, last + 2)}
            flux = {}
            for f in range(first, last + 1):
                alpha, beta, gamma = [spread(coef(i, level, f, lanes)) for i in range(3)]
                north = gamma > 0
                behind = jnp.where(north, inter[f - 1], inter[f + 1])
                upwind = jnp.where(north, a[f - 1], a[f])
                flux[f] = alpha * inter[f] + beta * behind + gamma * upwind
                if f > first:
                    results.append((f - 1, a[f - 1] - (flux[f] - flux[f - 1])))
        return results

    lax.fori_loop(0, levels * nj // group, body, 0)


def tile(j):
    return slice(j * LANES, (j + 1) * LANES)


def lon_pass(work, swept, coef, inter, west, flux, lane, finish):
    nj = swept.shape[3] // LANES
    each = range(nj)

    def interfaces(n):
        level, _, at = work[n]
        b = [swept[level, at, :, tile(j)] for j in each]
        w1, w2, e1 = from_west(b, 1, lane), from_west(b, 2, lane), from_east(b, lane)
        for j in each:
            inter[n, :, tile(j)] = 7.0 * (w1[j] + b[j]) - (w2[j] + e1[j])
            west[n, :, tile(j)] = w1[j]

    def fluxes(n):
        level, row, at = work[n]
        mid = [inter[n, :, tile(j)] for j in each]
        w1, e1 = from_west(mid, 1, lane), from_east(mid, lane)
        for j in each:
            alpha, beta, gamma = [spread(coef(i, level, row, tile(j))) for i in range(3)]
            right = gamma > 0
            behind = jnp.where(right, w1[j], e1[j])
            upwind = jnp.where(right, west[n, :, tile(j)], swept[level, at, :, tile(j)])
            flux[n, :, tile(j)] = alpha * mid[j] + beta * behind + gamma * upwind

    def update(n):
        level, _, at = work[n]
        here = [flux[n, :, tile(j)] for j in each]
        e1 = from_east(here, lane)
        return [swept[level, at, :, tile(j)] - (e1[j] - here[j]) for j in each]

    groups = len(work) // BLOCK
    for g in range(groups + 2):
        if g < groups:
            for q in range(BLOCK):
                interfaces(g * BLOCK + q)
        if 1 <= g <= groups:
            for q in range(BLOCK):
                fluxes((g - 1) * BLOCK + q)
        if g >= 2:
            finish(g - 2, [update((g - 2) * BLOCK + q) for q in range(BLOCK)])


def pack_block(block, packed, unit, units, count, lane):
    nlon = len(block[0]) * LANES
    width, mains, tail, per = packed_sizes(nlon, count)
    for d in range(count):
        j0, off = (d * width) // LANES, (d * width) % LANES
        for q, tiles in enumerate(block):
            turned = [pltpu.roll(tiles[j0 + m], LANES - off, 1) if off else tiles[j0 + m]
                      for m in range(mains + (1 if off else 0))]
            for m in range(mains):
                whole = jnp.where(lane < LANES - off, turned[m], turned[m + 1]) if off else turned[m]
                packed[d, (unit * BLOCK + q) * mains + m] = whole
        if tail:
            totals = {}
            for q, tiles in enumerate(block):
                at, place = divmod(unit * BLOCK + q, per)
                at += units * BLOCK * mains
                shift = (place * tail - off) % LANES
                moved = pltpu.roll(tiles[j0 + mains], shift, 1) if shift else tiles[j0 + mains]
                if place:
                    before = totals[at] if at in totals else packed[d, at]
                    moved = jnp.where(lane < place * tail, before, moved)
                totals[at] = moved
            for at, total in totals.items():
                packed[d, at] = total


def unpack_unit(chunk, place, unit, units, target, lead, mains, tail, per, lane):
    copy_tiles([((chunk, (place, unit * BLOCK * mains + i)), (target, lead + (i,))) for i in range(BLOCK * mains)])
    totals = {}
    for q in range(BLOCK if tail else 0):
        at, there = divmod(unit * BLOCK + q, per)
        to, here = divmod(q, per)
        shift = (here - there) * tail % LANES
        if to in totals and totals[to][1:] == (at, shift):
            continue
        source = chunk[place, units * BLOCK * mains + at]
        moved = pltpu.roll(source, shift, 1) if shift else source
        totals[to] = (jnp.where(lane < here * tail, totals[to][0], moved) if to in totals else moved, at, shift)
    for to, (total, _, _) in totals.items():
        target[lead + (BLOCK * mains + to,)] = total


def copy_tiles(pairs):
    values = [source[at] for (source, at), _ in pairs]
    for value, (_, (target, at)) in zip(values, pairs):
        target[at] = value


def hand_out(packed, outs, groups):
    me = lax.axis_index("lev")
    for group, out in zip(groups, outs):
        for place, k in enumerate(group):
            copy_tiles([((packed, (me ^ k, i)), (out, (place, i))) for i in range(packed.shape[1])])


def own_coefficients(rows, joined, winds, cx, cy):
    levels, held, nlon = cx.shape[1:]
    keep = jnp.where(lax.axis_index("lat") == 0, 0.0, 1.0)
    for level in range(levels):
        for way in range(2):
            for row in range(rows):
                winds[way, level, row:row + 1, :] = joined[way * rows + row, level:level + 1, :]
        winds[1, level, 0:1, :] = winds[1, level, 0:1, :] * keep
        for way, target in enumerate((cx, cy)):
            for j in range(nlon // LANES):
                parts = coefficients(winds[way, level, :, tile(j)])
                for p in range(3):
                    target[p, level, :, tile(j)] = parts[p]


def put_rows(target, level, at, rows):
    for q, row in enumerate(rows):
        for j, part in enumerate(row):
            target[level, at + q, :, tile(j)] = part


def interior_kernel(count, rows, groups, state, joined, *refs):
    outs, (first, cx, cy), refs = refs[:len(groups)], refs[len(groups):len(groups) + 3], refs[len(groups) + 3:]
    halos, (packed, winds, swept, inter, west, flux) = refs[:-6], refs[-6:]
    levels, nlon = state.shape[0], state.shape[3]
    nj = nlon // LANES
    lane = lane_ids()
    for slot in range(1, levels):
        fill_halos(rows, slot, state, joined, *halos[2 * slot - 2:2 * slot])
    own_coefficients(rows, joined, winds, cx, cy)
    coef_x = lambda i, level, r, lanes: cx[i, level, r:r + 1, lanes]
    coef_y = lambda i, level, f, lanes: cy[i, level, f:f + 1, lanes]

    def put(level, row, lanes, value):
        swept[level, row - REACH, :, lanes] = value

    lat_pass(levels, nj, [(REACH, rows - REACH)], lambda level, r, lanes: state[level, r, :, lanes], coef_y, put)
    work = [(level, row, row - REACH) for level in range(levels) for row in range(REACH, rows - REACH)]

    def keep_first(group, done):
        level, _, at = work[group * BLOCK]
        put_rows(first, level, at, done)

    lon_pass(work, swept, coef_x, inter, west, flux, lane, keep_first)
    lat_pass(levels, nj, [(HALO, rows - HALO)], lambda level, r, lanes: first[level, r - REACH, :, lanes], coef_y, put)
    work_last = [(level, row, row - REACH) for level in range(levels) for row in range(HALO, rows - HALO)]

    def send(group, done):
        pack_block(done, packed, group, len(work_last) // BLOCK, count, lane)

    lon_pass(work_last, swept, coef_x, inter, west, flux, lane, send)
    hand_out(packed, outs, groups)


def edge_kernel(count, rows, groups, slot, state, first_round, second_round, first, cx, cy, *refs):
    outs, (packed, beyond, swept, edge, inter, west, flux) = refs[-7 - len(groups):-7], refs[-7:]
    nlon = state.shape[3]
    nj = nlon // LANES
    lane = lane_ids()
    odd = lax.axis_index("lat") % 2 == 1

    def halo(south, *at):
        one, two = first_round[at], second_round[at]
        return jnp.where(odd, one, two) if south else jnp.where(odd, two, one)

    for end, south in enumerate((True, False)):
        for j in range(nj):
            parts = coefficients(halo(south, HALO, slice(None), tile(j)))
            for p in range(3):
                beyond[p, end, :, tile(j)] = parts[p]

    def coef_x(i, _, r, lanes):
        if 0 <= r < rows:
            return cx[i, slot, r:r + 1, lanes]
        end, at = (0, r + REACH) if r < 0 else (1, r - rows)
        return beyond[i, end, at:at + 1, lanes]

    def coef_y(i, _, f, lanes):
        if 0 <= f < rows:
            return cy[i, slot, f:f + 1, lanes]
        end, at = (0, f + 2 * REACH + 1) if f < 0 else (1, f - rows + REACH)
        return beyond[i, end, at:at + 1, lanes]

    def cell(_, r, lanes):
        if 0 <= r < rows:
            return state[slot, r, :, lanes]
        return halo(r < 0, r + HALO if r < 0 else r - rows, slice(None), lanes)

    ends = [(-REACH, REACH), (rows - REACH, rows + REACH)]
    ends_last = [(0, HALO), (rows - HALO, rows)]

    def place(row, ranges):
        (a, b), (c, _) = ranges
        return row - a if row < b else row - c + BLOCK

    def cell_first(_, r, lanes):
        if REACH <= r < rows - REACH:
            return first[slot, r - REACH, :, lanes]
        return edge[0, place(r, ends), :, lanes]

    def put(_, row, lanes, value):
        swept[0, place(row, ends), :, lanes] = value

    def put_last(_, row, lanes, value):
        swept[0, place(row, ends_last), :, lanes] = value

    def listed(ranges):
        return [(0, row, place(row, ranges)) for a, b in ranges for row in range(a, b)]

    def keep_edge(group, done):
        put_rows(edge, 0, group * BLOCK, done)

    def send(group, done):
        pack_block(done, packed, group, len(ends_last), count, lane)

    lat_pass(1, nj, ends, cell, coef_y, put)
    lon_pass(listed(ends), swept, coef_x, inter, west, flux, lane, keep_edge)
    lat_pass(1, nj, ends_last, cell_first, coef_y, put_last)
    lon_pass(listed(ends_last), swept, coef_x, inter, west, flux, lane, send)
    hand_out(packed, outs, groups)


def weights_kernel(weights, source, out):
    targets, rows, taps, width = weights.shape

    for row in range(rows):
        for k in range(targets):
            lowest, highest = max(k - (TAPS - 1), 0), min(k, targets - TAPS)
            w = weights[k, row]
            w = jnp.concatenate([w, jnp.zeros((SUB - taps, width), jnp.float32)], axis=0)
            at = jnp.broadcast_to(source[k, row:row + 1, :], (SUB, width))
            total = w
            for g in range(lowest + 1, highest + 1):
                total = jnp.where(at == g, pltpu.roll(w, g - lowest, 0), total)
            out[k, row] = total


def remap_kernel(count, plan, numbers, counts, *refs):
    chunks, weights, (out, levels, result, sems) = refs[:len(plan)], refs[len(plan)], refs[-4:]
    me = lax.axis_index("lev")
    targets, _, _, width = result.shape
    _, mains, tail, per = packed_sizes(width * count, count)
    lane = lane_ids()
    copies = []

    def leave(source, target):
        copy = pltpu.make_async_copy(source, target, sems.at[len(copies)])
        copy.start()
        copies.append(copy)

    def level_of(k, slot):
        d = me ^ k
        start = jnp.int32(0)
        for e in range(count):
            start = start + jnp.where(e < d, counts[e], 0)
        return jnp.where(slot < counts[d], start + slot, targets)

    for units, chunk in zip(plan, chunks):
        for unit, (k, slot, number) in enumerate(units):
            lead = (level_of(k, slot), numbers.index(number))
            unpack_unit(chunk, 0, unit, len(units), levels, lead, mains, tail, per, lane)

    for at, number in enumerate(numbers):
        for q in range(BLOCK):
            row = number * BLOCK + q
            for m in range(mains + (1 if tail else 0)):
                wide = LANES if m < mains else tail
                lanes = slice(m * LANES, m * LANES + wide)
                values = []
                for level in range(targets):
                    if m < mains:
                        values.append(levels[level, at, q * mains + m])
                    else:
                        last = levels[level, at, BLOCK * mains + q // per]
                        shift = (q % per) * tail
                        values.append(pltpu.roll(last, LANES - shift, 1) if shift else last)
                for k in range(targets):
                    lowest, highest = max(k - (TAPS - 1), 0), min(k, targets - TAPS) + TAPS - 1
                    total = None
                    for level in range(lowest, highest + 1):
                        j = level - lowest
                        term = jnp.broadcast_to(weights[k, row, j:j + 1, lanes], (SUB, wide)) * values[level][:, :wide]
                        total = term if total is None else total + term
                    result[k, at * BLOCK + q, :, lanes] = total
        for k in range(targets):
            leave(result.at[k, pl.ds(at * BLOCK, BLOCK)], out.at[k, pl.ds(number * BLOCK, BLOCK)])
    for copy in copies:
        copy.wait()


def mark_kernel(*refs):
    refs[-1][...] = jnp.zeros((SUB, LANES), jnp.float32)


def tiles_of(array):
    lead, levels, nlon = array.shape[:-2], array.shape[-2], array.shape[-1]
    split = array.reshape(lead + (levels, nlon // LANES, LANES))
    order = tuple(range(len(lead))) + (len(lead) + 1, len(lead), len(lead) + 2)
    split = with_layout_constraint(split, Layout(major_to_minor=order))
    return jnp.swapaxes(split, -3, -2).reshape(-1, LANES)


VMEM = pl.BlockSpec(memory_space=pltpu.VMEM)
ANY = pl.BlockSpec(memory_space=pl.ANY)
SMEM = pl.BlockSpec(memory_space=pltpu.SMEM)


def call(kernel, outs, args, specs=None, scratch=(), cost=None):
    return pl.pallas_call(
        kernel,
        out_shape=outs,
        in_specs=specs or [VMEM] * len(args),
        out_specs=jax.tree.map(lambda _: VMEM, outs),
        scratch_shapes=list(scratch),
        compiler_params=pltpu.CompilerParams(vmem_limit_bytes=16 << 20),
        cost_estimate=cost,
    )(*args)


def cost(flops, size):
    return pl.CostEstimate(flops=int(flops), bytes_accessed=int(size), transcendentals=0)


def f32(*shape):
    return jax.ShapeDtypeStruct(shape, jnp.float32)


def shards(tracers, wind_x, wind_y, level_counts, source_level, remap_weight):
    count = lax.axis_size("lev")
    bands = lax.axis_size("lat")
    number, depth, rows, nlon = tracers.shape
    targets, _, width = source_level.shape
    mains, tail, per = packed_sizes(nlon, count)[1:]
    blocks = rows // BLOCK
    inner = (rows - 2 * HALO) // BLOCK

    raw = tiles_of(jnp.transpose(tracers, (0, 2, 1, 3)))
    joined = jnp.concatenate([jnp.transpose(wind_x, (1, 0, 2)), jnp.transpose(wind_y, (1, 0, 2))], axis=0)
    halo = f32(HALO + 1, number, nlon)
    state, *sent = call(
        functools.partial(prep_kernel, rows),
        [f32(depth, rows, number, nlon), halo, halo], (raw, joined),
        cost=cost(1, 1))
    second = {i: ((i - 1) ^ 1) + 1 for i in range(1, bands - 1)}
    second_pairs = [(i * count + d, second[i] * count + d if i in second else i * count + (d ^ 1))
                    for i in range(bands) for d in range(count)]

    def beside(sent):
        return [lax.ppermute(sent[0], "lat", [(i, i ^ 1) for i in range(bands)]),
                lax.ppermute(sent[1], ("lat", "lev"), second_pairs)]

    rounds = [beside(sent)]
    taps = call(
        weights_kernel, f32(targets, rows, SUB, width),
        (jnp.transpose(remap_weight, (1, 2, 0, 3)), source_level),
        cost=cost(1, 1))

    def box(places, units):
        return places, packed_tiles(units, mains, tail, per), SUB, LANES

    def vmem(*shape):
        return pltpu.VMEM(shape, jnp.float32)

    held = -(-rows // SUB) * SUB
    coef = f32(3, depth, held, nlon)
    swept = vmem(depth, rows - 2 * REACH, number, nlon)
    stage = vmem(depth * (rows - 2 * REACH), number, nlon)
    chips = tuple(range(2, count, 2))
    groups = ((0,), (1,)) + tuple((k, k ^ 1) for k in chips)
    inner_units = depth * inner
    result = call(
        functools.partial(interior_kernel, count, rows, groups),
        [f32(*box(len(group), inner_units)) for group in groups]
        + [f32(depth, rows - 2 * REACH, number, nlon), coef, coef] + [halo] * (2 * depth - 2),
        (state, joined), scratch=[vmem(*box(count, inner_units)), vmem(2, depth, held, nlon), swept, stage, stage, stage],
        cost=cost(1, 1))
    middle, (first, cx, cy), sent = result[:len(groups)], result[len(groups):len(groups) + 3], result[len(groups) + 3:]
    rounds += [beside(sent[2 * i:2 * i + 2]) for i in range(depth - 1)]
    swept = vmem(1, 2 * HALO, number, nlon)
    stage = vmem(2 * HALO, number, nlon)

    def edge(slot, groups, after):
        args = (state, *rounds[slot], first, cx, cy, *after)
        return call(
            functools.partial(edge_kernel, count, rows, groups, slot),
            [f32(*box(len(group), 2)) for group in groups], args,
            specs=[VMEM] * (len(args) - len(after)) + [ANY] * len(after),
            scratch=[vmem(*box(count, 2)), vmem(3, 2, SUB, nlon), swept, swept, stage, stage, stage],
            cost=cost(60 * tracers.size, 8 * tracers.size))

    def swapped(sent, k):
        return lax.ppermute(sent, "lev", [(i, i ^ k) for i in range(count)])

    def units_of(k, places):
        return tuple((k, slot, block) for slot, block in places)

    def remap(listed, after):
        args = (level_counts, *(chunk for _, chunk in listed), taps, *after)
        return pl.pallas_call(
            functools.partial(remap_kernel, count, tuple(units for units, _ in listed), tuple(range(blocks))),
            out_shape=f32(targets, rows, number, width),
            in_specs=[SMEM] + [VMEM] * (len(args) - 1 - len(after)) + [ANY] * len(after),
            out_specs=ANY,
            scratch_shapes=[
                vmem(targets + 1, blocks, packed_tiles(1, mains, tail, per), SUB, LANES),
                vmem(targets, rows, number, width),
                pltpu.SemaphoreType.DMA((blocks * targets,)),
            ],
            compiler_params=pltpu.CompilerParams(vmem_limit_bytes=16 << 20),
            cost_estimate=cost(1, 1),
        )(*args)

    def mark(chunks):
        return pl.pallas_call(
            mark_kernel, out_shape=f32(SUB, LANES), in_specs=[ANY] * len(chunks), out_specs=VMEM, cost_estimate=cost(1, 1),
            compiler_params=pltpu.CompilerParams(vmem_limit_bytes=1 << 20),
        )(*chunks)

    places = tuple((slot, 1 + b) for slot in range(depth) for b in range(inner))
    arrived = [swapped(chunk, k) for k, chunk in zip(chips, middle[2:])]
    listed = [(units_of(k, places), chunk) for k, chunk in zip(chips, arrived)]
    listed.append((units_of(0, places), middle[0]))
    beside_me = [(units_of(1, places), middle[1])]
    after, marks = (taps,), []
    for slot in range(depth):
        own = ((slot, 0), (slot, blocks - 1))
        done = edge(slot, tuple((k,) for k in range(count)), after)
        crossing = [(units_of(k, own), swapped(done[k], k)) for k in range(count - 1, 1, -1)]
        listed += crossing + [(units_of(0, own), done[0])]
        beside_me.append((units_of(1, own), done[1]))
        marks.append(mark([chunk for _, chunk in crossing]))
        after = (done[0],)
    beside_me += [(units_of(k ^ 1, places), chunk) for k, chunk in zip(chips, arrived)]
    waiting = lax.optimization_barrier((*(chunk for _, chunk in beside_me), done[0]))
    listed += [(units, swapped(chunk[-1:], 1)) for (units, _), chunk in zip(beside_me, waiting)]
    out = remap(listed, marks)
    return jnp.transpose(out, (2, 0, 1, 3))


def solution(mesh):
    in_specs = (
        P(None, "lev", ("groups", "lat"), None),
        P("lev", ("groups", "lat"), None),
        P("lev", ("groups", "lat"), None),
        P(),
        P(None, ("groups", "lat"), "lev"),
        P(None, None, ("groups", "lat"), "lev"),
    )
    out_specs = P(None, None, ("groups", "lat"), "lev")
    return jax.shard_map(shards, mesh=mesh, in_specs=in_specs, out_specs=out_specs, check_vma=False)
```

```python
import functools

import jax
import jax.numpy as jnp
from jax import lax
from jax.experimental import pallas as pl
from jax.experimental.layout import Layout, with_layout_constraint
from jax.experimental.pallas import tpu as pltpu
from jax.sharding import PartitionSpec as P

SUBSTEPS = 2
TAPS = 4
REACH = 3
HALO = REACH * SUBSTEPS
BLOCK = 6
LANES = 128
SUB = 8


def spread(row):
    return jnp.broadcast_to(row, (SUB, LANES))


def lane_ids():
    return lax.broadcasted_iota(jnp.int32, (SUB, LANES), 1)


def from_west(tiles, steps, lane):
    turned = [pltpu.roll(t, steps, 1) for t in tiles]
    return [jnp.where(lane < steps, turned[j - 1], turned[j]) for j in range(len(tiles))]


def from_east(tiles, lane):
    turned = [pltpu.roll(t, LANES - 1, 1) for t in tiles]
    count = len(tiles)
    return [jnp.where(lane == LANES - 1, turned[(j + 1) % count], turned[j]) for j in range(count)]


def coefficients(wind):
    size = jnp.abs(wind)
    rest = 1.0 - size
    alpha = wind * rest * rest * (1.0 / 12.0)
    beta = wind * size * rest * (-1.0 / 12.0)
    gamma = wind * size * (3.0 - 2.0 * size)
    return alpha, beta, gamma


def packed_sizes(nlon, count):
    width = nlon // count
    mains, tail = width // LANES, width % LANES
    return width, mains, tail, LANES // tail if tail else 1


def packed_tiles(units, mains, tail, per):
    return units * BLOCK * mains + (-(-units * BLOCK // per) if tail else 0)


def fill_halos(rows, slot, state, winds, first_round, second_round):
    band, bands = lax.axis_index("lat"), lax.axis_size("lat")
    even = band % 2 == 0
    keep = jnp.where((band == 0) | (band == bands - 1), 0.0, 1.0)
    for target, north, scale in ((first_round, even, None), (second_round, jnp.logical_not(even), keep)):
        scaled = (lambda v: v) if scale is None else (lambda v: v * scale)
        row_t = jnp.where(north, rows - HALO, 0)
        row_x = jnp.where(north, rows - REACH, 0)
        row_y = jnp.where(north, rows - REACH - 1, 0)
        for row in range(HALO):
            target[row] = scaled(state[slot, row_t + row])
        for q in range(REACH):
            target[HALO, q:q + 1, :] = scaled(winds[row_x + q, slot:slot + 1, :])
        for q in range(REACH + 1):
            target[HALO, REACH + q:REACH + q + 1, :] = scaled(winds[rows + row_y + q, slot:slot + 1, :])


def prep_kernel(rows, tracers, winds, state, *halos):
    levels, nlon = state.shape[0], state.shape[3]
    nj = nlon // LANES
    row_stride = nj * levels
    tracer_stride = rows * row_stride

    def body(row, _):
        for level in range(levels):
            for j in range(nj):
                start = row * row_stride + j * levels + level
                state[level, row, :, tile(j)] = tracers[pl.ds(start, SUB, stride=tracer_stride), :]
        return 0

    lax.fori_loop(0, rows, body, 0)
    for slot in range(levels):
        fill_halos(rows, slot, state, winds, *halos[2 * slot:2 * slot + 2])


def lat_pass(levels, nj, ranges, cell, coef, store):
    group = 3 if nj % 3 == 0 else 1

    def body(i, _):
        level = i // (nj // group)
        results = []
        for u in range(group):
            lanes = pl.ds(pl.multiple_of(((i % (nj // group)) * group + u) * LANES, LANES), LANES)
            results += [(level, row, lanes, value) for row, value in one(level, lanes)]
        for result in results:
            store(*result)
        return 0

    def one(level, lanes):
        results = []
        for first, last in ranges:
            a = {r: cell(level, r, lanes) for r in range(first - REACH, last + REACH)}
            inter = {f: 7.0 * (a[f - 1] + a[f]) - (a[f - 2] + a[f + 1]) for f in range(first - 1, last + 2)}
            flux = {}
            for f in range(first, last + 1):
                alpha, beta, gamma = [spread(coef(i, level, f, lanes)) for i in range(3)]
                north = gamma > 0
                behind = jnp.where(north, inter[f - 1], inter[f + 1])
                upwind = jnp.where(north, a[f - 1], a[f])
                flux[f] = alpha * inter[f] + beta * behind + gamma * upwind
                if f > first:
                    results.append((f - 1, a[f - 1] - (flux[f] - flux[f - 1])))
        return results

    lax.fori_loop(0, levels * nj // group, body, 0)


def tile(j):
    return slice(j * LANES, (j + 1) * LANES)


def lon_pass(work, swept, coef, inter, west, flux, lane, finish):
    nj = swept.shape[3] // LANES
    each = range(nj)

    def interfaces(n):
        level, _, at = work[n]
        b = [swept[level, at, :, tile(j)] for j in each]
        w1, w2, e1 = from_west(b, 1, lane), from_west(b, 2, lane), from_east(b, lane)
        for j in each:
            inter[n, :, tile(j)] = 7.0 * (w1[j] + b[j]) - (w2[j] + e1[j])
            west[n, :, tile(j)] = w1[j]

    def fluxes(n):
        level, row, at = work[n]
        mid = [inter[n, :, tile(j)] for j in each]
        w1, e1 = from_west(mid, 1, lane), from_east(mid, lane)
        for j in each:
            alpha, beta, gamma = [spread(coef(i, level, row, tile(j))) for i in range(3)]
            right = gamma > 0
            behind = jnp.where(right, w1[j], e1[j])
            upwind = jnp.where(right, west[n, :, tile(j)], swept[level, at, :, tile(j)])
            flux[n, :, tile(j)] = alpha * mid[j] + beta * behind + gamma * upwind

    def update(n):
        level, _, at = work[n]
        here = [flux[n, :, tile(j)] for j in each]
        e1 = from_east(here, lane)
        return [swept[level, at, :, tile(j)] - (e1[j] - here[j]) for j in each]

    groups = len(work) // BLOCK
    for g in range(groups + 2):
        if g < groups:
            for q in range(BLOCK):
                interfaces(g * BLOCK + q)
        if 1 <= g <= groups:
            for q in range(BLOCK):
                fluxes((g - 1) * BLOCK + q)
        if g >= 2:
            finish(g - 2, [update((g - 2) * BLOCK + q) for q in range(BLOCK)])


def pack_block(block, packed, unit, units, count, lane):
    nlon = len(block[0]) * LANES
    width, mains, tail, per = packed_sizes(nlon, count)
    for d in range(count):
        j0, off = (d * width) // LANES, (d * width) % LANES
        for q, tiles in enumerate(block):
            turned = [pltpu.roll(tiles[j0 + m], LANES - off, 1) if off else tiles[j0 + m]
                      for m in range(mains + (1 if off else 0))]
            for m in range(mains):
                whole = jnp.where(lane < LANES - off, turned[m], turned[m + 1]) if off else turned[m]
                packed[d, (unit * BLOCK + q) * mains + m] = whole
        if tail:
            totals = {}
            for q, tiles in enumerate(block):
                at, place = divmod(unit * BLOCK + q, per)
                at += units * BLOCK * mains
                shift = (place * tail - off) % LANES
                moved = pltpu.roll(tiles[j0 + mains], shift, 1) if shift else tiles[j0 + mains]
                if place:
                    before = totals[at] if at in totals else packed[d, at]
                    moved = jnp.where(lane < place * tail, before, moved)
                totals[at] = moved
            for at, total in totals.items():
                packed[d, at] = total


def unpack_unit(chunk, place, unit, units, target, lead, mains, tail, per, lane):
    copy_tiles([((chunk, (place, unit * BLOCK * mains + i)), (target, lead + (i,))) for i in range(BLOCK * mains)])
    totals = {}
    for q in range(BLOCK if tail else 0):
        at, there = divmod(unit * BLOCK + q, per)
        to, here = divmod(q, per)
        shift = (here - there) * tail % LANES
        if to in totals and totals[to][1:] == (at, shift):
            continue
        source = chunk[place, units * BLOCK * mains + at]
        moved = pltpu.roll(source, shift, 1) if shift else source
        totals[to] = (jnp.where(lane < here * tail, totals[to][0], moved) if to in totals else moved, at, shift)
    for to, (total, _, _) in totals.items():
        target[lead + (BLOCK * mains + to,)] = total


def copy_tiles(pairs):
    values = [source[at] for (source, at), _ in pairs]
    for value, (_, (target, at)) in zip(values, pairs):
        target[at] = value


def hand_out(packed, outs, groups):
    me = lax.axis_index("lev")
    for group, out in zip(groups, outs):
        for place, k in enumerate(group):
            copy_tiles([((packed, (me ^ k, i)), (out, (place, i))) for i in range(packed.shape[1])])


def own_coefficients(rows, joined, winds, cx, cy):
    levels, held, nlon = cx.shape[1:]
    keep = jnp.where(lax.axis_index("lat") == 0, 0.0, 1.0)
    for level in range(levels):
        for way in range(2):
            for row in range(rows):
                winds[way, level, row:row + 1, :] = joined[way * rows + row, level:level + 1, :]
        winds[1, level, 0:1, :] = winds[1, level, 0:1, :] * keep
        for way, target in enumerate((cx, cy)):
            for j in range(nlon // LANES):
                parts = coefficients(winds[way, level, :, tile(j)])
                for p in range(3):
                    target[p, level, :, tile(j)] = parts[p]


def put_rows(target, level, at, rows):
    for q, row in enumerate(rows):
        for j, part in enumerate(row):
            target[level, at + q, :, tile(j)] = part


def interior_kernel(count, rows, groups, state, joined, *refs):
    outs, (first, cx, cy, packed, winds, swept, inter, west, flux) = refs[:len(groups)], refs[len(groups):]
    levels, nlon = state.shape[0], state.shape[3]
    nj = nlon // LANES
    lane = lane_ids()
    own_coefficients(rows, joined, winds, cx, cy)
    coef_x = lambda i, level, r, lanes: cx[i, level, r:r + 1, lanes]
    coef_y = lambda i, level, f, lanes: cy[i, level, f:f + 1, lanes]

    def put(level, row, lanes, value):
        swept[level, row - REACH, :, lanes] = value

    lat_pass(levels, nj, [(REACH, rows - REACH)], lambda level, r, lanes: state[level, r, :, lanes], coef_y, put)
    work = [(level, row, row - REACH) for level in range(levels) for row in range(REACH, rows - REACH)]

    def keep_first(group, done):
        level, _, at = work[group * BLOCK]
        put_rows(first, level, at, done)

    lon_pass(work, swept, coef_x, inter, west, flux, lane, keep_first)
    lat_pass(levels, nj, [(HALO, rows - HALO)], lambda level, r, lanes: first[level, r - REACH, :, lanes], coef_y, put)
    work_last = [(level, row, row - REACH) for level in range(levels) for row in range(HALO, rows - HALO)]

    def send(group, done):
        pack_block(done, packed, group, len(work_last) // BLOCK, count, lane)

    lon_pass(work_last, swept, coef_x, inter, west, flux, lane, send)
    hand_out(packed, outs, groups)


def edge_kernel(count, rows, groups, slot, state, first_round, second_round, first, cx, cy, *refs):
    outs, (packed, beyond, swept, edge, inter, west, flux) = refs[-7 - len(groups):-7], refs[-7:]
    nlon = state.shape[3]
    nj = nlon // LANES
    lane = lane_ids()
    odd = lax.axis_index("lat") % 2 == 1

    def halo(south, *at):
        one, two = first_round[at], second_round[at]
        return jnp.where(odd, one, two) if south else jnp.where(odd, two, one)

    for end, south in enumerate((True, False)):
        for j in range(nj):
            parts = coefficients(halo(south, HALO, slice(None), tile(j)))
            for p in range(3):
                beyond[p, end, :, tile(j)] = parts[p]

    def coef_x(i, _, r, lanes):
        if 0 <= r < rows:
            return cx[i, slot, r:r + 1, lanes]
        end, at = (0, r + REACH) if r < 0 else (1, r - rows)
        return beyond[i, end, at:at + 1, lanes]

    def coef_y(i, _, f, lanes):
        if 0 <= f < rows:
            return cy[i, slot, f:f + 1, lanes]
        end, at = (0, f + 2 * REACH + 1) if f < 0 else (1, f - rows + REACH)
        return beyond[i, end, at:at + 1, lanes]

    def cell(_, r, lanes):
        if 0 <= r < rows:
            return state[slot, r, :, lanes]
        return halo(r < 0, r + HALO if r < 0 else r - rows, slice(None), lanes)

    ends = [(-REACH, REACH), (rows - REACH, rows + REACH)]
    ends_last = [(0, HALO), (rows - HALO, rows)]

    def place(row, ranges):
        (a, b), (c, _) = ranges
        return row - a if row < b else row - c + BLOCK

    def cell_first(_, r, lanes):
        if REACH <= r < rows - REACH:
            return first[slot, r - REACH, :, lanes]
        return edge[0, place(r, ends), :, lanes]

    def put(_, row, lanes, value):
        swept[0, place(row, ends), :, lanes] = value

    def put_last(_, row, lanes, value):
        swept[0, place(row, ends_last), :, lanes] = value

    def listed(ranges):
        return [(0, row, place(row, ranges)) for a, b in ranges for row in range(a, b)]

    def keep_edge(group, done):
        put_rows(edge, 0, group * BLOCK, done)

    def send(group, done):
        pack_block(done, packed, group, len(ends_last), count, lane)

    lat_pass(1, nj, ends, cell, coef_y, put)
    lon_pass(listed(ends), swept, coef_x, inter, west, flux, lane, keep_edge)
    lat_pass(1, nj, ends_last, cell_first, coef_y, put_last)
    lon_pass(listed(ends_last), swept, coef_x, inter, west, flux, lane, send)
    hand_out(packed, outs, groups)


def weights_kernel(weights, source, out):
    targets, rows, taps, width = weights.shape

    for row in range(rows):
        for k in range(targets):
            lowest, highest = max(k - (TAPS - 1), 0), min(k, targets - TAPS)
            w = weights[k, row]
            w = jnp.concatenate([w, jnp.zeros((SUB - taps, width), jnp.float32)], axis=0)
            at = jnp.broadcast_to(source[k, row:row + 1, :], (SUB, width))
            total = w
            for g in range(lowest + 1, highest + 1):
                total = jnp.where(at == g, pltpu.roll(w, g - lowest, 0), total)
            out[k, row] = total


def remap_kernel(count, plan, numbers, counts, *refs):
    chunks, weights, (out, levels, result, sems) = refs[:len(plan)], refs[len(plan)], refs[-4:]
    me = lax.axis_index("lev")
    targets, _, _, width = result.shape
    _, mains, tail, per = packed_sizes(width * count, count)
    lane = lane_ids()
    copies = []

    def leave(source, target):
        copy = pltpu.make_async_copy(source, target, sems.at[len(copies)])
        copy.start()
        copies.append(copy)

    def level_of(k, slot):
        d = me ^ k
        start = jnp.int32(0)
        for e in range(count):
            start = start + jnp.where(e < d, counts[e], 0)
        return jnp.where(slot < counts[d], start + slot, targets)

    for units, chunk in zip(plan, chunks):
        for unit, (k, slot, number) in enumerate(units):
            lead = (level_of(k, slot), numbers.index(number))
            unpack_unit(chunk, 0, unit, len(units), levels, lead, mains, tail, per, lane)

    for at, number in enumerate(numbers):
        for q in range(BLOCK):
            row = number * BLOCK + q
            for m in range(mains + (1 if tail else 0)):
                wide = LANES if m < mains else tail
                lanes = slice(m * LANES, m * LANES + wide)
                values = []
                for level in range(targets):
                    if m < mains:
                        values.append(levels[level, at, q * mains + m])
                    else:
                        last = levels[level, at, BLOCK * mains + q // per]
                        shift = (q % per) * tail
                        values.append(pltpu.roll(last, LANES - shift, 1) if shift else last)
                for k in range(targets):
                    lowest, highest = max(k - (TAPS - 1), 0), min(k, targets - TAPS) + TAPS - 1
                    total = None
                    for level in range(lowest, highest + 1):
                        j = level - lowest
                        term = jnp.broadcast_to(weights[k, row, j:j + 1, lanes], (SUB, wide)) * values[level][:, :wide]
                        total = term if total is None else total + term
                    result[k, at * BLOCK + q, :, lanes] = total
        for k in range(targets):
            leave(result.at[k, pl.ds(at * BLOCK, BLOCK)], out.at[k, pl.ds(number * BLOCK, BLOCK)])
    for copy in copies:
        copy.wait()


def mark_kernel(*refs):
    refs[-1][...] = jnp.zeros((SUB, LANES), jnp.float32)


def tiles_of(array):
    lead, levels, nlon = array.shape[:-2], array.shape[-2], array.shape[-1]
    split = array.reshape(lead + (levels, nlon // LANES, LANES))
    order = tuple(range(len(lead))) + (len(lead) + 1, len(lead), len(lead) + 2)
    split = with_layout_constraint(split, Layout(major_to_minor=order))
    return jnp.swapaxes(split, -3, -2).reshape(-1, LANES)


VMEM = pl.BlockSpec(memory_space=pltpu.VMEM)
ANY = pl.BlockSpec(memory_space=pl.ANY)
SMEM = pl.BlockSpec(memory_space=pltpu.SMEM)


def call(kernel, outs, args, specs=None, scratch=(), cost=None):
    return pl.pallas_call(
        kernel,
        out_shape=outs,
        in_specs=specs or [VMEM] * len(args),
        out_specs=jax.tree.map(lambda _: VMEM, outs),
        scratch_shapes=list(scratch),
        compiler_params=pltpu.CompilerParams(vmem_limit_bytes=16 << 20),
        cost_estimate=cost,
    )(*args)


def cost(flops, size):
    return pl.CostEstimate(flops=int(flops), bytes_accessed=int(size), transcendentals=0)


def f32(*shape):
    return jax.ShapeDtypeStruct(shape, jnp.float32)


def shards(tracers, wind_x, wind_y, level_counts, source_level, remap_weight):
    count = lax.axis_size("lev")
    bands = lax.axis_size("lat")
    number, depth, rows, nlon = tracers.shape
    targets, _, width = source_level.shape
    mains, tail, per = packed_sizes(nlon, count)[1:]
    blocks = rows // BLOCK
    inner = (rows - 2 * HALO) // BLOCK

    raw = tiles_of(jnp.transpose(tracers, (0, 2, 1, 3)))
    joined = jnp.concatenate([jnp.transpose(wind_x, (1, 0, 2)), jnp.transpose(wind_y, (1, 0, 2))], axis=0)
    halo = f32(HALO + 1, number, nlon)
    state, *sent = call(
        functools.partial(prep_kernel, rows),
        [f32(depth, rows, number, nlon)] + [halo] * (2 * depth), (raw, joined),
        cost=cost(1, 1))
    second = {i: ((i - 1) ^ 1) + 1 for i in range(1, bands - 1)}
    second_pairs = [(i * count + d, second[i] * count + d if i in second else i * count + (d ^ 1))
                    for i in range(bands) for d in range(count)]

    def beside(sent):
        return [lax.ppermute(sent[0], "lat", [(i, i ^ 1) for i in range(bands)]),
                lax.ppermute(sent[1], ("lat", "lev"), second_pairs)]

    rounds = [beside(sent[2 * slot:2 * slot + 2]) for slot in range(depth)]
    taps = call(
        weights_kernel, f32(targets, rows, SUB, width),
        (jnp.transpose(remap_weight, (1, 2, 0, 3)), source_level),
        cost=cost(1, 1))

    def box(places, units):
        return places, packed_tiles(units, mains, tail, per), SUB, LANES

    def vmem(*shape):
        return pltpu.VMEM(shape, jnp.float32)

    held = -(-rows // SUB) * SUB
    coef = f32(3, depth, held, nlon)
    swept = vmem(depth, rows - 2 * REACH, number, nlon)
    stage = vmem(depth * (rows - 2 * REACH), number, nlon)
    chips = tuple(range(2, count, 2))
    groups = ((0,), (1,)) + tuple((k, k ^ 1) for k in chips)
    inner_units = depth * inner
    result = call(
        functools.partial(interior_kernel, count, rows, groups),
        [f32(*box(len(group), inner_units)) for group in groups]
        + [f32(depth, rows - 2 * REACH, number, nlon), coef, coef],
        (state, joined), scratch=[vmem(*box(count, inner_units)), vmem(2, depth, held, nlon), swept, stage, stage, stage],
        cost=cost(1, 1))
    middle, (first, cx, cy) = result[:len(groups)], result[len(groups):]
    swept = vmem(1, 2 * HALO, number, nlon)
    stage = vmem(2 * HALO, number, nlon)

    def edge(slot, groups, after):
        args = (state, *rounds[slot], first, cx, cy, *after)
        return call(
            functools.partial(edge_kernel, count, rows, groups, slot),
            [f32(*box(len(group), 2)) for group in groups], args,
            specs=[VMEM] * (len(args) - len(after)) + [ANY] * len(after),
            scratch=[vmem(*box(count, 2)), vmem(3, 2, SUB, nlon), swept, swept, stage, stage, stage],
            cost=cost(60 * tracers.size, 8 * tracers.size))

    def swapped(sent, k):
        return lax.ppermute(sent, "lev", [(i, i ^ k) for i in range(count)])

    def units_of(k, places):
        return tuple((k, slot, block) for slot, block in places)

    def remap(listed, after):
        args = (level_counts, *(chunk for _, chunk in listed), taps, *after)
        return pl.pallas_call(
            functools.partial(remap_kernel, count, tuple(units for units, _ in listed), tuple(range(blocks))),
            out_shape=f32(targets, rows, number, width),
            in_specs=[SMEM] + [VMEM] * (len(args) - 1 - len(after)) + [ANY] * len(after),
            out_specs=ANY,
            scratch_shapes=[
                vmem(targets + 1, blocks, packed_tiles(1, mains, tail, per), SUB, LANES),
                vmem(targets, rows, number, width),
                pltpu.SemaphoreType.DMA((blocks * targets,)),
            ],
            compiler_params=pltpu.CompilerParams(vmem_limit_bytes=16 << 20),
            cost_estimate=cost(1, 1),
        )(*args)

    def mark(chunks):
        return pl.pallas_call(
            mark_kernel, out_shape=f32(SUB, LANES), in_specs=[ANY] * len(chunks), out_specs=VMEM, cost_estimate=cost(1, 1),
            compiler_params=pltpu.CompilerParams(vmem_limit_bytes=1 << 20),
        )(*chunks)

    places = tuple((slot, 1 + b) for slot in range(depth) for b in range(inner))
    arrived = [swapped(chunk, k) for k, chunk in zip(chips, middle[2:])]
    listed = [(units_of(k, places), chunk) for k, chunk in zip(chips, arrived)]
    listed.append((units_of(0, places), middle[0]))
    beside_me = [(units_of(1, places), middle[1])]
    after, marks = (taps,), []
    for slot in range(depth):
        own = ((slot, 0), (slot, blocks - 1))
        done = edge(slot, tuple((k,) for k in range(count)), after)
        crossing = [(units_of(k, own), swapped(done[k], k)) for k in range(count - 1, 1, -1)]
        listed += crossing + [(units_of(0, own), done[0])]
        beside_me.append((units_of(1, own), done[1]))
        marks.append(mark([chunk for _, chunk in crossing]))
        after = (done[0],)
    beside_me += [(units_of(k ^ 1, places), chunk) for k, chunk in zip(chips, arrived)]
    waiting = lax.optimization_barrier((*(chunk for _, chunk in beside_me), done[0]))
    listed += [(units, swapped(chunk[-1:], 1)) for (units, _), chunk in zip(beside_me, waiting)]
    out = remap(listed, marks)
    return jnp.transpose(out, (2, 0, 1, 3))


def solution(mesh):
    in_specs = (
        P(None, "lev", ("groups", "lat"), None),
        P("lev", ("groups", "lat"), None),
        P("lev", ("groups", "lat"), None),
        P(),
        P(None, ("groups", "lat"), "lev"),
        P(None, None, ("groups", "lat"), "lev"),
    )
    out_specs = P(None, None, ("groups", "lat"), "lev")
    return jax.shard_map(shards, mesh=mesh, in_specs=in_specs, out_specs=out_specs, check_vma=False)
```

```python
import functools

import jax
import jax.numpy as jnp
from jax import lax
from jax.experimental import pallas as pl
from jax.experimental.layout import Layout, with_layout_constraint
from jax.experimental.pallas import tpu as pltpu
from jax.sharding import PartitionSpec as P

SUBSTEPS = 2
TAPS = 4
REACH = 3
HALO = REACH * SUBSTEPS
BLOCK = 6
LAG = 3
LANES = 128
SUB = 8


def spread(row):
    return jnp.broadcast_to(row, (SUB, LANES))


def lane_ids():
    return lax.broadcasted_iota(jnp.int32, (SUB, LANES), 1)


def from_west(tiles, steps, lane):
    turned = [pltpu.roll(t, steps, 1) for t in tiles]
    return [jnp.where(lane < steps, turned[j - 1], turned[j]) for j in range(len(tiles))]


def from_east(tiles, lane):
    turned = [pltpu.roll(t, LANES - 1, 1) for t in tiles]
    count = len(tiles)
    return [jnp.where(lane == LANES - 1, turned[(j + 1) % count], turned[j]) for j in range(count)]


def coefficients(wind):
    size = jnp.abs(wind)
    rest = 1.0 - size
    alpha = wind * rest * rest * (1.0 / 12.0)
    beta = wind * size * rest * (-1.0 / 12.0)
    gamma = wind * size * (3.0 - 2.0 * size)
    return alpha, beta, gamma


def packed_sizes(nlon, count):
    width = nlon // count
    mains, tail = width // LANES, width % LANES
    return width, mains, tail, LANES // tail if tail else 1


def packed_tiles(units, mains, tail, per):
    return units * BLOCK * mains + (-(-units * BLOCK // per) if tail else 0)


def fill_halos(rows, slot, state, winds, first_round, second_round):
    band, bands = lax.axis_index("lat"), lax.axis_size("lat")
    even = band % 2 == 0
    keep = jnp.where((band == 0) | (band == bands - 1), 0.0, 1.0)
    for target, north, scale in ((first_round, even, None), (second_round, jnp.logical_not(even), keep)):
        scaled = (lambda v: v) if scale is None else (lambda v: v * scale)
        row_t = jnp.where(north, rows - HALO, 0)
        row_x = jnp.where(north, rows - REACH, 0)
        row_y = jnp.where(north, rows - REACH - 1, 0)
        for row in range(HALO):
            target[row] = scaled(state[slot, row_t + row])
        for q in range(REACH):
            target[HALO, q:q + 1, :] = scaled(winds[row_x + q, slot:slot + 1, :])
        for q in range(REACH + 1):
            target[HALO, REACH + q:REACH + q + 1, :] = scaled(winds[rows + row_y + q, slot:slot + 1, :])


def prep_kernel(rows, tracers, winds, state, first_round, second_round):
    levels, nlon = state.shape[0], state.shape[3]
    nj = nlon // LANES
    row_stride = nj * levels
    tracer_stride = rows * row_stride

    def body(row, _):
        for level in range(levels):
            for j in range(nj):
                start = row * row_stride + j * levels + level
                state[level, row, :, tile(j)] = tracers[pl.ds(start, SUB, stride=tracer_stride), :]
        return 0

    lax.fori_loop(0, rows, body, 0)
    fill_halos(rows, 0, state, winds, first_round, second_round)


def lat_pass(levels, nj, ranges, cell, coef, store):
    group = 3 if nj % 3 == 0 else 1

    def body(i, _):
        level = i // (nj // group)
        results = []
        for u in range(group):
            lanes = pl.ds(pl.multiple_of(((i % (nj // group)) * group + u) * LANES, LANES), LANES)
            results += [(level, row, lanes, value) for row, value in one(level, lanes)]
        for result in results:
            store(*result)
        return 0

    def one(level, lanes):
        results = []
        for first, last in ranges:
            a = {r: cell(level, r, lanes) for r in range(first - REACH, last + REACH)}
            inter = {f: 7.0 * (a[f - 1] + a[f]) - (a[f - 2] + a[f + 1]) for f in range(first - 1, last + 2)}
            flux = {}
            for f in range(first, last + 1):
                alpha, beta, gamma = [spread(coef(i, level, f, lanes)) for i in range(3)]
                north = gamma > 0
                behind = jnp.where(north, inter[f - 1], inter[f + 1])
                upwind = jnp.where(north, a[f - 1], a[f])
                flux[f] = alpha * inter[f] + beta * behind + gamma * upwind
                if f > first:
                    results.append((f - 1, a[f - 1] - (flux[f] - flux[f - 1])))
        return results

    lax.fori_loop(0, levels * nj // group, body, 0)


def tile(j):
    return slice(j * LANES, (j + 1) * LANES)


def lon_pass(work, swept, coef, inter, west, flux, lane, finish):
    nj = swept.shape[3] // LANES
    each = range(nj)

    def interfaces(n):
        level, _, at = work[n]
        b = [swept[level, at, :, tile(j)] for j in each]
        w1, w2, e1 = from_west(b, 1, lane), from_west(b, 2, lane), from_east(b, lane)
        for j in each:
            inter[n, :, tile(j)] = 7.0 * (w1[j] + b[j]) - (w2[j] + e1[j])
            west[n, :, tile(j)] = w1[j]

    def fluxes(n):
        level, row, at = work[n]
        mid = [inter[n, :, tile(j)] for j in each]
        w1, e1 = from_west(mid, 1, lane), from_east(mid, lane)
        for j in each:
            alpha, beta, gamma = [spread(coef(i, level, row, tile(j))) for i in range(3)]
            right = gamma > 0
            behind = jnp.where(right, w1[j], e1[j])
            upwind = jnp.where(right, west[n, :, tile(j)], swept[level, at, :, tile(j)])
            flux[n, :, tile(j)] = alpha * mid[j] + beta * behind + gamma * upwind

    def update(n):
        level, _, at = work[n]
        here = [flux[n, :, tile(j)] for j in each]
        e1 = from_east(here, lane)
        return [swept[level, at, :, tile(j)] - (e1[j] - here[j]) for j in each]

    for n in range(len(work) + 2 * LAG):
        if n < len(work):
            interfaces(n)
        if LAG <= n < len(work) + LAG:
            fluxes(n - LAG)
        if n >= 2 * LAG:
            finish(n - 2 * LAG, update(n - 2 * LAG))


def packer(packed, rows, count, lane):
    tails = {}

    def pack(n, tiles):
        width, mains, tail, per = packed_sizes(len(tiles) * LANES, count)
        for d in range(count):
            j0, off = (d * width) // LANES, (d * width) % LANES
            turned = [pltpu.roll(tiles[j0 + m], LANES - off, 1) if off else tiles[j0 + m]
                      for m in range(mains + (1 if off else 0))]
            for m in range(mains):
                whole = jnp.where(lane < LANES - off, turned[m], turned[m + 1]) if off else turned[m]
                packed[d, n * mains + m] = whole
            if tail:
                at, place = divmod(n, per)
                shift = (place * tail - off) % LANES
                moved = pltpu.roll(tiles[j0 + mains], shift, 1) if shift else tiles[j0 + mains]
                tails[d] = jnp.where(lane < place * tail, tails[d], moved) if place else moved
                if place == per - 1 or n == rows - 1:
                    packed[d, rows * mains + at] = tails[d]

    return pack


def unpack_unit(chunk, place, unit, units, target, lead, mains, tail, per, lane):
    copy_tiles([((chunk, (place, unit * BLOCK * mains + i)), (target, lead + (i,))) for i in range(BLOCK * mains)])
    totals = {}
    for q in range(BLOCK if tail else 0):
        at, there = divmod(unit * BLOCK + q, per)
        to, here = divmod(q, per)
        shift = (here - there) * tail % LANES
        if to in totals and totals[to][1:] == (at, shift):
            continue
        source = chunk[place, units * BLOCK * mains + at]
        moved = pltpu.roll(source, shift, 1) if shift else source
        totals[to] = (jnp.where(lane < here * tail, totals[to][0], moved) if to in totals else moved, at, shift)
    for to, (total, _, _) in totals.items():
        target[lead + (BLOCK * mains + to,)] = total


def copy_tiles(pairs):
    values = [source[at] for (source, at), _ in pairs]
    for value, (_, (target, at)) in zip(values, pairs):
        target[at] = value


def hand_out(packed, outs, groups):
    me = lax.axis_index("lev")
    for group, out in zip(groups, outs):
        for place, k in enumerate(group):
            copy_tiles([((packed, (me ^ k, i)), (out, (place, i))) for i in range(packed.shape[1])])


def own_coefficients(rows, joined, winds, cx, cy):
    levels, held, nlon = cx.shape[1:]
    keep = jnp.where(lax.axis_index("lat") == 0, 0.0, 1.0)
    for level in range(levels):
        for way in range(2):
            for row in range(rows):
                winds[way, level, row:row + 1, :] = joined[way * rows + row, level:level + 1, :]
        winds[1, level, 0:1, :] = winds[1, level, 0:1, :] * keep
        for way, target in enumerate((cx, cy)):
            for j in range(nlon // LANES):
                parts = coefficients(winds[way, level, :, tile(j)])
                for p in range(3):
                    target[p, level, :, tile(j)] = parts[p]


def put_row(target, level, at, row):
    for j, part in enumerate(row):
        target[level, at, :, tile(j)] = part


def interior_kernel(count, rows, groups, state, joined, *refs):
    outs, (first, cx, cy), refs = refs[:len(groups)], refs[len(groups):len(groups) + 3], refs[len(groups) + 3:]
    halos, (packed, winds, swept, inter, west, flux) = refs[:-6], refs[-6:]
    levels, nlon = state.shape[0], state.shape[3]
    nj = nlon // LANES
    lane = lane_ids()
    for slot in range(1, levels):
        fill_halos(rows, slot, state, joined, *halos[2 * slot - 2:2 * slot])
    own_coefficients(rows, joined, winds, cx, cy)
    coef_x = lambda i, level, r, lanes: cx[i, level, r:r + 1, lanes]
    coef_y = lambda i, level, f, lanes: cy[i, level, f:f + 1, lanes]

    def put(level, row, lanes, value):
        swept[level, row - REACH, :, lanes] = value

    lat_pass(levels, nj, [(REACH, rows - REACH)], lambda level, r, lanes: state[level, r, :, lanes], coef_y, put)
    work = [(level, row, row - REACH) for level in range(levels) for row in range(REACH, rows - REACH)]

    def keep_first(n, done):
        level, _, at = work[n]
        put_row(first, level, at, done)

    lon_pass(work, swept, coef_x, inter, west, flux, lane, keep_first)
    lat_pass(levels, nj, [(HALO, rows - HALO)], lambda level, r, lanes: first[level, r - REACH, :, lanes], coef_y, put)
    work_last = [(level, row, row - REACH) for level in range(levels) for row in range(HALO, rows - HALO)]

    lon_pass(work_last, swept, coef_x, inter, west, flux, lane, packer(packed, len(work_last), count, lane))
    hand_out(packed, outs, groups)


def edge_kernel(count, rows, groups, slot, state, first_round, second_round, first, cx, cy, *refs):
    outs, (packed, beyond, swept, edge, inter, west, flux) = refs[-7 - len(groups):-7], refs[-7:]
    nlon = state.shape[3]
    nj = nlon // LANES
    lane = lane_ids()
    odd = lax.axis_index("lat") % 2 == 1

    def halo(south, *at):
        one, two = first_round[at], second_round[at]
        return jnp.where(odd, one, two) if south else jnp.where(odd, two, one)

    for end, south in enumerate((True, False)):
        for j in range(nj):
            parts = coefficients(halo(south, HALO, slice(None), tile(j)))
            for p in range(3):
                beyond[p, end, :, tile(j)] = parts[p]

    def coef_x(i, _, r, lanes):
        if 0 <= r < rows:
            return cx[i, slot, r:r + 1, lanes]
        end, at = (0, r + REACH) if r < 0 else (1, r - rows)
        return beyond[i, end, at:at + 1, lanes]

    def coef_y(i, _, f, lanes):
        if 0 <= f < rows:
            return cy[i, slot, f:f + 1, lanes]
        end, at = (0, f + 2 * REACH + 1) if f < 0 else (1, f - rows + REACH)
        return beyond[i, end, at:at + 1, lanes]

    def cell(_, r, lanes):
        if 0 <= r < rows:
            return state[slot, r, :, lanes]
        return halo(r < 0, r + HALO if r < 0 else r - rows, slice(None), lanes)

    ends = [(-REACH, REACH), (rows - REACH, rows + REACH)]
    ends_last = [(0, HALO), (rows - HALO, rows)]

    def place(row, ranges):
        (a, b), (c, _) = ranges
        return row - a if row < b else row - c + BLOCK

    def cell_first(_, r, lanes):
        if REACH <= r < rows - REACH:
            return first[slot, r - REACH, :, lanes]
        return edge[0, place(r, ends), :, lanes]

    def put(_, row, lanes, value):
        swept[0, place(row, ends), :, lanes] = value

    def put_last(_, row, lanes, value):
        swept[0, place(row, ends_last), :, lanes] = value

    def listed(ranges):
        return [(0, row, place(row, ranges)) for a, b in ranges for row in range(a, b)]

    def keep_edge(n, done):
        put_row(edge, 0, n, done)

    lat_pass(1, nj, ends, cell, coef_y, put)
    lon_pass(listed(ends), swept, coef_x, inter, west, flux, lane, keep_edge)
    lat_pass(1, nj, ends_last, cell_first, coef_y, put_last)
    lon_pass(listed(ends_last), swept, coef_x, inter, west, flux, lane, packer(packed, 2 * HALO, count, lane))
    hand_out(packed, outs, groups)


def weights_kernel(weights, source, out):
    targets, rows, taps, width = weights.shape

    for row in range(rows):
        for k in range(targets):
            lowest, highest = max(k - (TAPS - 1), 0), min(k, targets - TAPS)
            w = weights[k, row]
            w = jnp.concatenate([w, jnp.zeros((SUB - taps, width), jnp.float32)], axis=0)
            at = jnp.broadcast_to(source[k, row:row + 1, :], (SUB, width))
            total = w
            for g in range(lowest + 1, highest + 1):
                total = jnp.where(at == g, pltpu.roll(w, g - lowest, 0), total)
            out[k, row] = total


def remap_kernel(count, plan, numbers, counts, *refs):
    chunks, weights, (out, levels, result, sems) = refs[:len(plan)], refs[len(plan)], refs[-4:]
    me = lax.axis_index("lev")
    targets, _, _, width = result.shape
    _, mains, tail, per = packed_sizes(width * count, count)
    lane = lane_ids()
    copies = []

    def leave(source, target):
        copy = pltpu.make_async_copy(source, target, sems.at[len(copies)])
        copy.start()
        copies.append(copy)

    def level_of(k, slot):
        d = me ^ k
        start = jnp.int32(0)
        for e in range(count):
            start = start + jnp.where(e < d, counts[e], 0)
        return jnp.where(slot < counts[d], start + slot, targets)

    for units, chunk in zip(plan, chunks):
        for unit, (k, slot, number) in enumerate(units):
            lead = (level_of(k, slot), numbers.index(number))
            unpack_unit(chunk, 0, unit, len(units), levels, lead, mains, tail, per, lane)

    for at, number in enumerate(numbers):
        for q in range(BLOCK):
            row = number * BLOCK + q
            for m in range(mains + (1 if tail else 0)):
                wide = LANES if m < mains else tail
                lanes = slice(m * LANES, m * LANES + wide)
                values = []
                for level in range(targets):
                    if m < mains:
                        values.append(levels[level, at, q * mains + m])
                    else:
                        last = levels[level, at, BLOCK * mains + q // per]
                        shift = (q % per) * tail
                        values.append(pltpu.roll(last, LANES - shift, 1) if shift else last)
                for k in range(targets):
                    lowest, highest = max(k - (TAPS - 1), 0), min(k, targets - TAPS) + TAPS - 1
                    total = None
                    for level in range(lowest, highest + 1):
                        j = level - lowest
                        term = jnp.broadcast_to(weights[k, row, j:j + 1, lanes], (SUB, wide)) * values[level][:, :wide]
                        total = term if total is None else total + term
                    result[k, at * BLOCK + q, :, lanes] = total
            leave(result.at[:, pl.ds(at * BLOCK + q, 1)], out.at[:, pl.ds(row, 1)])
    for copy in copies:
        copy.wait()


def mark_kernel(*refs):
    refs[-1][...] = jnp.zeros((SUB, LANES), jnp.float32)


def tiles_of(array):
    lead, levels, nlon = array.shape[:-2], array.shape[-2], array.shape[-1]
    split = array.reshape(lead + (levels, nlon // LANES, LANES))
    order = tuple(range(len(lead))) + (len(lead) + 1, len(lead), len(lead) + 2)
    split = with_layout_constraint(split, Layout(major_to_minor=order))
    return jnp.swapaxes(split, -3, -2).reshape(-1, LANES)


VMEM = pl.BlockSpec(memory_space=pltpu.VMEM)
ANY = pl.BlockSpec(memory_space=pl.ANY)
SMEM = pl.BlockSpec(memory_space=pltpu.SMEM)


def call(kernel, outs, args, specs=None, scratch=(), cost=None):
    return pl.pallas_call(
        kernel,
        out_shape=outs,
        in_specs=specs or [VMEM] * len(args),
        out_specs=jax.tree.map(lambda _: VMEM, outs),
        scratch_shapes=list(scratch),
        compiler_params=pltpu.CompilerParams(vmem_limit_bytes=16 << 20),
        cost_estimate=cost,
    )(*args)


def cost(flops, size):
    return pl.CostEstimate(flops=int(flops), bytes_accessed=int(size), transcendentals=0)


def f32(*shape):
    return jax.ShapeDtypeStruct(shape, jnp.float32)


def shards(tracers, wind_x, wind_y, level_counts, source_level, remap_weight):
    count = lax.axis_size("lev")
    bands = lax.axis_size("lat")
    number, depth, rows, nlon = tracers.shape
    targets, _, width = source_level.shape
    mains, tail, per = packed_sizes(nlon, count)[1:]
    blocks = rows // BLOCK
    inner = (rows - 2 * HALO) // BLOCK

    raw = tiles_of(jnp.transpose(tracers, (0, 2, 1, 3)))
    joined = jnp.concatenate([jnp.transpose(wind_x, (1, 0, 2)), jnp.transpose(wind_y, (1, 0, 2))], axis=0)
    halo = f32(HALO + 1, number, nlon)
    state, *sent = call(
        functools.partial(prep_kernel, rows),
        [f32(depth, rows, number, nlon), halo, halo], (raw, joined),
        cost=cost(1, 1))
    second = {i: ((i - 1) ^ 1) + 1 for i in range(1, bands - 1)}
    second_pairs = [(i * count + d, second[i] * count + d if i in second else i * count + (d ^ 1))
                    for i in range(bands) for d in range(count)]

    def beside(sent):
        return [lax.ppermute(sent[0], "lat", [(i, i ^ 1) for i in range(bands)]),
                lax.ppermute(sent[1], ("lat", "lev"), second_pairs)]

    rounds = [beside(sent)]
    taps = call(
        weights_kernel, f32(targets, rows, SUB, width),
        (jnp.transpose(remap_weight, (1, 2, 0, 3)), source_level),
        cost=cost(1, 1))

    def box(places, units):
        return places, packed_tiles(units, mains, tail, per), SUB, LANES

    def vmem(*shape):
        return pltpu.VMEM(shape, jnp.float32)

    held = -(-rows // SUB) * SUB
    coef = f32(3, depth, held, nlon)
    swept = vmem(depth, rows - 2 * REACH, number, nlon)
    stage = vmem(depth * (rows - 2 * REACH), number, nlon)
    chips = tuple(range(2, count, 2))
    groups = ((0,), (1,)) + tuple((k, k ^ 1) for k in chips)
    inner_units = depth * inner
    result = call(
        functools.partial(interior_kernel, count, rows, groups),
        [f32(*box(len(group), inner_units)) for group in groups]
        + [f32(depth, rows - 2 * REACH, number, nlon), coef, coef] + [halo] * (2 * depth - 2),
        (state, joined), scratch=[vmem(*box(count, inner_units)), vmem(2, depth, held, nlon), swept, stage, stage, stage],
        cost=cost(1, 1))
    middle, (first, cx, cy), sent = result[:len(groups)], result[len(groups):len(groups) + 3], result[len(groups) + 3:]
    rounds += [beside(sent[2 * i:2 * i + 2]) for i in range(depth - 1)]
    swept = vmem(1, 2 * HALO, number, nlon)
    stage = vmem(2 * HALO, number, nlon)

    def edge(slot, groups, after):
        args = (state, *rounds[slot], first, cx, cy, *after)
        return call(
            functools.partial(edge_kernel, count, rows, groups, slot),
            [f32(*box(len(group), 2)) for group in groups], args,
            specs=[VMEM] * (len(args) - len(after)) + [ANY] * len(after),
            scratch=[vmem(*box(count, 2)), vmem(3, 2, SUB, nlon), swept, swept, stage, stage, stage],
            cost=cost(60 * tracers.size, 8 * tracers.size))

    def swapped(sent, k):
        return lax.ppermute(sent, "lev", [(i, i ^ k) for i in range(count)])

    def units_of(k, places):
        return tuple((k, slot, block) for slot, block in places)

    def remap(listed, after):
        args = (level_counts, *(chunk for _, chunk in listed), taps, *after)
        return pl.pallas_call(
            functools.partial(remap_kernel, count, tuple(units for units, _ in listed), tuple(range(blocks))),
            out_shape=f32(targets, rows, number, width),
            in_specs=[SMEM] + [VMEM] * (len(args) - 1 - len(after)) + [ANY] * len(after),
            out_specs=ANY,
            scratch_shapes=[
                vmem(targets + 1, blocks, packed_tiles(1, mains, tail, per), SUB, LANES),
                vmem(targets, rows, number, width),
                pltpu.SemaphoreType.DMA((rows,)),
            ],
            compiler_params=pltpu.CompilerParams(vmem_limit_bytes=16 << 20),
            cost_estimate=cost(1, 1),
        )(*args)

    def mark(chunks):
        return pl.pallas_call(
            mark_kernel, out_shape=f32(SUB, LANES), in_specs=[ANY] * len(chunks), out_specs=VMEM, cost_estimate=cost(1, 1),
            compiler_params=pltpu.CompilerParams(vmem_limit_bytes=1 << 20),
        )(*chunks)

    places = tuple((slot, 1 + b) for slot in range(depth) for b in range(inner))
    arrived = [swapped(chunk, k) for k, chunk in zip(chips, middle[2:])]
    listed = [(units_of(k, places), chunk) for k, chunk in zip(chips, arrived)]
    listed.append((units_of(0, places), middle[0]))
    beside_me = [(units_of(1, places), middle[1])]
    after, marks = (taps,), []
    for slot in range(depth):
        own = ((slot, 0), (slot, blocks - 1))
        done = edge(slot, tuple((k,) for k in range(count)), after)
        crossing = [(units_of(k, own), swapped(done[k], k)) for k in range(count - 1, 1, -1)]
        listed += crossing + [(units_of(0, own), done[0])]
        beside_me.append((units_of(1, own), done[1]))
        marks.append(mark([chunk for _, chunk in crossing]))
        after = (done[0],)
    beside_me += [(units_of(k ^ 1, places), chunk) for k, chunk in zip(chips, arrived)]
    waiting = lax.optimization_barrier((*(chunk for _, chunk in beside_me), done[0]))
    listed += [(units, swapped(chunk[-1:], 1)) for (units, _), chunk in zip(beside_me, waiting)]
    out = remap(listed, marks)
    return jnp.transpose(out, (2, 0, 1, 3))


def solution(mesh):
    in_specs = (
        P(None, "lev", ("groups", "lat"), None),
        P("lev", ("groups", "lat"), None),
        P("lev", ("groups", "lat"), None),
        P(),
        P(None, ("groups", "lat"), "lev"),
        P(None, None, ("groups", "lat"), "lev"),
    )
    out_specs = P(None, None, ("groups", "lat"), "lev")
    return jax.shard_map(shards, mesh=mesh, in_specs=in_specs, out_specs=out_specs, check_vma=False)
```

```python
import functools

import jax
import jax.numpy as jnp
from jax import lax
from jax.experimental import pallas as pl
from jax.experimental.layout import Layout, with_layout_constraint
from jax.experimental.pallas import tpu as pltpu
from jax.sharding import PartitionSpec as P

SUBSTEPS = 2
TAPS = 4
REACH = 3
HALO = REACH * SUBSTEPS
BLOCK = 6
LANES = 128
SUB = 8


def spread(row):
    return jnp.broadcast_to(row, (SUB, LANES))


def lane_ids():
    return lax.broadcasted_iota(jnp.int32, (SUB, LANES), 1)


def from_west(tiles, steps, lane):
    turned = [pltpu.roll(t, steps, 1) for t in tiles]
    return [jnp.where(lane < steps, turned[j - 1], turned[j]) for j in range(len(tiles))]


def from_east(tiles, lane):
    turned = [pltpu.roll(t, LANES - 1, 1) for t in tiles]
    count = len(tiles)
    return [jnp.where(lane == LANES - 1, turned[(j + 1) % count], turned[j]) for j in range(count)]


def coefficients(wind):
    size = jnp.abs(wind)
    rest = 1.0 - size
    alpha = wind * rest * rest * (1.0 / 12.0)
    beta = wind * size * rest * (-1.0 / 12.0)
    gamma = wind * size * (3.0 - 2.0 * size)
    return alpha, beta, gamma


def packed_sizes(nlon, count):
    width = nlon // count
    mains, tail = width // LANES, width % LANES
    return width, mains, tail, LANES // tail if tail else 1


def packed_tiles(units, mains, tail, per):
    return units * BLOCK * mains + (-(-units * BLOCK // per) if tail else 0)


def fill_halos(rows, slot, state, winds, first_round, second_round):
    band, bands = lax.axis_index("lat"), lax.axis_size("lat")
    even = band % 2 == 0
    keep = jnp.where((band == 0) | (band == bands - 1), 0.0, 1.0)
    for target, north, scale in ((first_round, even, None), (second_round, jnp.logical_not(even), keep)):
        scaled = (lambda v: v) if scale is None else (lambda v: v * scale)
        row_t = jnp.where(north, rows - HALO, 0)
        row_x = jnp.where(north, rows - REACH, 0)
        row_y = jnp.where(north, rows - REACH - 1, 0)
        for row in range(HALO):
            target[row] = scaled(state[slot, row_t + row])
        for q in range(REACH):
            target[HALO, q:q + 1, :] = scaled(winds[row_x + q, slot:slot + 1, :])
        for q in range(REACH + 1):
            target[HALO, REACH + q:REACH + q + 1, :] = scaled(winds[rows + row_y + q, slot:slot + 1, :])


def prep_kernel(rows, tracers, winds, state, first_round, second_round):
    levels, nlon = state.shape[0], state.shape[3]
    nj = nlon // LANES
    row_stride = nj * levels
    tracer_stride = rows * row_stride

    def body(row, _):
        for level in range(levels):
            for j in range(nj):
                start = row * row_stride + j * levels + level
                state[level, row, :, tile(j)] = tracers[pl.ds(start, SUB, stride=tracer_stride), :]
        return 0

    lax.fori_loop(0, rows, body, 0)
    fill_halos(rows, 0, state, winds, first_round, second_round)


def lat_pass(levels, nj, ranges, cell, coef, store):
    group = 3 if nj % 3 == 0 else 1

    def body(i, _):
        level = i // (nj // group)
        results = []
        for u in range(group):
            lanes = pl.ds(pl.multiple_of(((i % (nj // group)) * group + u) * LANES, LANES), LANES)
            results += [(level, row, lanes, value) for row, value in one(level, lanes)]
        for result in results:
            store(*result)
        return 0

    def one(level, lanes):
        results = []
        for first, last in ranges:
            a = {r: cell(level, r, lanes) for r in range(first - REACH, last + REACH)}
            inter = {f: 7.0 * (a[f - 1] + a[f]) - (a[f - 2] + a[f + 1]) for f in range(first - 1, last + 2)}
            flux = {}
            for f in range(first, last + 1):
                alpha, beta, gamma = [spread(coef(i, level, f, lanes)) for i in range(3)]
                north = gamma > 0
                behind = jnp.where(north, inter[f - 1], inter[f + 1])
                upwind = jnp.where(north, a[f - 1], a[f])
                flux[f] = alpha * inter[f] + beta * behind + gamma * upwind
                if f > first:
                    results.append((f - 1, a[f - 1] - (flux[f] - flux[f - 1])))
        return results

    lax.fori_loop(0, levels * nj // group, body, 0)


def tile(j):
    return slice(j * LANES, (j + 1) * LANES)


def lon_pass(work, swept, coef, inter, west, flux, lane, finish):
    nj = swept.shape[3] // LANES
    each = range(nj)

    def interfaces(n):
        level, _, at = work[n]
        b = [swept[level, at, :, tile(j)] for j in each]
        w1, w2, e1 = from_west(b, 1, lane), from_west(b, 2, lane), from_east(b, lane)
        for j in each:
            inter[n, :, tile(j)] = 7.0 * (w1[j] + b[j]) - (w2[j] + e1[j])
            west[n, :, tile(j)] = w1[j]

    def fluxes(n):
        level, row, at = work[n]
        mid = [inter[n, :, tile(j)] for j in each]
        w1, e1 = from_west(mid, 1, lane), from_east(mid, lane)
        for j in each:
            alpha, beta, gamma = [spread(coef(i, level, row, tile(j))) for i in range(3)]
            right = gamma > 0
            behind = jnp.where(right, w1[j], e1[j])
            upwind = jnp.where(right, west[n, :, tile(j)], swept[level, at, :, tile(j)])
            flux[n, :, tile(j)] = alpha * mid[j] + beta * behind + gamma * upwind

    def update(n):
        level, _, at = work[n]
        here = [flux[n, :, tile(j)] for j in each]
        e1 = from_east(here, lane)
        return [swept[level, at, :, tile(j)] - (e1[j] - here[j]) for j in each]

    for n in range(len(work)):
        interfaces(n)
    for n in range(len(work)):
        fluxes(n)
    for g in range(len(work) // BLOCK):
        finish(g, [update(g * BLOCK + q) for q in range(BLOCK)])


def pack_block(block, packed, unit, units, count, lane):
    nlon = len(block[0]) * LANES
    width, mains, tail, per = packed_sizes(nlon, count)
    for d in range(count):
        j0, off = (d * width) // LANES, (d * width) % LANES
        for q, tiles in enumerate(block):
            turned = [pltpu.roll(tiles[j0 + m], LANES - off, 1) if off else tiles[j0 + m]
                      for m in range(mains + (1 if off else 0))]
            for m in range(mains):
                whole = jnp.where(lane < LANES - off, turned[m], turned[m + 1]) if off else turned[m]
                packed[d, (unit * BLOCK + q) * mains + m] = whole
        if tail:
            totals = {}
            for q, tiles in enumerate(block):
                at, place = divmod(unit * BLOCK + q, per)
                at += units * BLOCK * mains
                shift = (place * tail - off) % LANES
                moved = pltpu.roll(tiles[j0 + mains], shift, 1) if shift else tiles[j0 + mains]
                if place:
                    before = totals[at] if at in totals else packed[d, at]
                    moved = jnp.where(lane < place * tail, before, moved)
                totals[at] = moved
            for at, total in totals.items():
                packed[d, at] = total


def unpack_unit(chunk, place, unit, units, target, lead, mains, tail, per, lane):
    copy_tiles([((chunk, (place, unit * BLOCK * mains + i)), (target, lead + (i,))) for i in range(BLOCK * mains)])
    totals = {}
    for q in range(BLOCK if tail else 0):
        at, there = divmod(unit * BLOCK + q, per)
        to, here = divmod(q, per)
        shift = (here - there) * tail % LANES
        if to in totals and totals[to][1:] == (at, shift):
            continue
        source = chunk[place, units * BLOCK * mains + at]
        moved = pltpu.roll(source, shift, 1) if shift else source
        totals[to] = (jnp.where(lane < here * tail, totals[to][0], moved) if to in totals else moved, at, shift)
    for to, (total, _, _) in totals.items():
        target[lead + (BLOCK * mains + to,)] = total


def copy_tiles(pairs):
    values = [source[at] for (source, at), _ in pairs]
    for value, (_, (target, at)) in zip(values, pairs):
        target[at] = value


def hand_out(packed, outs, groups):
    me = lax.axis_index("lev")
    for group, out in zip(groups, outs):
        for place, k in enumerate(group):
            copy_tiles([((packed, (me ^ k, i)), (out, (place, i))) for i in range(packed.shape[1])])


def own_coefficients(rows, joined, winds, cx, cy):
    levels, held, nlon = cx.shape[1:]
    keep = jnp.where(lax.axis_index("lat") == 0, 0.0, 1.0)
    for level in range(levels):
        for way in range(2):
            for row in range(rows):
                winds[way, level, row:row + 1, :] = joined[way * rows + row, level:level + 1, :]
        winds[1, level, 0:1, :] = winds[1, level, 0:1, :] * keep
        for way, target in enumerate((cx, cy)):
            for j in range(nlon // LANES):
                parts = coefficients(winds[way, level, :, tile(j)])
                for p in range(3):
                    target[p, level, :, tile(j)] = parts[p]


def put_rows(target, level, at, rows):
    for q, row in enumerate(rows):
        for j, part in enumerate(row):
            target[level, at + q, :, tile(j)] = part


def interior_kernel(count, rows, groups, state, joined, *refs):
    outs, (first, cx, cy), refs = refs[:len(groups)], refs[len(groups):len(groups) + 3], refs[len(groups) + 3:]
    halos, (packed, winds, swept, inter, west, flux) = refs[:-6], refs[-6:]
    levels, nlon = state.shape[0], state.shape[3]
    nj = nlon // LANES
    lane = lane_ids()
    for slot in range(1, levels):
        fill_halos(rows, slot, state, joined, *halos[2 * slot - 2:2 * slot])
    own_coefficients(rows, joined, winds, cx, cy)
    coef_x = lambda i, level, r, lanes: cx[i, level, r:r + 1, lanes]
    coef_y = lambda i, level, f, lanes: cy[i, level, f:f + 1, lanes]

    def put(level, row, lanes, value):
        swept[level, row - REACH, :, lanes] = value

    lat_pass(levels, nj, [(REACH, rows - REACH)], lambda level, r, lanes: state[level, r, :, lanes], coef_y, put)
    work = [(level, row, row - REACH) for level in range(levels) for row in range(REACH, rows - REACH)]

    def keep_first(group, done):
        level, _, at = work[group * BLOCK]
        put_rows(first, level, at, done)

    lon_pass(work, swept, coef_x, inter, west, flux, lane, keep_first)
    lat_pass(levels, nj, [(HALO, rows - HALO)], lambda level, r, lanes: first[level, r - REACH, :, lanes], coef_y, put)
    work_last = [(level, row, row - REACH) for level in range(levels) for row in range(HALO, rows - HALO)]

    def send(group, done):
        pack_block(done, packed, group, len(work_last) // BLOCK, count, lane)

    lon_pass(work_last, swept, coef_x, inter, west, flux, lane, send)
    hand_out(packed, outs, groups)


def edge_kernel(count, rows, groups, slot, state, first_round, second_round, first, cx, cy, *refs):
    outs, (packed, beyond, swept, edge, inter, west, flux) = refs[-7 - len(groups):-7], refs[-7:]
    nlon = state.shape[3]
    nj = nlon // LANES
    lane = lane_ids()
    odd = lax.axis_index("lat") % 2 == 1

    def halo(south, *at):
        one, two = first_round[at], second_round[at]
        return jnp.where(odd, one, two) if south else jnp.where(odd, two, one)

    for end, south in enumerate((True, False)):
        for j in range(nj):
            parts = coefficients(halo(south, HALO, slice(None), tile(j)))
            for p in range(3):
                beyond[p, end, :, tile(j)] = parts[p]

    def coef_x(i, _, r, lanes):
        if 0 <= r < rows:
            return cx[i, slot, r:r + 1, lanes]
        end, at = (0, r + REACH) if r < 0 else (1, r - rows)
        return beyond[i, end, at:at + 1, lanes]

    def coef_y(i, _, f, lanes):
        if 0 <= f < rows:
            return cy[i, slot, f:f + 1, lanes]
        end, at = (0, f + 2 * REACH + 1) if f < 0 else (1, f - rows + REACH)
        return beyond[i, end, at:at + 1, lanes]

    def cell(_, r, lanes):
        if 0 <= r < rows:
            return state[slot, r, :, lanes]
        return halo(r < 0, r + HALO if r < 0 else r - rows, slice(None), lanes)

    ends = [(-REACH, REACH), (rows - REACH, rows + REACH)]
    ends_last = [(0, HALO), (rows - HALO, rows)]

    def place(row, ranges):
        (a, b), (c, _) = ranges
        return row - a if row < b else row - c + BLOCK

    def cell_first(_, r, lanes):
        if REACH <= r < rows - REACH:
            return first[slot, r - REACH, :, lanes]
        return edge[0, place(r, ends), :, lanes]

    def put(_, row, lanes, value):
        swept[0, place(row, ends), :, lanes] = value

    def put_last(_, row, lanes, value):
        swept[0, place(row, ends_last), :, lanes] = value

    def listed(ranges):
        return [(0, row, place(row, ranges)) for a, b in ranges for row in range(a, b)]

    def keep_edge(group, done):
        put_rows(edge, 0, group * BLOCK, done)

    def send(group, done):
        pack_block(done, packed, group, len(ends_last), count, lane)

    lat_pass(1, nj, ends, cell, coef_y, put)
    lon_pass(listed(ends), swept, coef_x, inter, west, flux, lane, keep_edge)
    lat_pass(1, nj, ends_last, cell_first, coef_y, put_last)
    lon_pass(listed(ends_last), swept, coef_x, inter, west, flux, lane, send)
    hand_out(packed, outs, groups)


def weights_kernel(weights, source, out):
    targets, rows, taps, width = weights.shape

    for row in range(rows):
        for k in range(targets):
            lowest, highest = max(k - (TAPS - 1), 0), min(k, targets - TAPS)
            w = weights[k, row]
            w = jnp.concatenate([w, jnp.zeros((SUB - taps, width), jnp.float32)], axis=0)
            at = jnp.broadcast_to(source[k, row:row + 1, :], (SUB, width))
            total = w
            for g in range(lowest + 1, highest + 1):
                total = jnp.where(at == g, pltpu.roll(w, g - lowest, 0), total)
            out[k, row] = total


def remap_kernel(count, plan, numbers, counts, *refs):
    chunks, weights, (out, levels, result, sems) = refs[:len(plan)], refs[len(plan)], refs[-4:]
    me = lax.axis_index("lev")
    targets, _, _, width = result.shape
    _, mains, tail, per = packed_sizes(width * count, count)
    lane = lane_ids()
    copies = []

    def leave(source, target):
        copy = pltpu.make_async_copy(source, target, sems.at[len(copies)])
        copy.start()
        copies.append(copy)

    def level_of(k, slot):
        d = me ^ k
        start = jnp.int32(0)
        for e in range(count):
            start = start + jnp.where(e < d, counts[e], 0)
        return jnp.where(slot < counts[d], start + slot, targets)

    for units, chunk in zip(plan, chunks):
        for unit, (k, slot, number) in enumerate(units):
            lead = (level_of(k, slot), numbers.index(number))
            unpack_unit(chunk, 0, unit, len(units), levels, lead, mains, tail, per, lane)

    for at, number in enumerate(numbers):
        for q in range(BLOCK):
            row = number * BLOCK + q
            for m in range(mains + (1 if tail else 0)):
                wide = LANES if m < mains else tail
                lanes = slice(m * LANES, m * LANES + wide)
                values = []
                for level in range(targets):
                    if m < mains:
                        values.append(levels[level, at, q * mains + m])
                    else:
                        last = levels[level, at, BLOCK * mains + q // per]
                        shift = (q % per) * tail
                        values.append(pltpu.roll(last, LANES - shift, 1) if shift else last)
                for k in range(targets):
                    lowest, highest = max(k - (TAPS - 1), 0), min(k, targets - TAPS) + TAPS - 1
                    total = None
                    for level in range(lowest, highest + 1):
                        j = level - lowest
                        term = jnp.broadcast_to(weights[k, row, j:j + 1, lanes], (SUB, wide)) * values[level][:, :wide]
                        total = term if total is None else total + term
                    result[k, at * BLOCK + q, :, lanes] = total
            leave(result.at[:, pl.ds(at * BLOCK + q, 1)], out.at[:, pl.ds(row, 1)])
    for copy in copies:
        copy.wait()


def mark_kernel(*refs):
    refs[-1][...] = jnp.zeros((SUB, LANES), jnp.float32)


def tiles_of(array):
    lead, levels, nlon = array.shape[:-2], array.shape[-2], array.shape[-1]
    split = array.reshape(lead + (levels, nlon // LANES, LANES))
    order = tuple(range(len(lead))) + (len(lead) + 1, len(lead), len(lead) + 2)
    split = with_layout_constraint(split, Layout(major_to_minor=order))
    return jnp.swapaxes(split, -3, -2).reshape(-1, LANES)


VMEM = pl.BlockSpec(memory_space=pltpu.VMEM)
ANY = pl.BlockSpec(memory_space=pl.ANY)
SMEM = pl.BlockSpec(memory_space=pltpu.SMEM)


def call(kernel, outs, args, specs=None, scratch=(), cost=None):
    return pl.pallas_call(
        kernel,
        out_shape=outs,
        in_specs=specs or [VMEM] * len(args),
        out_specs=jax.tree.map(lambda _: VMEM, outs),
        scratch_shapes=list(scratch),
        compiler_params=pltpu.CompilerParams(vmem_limit_bytes=16 << 20),
        cost_estimate=cost,
    )(*args)


def cost(flops, size):
    return pl.CostEstimate(flops=int(flops), bytes_accessed=int(size), transcendentals=0)


def f32(*shape):
    return jax.ShapeDtypeStruct(shape, jnp.float32)


def shards(tracers, wind_x, wind_y, level_counts, source_level, remap_weight):
    count = lax.axis_size("lev")
    bands = lax.axis_size("lat")
    number, depth, rows, nlon = tracers.shape
    targets, _, width = source_level.shape
    mains, tail, per = packed_sizes(nlon, count)[1:]
    blocks = rows // BLOCK
    inner = (rows - 2 * HALO) // BLOCK

    raw = tiles_of(jnp.transpose(tracers, (0, 2, 1, 3)))
    joined = jnp.concatenate([jnp.transpose(wind_x, (1, 0, 2)), jnp.transpose(wind_y, (1, 0, 2))], axis=0)
    halo = f32(HALO + 1, number, nlon)
    state, *sent = call(
        functools.partial(prep_kernel, rows),
        [f32(depth, rows, number, nlon), halo, halo], (raw, joined),
        cost=cost(1, 1))
    second = {i: ((i - 1) ^ 1) + 1 for i in range(1, bands - 1)}
    second_pairs = [(i * count + d, second[i] * count + d if i in second else i * count + (d ^ 1))
                    for i in range(bands) for d in range(count)]

    def beside(sent):
        return [lax.ppermute(sent[0], "lat", [(i, i ^ 1) for i in range(bands)]),
                lax.ppermute(sent[1], ("lat", "lev"), second_pairs)]

    rounds = [beside(sent)]
    taps = call(
        weights_kernel, f32(targets, rows, SUB, width),
        (jnp.transpose(remap_weight, (1, 2, 0, 3)), source_level),
        cost=cost(1, 1))

    def box(places, units):
        return places, packed_tiles(units, mains, tail, per), SUB, LANES

    def vmem(*shape):
        return pltpu.VMEM(shape, jnp.float32)

    held = -(-rows // SUB) * SUB
    coef = f32(3, depth, held, nlon)
    swept = vmem(depth, rows - 2 * REACH, number, nlon)
    stage = vmem(depth * (rows - 2 * REACH), number, nlon)
    chips = tuple(range(2, count, 2))
    groups = ((0,), (1,)) + tuple((k, k ^ 1) for k in chips)
    inner_units = depth * inner
    result = call(
        functools.partial(interior_kernel, count, rows, groups),
        [f32(*box(len(group), inner_units)) for group in groups]
        + [f32(depth, rows - 2 * REACH, number, nlon), coef, coef] + [halo] * (2 * depth - 2),
        (state, joined), scratch=[vmem(*box(count, inner_units)), vmem(2, depth, held, nlon), swept, stage, stage, stage],
        cost=cost(1, 1))
    middle, (first, cx, cy), sent = result[:len(groups)], result[len(groups):len(groups) + 3], result[len(groups) + 3:]
    rounds += [beside(sent[2 * i:2 * i + 2]) for i in range(depth - 1)]
    swept = vmem(1, 2 * HALO, number, nlon)
    stage = vmem(2 * HALO, number, nlon)

    def edge(slot, groups, after):
        args = (state, *rounds[slot], first, cx, cy, *after)
        return call(
            functools.partial(edge_kernel, count, rows, groups, slot),
            [f32(*box(len(group), 2)) for group in groups], args,
            specs=[VMEM] * (len(args) - len(after)) + [ANY] * len(after),
            scratch=[vmem(*box(count, 2)), vmem(3, 2, SUB, nlon), swept, swept, stage, stage, stage],
            cost=cost(60 * tracers.size, 8 * tracers.size))

    def swapped(sent, k):
        return lax.ppermute(sent, "lev", [(i, i ^ k) for i in range(count)])

    def units_of(k, places):
        return tuple((k, slot, block) for slot, block in places)

    def remap(listed, after):
        args = (level_counts, *(chunk for _, chunk in listed), taps, *after)
        return pl.pallas_call(
            functools.partial(remap_kernel, count, tuple(units for units, _ in listed), tuple(range(blocks))),
            out_shape=f32(targets, rows, number, width),
            in_specs=[SMEM] + [VMEM] * (len(args) - 1 - len(after)) + [ANY] * len(after),
            out_specs=ANY,
            scratch_shapes=[
                vmem(targets + 1, blocks, packed_tiles(1, mains, tail, per), SUB, LANES),
                vmem(targets, rows, number, width),
                pltpu.SemaphoreType.DMA((rows,)),
            ],
            compiler_params=pltpu.CompilerParams(vmem_limit_bytes=16 << 20),
            cost_estimate=cost(1, 1),
        )(*args)

    def mark(chunks):
        return pl.pallas_call(
            mark_kernel, out_shape=f32(SUB, LANES), in_specs=[ANY] * len(chunks), out_specs=VMEM, cost_estimate=cost(1, 1),
            compiler_params=pltpu.CompilerParams(vmem_limit_bytes=1 << 20),
        )(*chunks)

    places = tuple((slot, 1 + b) for slot in range(depth) for b in range(inner))
    arrived = [swapped(chunk, k) for k, chunk in zip(chips, middle[2:])]
    listed = [(units_of(k, places), chunk) for k, chunk in zip(chips, arrived)]
    listed.append((units_of(0, places), middle[0]))
    beside_me = [(units_of(1, places), middle[1])]
    after, marks = (taps,), []
    for slot in range(depth):
        own = ((slot, 0), (slot, blocks - 1))
        done = edge(slot, tuple((k,) for k in range(count)), after)
        crossing = [(units_of(k, own), swapped(done[k], k)) for k in range(count - 1, 1, -1)]
        listed += crossing + [(units_of(0, own), done[0])]
        beside_me.append((units_of(1, own), done[1]))
        marks.append(mark([chunk for _, chunk in crossing]))
        after = (done[0],)
    beside_me += [(units_of(k ^ 1, places), chunk) for k, chunk in zip(chips, arrived)]
    waiting = lax.optimization_barrier((*(chunk for _, chunk in beside_me), done[0]))
    listed += [(units, swapped(chunk[-1:], 1)) for (units, _), chunk in zip(beside_me, waiting)]
    out = remap(listed, marks)
    return jnp.transpose(out, (2, 0, 1, 3))


def solution(mesh):
    in_specs = (
        P(None, "lev", ("groups", "lat"), None),
        P("lev", ("groups", "lat"), None),
        P("lev", ("groups", "lat"), None),
        P(),
        P(None, ("groups", "lat"), "lev"),
        P(None, None, ("groups", "lat"), "lev"),
    )
    out_specs = P(None, None, ("groups", "lat"), "lev")
    return jax.shard_map(shards, mesh=mesh, in_specs=in_specs, out_specs=out_specs, check_vma=False)
```

```python
import functools

import jax
import jax.numpy as jnp
from jax import lax
from jax.experimental import pallas as pl
from jax.experimental.layout import Layout, with_layout_constraint
from jax.experimental.pallas import tpu as pltpu
from jax.sharding import PartitionSpec as P

SUBSTEPS = 2
TAPS = 4
REACH = 3
HALO = REACH * SUBSTEPS
BLOCK = 6
LANES = 128
SUB = 8


def spread(row):
    return jnp.broadcast_to(row, (SUB, LANES))


def lane_ids():
    return lax.broadcasted_iota(jnp.int32, (SUB, LANES), 1)


def from_west(tiles, steps, lane):
    turned = [pltpu.roll(t, steps, 1) for t in tiles]
    return [jnp.where(lane < steps, turned[j - 1], turned[j]) for j in range(len(tiles))]


def from_east(tiles, lane):
    turned = [pltpu.roll(t, LANES - 1, 1) for t in tiles]
    count = len(tiles)
    return [jnp.where(lane == LANES - 1, turned[(j + 1) % count], turned[j]) for j in range(count)]


def coefficients(wind):
    size = jnp.abs(wind)
    rest = 1.0 - size
    alpha = wind * rest * rest * (1.0 / 12.0)
    beta = wind * size * rest * (-1.0 / 12.0)
    gamma = wind * size * (3.0 - 2.0 * size)
    return alpha, beta, gamma


def packed_sizes(nlon, count):
    width = nlon // count
    mains, tail = width // LANES, width % LANES
    return width, mains, tail, LANES // tail if tail else 1


def packed_tiles(units, mains, tail, per):
    return units * BLOCK * mains + (-(-units * BLOCK // per) if tail else 0)


def fill_halos(rows, slot, state, winds, first_round, second_round):
    band, bands = lax.axis_index("lat"), lax.axis_size("lat")
    even = band % 2 == 0
    keep = jnp.where((band == 0) | (band == bands - 1), 0.0, 1.0)
    for target, north, scale in ((first_round, even, None), (second_round, jnp.logical_not(even), keep)):
        scaled = (lambda v: v) if scale is None else (lambda v: v * scale)
        row_t = jnp.where(north, rows - HALO, 0)
        row_x = jnp.where(north, rows - REACH, 0)
        row_y = jnp.where(north, rows - REACH - 1, 0)
        for row in range(HALO):
            target[row] = scaled(state[slot, row_t + row])
        for q in range(REACH):
            target[HALO, q:q + 1, :] = scaled(winds[row_x + q, slot:slot + 1, :])
        for q in range(REACH + 1):
            target[HALO, REACH + q:REACH + q + 1, :] = scaled(winds[rows + row_y + q, slot:slot + 1, :])


def prep_kernel(rows, tracers, winds, state, first_round, second_round):
    levels, nlon = state.shape[0], state.shape[3]
    nj = nlon // LANES
    row_stride = nj * levels
    tracer_stride = rows * row_stride

    def body(row, _):
        for level in range(levels):
            for j in range(nj):
                start = row * row_stride + j * levels + level
                state[level, row, :, tile(j)] = tracers[pl.ds(start, SUB, stride=tracer_stride), :]
        return 0

    lax.fori_loop(0, rows, body, 0)
    fill_halos(rows, 0, state, winds, first_round, second_round)


def lat_pass(levels, nj, ranges, cell, coef, store):
    group = 3 if nj % 3 == 0 else 1

    def body(level, _):
        for start in range(0, nj, group):
            results = []
            for j in range(start, start + group):
                results += [(level, row, tile(j), value) for row, value in one(level, tile(j))]
            for result in results:
                store(*result)
        return 0

    def one(level, lanes):
        results = []
        for first, last in ranges:
            a = {r: cell(level, r, lanes) for r in range(first - REACH, last + REACH)}
            inter = {f: 7.0 * (a[f - 1] + a[f]) - (a[f - 2] + a[f + 1]) for f in range(first - 1, last + 2)}
            flux = {}
            for f in range(first, last + 1):
                alpha, beta, gamma = [spread(coef(i, level, f, lanes)) for i in range(3)]
                north = gamma > 0
                behind = jnp.where(north, inter[f - 1], inter[f + 1])
                upwind = jnp.where(north, a[f - 1], a[f])
                flux[f] = alpha * inter[f] + beta * behind + gamma * upwind
                if f > first:
                    results.append((f - 1, a[f - 1] - (flux[f] - flux[f - 1])))
        return results

    lax.fori_loop(0, levels, body, 0)


def tile(j):
    return slice(j * LANES, (j + 1) * LANES)


def lon_pass(work, swept, coef, inter, west, flux, lane, finish):
    nj = swept.shape[3] // LANES
    each = range(nj)

    def interfaces(n):
        level, _, at = work[n]
        b = [swept[level, at, :, tile(j)] for j in each]
        w1, w2, e1 = from_west(b, 1, lane), from_west(b, 2, lane), from_east(b, lane)
        for j in each:
            inter[n, :, tile(j)] = 7.0 * (w1[j] + b[j]) - (w2[j] + e1[j])
            west[n, :, tile(j)] = w1[j]

    def fluxes(n):
        level, row, at = work[n]
        mid = [inter[n, :, tile(j)] for j in each]
        w1, e1 = from_west(mid, 1, lane), from_east(mid, lane)
        for j in each:
            alpha, beta, gamma = [spread(coef(i, level, row, tile(j))) for i in range(3)]
            right = gamma > 0
            behind = jnp.where(right, w1[j], e1[j])
            upwind = jnp.where(right, west[n, :, tile(j)], swept[level, at, :, tile(j)])
            flux[n, :, tile(j)] = alpha * mid[j] + beta * behind + gamma * upwind

    def update(n):
        level, _, at = work[n]
        here = [flux[n, :, tile(j)] for j in each]
        e1 = from_east(here, lane)
        return [swept[level, at, :, tile(j)] - (e1[j] - here[j]) for j in each]

    for n in range(len(work)):
        interfaces(n)
    for n in range(len(work)):
        fluxes(n)
    for g in range(len(work) // BLOCK):
        finish(g, [update(g * BLOCK + q) for q in range(BLOCK)])


def pack_block(block, packed, unit, units, count, lane):
    nlon = len(block[0]) * LANES
    width, mains, tail, per = packed_sizes(nlon, count)
    for d in range(count):
        j0, off = (d * width) // LANES, (d * width) % LANES
        for q, tiles in enumerate(block):
            turned = [pltpu.roll(tiles[j0 + m], LANES - off, 1) if off else tiles[j0 + m]
                      for m in range(mains + (1 if off else 0))]
            for m in range(mains):
                whole = jnp.where(lane < LANES - off, turned[m], turned[m + 1]) if off else turned[m]
                packed[d, (unit * BLOCK + q) * mains + m] = whole
        if tail:
            totals = {}
            for q, tiles in enumerate(block):
                at, place = divmod(unit * BLOCK + q, per)
                at += units * BLOCK * mains
                shift = (place * tail - off) % LANES
                moved = pltpu.roll(tiles[j0 + mains], shift, 1) if shift else tiles[j0 + mains]
                if place:
                    before = totals[at] if at in totals else packed[d, at]
                    moved = jnp.where(lane < place * tail, before, moved)
                totals[at] = moved
            for at, total in totals.items():
                packed[d, at] = total


def unpack_unit(chunk, place, unit, units, target, lead, mains, tail, per, lane):
    copy_tiles([((chunk, (place, unit * BLOCK * mains + i)), (target, lead + (i,))) for i in range(BLOCK * mains)])
    totals = {}
    for q in range(BLOCK if tail else 0):
        at, there = divmod(unit * BLOCK + q, per)
        to, here = divmod(q, per)
        shift = (here - there) * tail % LANES
        if to in totals and totals[to][1:] == (at, shift):
            continue
        source = chunk[place, units * BLOCK * mains + at]
        moved = pltpu.roll(source, shift, 1) if shift else source
        totals[to] = (jnp.where(lane < here * tail, totals[to][0], moved) if to in totals else moved, at, shift)
    for to, (total, _, _) in totals.items():
        target[lead + (BLOCK * mains + to,)] = total


def copy_tiles(pairs):
    values = [source[at] for (source, at), _ in pairs]
    for value, (_, (target, at)) in zip(values, pairs):
        target[at] = value


def hand_out(packed, outs, groups):
    me = lax.axis_index("lev")
    for group, out in zip(groups, outs):
        for place, k in enumerate(group):
            copy_tiles([((packed, (me ^ k, i)), (out, (place, i))) for i in range(packed.shape[1])])


def own_coefficients(rows, joined, winds, cx, cy):
    levels, held, nlon = cx.shape[1:]
    keep = jnp.where(lax.axis_index("lat") == 0, 0.0, 1.0)
    for level in range(levels):
        for way in range(2):
            for row in range(rows):
                winds[way, level, row:row + 1, :] = joined[way * rows + row, level:level + 1, :]
        winds[1, level, 0:1, :] = winds[1, level, 0:1, :] * keep
        for way, target in enumerate((cx, cy)):
            for j in range(nlon // LANES):
                parts = coefficients(winds[way, level, :, tile(j)])
                for p in range(3):
                    target[p, level, :, tile(j)] = parts[p]


def put_rows(target, level, at, rows):
    for q, row in enumerate(rows):
        for j, part in enumerate(row):
            target[level, at + q, :, tile(j)] = part


def interior_kernel(count, rows, groups, state, joined, *refs):
    outs, (first, cx, cy), refs = refs[:len(groups)], refs[len(groups):len(groups) + 3], refs[len(groups) + 3:]
    halos, (packed, winds, swept, inter, west, flux) = refs[:-6], refs[-6:]
    levels, nlon = state.shape[0], state.shape[3]
    nj = nlon // LANES
    lane = lane_ids()
    for slot in range(1, levels):
        fill_halos(rows, slot, state, joined, *halos[2 * slot - 2:2 * slot])
    own_coefficients(rows, joined, winds, cx, cy)
    coef_x = lambda i, level, r, lanes: cx[i, level, r:r + 1, lanes]
    coef_y = lambda i, level, f, lanes: cy[i, level, f:f + 1, lanes]

    def put(level, row, lanes, value):
        swept[level, row - REACH, :, lanes] = value

    lat_pass(levels, nj, [(REACH, rows - REACH)], lambda level, r, lanes: state[level, r, :, lanes], coef_y, put)
    work = [(level, row, row - REACH) for level in range(levels) for row in range(REACH, rows - REACH)]

    def keep_first(group, done):
        level, _, at = work[group * BLOCK]
        put_rows(first, level, at, done)

    lon_pass(work, swept, coef_x, inter, west, flux, lane, keep_first)
    lat_pass(levels, nj, [(HALO, rows - HALO)], lambda level, r, lanes: first[level, r - REACH, :, lanes], coef_y, put)
    work_last = [(level, row, row - REACH) for level in range(levels) for row in range(HALO, rows - HALO)]

    def send(group, done):
        pack_block(done, packed, group, len(work_last) // BLOCK, count, lane)

    lon_pass(work_last, swept, coef_x, inter, west, flux, lane, send)
    hand_out(packed, outs, groups)


def edge_kernel(count, rows, groups, slot, state, first_round, second_round, first, cx, cy, *refs):
    outs, (packed, beyond, swept, edge, inter, west, flux) = refs[-7 - len(groups):-7], refs[-7:]
    nlon = state.shape[3]
    nj = nlon // LANES
    lane = lane_ids()
    odd = lax.axis_index("lat") % 2 == 1

    def halo(south, *at):
        one, two = first_round[at], second_round[at]
        return jnp.where(odd, one, two) if south else jnp.where(odd, two, one)

    for end, south in enumerate((True, False)):
        for j in range(nj):
            parts = coefficients(halo(south, HALO, slice(None), tile(j)))
            for p in range(3):
                beyond[p, end, :, tile(j)] = parts[p]

    def coef_x(i, _, r, lanes):
        if 0 <= r < rows:
            return cx[i, slot, r:r + 1, lanes]
        end, at = (0, r + REACH) if r < 0 else (1, r - rows)
        return beyond[i, end, at:at + 1, lanes]

    def coef_y(i, _, f, lanes):
        if 0 <= f < rows:
            return cy[i, slot, f:f + 1, lanes]
        end, at = (0, f + 2 * REACH + 1) if f < 0 else (1, f - rows + REACH)
        return beyond[i, end, at:at + 1, lanes]

    def cell(_, r, lanes):
        if 0 <= r < rows:
            return state[slot, r, :, lanes]
        return halo(r < 0, r + HALO if r < 0 else r - rows, slice(None), lanes)

    ends = [(-REACH, REACH), (rows - REACH, rows + REACH)]
    ends_last = [(0, HALO), (rows - HALO, rows)]

    def place(row, ranges):
        (a, b), (c, _) = ranges
        return row - a if row < b else row - c + BLOCK

    def cell_first(_, r, lanes):
        if REACH <= r < rows - REACH:
            return first[slot, r - REACH, :, lanes]
        return edge[0, place(r, ends), :, lanes]

    def put(_, row, lanes, value):
        swept[0, place(row, ends), :, lanes] = value

    def put_last(_, row, lanes, value):
        swept[0, place(row, ends_last), :, lanes] = value

    def listed(ranges):
        return [(0, row, place(row, ranges)) for a, b in ranges for row in range(a, b)]

    def keep_edge(group, done):
        put_rows(edge, 0, group * BLOCK, done)

    def send(group, done):
        pack_block(done, packed, group, len(ends_last), count, lane)

    lat_pass(1, nj, ends, cell, coef_y, put)
    lon_pass(listed(ends), swept, coef_x, inter, west, flux, lane, keep_edge)
    lat_pass(1, nj, ends_last, cell_first, coef_y, put_last)
    lon_pass(listed(ends_last), swept, coef_x, inter, west, flux, lane, send)
    hand_out(packed, outs, groups)


def weights_kernel(weights, source, out):
    targets, rows, taps, width = weights.shape

    for row in range(rows):
        for k in range(targets):
            lowest, highest = max(k - (TAPS - 1), 0), min(k, targets - TAPS)
            w = weights[k, row]
            w = jnp.concatenate([w, jnp.zeros((SUB - taps, width), jnp.float32)], axis=0)
            at = jnp.broadcast_to(source[k, row:row + 1, :], (SUB, width))
            total = w
            for g in range(lowest + 1, highest + 1):
                total = jnp.where(at == g, pltpu.roll(w, g - lowest, 0), total)
            out[k, row] = total


def remap_kernel(count, plan, numbers, counts, *refs):
    chunks, weights, (out, levels, result, sems) = refs[:len(plan)], refs[len(plan)], refs[-4:]
    me = lax.axis_index("lev")
    targets, _, _, width = result.shape
    _, mains, tail, per = packed_sizes(width * count, count)
    lane = lane_ids()
    copies = []

    def leave(source, target):
        copy = pltpu.make_async_copy(source, target, sems.at[len(copies)])
        copy.start()
        copies.append(copy)

    def level_of(k, slot):
        d = me ^ k
        start = jnp.int32(0)
        for e in range(count):
            start = start + jnp.where(e < d, counts[e], 0)
        return jnp.where(slot < counts[d], start + slot, targets)

    for units, chunk in zip(plan, chunks):
        for unit, (k, slot, number) in enumerate(units):
            lead = (level_of(k, slot), numbers.index(number))
            unpack_unit(chunk, 0, unit, len(units), levels, lead, mains, tail, per, lane)

    for at, number in enumerate(numbers):
        for q in range(BLOCK):
            row = number * BLOCK + q
            for m in range(mains + (1 if tail else 0)):
                wide = LANES if m < mains else tail
                lanes = slice(m * LANES, m * LANES + wide)
                values = []
                for level in range(targets):
                    if m < mains:
                        values.append(levels[level, at, q * mains + m])
                    else:
                        last = levels[level, at, BLOCK * mains + q // per]
                        shift = (q % per) * tail
                        values.append(pltpu.roll(last, LANES - shift, 1) if shift else last)
                for k in range(targets):
                    lowest, highest = max(k - (TAPS - 1), 0), min(k, targets - TAPS) + TAPS - 1
                    total = None
                    for level in range(lowest, highest + 1):
                        j = level - lowest
                        term = jnp.broadcast_to(weights[k, row, j:j + 1, lanes], (SUB, wide)) * values[level][:, :wide]
                        total = term if total is None else total + term
                    result[k, at * BLOCK + q, :, lanes] = total
            leave(result.at[:, pl.ds(at * BLOCK + q, 1)], out.at[:, pl.ds(row, 1)])
    for copy in copies:
        copy.wait()


def mark_kernel(*refs):
    refs[-1][...] = jnp.zeros((SUB, LANES), jnp.float32)


def tiles_of(array):
    lead, levels, nlon = array.shape[:-2], array.shape[-2], array.shape[-1]
    split = array.reshape(lead + (levels, nlon // LANES, LANES))
    order = tuple(range(len(lead))) + (len(lead) + 1, len(lead), len(lead) + 2)
    split = with_layout_constraint(split, Layout(major_to_minor=order))
    return jnp.swapaxes(split, -3, -2).reshape(-1, LANES)


VMEM = pl.BlockSpec(memory_space=pltpu.VMEM)
ANY = pl.BlockSpec(memory_space=pl.ANY)
SMEM = pl.BlockSpec(memory_space=pltpu.SMEM)


def call(kernel, outs, args, specs=None, scratch=(), cost=None):
    return pl.pallas_call(
        kernel,
        out_shape=outs,
        in_specs=specs or [VMEM] * len(args),
        out_specs=jax.tree.map(lambda _: VMEM, outs),
        scratch_shapes=list(scratch),
        compiler_params=pltpu.CompilerParams(vmem_limit_bytes=16 << 20),
        cost_estimate=cost,
    )(*args)


def cost(flops, size):
    return pl.CostEstimate(flops=int(flops), bytes_accessed=int(size), transcendentals=0)


def f32(*shape):
    return jax.ShapeDtypeStruct(shape, jnp.float32)


def shards(tracers, wind_x, wind_y, level_counts, source_level, remap_weight):
    count = lax.axis_size("lev")
    bands = lax.axis_size("lat")
    number, depth, rows, nlon = tracers.shape
    targets, _, width = source_level.shape
    mains, tail, per = packed_sizes(nlon, count)[1:]
    blocks = rows // BLOCK
    inner = (rows - 2 * HALO) // BLOCK

    raw = tiles_of(jnp.transpose(tracers, (0, 2, 1, 3)))
    joined = jnp.concatenate([jnp.transpose(wind_x, (1, 0, 2)), jnp.transpose(wind_y, (1, 0, 2))], axis=0)
    halo = f32(HALO + 1, number, nlon)
    state, *sent = call(
        functools.partial(prep_kernel, rows),
        [f32(depth, rows, number, nlon), halo, halo], (raw, joined),
        cost=cost(1, 1))
    second = {i: ((i - 1) ^ 1) + 1 for i in range(1, bands - 1)}
    second_pairs = [(i * count + d, second[i] * count + d if i in second else i * count + (d ^ 1))
                    for i in range(bands) for d in range(count)]

    def beside(sent):
        return [lax.ppermute(sent[0], "lat", [(i, i ^ 1) for i in range(bands)]),
                lax.ppermute(sent[1], ("lat", "lev"), second_pairs)]

    rounds = [beside(sent)]
    taps = call(
        weights_kernel, f32(targets, rows, SUB, width),
        (jnp.transpose(remap_weight, (1, 2, 0, 3)), source_level),
        cost=cost(1, 1))

    def box(places, units):
        return places, packed_tiles(units, mains, tail, per), SUB, LANES

    def vmem(*shape):
        return pltpu.VMEM(shape, jnp.float32)

    held = -(-rows // SUB) * SUB
    coef = f32(3, depth, held, nlon)
    swept = vmem(depth, rows - 2 * REACH, number, nlon)
    stage = vmem(depth * (rows - 2 * REACH), number, nlon)
    chips = tuple(range(2, count, 2))
    groups = ((0,), (1,)) + tuple((k, k ^ 1) for k in chips)
    inner_units = depth * inner
    result = call(
        functools.partial(interior_kernel, count, rows, groups),
        [f32(*box(len(group), inner_units)) for group in groups]
        + [f32(depth, rows - 2 * REACH, number, nlon), coef, coef] + [halo] * (2 * depth - 2),
        (state, joined), scratch=[vmem(*box(count, inner_units)), vmem(2, depth, held, nlon), swept, stage, stage, stage],
        cost=cost(1, 1))
    middle, (first, cx, cy), sent = result[:len(groups)], result[len(groups):len(groups) + 3], result[len(groups) + 3:]
    rounds += [beside(sent[2 * i:2 * i + 2]) for i in range(depth - 1)]
    swept = vmem(1, 2 * HALO, number, nlon)
    stage = vmem(2 * HALO, number, nlon)

    def edge(slot, groups, after):
        args = (state, *rounds[slot], first, cx, cy, *after)
        return call(
            functools.partial(edge_kernel, count, rows, groups, slot),
            [f32(*box(len(group), 2)) for group in groups], args,
            specs=[VMEM] * (len(args) - len(after)) + [ANY] * len(after),
            scratch=[vmem(*box(count, 2)), vmem(3, 2, SUB, nlon), swept, swept, stage, stage, stage],
            cost=cost(60 * tracers.size, 8 * tracers.size))

    def swapped(sent, k):
        return lax.ppermute(sent, "lev", [(i, i ^ k) for i in range(count)])

    def units_of(k, places):
        return tuple((k, slot, block) for slot, block in places)

    def remap(listed, after):
        args = (level_counts, *(chunk for _, chunk in listed), taps, *after)
        return pl.pallas_call(
            functools.partial(remap_kernel, count, tuple(units for units, _ in listed), tuple(range(blocks))),
            out_shape=f32(targets, rows, number, width),
            in_specs=[SMEM] + [VMEM] * (len(args) - 1 - len(after)) + [ANY] * len(after),
            out_specs=ANY,
            scratch_shapes=[
                vmem(targets + 1, blocks, packed_tiles(1, mains, tail, per), SUB, LANES),
                vmem(targets, rows, number, width),
                pltpu.SemaphoreType.DMA((rows,)),
            ],
            compiler_params=pltpu.CompilerParams(vmem_limit_bytes=16 << 20),
            cost_estimate=cost(1, 1),
        )(*args)

    def mark(chunks):
        return pl.pallas_call(
            mark_kernel, out_shape=f32(SUB, LANES), in_specs=[ANY] * len(chunks), out_specs=VMEM, cost_estimate=cost(1, 1),
            compiler_params=pltpu.CompilerParams(vmem_limit_bytes=1 << 20),
        )(*chunks)

    places = tuple((slot, 1 + b) for slot in range(depth) for b in range(inner))
    arrived = [swapped(chunk, k) for k, chunk in zip(chips, middle[2:])]
    listed = [(units_of(k, places), chunk) for k, chunk in zip(chips, arrived)]
    listed.append((units_of(0, places), middle[0]))
    beside_me = [(units_of(1, places), middle[1])]
    after, marks = (taps,), []
    for slot in range(depth):
        own = ((slot, 0), (slot, blocks - 1))
        done = edge(slot, tuple((k,) for k in range(count)), after)
        crossing = [(units_of(k, own), swapped(done[k], k)) for k in range(count - 1, 1, -1)]
        listed += crossing + [(units_of(0, own), done[0])]
        beside_me.append((units_of(1, own), done[1]))
        marks.append(mark([chunk for _, chunk in crossing]))
        after = (done[0],)
    beside_me += [(units_of(k ^ 1, places), chunk) for k, chunk in zip(chips, arrived)]
    waiting = lax.optimization_barrier((*(chunk for _, chunk in beside_me), done[0]))
    listed += [(units, swapped(chunk[-1:], 1)) for (units, _), chunk in zip(beside_me, waiting)]
    out = remap(listed, marks)
    return jnp.transpose(out, (2, 0, 1, 3))


def solution(mesh):
    in_specs = (
        P(None, "lev", ("groups", "lat"), None),
        P("lev", ("groups", "lat"), None),
        P("lev", ("groups", "lat"), None),
        P(),
        P(None, ("groups", "lat"), "lev"),
        P(None, None, ("groups", "lat"), "lev"),
    )
    out_specs = P(None, None, ("groups", "lat"), "lev")
    return jax.shard_map(shards, mesh=mesh, in_specs=in_specs, out_specs=out_specs, check_vma=False)
```

```python
import functools

import jax
import jax.numpy as jnp
from jax import lax
from jax.experimental import pallas as pl
from jax.experimental.layout import Layout, with_layout_constraint
from jax.experimental.pallas import tpu as pltpu
from jax.sharding import PartitionSpec as P

SUBSTEPS = 2
TAPS = 4
REACH = 3
HALO = REACH * SUBSTEPS
BLOCK = 6
LANES = 128
SUB = 8


def spread(row):
    return jnp.broadcast_to(row, (SUB, LANES))


def lane_ids():
    return lax.broadcasted_iota(jnp.int32, (SUB, LANES), 1)


def from_west(tiles, steps, lane):
    turned = [pltpu.roll(t, steps, 1) for t in tiles]
    return [jnp.where(lane < steps, turned[j - 1], turned[j]) for j in range(len(tiles))]


def from_east(tiles, lane):
    turned = [pltpu.roll(t, LANES - 1, 1) for t in tiles]
    count = len(tiles)
    return [jnp.where(lane == LANES - 1, turned[(j + 1) % count], turned[j]) for j in range(count)]


def coefficients(wind):
    size = jnp.abs(wind)
    rest = 1.0 - size
    alpha = wind * rest * rest * (1.0 / 12.0)
    beta = wind * size * rest * (-1.0 / 12.0)
    gamma = wind * size * (3.0 - 2.0 * size)
    return alpha, beta, gamma


def packed_sizes(nlon, count):
    width = nlon // count
    mains, tail = width // LANES, width % LANES
    return width, mains, tail, LANES // tail if tail else 1


def packed_tiles(units, mains, tail, per):
    return units * BLOCK * mains + (-(-units * BLOCK // per) if tail else 0)


def fill_halos(rows, slot, state, winds, first_round, second_round):
    band, bands = lax.axis_index("lat"), lax.axis_size("lat")
    even = band % 2 == 0
    keep = jnp.where((band == 0) | (band == bands - 1), 0.0, 1.0)
    for target, north, scale in ((first_round, even, None), (second_round, jnp.logical_not(even), keep)):
        scaled = (lambda v: v) if scale is None else (lambda v: v * scale)
        row_t = jnp.where(north, rows - HALO, 0)
        row_x = jnp.where(north, rows - REACH, 0)
        row_y = jnp.where(north, rows - REACH - 1, 0)
        for row in range(HALO):
            target[row] = scaled(state[slot, row_t + row])
        for q in range(REACH):
            target[HALO, q:q + 1, :] = scaled(winds[row_x + q, slot:slot + 1, :])
        for q in range(REACH + 1):
            target[HALO, REACH + q:REACH + q + 1, :] = scaled(winds[rows + row_y + q, slot:slot + 1, :])


def prep_kernel(rows, tracers, winds, state, *halos):
    levels, nlon = state.shape[0], state.shape[3]
    nj = nlon // LANES
    row_stride = nj * levels
    tracer_stride = rows * row_stride

    def body(row, _):
        for level in range(levels):
            for j in range(nj):
                start = row * row_stride + j * levels + level
                state[level, row, :, tile(j)] = tracers[pl.ds(start, SUB, stride=tracer_stride), :]
        return 0

    lax.fori_loop(0, rows, body, 0)
    for slot in range(levels):
        fill_halos(rows, slot, state, winds, *halos[2 * slot:2 * slot + 2])


def lat_pass(levels, nj, ranges, cell, coef, store):
    group = 3 if nj % 3 == 0 else 1

    def body(level, _):
        for start in range(0, nj, group):
            results = []
            for j in range(start, start + group):
                results += [(level, row, tile(j), value) for row, value in one(level, tile(j))]
            for result in results:
                store(*result)
        return 0

    def one(level, lanes):
        results = []
        for first, last in ranges:
            a = {r: cell(level, r, lanes) for r in range(first - REACH, last + REACH)}
            inter = {f: 7.0 * (a[f - 1] + a[f]) - (a[f - 2] + a[f + 1]) for f in range(first - 1, last + 2)}
            flux = {}
            for f in range(first, last + 1):
                alpha, beta, gamma = [spread(coef(i, level, f, lanes)) for i in range(3)]
                north = gamma > 0
                behind = jnp.where(north, inter[f - 1], inter[f + 1])
                upwind = jnp.where(north, a[f - 1], a[f])
                flux[f] = alpha * inter[f] + beta * behind + gamma * upwind
                if f > first:
                    results.append((f - 1, a[f - 1] - (flux[f] - flux[f - 1])))
        return results

    lax.fori_loop(0, levels, body, 0)


def tile(j):
    return slice(j * LANES, (j + 1) * LANES)


def lon_pass(work, swept, coef, inter, west, flux, lane, finish):
    nj = swept.shape[3] // LANES
    each = range(nj)

    def interfaces(n):
        level, _, at = work[n]
        b = [swept[level, at, :, tile(j)] for j in each]
        w1, w2, e1 = from_west(b, 1, lane), from_west(b, 2, lane), from_east(b, lane)
        for j in each:
            inter[n, :, tile(j)] = 7.0 * (w1[j] + b[j]) - (w2[j] + e1[j])
            west[n, :, tile(j)] = w1[j]

    def fluxes(n):
        level, row, at = work[n]
        mid = [inter[n, :, tile(j)] for j in each]
        w1, e1 = from_west(mid, 1, lane), from_east(mid, lane)
        for j in each:
            alpha, beta, gamma = [spread(coef(i, level, row, tile(j))) for i in range(3)]
            right = gamma > 0
            behind = jnp.where(right, w1[j], e1[j])
            upwind = jnp.where(right, west[n, :, tile(j)], swept[level, at, :, tile(j)])
            flux[n, :, tile(j)] = alpha * mid[j] + beta * behind + gamma * upwind

    def update(n):
        level, _, at = work[n]
        here = [flux[n, :, tile(j)] for j in each]
        e1 = from_east(here, lane)
        return [swept[level, at, :, tile(j)] - (e1[j] - here[j]) for j in each]

    for n in range(len(work)):
        interfaces(n)
    for n in range(len(work)):
        fluxes(n)
    for g in range(len(work) // BLOCK):
        finish(g, [update(g * BLOCK + q) for q in range(BLOCK)])


def pack_block(block, packed, unit, units, count, lane):
    nlon = len(block[0]) * LANES
    width, mains, tail, per = packed_sizes(nlon, count)
    for d in range(count):
        j0, off = (d * width) // LANES, (d * width) % LANES
        for q, tiles in enumerate(block):
            turned = [pltpu.roll(tiles[j0 + m], LANES - off, 1) if off else tiles[j0 + m]
                      for m in range(mains + (1 if off else 0))]
            for m in range(mains):
                whole = jnp.where(lane < LANES - off, turned[m], turned[m + 1]) if off else turned[m]
                packed[d, (unit * BLOCK + q) * mains + m] = whole
        if tail:
            totals = {}
            for q, tiles in enumerate(block):
                at, place = divmod(unit * BLOCK + q, per)
                at += units * BLOCK * mains
                shift = (place * tail - off) % LANES
                moved = pltpu.roll(tiles[j0 + mains], shift, 1) if shift else tiles[j0 + mains]
                if place:
                    before = totals[at] if at in totals else packed[d, at]
                    moved = jnp.where(lane < place * tail, before, moved)
                totals[at] = moved
            for at, total in totals.items():
                packed[d, at] = total


def unpack_unit(chunk, place, unit, units, target, lead, mains, tail, per, lane):
    copy_tiles([((chunk, (place, unit * BLOCK * mains + i)), (target, lead + (i,))) for i in range(BLOCK * mains)])
    totals = {}
    for q in range(BLOCK if tail else 0):
        at, there = divmod(unit * BLOCK + q, per)
        to, here = divmod(q, per)
        shift = (here - there) * tail % LANES
        if to in totals and totals[to][1:] == (at, shift):
            continue
        source = chunk[place, units * BLOCK * mains + at]
        moved = pltpu.roll(source, shift, 1) if shift else source
        totals[to] = (jnp.where(lane < here * tail, totals[to][0], moved) if to in totals else moved, at, shift)
    for to, (total, _, _) in totals.items():
        target[lead + (BLOCK * mains + to,)] = total


def copy_tiles(pairs):
    values = [source[at] for (source, at), _ in pairs]
    for value, (_, (target, at)) in zip(values, pairs):
        target[at] = value


def hand_out(packed, outs, groups):
    me = lax.axis_index("lev")
    for group, out in zip(groups, outs):
        for place, k in enumerate(group):
            copy_tiles([((packed, (me ^ k, i)), (out, (place, i))) for i in range(packed.shape[1])])


def own_coefficients(rows, joined, winds, cx, cy):
    levels, held, nlon = cx.shape[1:]
    keep = jnp.where(lax.axis_index("lat") == 0, 0.0, 1.0)
    for level in range(levels):
        for way in range(2):
            for row in range(rows):
                winds[way, level, row:row + 1, :] = joined[way * rows + row, level:level + 1, :]
        winds[1, level, 0:1, :] = winds[1, level, 0:1, :] * keep
        for way, target in enumerate((cx, cy)):
            for j in range(nlon // LANES):
                parts = coefficients(winds[way, level, :, tile(j)])
                for p in range(3):
                    target[p, level, :, tile(j)] = parts[p]


def put_rows(target, level, at, rows):
    for q, row in enumerate(rows):
        for j, part in enumerate(row):
            target[level, at + q, :, tile(j)] = part


def interior_kernel(count, rows, groups, state, joined, *refs):
    outs, (first, cx, cy, packed, winds, swept, inter, west, flux) = refs[:len(groups)], refs[len(groups):]
    levels, nlon = state.shape[0], state.shape[3]
    nj = nlon // LANES
    lane = lane_ids()
    own_coefficients(rows, joined, winds, cx, cy)
    coef_x = lambda i, level, r, lanes: cx[i, level, r:r + 1, lanes]
    coef_y = lambda i, level, f, lanes: cy[i, level, f:f + 1, lanes]

    def put(level, row, lanes, value):
        swept[level, row - REACH, :, lanes] = value

    lat_pass(levels, nj, [(REACH, rows - REACH)], lambda level, r, lanes: state[level, r, :, lanes], coef_y, put)
    work = [(level, row, row - REACH) for level in range(levels) for row in range(REACH, rows - REACH)]

    def keep_first(group, done):
        level, _, at = work[group * BLOCK]
        put_rows(first, level, at, done)

    lon_pass(work, swept, coef_x, inter, west, flux, lane, keep_first)
    lat_pass(levels, nj, [(HALO, rows - HALO)], lambda level, r, lanes: first[level, r - REACH, :, lanes], coef_y, put)
    work_last = [(level, row, row - REACH) for level in range(levels) for row in range(HALO, rows - HALO)]

    def send(group, done):
        pack_block(done, packed, group, len(work_last) // BLOCK, count, lane)

    lon_pass(work_last, swept, coef_x, inter, west, flux, lane, send)
    hand_out(packed, outs, groups)


def edge_kernel(count, rows, groups, slot, state, first_round, second_round, first, cx, cy, *refs):
    outs, (packed, beyond, swept, edge, inter, west, flux) = refs[-7 - len(groups):-7], refs[-7:]
    nlon = state.shape[3]
    nj = nlon // LANES
    lane = lane_ids()
    odd = lax.axis_index("lat") % 2 == 1

    def halo(south, *at):
        one, two = first_round[at], second_round[at]
        return jnp.where(odd, one, two) if south else jnp.where(odd, two, one)

    for end, south in enumerate((True, False)):
        for j in range(nj):
            parts = coefficients(halo(south, HALO, slice(None), tile(j)))
            for p in range(3):
                beyond[p, end, :, tile(j)] = parts[p]

    def coef_x(i, _, r, lanes):
        if 0 <= r < rows:
            return cx[i, slot, r:r + 1, lanes]
        end, at = (0, r + REACH) if r < 0 else (1, r - rows)
        return beyond[i, end, at:at + 1, lanes]

    def coef_y(i, _, f, lanes):
        if 0 <= f < rows:
            return cy[i, slot, f:f + 1, lanes]
        end, at = (0, f + 2 * REACH + 1) if f < 0 else (1, f - rows + REACH)
        return beyond[i, end, at:at + 1, lanes]

    def cell(_, r, lanes):
        if 0 <= r < rows:
            return state[slot, r, :, lanes]
        return halo(r < 0, r + HALO if r < 0 else r - rows, slice(None), lanes)

    ends = [(-REACH, REACH), (rows - REACH, rows + REACH)]
    ends_last = [(0, HALO), (rows - HALO, rows)]

    def place(row, ranges):
        (a, b), (c, _) = ranges
        return row - a if row < b else row - c + BLOCK

    def cell_first(_, r, lanes):
        if REACH <= r < rows - REACH:
            return first[slot, r - REACH, :, lanes]
        return edge[0, place(r, ends), :, lanes]

    def put(_, row, lanes, value):
        swept[0, place(row, ends), :, lanes] = value

    def put_last(_, row, lanes, value):
        swept[0, place(row, ends_last), :, lanes] = value

    def listed(ranges):
        return [(0, row, place(row, ranges)) for a, b in ranges for row in range(a, b)]

    def keep_edge(group, done):
        put_rows(edge, 0, group * BLOCK, done)

    def send(group, done):
        pack_block(done, packed, group, len(ends_last), count, lane)

    lat_pass(1, nj, ends, cell, coef_y, put)
    lon_pass(listed(ends), swept, coef_x, inter, west, flux, lane, keep_edge)
    lat_pass(1, nj, ends_last, cell_first, coef_y, put_last)
    lon_pass(listed(ends_last), swept, coef_x, inter, west, flux, lane, send)
    hand_out(packed, outs, groups)


def weights_kernel(weights, source, out):
    targets, rows, taps, width = weights.shape

    for row in range(rows):
        for k in range(targets):
            lowest, highest = max(k - (TAPS - 1), 0), min(k, targets - TAPS)
            w = weights[k, row]
            w = jnp.concatenate([w, jnp.zeros((SUB - taps, width), jnp.float32)], axis=0)
            at = jnp.broadcast_to(source[k, row:row + 1, :], (SUB, width))
            total = w
            for g in range(lowest + 1, highest + 1):
                total = jnp.where(at == g, pltpu.roll(w, g - lowest, 0), total)
            out[k, row] = total


def remap_kernel(count, plan, numbers, counts, *refs):
    chunks, weights, (out, levels, result, sems) = refs[:len(plan)], refs[len(plan)], refs[-4:]
    me = lax.axis_index("lev")
    targets, _, _, width = result.shape
    _, mains, tail, per = packed_sizes(width * count, count)
    lane = lane_ids()
    copies = []

    def leave(source, target):
        copy = pltpu.make_async_copy(source, target, sems.at[len(copies)])
        copy.start()
        copies.append(copy)

    def level_of(k, slot):
        d = me ^ k
        start = jnp.int32(0)
        for e in range(count):
            start = start + jnp.where(e < d, counts[e], 0)
        return jnp.where(slot < counts[d], start + slot, targets)

    for units, chunk in zip(plan, chunks):
        for unit, (k, slot, number) in enumerate(units):
            lead = (level_of(k, slot), numbers.index(number))
            unpack_unit(chunk, 0, unit, len(units), levels, lead, mains, tail, per, lane)

    for at, number in enumerate(numbers):
        for q in range(BLOCK):
            row = number * BLOCK + q
            for m in range(mains + (1 if tail else 0)):
                wide = LANES if m < mains else tail
                lanes = slice(m * LANES, m * LANES + wide)
                values = []
                for level in range(targets):
                    if m < mains:
                        values.append(levels[level, at, q * mains + m])
                    else:
                        last = levels[level, at, BLOCK * mains + q // per]
                        shift = (q % per) * tail
                        values.append(pltpu.roll(last, LANES - shift, 1) if shift else last)
                for k in range(targets):
                    lowest, highest = max(k - (TAPS - 1), 0), min(k, targets - TAPS) + TAPS - 1
                    total = None
                    for level in range(lowest, highest + 1):
                        j = level - lowest
                        term = jnp.broadcast_to(weights[k, row, j:j + 1, lanes], (SUB, wide)) * values[level][:, :wide]
                        total = term if total is None else total + term
                    result[k, at * BLOCK + q, :, lanes] = total
            leave(result.at[:, pl.ds(at * BLOCK + q, 1)], out.at[:, pl.ds(row, 1)])
    for copy in copies:
        copy.wait()


def mark_kernel(*refs):
    refs[-1][...] = jnp.zeros((SUB, LANES), jnp.float32)


def tiles_of(array):
    lead, levels, nlon = array.shape[:-2], array.shape[-2], array.shape[-1]
    split = array.reshape(lead + (levels, nlon // LANES, LANES))
    order = tuple(range(len(lead))) + (len(lead) + 1, len(lead), len(lead) + 2)
    split = with_layout_constraint(split, Layout(major_to_minor=order))
    return jnp.swapaxes(split, -3, -2).reshape(-1, LANES)


VMEM = pl.BlockSpec(memory_space=pltpu.VMEM)
ANY = pl.BlockSpec(memory_space=pl.ANY)
SMEM = pl.BlockSpec(memory_space=pltpu.SMEM)


def call(kernel, outs, args, specs=None, scratch=(), cost=None):
    return pl.pallas_call(
        kernel,
        out_shape=outs,
        in_specs=specs or [VMEM] * len(args),
        out_specs=jax.tree.map(lambda _: VMEM, outs),
        scratch_shapes=list(scratch),
        compiler_params=pltpu.CompilerParams(vmem_limit_bytes=16 << 20),
        cost_estimate=cost,
    )(*args)


def cost(flops, size):
    return pl.CostEstimate(flops=int(flops), bytes_accessed=int(size), transcendentals=0)


def f32(*shape):
    return jax.ShapeDtypeStruct(shape, jnp.float32)


def shards(tracers, wind_x, wind_y, level_counts, source_level, remap_weight):
    count = lax.axis_size("lev")
    bands = lax.axis_size("lat")
    number, depth, rows, nlon = tracers.shape
    targets, _, width = source_level.shape
    mains, tail, per = packed_sizes(nlon, count)[1:]
    blocks = rows // BLOCK
    inner = (rows - 2 * HALO) // BLOCK

    raw = tiles_of(jnp.transpose(tracers, (0, 2, 1, 3)))
    joined = jnp.concatenate([jnp.transpose(wind_x, (1, 0, 2)), jnp.transpose(wind_y, (1, 0, 2))], axis=0)
    halo = f32(HALO + 1, number, nlon)
    state, *sent = call(
        functools.partial(prep_kernel, rows),
        [f32(depth, rows, number, nlon)] + [halo] * (2 * depth), (raw, joined),
        cost=cost(1, 1))
    second = {i: ((i - 1) ^ 1) + 1 for i in range(1, bands - 1)}
    second_pairs = [(i * count + d, second[i] * count + d if i in second else i * count + (d ^ 1))
                    for i in range(bands) for d in range(count)]

    def beside(sent):
        return [lax.ppermute(sent[0], "lat", [(i, i ^ 1) for i in range(bands)]),
                lax.ppermute(sent[1], ("lat", "lev"), second_pairs)]

    rounds = [beside(sent[2 * slot:2 * slot + 2]) for slot in range(depth)]
    taps = call(
        weights_kernel, f32(targets, rows, SUB, width),
        (jnp.transpose(remap_weight, (1, 2, 0, 3)), source_level),
        cost=cost(1, 1))

    def box(places, units):
        return places, packed_tiles(units, mains, tail, per), SUB, LANES

    def vmem(*shape):
        return pltpu.VMEM(shape, jnp.float32)

    held = -(-rows // SUB) * SUB
    coef = f32(3, depth, held, nlon)
    swept = vmem(depth, rows - 2 * REACH, number, nlon)
    stage = vmem(depth * (rows - 2 * REACH), number, nlon)
    chips = tuple(range(2, count, 2))
    groups = ((0,), (1,)) + tuple((k, k ^ 1) for k in chips)
    inner_units = depth * inner
    result = call(
        functools.partial(interior_kernel, count, rows, groups),
        [f32(*box(len(group), inner_units)) for group in groups]
        + [f32(depth, rows - 2 * REACH, number, nlon), coef, coef],
        (state, joined), scratch=[vmem(*box(count, inner_units)), vmem(2, depth, held, nlon), swept, stage, stage, stage],
        cost=cost(1, 1))
    middle, (first, cx, cy) = result[:len(groups)], result[len(groups):]
    swept = vmem(1, 2 * HALO, number, nlon)
    stage = vmem(2 * HALO, number, nlon)

    def edge(slot, groups, after):
        args = (state, *rounds[slot], first, cx, cy, *after)
        return call(
            functools.partial(edge_kernel, count, rows, groups, slot),
            [f32(*box(len(group), 2)) for group in groups], args,
            specs=[VMEM] * (len(args) - len(after)) + [ANY] * len(after),
            scratch=[vmem(*box(count, 2)), vmem(3, 2, SUB, nlon), swept, swept, stage, stage, stage],
            cost=cost(60 * tracers.size, 8 * tracers.size))

    def swapped(sent, k):
        return lax.ppermute(sent, "lev", [(i, i ^ k) for i in range(count)])

    def units_of(k, places):
        return tuple((k, slot, block) for slot, block in places)

    def remap(listed, after):
        args = (level_counts, *(chunk for _, chunk in listed), taps, *after)
        return pl.pallas_call(
            functools.partial(remap_kernel, count, tuple(units for units, _ in listed), tuple(range(blocks))),
            out_shape=f32(targets, rows, number, width),
            in_specs=[SMEM] + [VMEM] * (len(args) - 1 - len(after)) + [ANY] * len(after),
            out_specs=ANY,
            scratch_shapes=[
                vmem(targets + 1, blocks, packed_tiles(1, mains, tail, per), SUB, LANES),
                vmem(targets, rows, number, width),
                pltpu.SemaphoreType.DMA((rows,)),
            ],
            compiler_params=pltpu.CompilerParams(vmem_limit_bytes=16 << 20),
            cost_estimate=cost(1, 1),
        )(*args)

    def mark(chunks):
        return pl.pallas_call(
            mark_kernel, out_shape=f32(SUB, LANES), in_specs=[ANY] * len(chunks), out_specs=VMEM, cost_estimate=cost(1, 1),
            compiler_params=pltpu.CompilerParams(vmem_limit_bytes=1 << 20),
        )(*chunks)

    places = tuple((slot, 1 + b) for slot in range(depth) for b in range(inner))
    arrived = [swapped(chunk, k) for k, chunk in zip(chips, middle[2:])]
    listed = [(units_of(k, places), chunk) for k, chunk in zip(chips, arrived)]
    listed.append((units_of(0, places), middle[0]))
    beside_me = [(units_of(1, places), middle[1])]
    after, marks = (taps,), []
    for slot in range(depth):
        own = ((slot, 0), (slot, blocks - 1))
        done = edge(slot, tuple((k,) for k in range(count)), after)
        crossing = [(units_of(k, own), swapped(done[k], k)) for k in range(count - 1, 1, -1)]
        listed += crossing + [(units_of(0, own), done[0])]
        beside_me.append((units_of(1, own), done[1]))
        marks.append(mark([chunk for _, chunk in crossing]))
        after = (done[0],)
    beside_me += [(units_of(k ^ 1, places), chunk) for k, chunk in zip(chips, arrived)]
    waiting = lax.optimization_barrier((*(chunk for _, chunk in beside_me), done[0]))
    listed += [(units, swapped(chunk[-1:], 1)) for (units, _), chunk in zip(beside_me, waiting)]
    out = remap(listed, marks)
    return jnp.transpose(out, (2, 0, 1, 3))


def solution(mesh):
    in_specs = (
        P(None, "lev", ("groups", "lat"), None),
        P("lev", ("groups", "lat"), None),
        P("lev", ("groups", "lat"), None),
        P(),
        P(None, ("groups", "lat"), "lev"),
        P(None, None, ("groups", "lat"), "lev"),
    )
    out_specs = P(None, None, ("groups", "lat"), "lev")
    return jax.shard_map(shards, mesh=mesh, in_specs=in_specs, out_specs=out_specs, check_vma=False)
```
